32 devices in a mesh: seq: 16 (over z, y, x), head: 2 (over core).
Axes of the slice: x: 2, y: 2, z: 4, core: 2. Of those that a mesh axis runs over, the one named last changes fastest.
Arguments:
- queries: bfloat16 [16384, 1024], P('seq', 'head'), may hold values from -8 to 8
- key_rows: bfloat16 [16384, 1024], P('seq', 'head'), may hold values from -8 to 8
- value_rows: bfloat16 [16384, 1024], P('seq', 'head'), may hold values from -6 to 6
- out_weight: bfloat16 [1024, 1024], P('head'), may hold values from -0.1875 to 0.1875
- cotangent: bfloat16 [16384, 1024], P('seq'), may hold values from -6 to 6
Outputs:
- mixed: bfloat16 [16384, 1024], P('seq', 'head')
- query_grad: bfloat16 [16384, 1024], P('seq', 'head')
- key_grad: bfloat16 [16384, 1024], P('seq', 'head')
- value_grad: bfloat16 [16384, 1024], P('seq', 'head')
- weight_grad: float32 [1024, 1024], P('head')
The draws below stay inside these ranges and needn't reach their ends.
All inputs are finite; a program needn't handle non-finite values.
Results may differ from the reference program's by a relative error of at most 0.02.
Values may be sent and summed in bfloat16 or wider, within the bound.
No kernel may reach another device: no remote copies, remote signals or barrier semaphores. Data moves between devices by JAX's collectives and lax.ppermute only.
A program may use at most 256 MiB of HBM per device.

```python
import jax
import jax.numpy as jnp
from jax import lax

HEADS = 16
DH = 64
D = 1024
LANDMARKS = 256
ITERS = 2
TOKENS = 16384
SEGMENT = 64


def segment_means(key):
    means = jax.random.normal(key, (LANDMARKS, D), jnp.float32) * 0.9
    return jnp.broadcast_to(means[:, None, :], (LANDMARKS, SEGMENT, D)).reshape(TOKENS, D)


def draw_queries(key, part):
    means = segment_means(key)
    key = jax.random.fold_in(key, 11)
    values = means + jax.random.normal(key, (TOKENS, D), jnp.float32)
    return jnp.clip(values, -8.0, 8.0).astype(jnp.bfloat16)


def draw_key_rows(key, part):
    means = segment_means(key)
    key = jax.random.fold_in(key, 13)
    values = means + jax.random.normal(key, (TOKENS, D), jnp.float32)
    return jnp.clip(values, -8.0, 8.0).astype(jnp.bfloat16)


def level_of(rng, dims, pieces, low, high):
    def one(dim, blocks):
        draws = jax.random.uniform(jax.random.fold_in(jax.random.fold_in(rng, 6), dim), (blocks,), jnp.float32, low / len(pieces), high / len(pieces))
        return jnp.repeat(jnp.exp(draws), dims[dim] // blocks).reshape((-1,) + (1,) * (len(dims) - dim - 1))

    loudness = one(*pieces[0])
    for cut in pieces[1:]:
        loudness = loudness * one(*cut)
    return loudness


def gaussian(rng, shape, spread, bound, cuts=(), kind=jnp.bfloat16):
    drawn = spread * jax.random.normal(rng, shape, jnp.float32)
    if cuts:
        drawn = drawn * level_of(rng, shape, cuts, -0.22, 0.18)
    return jnp.clip(drawn, -bound, bound).astype(kind)


def setup_inputs(seed: int = 0) -> dict:
    splits = jax.random.split(jax.random.key(seed), 6)
    return {
        "queries": draw_queries(jax.random.fold_in(splits[5], 71), 0),
        "key_rows": draw_key_rows(jax.random.fold_in(splits[5], 71), 0),
        "value_rows": gaussian(splits[2], (TOKENS, D), 1.0, 6.0, ((0, 16), (1, 2))),
        "out_weight": gaussian(splits[3], (D, D), D ** -0.5, 0.1875, ((0, 2),)),
        "cotangent": gaussian(splits[4], (TOKENS, D), 1.0, 6.0, ((0, 16),)),
    }


softmax_scale_factor = 0.125

def product_high(left, right):
    return jnp.dot(left, right, precision=lax.Precision.HIGHEST)

def pseudo_inverse(amat):
    column_top = lax.stop_gradient(jnp.max(lax.optimization_barrier(jnp.sum(amat, axis=0))))
    current = amat.T / column_top
    ident = jnp.eye(amat.shape[0], dtype=amat.dtype)
    for iteration in range(ITERS):
        apply_z = product_high(amat, current)
        inner = 7.0 * ident - apply_z
        inner = 15.0 * ident - product_high(apply_z, inner)
        inner = 13.0 * ident - product_high(apply_z, inner)
        current = 0.25 * product_high(current, inner)
    return current

def one_head(query_h, key_h, value_h, grad_h):
    float_single = jnp.float32
    bf16 = jnp.bfloat16
    landmark_queries = lax.optimization_barrier(jnp.mean(query_h.astype(float_single).reshape(LANDMARKS, SEGMENT, DH), axis=1)).astype(bf16)
    landmark_keys = lax.optimization_barrier(jnp.mean(key_h.astype(float_single).reshape(LANDMARKS, SEGMENT, DH), axis=1)).astype(bf16)
    kernel_f = jax.nn.softmax(jnp.dot(query_h, landmark_keys.T, preferred_element_type=float_single) * softmax_scale_factor, axis=1)
    kernel_fb = kernel_f.astype(bf16)
    scores_b = jnp.dot(landmark_queries, key_h.T, preferred_element_type=float_single) * softmax_scale_factor
    weights_p = jnp.exp(scores_b - lax.optimization_barrier(jnp.max(scores_b, axis=1, keepdims=True)))
    totals = lax.optimization_barrier(jnp.sum(weights_p, axis=1, keepdims=True))
    weights_pb = weights_p.astype(bf16)
    landmark_value_rows = jnp.dot(weights_pb, value_h, preferred_element_type=float_single) / totals
    kernel_a = jax.nn.softmax(jnp.dot(landmark_queries, landmark_keys.T, preferred_element_type=float_single) * softmax_scale_factor, axis=1)
    approximate_inverse, pull_back = jax.vjp(pseudo_inverse, kernel_a)
    mixing_matrix = product_high(approximate_inverse, landmark_value_rows)
    mixer_b = mixing_matrix.astype(bf16)
    attn_h = jnp.dot(kernel_fb, mixer_b, preferred_element_type=float_single).astype(bf16)
    mixing_matrix_gradient = jnp.dot(kernel_fb.T, grad_h, preferred_element_type=float_single)
    grad_f = jnp.dot(grad_h, mixer_b.T, preferred_element_type=float_single)
    grad_sf = (kernel_f * (grad_f - lax.optimization_barrier(jnp.sum(kernel_f * grad_f, axis=1, keepdims=True)))).astype(bf16)
    query_f = jnp.dot(grad_sf, landmark_keys, preferred_element_type=float_single) * softmax_scale_factor
    land_k_f = jnp.dot(grad_sf.T, query_h, preferred_element_type=float_single) * softmax_scale_factor
    inverse_matrix_gradient = product_high(mixing_matrix_gradient, landmark_value_rows.T)
    landmark_value_gradient = product_high(approximate_inverse.T, mixing_matrix_gradient)
    grad_a = pull_back(inverse_matrix_gradient)[0]
    query_kernel_gradient = kernel_a * (grad_a - lax.optimization_barrier(jnp.sum(kernel_a * grad_a, axis=1, keepdims=True)))
    landmark_query_kernel = product_high(query_kernel_gradient, landmark_keys.astype(float_single)) * softmax_scale_factor
    landmark_key_kernel = product_high(query_kernel_gradient.T, landmark_queries.astype(float_single)) * softmax_scale_factor
    grad_norm = landmark_value_gradient / totals
    grad_norm_b = grad_norm.astype(bf16)
    center = lax.optimization_barrier(jnp.sum(grad_norm * landmark_value_rows, axis=1, keepdims=True))
    grad_sb = (weights_p * (jnp.dot(grad_norm_b, value_h.T, preferred_element_type=float_single) - center)).astype(bf16)
    land_q_b = jnp.dot(grad_sb, key_h, preferred_element_type=float_single) * softmax_scale_factor
    key_b = jnp.dot(grad_sb.T, landmark_queries, preferred_element_type=float_single) * softmax_scale_factor
    value_out = jnp.dot(weights_pb.T, grad_norm_b, preferred_element_type=float_single).astype(bf16)
    land_q_all = land_q_b + landmark_query_kernel
    land_k_all = land_k_f + landmark_key_kernel
    query_out = (query_f + jnp.repeat(land_q_all / SEGMENT, SEGMENT, axis=0)).astype(bf16)
    key_out = (key_b + jnp.repeat(land_k_all / SEGMENT, SEGMENT, axis=0)).astype(bf16)
    return (attn_h, query_out, key_out, value_out)

def reference(queries, key_rows, value_rows, out_weight, cotangent):
    grad_attn = jnp.dot(cotangent, out_weight.T, preferred_element_type=jnp.float32).astype(jnp.bfloat16)

    def split_heads(array):
        return array.reshape(TOKENS, HEADS, DH).transpose(1, 0, 2)

    def join_heads(array):
        return array.transpose(1, 0, 2).reshape(TOKENS, D)
    attn, query_grad, key_grad, value_grad = lax.map(lambda items: one_head(items[0], items[1], items[2], items[3]), (split_heads(queries), split_heads(key_rows), split_heads(value_rows), split_heads(grad_attn)))
    attn = join_heads(attn)
    mixed = jnp.dot(attn, out_weight, preferred_element_type=jnp.float32).astype(jnp.bfloat16)
    weight_grad = jnp.dot(attn.T, cotangent, preferred_element_type=jnp.float32)
    return (mixed, join_heads(query_grad), join_heads(key_grad), join_heads(value_grad), weight_grad)
```

```python
import functools

import jax
import jax.numpy as jnp
from jax import lax
from jax.experimental import pallas as pl
from jax.experimental.pallas import tpu as pltpu
from jax.sharding import PartitionSpec as P

DH = 64
PAIR = 2 * DH
LANDMARKS = 256
ITERS = 2
SCALE = 0.125
CHUNK = 128
EXTRA = 16
F32 = jnp.float32
BF16 = jnp.bfloat16
PARAMS = pltpu.CompilerParams(vmem_limit_bytes=24 * 1024 * 1024)


def dot(left, right, dims=((1,), (0,))):
    return lax.dot_general(left, right, (dims, ((), ())), preferred_element_type=F32)


NT = ((1,), (1,))
TN = ((0,), (0,))


def halves(value):
    high = value.astype(BF16)
    return high, (value - high.astype(F32)).astype(BF16)


def dot_exact(left, right, dims=((1,), (0,))):
    return dot(left[0], right[0], dims) + (
        dot(left[0], right[1], dims) + dot(left[1], right[0], dims)
    )


def turned(pair):
    return pair[0].T, pair[1].T


def keep_rows(block, which):
    rows = lax.broadcasted_iota(jnp.int32, block.shape, 0) // DH
    return jnp.where(rows == which, block, jnp.zeros_like(block))


def keep_lanes(block, which):
    lanes = lax.broadcasted_iota(jnp.int32, block.shape, 1) // DH
    return jnp.where(lanes == which, block, jnp.zeros_like(block))


def fold(block, op):
    parts = block.reshape(block.shape[0] // 8, 8, block.shape[1])
    return op(parts, axis=0)


def exchange(block, mask, n):
    return lax.ppermute(block, "seq", [(i, i ^ mask) for i in range(n)])


def bit_groups(n):
    bits = n.bit_length() - 1
    groups = []
    while bits > 0:
        take = 2 if bits % 2 == 0 else 1
        bits -= take
        groups.append((bits, 1 << take))
    return groups


def gather_lists(block, n):
    got = [block]
    held = block[None]
    for shift, size in bit_groups(n):
        if len(got) > 1:
            held = jnp.stack(got, axis=1).reshape((-1,) + block.shape)
        got = [held] + [exchange(held, m << shift, n) for m in range(1, size)]
    return got


def gather_ordered(block, n, me):
    got = gather_lists(block, n)
    held = jnp.stack(got, axis=1).reshape((n,) + block.shape)
    return held.at[jnp.arange(n) ^ me].get(mode="promise_in_bounds")


def split_by_partner(blocks, n, me):
    size = bit_groups(n)[-1][1]
    return [
        blocks.at[(jnp.arange(n // size) * size + m) ^ me].get(mode="promise_in_bounds")
        for m in range(size)
    ]


def scatter_step(pieces, shift, size, n):
    got = [pieces[0]] + [exchange(pieces[m], m << shift, n) for m in range(1, size)]
    return sum(part.astype(F32) for part in got)


def scatter_pieces(pieces, n, groups):
    for step, (shift, size) in enumerate(groups):
        held = scatter_step(pieces, shift, size, n)
        if step + 1 < len(groups):
            following = groups[step + 1][1]
            held = held.astype(BF16).reshape((-1, following) + held.shape[1:])
            pieces = [held[:, m] for m in range(following)]
    return held


def means_kernel(seg_len, q_ref, k_ref, out_ref, in_ref, sum_ref, sems):
    rows, columns = q_ref.shape
    steps = sems.shape[1]
    height = rows // steps
    copies = {}
    for c in range(steps):
        part = pl.ds(c * height, height)
        for side, ref in enumerate((q_ref, k_ref)):
            copies[side, c] = pltpu.make_async_copy(ref.at[part], in_ref.at[side, part], sems.at[side, c])
            copies[side, c].start()
    for c in range(steps):
        for side in range(2):
            copies[side, c].wait()
            span = slice(side * columns, (side + 1) * columns)
            for s in range(c * height // seg_len, (c + 1) * height // seg_len):
                total = fold(in_ref[side, s * seg_len : (s + 1) * seg_len, :].astype(F32), jnp.sum)
                sum_ref[s : s + 1, span] = jnp.sum(total, axis=0, keepdims=True)
    out_ref[...] = (sum_ref[...] * (1.0 / seg_len)).astype(BF16)


def forward_kernel(n, heads, count, me_ref, q_ref, k_ref, v_ref, g_ref, *refs):
    size = bit_groups(n)[-1][1]
    in_refs = refs[:count]
    fb_ref, pb_ref, top_ref, land_ref = refs[count : count + 4]
    out_refs = refs[count + 4 : count + 4 + size]
    score_ref, message_ref = refs[count + 4 + size :]
    pair = pl.program_id(0)
    columns = land_ref.shape[1] // 2

    @pl.when(pair == 0)
    def _():
        for m in range(count):
            held, height, _ = in_refs[m].shape
            for t in range(held):
                at = pl.multiple_of(((t * count + m) ^ me_ref[1]) * height, height)
                land_ref[pl.ds(at, height), :] = in_refs[m][t]

    here = pl.multiple_of(pair * PAIR, PAIR)
    lq_pair = land_ref[:, pl.ds(here, PAIR)]
    lk_pair = land_ref[:, pl.ds(columns + here, PAIR)]
    rows = q_ref.shape[0]
    parts = n // heads
    cols = DH // parts
    gt = g_ref[...].T
    vt = v_ref[...].T
    for h in range(2):
        lk = keep_lanes(lk_pair * SCALE, h).astype(BF16)
        lq = keep_lanes(lq_pair * SCALE, h).astype(BF16)
        span = slice(h * LANDMARKS, (h + 1) * LANDMARKS)
        top = None
        for c in range(0, rows, CHUNK):
            part = slice(c, c + CHUNK)
            sb = dot(k_ref[part, :], lq, NT)
            score_ref[part, :] = sb
            high = fold(sb, jnp.max)
            top = high if top is None else jnp.maximum(top, high)
            sf = dot(q_ref[part, :], lk, NT)
            e = jnp.exp(sf - jnp.max(sf, axis=1, keepdims=True))
            fb_ref[part, span] = (e * (1.0 / jnp.sum(e, axis=1, keepdims=True))).astype(BF16)
        top = jnp.max(top, axis=0, keepdims=True).astype(BF16).astype(F32)
        total = None
        for c in range(0, rows, CHUNK):
            part = slice(c, c + CHUNK)
            p = jnp.exp(score_ref[part, :] - top)
            add = fold(p, jnp.sum)
            total = add if total is None else total + add
            pb_ref[part, span] = p.astype(BF16)
        total = jnp.sum(total, axis=0, keepdims=True)
        top_ref[0, h : h + 1, :] = top
        grads = dot(gt[h * DH : (h + 1) * DH], fb_ref[:, span])
        vals = dot(vt[h * DH : (h + 1) * DH], pb_ref[:, span])
        high, low = halves(total)
        extra = three_rows(top, high.astype(F32), low.astype(F32))
        for p in range(parts):
            cut = slice(p * cols, (p + 1) * cols)
            message_ref[(2 * pair + h) * parts + p] = jnp.concatenate(
                [vals[cut], grads[cut], extra], axis=0
            ).astype(BF16)

    @pl.when(pair == pl.num_programs(0) - 1)
    def _():
        for m in range(size):
            for t in range(n // size):
                out_refs[m][t] = message_ref[(t * size + m) ^ me_ref[0]]


def merge(items, cols):
    tops = [item[2 * cols : 2 * cols + 1] for item in items]
    peak = functools.reduce(jnp.maximum, tops)
    vals = grads = total = 0.0
    for item, top in zip(items, tops):
        factor = jnp.exp(top - peak)
        vals = vals + item[:cols] * factor
        grads = grads + item[cols : 2 * cols]
        total = total + (
            item[2 * cols + 1 : 2 * cols + 2] + item[2 * cols + 2 : 2 * cols + 3]
        ) * factor
    return vals, grads, peak, total


def three_rows(first, second, third):
    row = lax.broadcasted_iota(jnp.int32, (EXTRA, LANDMARKS), 0)
    return jnp.where(row == 0, first, jnp.where(row == 1, second, jnp.where(row == 2, third, 0.0)))


def merge_kernel(cols, count, *refs):
    in_refs, out_refs = refs[:count], refs[count:]
    following = len(out_refs)
    for t in range(in_refs[0].shape[0]):
        vals, grads, peak, total = merge([ref[t].astype(F32) for ref in in_refs], cols)
        high, low = halves(total)
        extra = three_rows(peak, high.astype(F32), low.astype(F32))
        out_refs[t % following][t // following] = jnp.concatenate(
            [vals, grads, extra], axis=0
        ).astype(BF16)


def mix_kernel(cols, count, *refs):
    in_refs, z_ref = refs[:count], refs[count]
    reply_ref, values_ref, grads_ref = refs[count + 1 :]
    vals, grads, peak, total = merge([ref[0].astype(F32) for ref in in_refs], cols)
    inverse = halves(z_ref[0])
    values = vals / total
    mixer = dot_exact(halves(values), inverse, NT)
    norm = dot_exact(halves(grads), inverse) / total
    high, low = halves(jnp.sum(norm * values, axis=0, keepdims=True))
    extra = three_rows(peak, high.astype(F32), low.astype(F32))
    reply_ref[0] = jnp.concatenate([mixer, norm, extra], axis=0).astype(BF16)
    values_ref[...] = values
    grads_ref[...] = grads


def soft_rows(scores):
    e = jnp.exp(scores - jnp.max(scores, axis=1, keepdims=True))
    return e / jnp.sum(e, axis=1, keepdims=True)


def eye():
    shape = (LANDMARKS, LANDMARKS)
    same = lax.broadcasted_iota(jnp.int32, shape, 0) == lax.broadcasted_iota(jnp.int32, shape, 1)
    return same.astype(F32)


def column_top(amat):
    return jnp.max(jnp.sum(amat, axis=0, keepdims=True), axis=1, keepdims=True)


def newton_kernel(own_ref, lq_ref, lk_ref, saved_ref, z_ref):
    which = own_ref[1]
    amat = soft_rows(dot(keep_lanes(lq_ref[...] * SCALE, which).astype(BF16), lk_ref[...], NT))
    saved_ref[0] = amat
    current = amat.T / column_top(amat)
    ident = eye()
    amat = halves(amat)
    for i in range(ITERS):
        saved_ref[1 + 4 * i] = current
        z = halves(current)
        x_full = dot_exact(amat, z)
        saved_ref[2 + 4 * i] = x_full
        x = halves(x_full)
        inner = 15.0 * ident - dot_exact(x, halves(7.0 * ident - x_full))
        saved_ref[3 + 4 * i] = inner
        inner = 13.0 * ident - dot_exact(x, halves(inner))
        saved_ref[4 + 4 * i] = inner
        current = 0.25 * dot_exact(z, halves(inner))
    z_ref[0] = current


def newton_grad_kernel(own_ref, saved_ref, values_ref, grads_ref, lq_ref, lk_ref, q_ref, k_ref):
    which = own_ref[1]
    ident = eye()
    amat = saved_ref[0]
    amat_t = turned(halves(amat))
    grad_z = dot_exact(halves(grads_ref[...]), halves(values_ref[...]), TN)
    grad_a = jnp.zeros_like(amat)
    for i in reversed(range(ITERS)):
        z = halves(saved_ref[1 + 4 * i])
        x_full = saved_ref[2 + 4 * i]
        x_t = turned(halves(x_full))
        first = halves(7.0 * ident - x_full)
        second = halves(saved_ref[3 + 4 * i])
        third = halves(saved_ref[4 + 4 * i])
        dz = halves(0.25 * grad_z)
        d_third = halves(dot_exact(turned(z), dz))
        d_second = halves(-dot_exact(x_t, d_third))
        d_x = -dot_exact(d_third, second, NT) - dot_exact(d_second, first, NT)
        d_x = halves(d_x + dot_exact(x_t, d_second))
        grad_a = grad_a + dot_exact(d_x, z, NT)
        grad_z = dot_exact(dz, third, NT) + dot_exact(amat_t, d_x)
    grad_a = grad_a + grad_z.T / column_top(amat)
    grad_s = amat * (grad_a - jnp.sum(amat * grad_a, axis=1, keepdims=True)) * SCALE
    high, low = halves(grad_s)
    lq = keep_lanes(lq_ref[...], which)
    lk = keep_lanes(lk_ref[...], which)
    q_ref[...] = dot(high, lk) + dot(low, lk)
    k_ref[...] = dot(high.T, lq) + dot(low.T, lq)


def attend_kernel(n, heads, me_ref, fb_ref, top_ref, cot_ref, *refs):
    size = bit_groups(n)[-1][1]
    parts = n // heads
    cols = DH // parts
    reply_refs = refs[:size]
    attn_ref, mixer_ref, norm_ref, center_ref = refs[size : size + 4]
    out_refs = refs[size + 4 : 2 * size + 4]
    w_ref, d_ref, e_ref, sum_ref, all_ref = refs[2 * size + 4 :]
    pair = pl.program_id(0)

    @pl.when(pair == 0)
    def _():
        for m in range(size):
            for t in range(n // size):
                reply = reply_refs[m][t].astype(F32)
                at = (t * size + m) ^ me_ref[0]
                w_ref[at] = reply[:cols]
                d_ref[at] = reply[cols : 2 * cols]
                e_ref[at] = reply[2 * cols : 2 * cols + 8]
        for h in range(heads):
            cut = slice(h * parts, (h + 1) * parts)
            span = slice(h * DH, (h + 1) * DH)
            mixer_ref[span, :] = w_ref[cut].reshape(DH, LANDMARKS).astype(BF16)
            extra = e_ref[cut]
            top = top_ref[h // 2, h % 2 : h % 2 + 1, :]
            factor = jnp.exp(top - extra[0, 0:1, :])
            norm_ref[span, :] = (d_ref[cut].reshape(DH, LANDMARKS) * factor).astype(BF16)
            sums = jnp.sum(extra, axis=0)
            center_ref[h : h + 1, :] = (sums[1:2] + sums[2:3]) * factor

    mixer = mixer_ref[pl.ds(pl.multiple_of(pair * PAIR, PAIR), PAIR), :]
    attn = dot(fb_ref[:, :LANDMARKS], keep_rows(mixer, 0), NT) + dot(
        fb_ref[:, LANDMARKS:], keep_rows(mixer, 1), NT
    )
    attn = attn.astype(BF16)
    attn_ref[...] = attn
    all_ref[pl.ds(pl.multiple_of(pair * PAIR, PAIR), PAIR), :] = attn.T

    @pl.when(pair == pl.num_programs(0) - 1)
    def _():
        block, split = sum_ref.shape[1], n // sum_ref.shape[0]
        width = cot_ref.shape[1]
        sum_ref[...] = dot(all_ref[...], cot_ref[...]).reshape(sum_ref.shape)
        for m in range(size):
            for t in range(n // size):
                at = (t * size + m) ^ me_ref[0]
                if split == 1:
                    out_refs[m][t] = sum_ref[at].astype(BF16)
                else:
                    side = pl.multiple_of((at % split) * (width // split), width // split)
                    out_refs[m][t] = sum_ref[at // split, :, pl.ds(side, width // split)].astype(BF16)


def query_kernel(own_ref, q_ref, g_ref, fb_ref, lk_ref, mixer_ref, more_ref, out_ref, land_ref, ds_ref):
    rows = q_ref.shape[0]
    lk = lk_ref[...] * SCALE
    for h in range(2):
        span = slice(h * LANDMARKS, (h + 1) * LANDMARKS)
        mixer = keep_rows(mixer_ref[...], h)
        for c in range(0, rows, CHUNK):
            part = slice(c, c + CHUNK)
            f = fb_ref[part, span].astype(F32)
            df = dot(g_ref[part, :], mixer)
            ds_ref[part, span] = (f * (df - jnp.sum(f * df, axis=1, keepdims=True))).astype(BF16)
    out_ref[...] = (
        dot(ds_ref[:, :LANDMARKS], keep_lanes(lk, 0).astype(BF16))
        + dot(ds_ref[:, LANDMARKS:], keep_lanes(lk, 1).astype(BF16))
    ).astype(BF16)
    qt = q_ref[...].T
    sums = jnp.concatenate(
        [dot(qt[:DH], ds_ref[:, :LANDMARKS]), dot(qt[DH:], ds_ref[:, LANDMARKS:])], axis=0
    )
    here = (own_ref[0] == pl.program_id(0)).astype(F32)
    land_ref[...] = (sums.T * SCALE + more_ref[...] * here).astype(BF16)


def key_half_kernel(
    first, own_ref, k_ref, v_ref, pb_ref, lq_ref, norm_ref, center_ref, more_ref, *refs
):
    out_ref, value_ref, land_ref, ds_ref = refs[-4:]
    key_pair(first, own_ref, k_ref, v_ref, pb_ref, lq_ref, norm_ref, center_ref, more_ref, out_ref, value_ref, land_ref, ds_ref)


def key_rest_kernel(
    first, own_ref, k_ref, v_ref, pb_ref, lq_ref, norm_ref, center_ref, more_ref, *refs
):
    early_ref, other_ref, _, _, out_ref, value_ref = refs[:6]
    out_refs, (land_ref, ds_ref) = refs[6:-2], refs[-2:]
    size = len(out_refs)
    columns = other_ref.shape[1]
    pair = pl.program_id(0)
    at_pair = pl.ds(pl.multiple_of(pair * PAIR, PAIR), PAIR)
    key_pair(
        first, own_ref, k_ref, v_ref, pb_ref, lq_ref, norm_ref, center_ref, more_ref,
        out_ref, value_ref, land_ref.at[:, at_pair], ds_ref,
    )

    @pl.when(pair == pl.num_programs(0) - 1)
    def _():
        early = early_ref.shape[1]
        for m in range(size):
            held, height, _ = out_refs[m].shape
            for t in range(held):
                at = pl.multiple_of(((t * size + m) ^ own_ref[2]) * height, height)
                out_refs[m][t, :, :early] = early_ref[pl.ds(at, height), :]
                out_refs[m][t, :, early:columns] = land_ref[pl.ds(at, height), :]
                out_refs[m][t, :, columns:] = other_ref[pl.ds(at, height), :]


def key_pair(
    first, own_ref, k_ref, v_ref, pb_ref, lq_ref, norm_ref, center_ref, more_ref, out_ref, value_ref, land_ref, ds_ref
):
    rows = k_ref.shape[0]
    lq = lq_ref[...] * SCALE
    pair = first + pl.program_id(0)
    for h in range(2):
        span = slice(h * LANDMARKS, (h + 1) * LANDMARKS)
        norm = keep_rows(norm_ref[...], h)
        center = center_ref[pl.ds(2 * pair + h, 1), :]
        for c in range(0, rows, CHUNK):
            part = slice(c, c + CHUNK)
            dp = dot(v_ref[part, :], norm)
            ds_ref[part, span] = (pb_ref[part, span].astype(F32) * (dp - center)).astype(BF16)
    out_ref[...] = (
        dot(ds_ref[:, :LANDMARKS], keep_lanes(lq, 0).astype(BF16))
        + dot(ds_ref[:, LANDMARKS:], keep_lanes(lq, 1).astype(BF16))
    ).astype(BF16)
    value_ref[...] = (
        dot(pb_ref[:, :LANDMARKS], keep_rows(norm_ref[...], 0), NT)
        + dot(pb_ref[:, LANDMARKS:], keep_rows(norm_ref[...], 1), NT)
    ).astype(BF16)
    kt = k_ref[...].T
    sums = jnp.concatenate(
        [dot(kt[:DH], ds_ref[:, :LANDMARKS]), dot(kt[DH:], ds_ref[:, LANDMARKS:])], axis=0
    )
    here = (own_ref[0] == pair).astype(F32)
    land_ref[...] = (sums.T * SCALE + more_ref[...] * here).astype(BF16)


def unpack_kernel(size, split, me_ref, *refs):
    out_ref = refs[-1]
    block, width = refs[0].shape[1:]
    for m in range(size):
        at = m ^ (me_ref[0] % size)
        row = pl.ds(pl.multiple_of((at // split) * block, block), block)
        column = pl.ds(pl.multiple_of((at % split) * width, width), width)
        if split == 1:
            out_ref[row, :] = refs[m][0].astype(F32)
        else:
            out_ref[row, column] = refs[m][0].astype(F32)


def held_in_hbm(x):
    return pltpu.with_memory_space_constraint(x, pltpu.HBM)


def whole(shape):
    return pl.BlockSpec(shape, lambda *_: (0,) * len(shape))


def shape_of(shape, dtype):
    return jax.ShapeDtypeStruct(shape, dtype)


def call(kernel, grid, scalars, ins, in_specs, outs, out_specs, scratch=(), flops=0, name=None, aliases={}):
    return pl.pallas_call(
        kernel,
        grid_spec=pltpu.PrefetchScalarGridSpec(
            num_scalar_prefetch=len(scalars),
            grid=grid,
            in_specs=in_specs,
            out_specs=out_specs,
            scratch_shapes=list(scratch),
        ),
        out_shape=outs,
        compiler_params=PARAMS,
        input_output_aliases=aliases,
        cost_estimate=pl.CostEstimate(flops=flops, bytes_accessed=4 << 20, transcendentals=0),
        name=name,
    )(*scalars, *ins)


def local(queries, key_rows, value_rows, out_weight, cotangent):
    rows, columns = queries.shape
    width = out_weight.shape[1]
    heads = columns // DH
    pairs = columns // PAIR
    n = lax.axis_size("seq")
    me = lax.axis_index("seq")
    mine = lax.axis_index("head")
    land_dev = LANDMARKS // n
    seg_len = rows // land_dev
    parts = n // heads
    cols = DH // parts
    size = bit_groups(n)[-1][1]
    height = 2 * cols + EXTRA
    own_head = me // parts
    own_arr = jnp.stack([own_head // 2, own_head % 2, me * 0 if land_dev % 16 else me]).astype(jnp.int32)

    steps = 4
    in_hbm = pl.BlockSpec(memory_space=pltpu.HBM)
    own = call(
        functools.partial(means_kernel, seg_len),
        (1,),
        [],
        [held_in_hbm(queries), held_in_hbm(key_rows)],
        [in_hbm, in_hbm],
        shape_of((land_dev, 2 * columns), BF16),
        whole((land_dev, 2 * columns)),
        [
            pltpu.VMEM((2, rows, columns), BF16),
            pltpu.VMEM((land_dev, 2 * columns), F32),
            pltpu.SemaphoreType.DMA((2, steps)),
        ],
        name="means",
    )
    grad_attn = dot(cotangent, out_weight, NT).astype(BF16)
    sorted_here = land_dev % 16 == 0
    if sorted_here:
        lands = gather_lists(own, n)
    else:
        lands = [gather_ordered(own, n, me).reshape(LANDMARKS // 16, 16, 2 * columns)]
    me_arr = jnp.stack([me, me if sorted_here else me * 0]).astype(jnp.int32)

    token_pair = pl.BlockSpec((rows, PAIR), lambda j, *_: (0, j))
    factor_pair = pl.BlockSpec((rows, 2 * LANDMARKS), lambda j, *_: (0, j))
    lq_pair = pl.BlockSpec((LANDMARKS, PAIR), lambda j, *_: (0, j))
    lk_pair = pl.BlockSpec((LANDMARKS, PAIR), lambda j, *_: (0, j + pairs))
    factors = pltpu.HBM((rows, heads * LANDMARKS), BF16)
    piece = shape_of((n // size, height, LANDMARKS), BF16)

    fb, pb, tops, land, *pieces = call(
        functools.partial(forward_kernel, n, heads, len(lands)),
        (pairs,),
        [me_arr],
        [held_in_hbm(x) for x in (queries, key_rows, value_rows, grad_attn)] + lands,
        [token_pair] * 4 + [whole(lands[0].shape)] * len(lands),
        [
            factors,
            factors,
            shape_of((pairs, 8, LANDMARKS), F32),
            shape_of((LANDMARKS, 2 * columns), BF16),
        ]
        + [piece] * size,
        [
            factor_pair,
            factor_pair,
            pl.BlockSpec((1, 8, LANDMARKS), lambda j, *_: (j, 0, 0)),
            whole((LANDMARKS, 2 * columns)),
        ]
        + [whole(piece.shape)] * size,
        [
            pltpu.VMEM((rows, LANDMARKS), F32),
            pltpu.VMEM((n, height, LANDMARKS), BF16),
        ],
        flops=8 << 30,
        name="forward",
    )

    square = (LANDMARKS, LANDMARKS)
    own_lq = pl.BlockSpec((LANDMARKS, PAIR), lambda i, own: (0, own[0]))
    own_lk = pl.BlockSpec((LANDMARKS, PAIR), lambda i, own: (0, own[0] + pairs))
    kept = shape_of((1 + 4 * ITERS,) + square, F32)
    saved, inverse = call(
        newton_kernel,
        (1,),
        [own_arr],
        [land, land],
        [own_lq, own_lk],
        [kept, shape_of((1,) + square, F32)],
        [whole(kept.shape), whole((1,) + square)],
        flops=4 << 30,
        name="newton",
    )

    groups = bit_groups(n)[::-1]
    for step, (shift, count) in enumerate(groups):
        got = [pieces[0]] + [exchange(pieces[m], m << shift, n) for m in range(1, count)]
        specs = [whole(got[0].shape)] * count
        if step == 0:
            got, inverse, saved = lax.optimization_barrier((got, inverse, saved))
        if step + 1 < len(groups):
            following = groups[step + 1][1]
            piece = shape_of((got[0].shape[0] // following, height, LANDMARKS), BF16)
            pieces = call(
                functools.partial(merge_kernel, cols, count),
                (1,),
                [],
                got,
                specs,
                [piece] * following,
                [whole(piece.shape)] * following,
                name="merge",
            )
    small = shape_of((cols, LANDMARKS), F32)
    reply, values, grads = call(
        functools.partial(mix_kernel, cols, count),
        (1,),
        [],
        got + [inverse],
        specs + [whole((1,) + square)],
        [piece, small, small],
        [whole(piece.shape), whole(small.shape), whole(small.shape)],
        name="mix",
    )
    replies = gather_lists(reply[0], n)

    more = shape_of((LANDMARKS, PAIR), F32)
    more_q, more_k = call(
        newton_grad_kernel,
        (1,),
        [own_arr],
        [saved, values, grads, land, land],
        [whole(kept.shape), whole(small.shape), whole(small.shape), own_lq, own_lk],
        [more, more],
        [whole(more.shape)] * 2,
        flops=8 << 30,
        name="newton_grad",
    )

    block = max(columns // n, 16)
    split = n * block // columns
    flat = shape_of((columns, LANDMARKS), BF16)
    weight_piece = shape_of((n // size, block, width // split), BF16)
    attn, mixer, norm, center, *weight_pieces = call(
        functools.partial(attend_kernel, n, heads),
        (pairs,),
        [me_arr],
        [fb, tops, cotangent] + replies,
        [factor_pair, whole(tops.shape), whole(cotangent.shape)] + [whole(replies[0].shape)] * size,
        [shape_of((rows, columns), BF16), flat, flat, shape_of((heads, LANDMARKS), F32)]
        + [weight_piece] * size,
        [token_pair, whole(flat.shape), whole(flat.shape), whole((heads, LANDMARKS))]
        + [whole(weight_piece.shape)] * size,
        [
            pltpu.VMEM((n, cols, LANDMARKS), F32),
            pltpu.VMEM((n, cols, LANDMARKS), F32),
            pltpu.VMEM((n, 8, LANDMARKS), F32),
            pltpu.VMEM((columns // block, block, width), F32),
            pltpu.VMEM((columns, rows), BF16),
        ],
        flops=4 << 30,
        name="attend",
    )
    (shift, count), later = groups[0], groups[1:]
    weight_sum = scatter_step(weight_pieces, shift, count, n).astype(BF16)
    (pb, key_rows, value_rows), weight_sum = lax.optimization_barrier(
        ((pb, key_rows, value_rows), weight_sum)
    )
    following = later[0][1]
    weight_sum = weight_sum.reshape((-1, following) + weight_sum.shape[1:])
    weight_own = scatter_pieces([weight_sum[:, m] for m in range(following)], n, later)[0].astype(BF16)
    half = width // 2
    there = dot(attn, lax.dynamic_slice_in_dim(out_weight, (1 - mine) * half, half, 1))
    arrived = lax.ppermute(there.astype(BF16), "head", [(0, 1), (1, 0)])
    here = dot(attn, lax.dynamic_slice_in_dim(out_weight, mine * half, half, 1))
    mixed = (here + arrived.astype(F32)).astype(BF16)

    flat_pair = pl.BlockSpec((PAIR, LANDMARKS), lambda j, *_: (j, 0))
    land_pair = pl.BlockSpec((LANDMARKS, PAIR), lambda j, *_: (0, j))
    tokens = shape_of((rows, columns), BF16)
    land_shape = shape_of((LANDMARKS, columns), BF16)
    products = [pltpu.VMEM((rows, 2 * LANDMARKS), BF16)]
    query_f, land_k = call(
        query_kernel,
        (pairs,),
        [own_arr],
        [queries, grad_attn, fb, land, mixer, more_k],
        [token_pair, token_pair, factor_pair, lk_pair, flat_pair, whole(more.shape)],
        [tokens, land_shape],
        [token_pair, land_pair],
        products,
        flops=6 << 30,
        name="query_grad",
    )
    if sorted_here:
        land_piece, count = shape_of((n // size, land_dev, 2 * columns), BF16), size
    else:
        land_piece, count = shape_of((LANDMARKS // 16, 16, 2 * columns), BF16), 1
    some = pairs // 2
    key_in = [key_rows, value_rows, pb, land, norm, center, more_q]

    def key_specs(first):
        pair_of = lambda j, *_: (0, j + first)
        tokens_at = pl.BlockSpec((rows, PAIR), pair_of)
        factors_at = pl.BlockSpec((rows, 2 * LANDMARKS), pair_of)
        land_at = pl.BlockSpec((LANDMARKS, PAIR), pair_of)
        flat_at = pl.BlockSpec((PAIR, LANDMARKS), lambda j, *_: (j + first, 0))
        return [tokens_at, tokens_at, factors_at, land_at, flat_at, whole((heads, LANDMARKS)), whole(more.shape)]

    specs = key_specs(0)
    half_shape = shape_of((LANDMARKS, some * PAIR), BF16)
    tokens_hbm = pltpu.HBM((rows, columns), BF16)
    key_b, value_grad, land_early = call(
        functools.partial(key_half_kernel, 0),
        (some,),
        [own_arr],
        key_in,
        specs,
        [tokens_hbm, tokens_hbm, half_shape],
        [specs[0], specs[0], land_pair],
        products,
        flops=3 << 30,
        name="key_grad",
    )
    (pb, land_early), weight_own = lax.optimization_barrier(((pb, land_early), weight_own))
    key_in[2] = pb
    specs = key_specs(some)
    key_b, value_grad, *land_pieces = call(
        functools.partial(key_rest_kernel, some),
        (pairs - some,),
        [own_arr],
        key_in + [land_early, land_k, held_in_hbm(key_b), held_in_hbm(value_grad)],
        specs + [whole(half_shape.shape), whole(land_shape.shape), in_hbm, in_hbm],
        [tokens_hbm, tokens_hbm] + [land_piece] * count,
        [specs[0], specs[0]] + [whole(land_piece.shape)] * count,
        [pltpu.VMEM((LANDMARKS, (pairs - some) * PAIR), BF16)] + products,
        flops=3 << 30,
        name="key_grad_rest",
        aliases={len(key_in) + 3: 0, len(key_in) + 4: 1},
    )
    if not sorted_here:
        land_pieces = split_by_partner(land_pieces[0].reshape(n, land_dev, 2 * columns), n, me)
    land_own = scatter_pieces(land_pieces, n, groups)[0] * (1.0 / seg_len)

    def finish(token_part, land_part):
        return (
            (token_part.reshape(land_dev, seg_len, columns) + land_part[:, None, :])
            .astype(BF16)
            .reshape(rows, columns)
        )

    weights = gather_lists(weight_own, n)
    weights, mixed = lax.optimization_barrier((weights, mixed))
    weight_grad = call(
        functools.partial(unpack_kernel, size, split),
        (n // size,),
        [me_arr],
        weights,
        [pl.BlockSpec((1,) + weights[0].shape[1:], lambda t, me: (t, 0, 0))] * size,
        shape_of((columns, width), F32),
        pl.BlockSpec((size * block // split, width), lambda t, me: (t ^ (me[0] // size), 0)),
        name="unpack",
    )
    query_grad = finish(query_f, land_own[:, :columns])
    key_grad = finish(key_b, land_own[:, columns:])
    return (mixed, query_grad, key_grad, value_grad, weight_grad)


def solution(mesh):
    return jax.shard_map(
        local,
        mesh=mesh,
        in_specs=(
            P("seq", "head"),
            P("seq", "head"),
            P("seq", "head"),
            P("head", None),
            P("seq", None),
        ),
        out_specs=(
            P("seq", "head"),
            P("seq", "head"),
            P("seq", "head"),
            P("seq", "head"),
            P("head", None),
        ),
        check_vma=False,
    )
```

```python
import functools

import jax
import jax.numpy as jnp
from jax import lax
from jax.experimental import pallas as pl
from jax.experimental.pallas import tpu as pltpu
from jax.sharding import PartitionSpec as P

DH = 64
PAIR = 2 * DH
LANDMARKS = 256
ITERS = 2
SCALE = 0.125
CHUNK = 256
EXTRA = 16
F32 = jnp.float32
BF16 = jnp.bfloat16
PARAMS = pltpu.CompilerParams(vmem_limit_bytes=24 * 1024 * 1024)


def dot(left, right, dims=((1,), (0,))):
    return lax.dot_general(left, right, (dims, ((), ())), preferred_element_type=F32)


NT = ((1,), (1,))
TN = ((0,), (0,))


def halves(value):
    high = value.astype(BF16)
    return high, (value - high.astype(F32)).astype(BF16)


def dot_exact(left, right, dims=((1,), (0,))):
    return dot(left[0], right[0], dims) + (
        dot(left[0], right[1], dims) + dot(left[1], right[0], dims)
    )


def turned(pair):
    return pair[0].T, pair[1].T


def keep_rows(block, which):
    rows = lax.broadcasted_iota(jnp.int32, block.shape, 0) // DH
    return jnp.where(rows == which, block, jnp.zeros_like(block))


def keep_lanes(block, which):
    lanes = lax.broadcasted_iota(jnp.int32, block.shape, 1) // DH
    return jnp.where(lanes == which, block, jnp.zeros_like(block))


def fold(block, op):
    parts = block.reshape(block.shape[0] // 8, 8, block.shape[1])
    return op(parts, axis=0)


def exchange(block, mask, n):
    return lax.ppermute(block, "seq", [(i, i ^ mask) for i in range(n)])


def bit_groups(n):
    bits = n.bit_length() - 1
    groups = []
    while bits > 0:
        take = 2 if bits % 2 == 0 else 1
        bits -= take
        groups.append((bits, 1 << take))
    return groups


def gather_first(block, n):
    shift, size = bit_groups(n)[0]
    held = block[None]
    return [held] + [exchange(held, m << shift, n) for m in range(1, size)]


def gather_rest(got, n):
    for shift, size in bit_groups(n)[1:]:
        held = jnp.stack(got, axis=1).reshape((-1,) + got[0].shape[1:])
        got = [held] + [exchange(held, m << shift, n) for m in range(1, size)]
    return got


def gather_lists(block, n):
    return gather_rest(gather_first(block, n), n)


def gather_ordered(block, n, me):
    got = gather_lists(block, n)
    held = jnp.stack(got, axis=1).reshape((n,) + block.shape)
    return held.at[jnp.arange(n) ^ me].get(mode="promise_in_bounds")


def split_by_partner(blocks, n, me):
    size = bit_groups(n)[-1][1]
    return [
        blocks.at[(jnp.arange(n // size) * size + m) ^ me].get(mode="promise_in_bounds")
        for m in range(size)
    ]


def scatter_step(pieces, shift, size, n):
    got = [pieces[0]] + [exchange(pieces[m], m << shift, n) for m in range(1, size)]
    return sum(part.astype(F32) for part in got)


def scatter_pieces(pieces, n, groups):
    for step, (shift, size) in enumerate(groups):
        held = scatter_step(pieces, shift, size, n)
        if step + 1 < len(groups):
            following = groups[step + 1][1]
            held = held.astype(BF16).reshape((-1, following) + held.shape[1:])
            pieces = [held[:, m] for m in range(following)]
    return held


def means_kernel(seg_len, q_ref, k_ref, out_ref, in_ref, sum_ref, sems):
    rows, columns = q_ref.shape
    steps = sems.shape[1]
    height = rows // steps
    copies = {}
    for c in range(steps):
        part = pl.ds(c * height, height)
        for side, ref in enumerate((q_ref, k_ref)):
            copies[side, c] = pltpu.make_async_copy(ref.at[part], in_ref.at[side, part], sems.at[side, c])
            copies[side, c].start()
    for c in range(steps):
        for side in range(2):
            copies[side, c].wait()
            span = slice(side * columns, (side + 1) * columns)
            for s in range(c * height // seg_len, (c + 1) * height // seg_len):
                total = fold(in_ref[side, s * seg_len : (s + 1) * seg_len, :].astype(F32), jnp.sum)
                sum_ref[s : s + 1, span] = jnp.sum(total, axis=0, keepdims=True)
    out_ref[...] = (sum_ref[...] * (1.0 / seg_len)).astype(BF16)


def forward_kernel(n, heads, count, me_ref, q_ref, k_ref, v_ref, g_ref, *refs):
    size = bit_groups(n)[-1][1]
    in_refs = refs[:count]
    fb_ref, pb_ref, top_ref, land_ref = refs[count : count + 4]
    out_refs = refs[count + 4 : count + 4 + size]
    score_ref, message_ref = refs[count + 4 + size :]
    pair = pl.program_id(0)
    columns = land_ref.shape[1] // 2

    @pl.when(pair == 0)
    def _():
        for m in range(count):
            held, height, _ = in_refs[m].shape
            for t in range(held):
                at = pl.multiple_of(((t * count + m) ^ me_ref[1]) * height, height)
                land_ref[pl.ds(at, height), :] = in_refs[m][t]

    here = pl.multiple_of(pair * PAIR, PAIR)
    lq_pair = land_ref[:, pl.ds(here, PAIR)]
    lk_pair = land_ref[:, pl.ds(columns + here, PAIR)]
    rows = q_ref.shape[0]
    parts = n // heads
    cols = DH // parts
    gt = g_ref[...].T
    vt = v_ref[...].T
    for h in range(2):
        lk = keep_lanes(lk_pair * SCALE, h).astype(BF16)
        lq = keep_lanes(lq_pair * SCALE, h).astype(BF16)
        span = slice(h * LANDMARKS, (h + 1) * LANDMARKS)
        top = None
        for c in range(0, rows, CHUNK):
            part = slice(c, c + CHUNK)
            sb = dot(k_ref[part, :], lq, NT)
            score_ref[part, :] = sb
            high = fold(sb, jnp.max)
            top = high if top is None else jnp.maximum(top, high)
            sf = dot(q_ref[part, :], lk, NT)
            e = jnp.exp(sf - jnp.max(sf, axis=1, keepdims=True))
            fb_ref[part, span] = (e * (1.0 / jnp.sum(e, axis=1, keepdims=True))).astype(BF16)
        top = jnp.max(top, axis=0, keepdims=True).astype(BF16).astype(F32)
        total = None
        for c in range(0, rows, CHUNK):
            part = slice(c, c + CHUNK)
            p = jnp.exp(score_ref[part, :] - top)
            add = fold(p, jnp.sum)
            total = add if total is None else total + add
            pb_ref[part, span] = p.astype(BF16)
        total = jnp.sum(total, axis=0, keepdims=True)
        top_ref[0, h : h + 1, :] = top
        grads = dot(gt[h * DH : (h + 1) * DH], fb_ref[:, span])
        vals = dot(vt[h * DH : (h + 1) * DH], pb_ref[:, span])
        high, low = halves(total)
        extra = three_rows(top, high.astype(F32), low.astype(F32))
        for p in range(parts):
            cut = slice(p * cols, (p + 1) * cols)
            message_ref[(2 * pair + h) * parts + p] = jnp.concatenate(
                [vals[cut], grads[cut], extra], axis=0
            ).astype(BF16)

    @pl.when(pair == pl.num_programs(0) - 1)
    def _():
        for m in range(size):
            for t in range(n // size):
                out_refs[m][t] = message_ref[(t * size + m) ^ me_ref[0]]


def merge(items, cols):
    tops = [item[2 * cols : 2 * cols + 1] for item in items]
    peak = functools.reduce(jnp.maximum, tops)
    vals = grads = total = 0.0
    for item, top in zip(items, tops):
        factor = jnp.exp(top - peak)
        vals = vals + item[:cols] * factor
        grads = grads + item[cols : 2 * cols]
        total = total + (
            item[2 * cols + 1 : 2 * cols + 2] + item[2 * cols + 2 : 2 * cols + 3]
        ) * factor
    return vals, grads, peak, total


def three_rows(first, second, third):
    row = lax.broadcasted_iota(jnp.int32, (EXTRA, LANDMARKS), 0)
    return jnp.where(row == 0, first, jnp.where(row == 1, second, jnp.where(row == 2, third, 0.0)))


def merge_kernel(cols, count, *refs):
    in_refs, out_refs = refs[:count], refs[count:]
    following = len(out_refs)
    for t in range(in_refs[0].shape[0]):
        vals, grads, peak, total = merge([ref[t].astype(F32) for ref in in_refs], cols)
        high, low = halves(total)
        extra = three_rows(peak, high.astype(F32), low.astype(F32))
        out_refs[t % following][t // following] = jnp.concatenate(
            [vals, grads, extra], axis=0
        ).astype(BF16)


def mix_kernel(cols, count, *refs):
    in_refs, z_ref = refs[:count], refs[count]
    reply_ref, values_ref, grads_ref = refs[count + 1 :]
    vals, grads, peak, total = merge([ref[0].astype(F32) for ref in in_refs], cols)
    inverse = halves(z_ref[0])
    values = vals / total
    mixer = dot_exact(halves(values), inverse, NT)
    norm = dot_exact(halves(grads), inverse) / total
    high, low = halves(jnp.sum(norm * values, axis=0, keepdims=True))
    extra = three_rows(peak, high.astype(F32), low.astype(F32))
    reply_ref[0] = jnp.concatenate([mixer, norm, extra], axis=0).astype(BF16)
    values_ref[...] = values
    grads_ref[...] = grads


def soft_rows(scores):
    e = jnp.exp(scores - jnp.max(scores, axis=1, keepdims=True))
    return e / jnp.sum(e, axis=1, keepdims=True)


def eye():
    shape = (LANDMARKS, LANDMARKS)
    same = lax.broadcasted_iota(jnp.int32, shape, 0) == lax.broadcasted_iota(jnp.int32, shape, 1)
    return same.astype(F32)


def column_top(amat):
    return jnp.max(jnp.sum(amat, axis=0, keepdims=True), axis=1, keepdims=True)


def newton_kernel(own_ref, lq_ref, lk_ref, saved_ref, z_ref):
    which = own_ref[1]
    amat = soft_rows(dot(keep_lanes(lq_ref[...] * SCALE, which).astype(BF16), lk_ref[...], NT))
    saved_ref[0] = amat
    current = amat.T / column_top(amat)
    ident = eye()
    amat = halves(amat)
    for i in range(ITERS):
        saved_ref[1 + 4 * i] = current
        z = halves(current)
        x_full = dot_exact(amat, z)
        saved_ref[2 + 4 * i] = x_full
        x = halves(x_full)
        inner = 15.0 * ident - dot_exact(x, halves(7.0 * ident - x_full))
        saved_ref[3 + 4 * i] = inner
        inner = 13.0 * ident - dot_exact(x, halves(inner))
        saved_ref[4 + 4 * i] = inner
        current = 0.25 * dot_exact(z, halves(inner))
    z_ref[0] = current


def newton_grad_kernel(own_ref, saved_ref, values_ref, grads_ref, lq_ref, lk_ref, q_ref, k_ref):
    which = own_ref[1]
    ident = eye()
    amat = saved_ref[0]
    amat_t = turned(halves(amat))
    grad_z = dot_exact(halves(grads_ref[...]), halves(values_ref[...]), TN)
    grad_a = jnp.zeros_like(amat)
    for i in reversed(range(ITERS)):
        z = halves(saved_ref[1 + 4 * i])
        x_full = saved_ref[2 + 4 * i]
        x_t = turned(halves(x_full))
        first = halves(7.0 * ident - x_full)
        second = halves(saved_ref[3 + 4 * i])
        third = halves(saved_ref[4 + 4 * i])
        dz = halves(0.25 * grad_z)
        d_third = halves(dot_exact(turned(z), dz))
        d_second = halves(-dot_exact(x_t, d_third))
        d_x = -dot_exact(d_third, second, NT) - dot_exact(d_second, first, NT)
        d_x = halves(d_x + dot_exact(x_t, d_second))
        grad_a = grad_a + dot_exact(d_x, z, NT)
        grad_z = dot_exact(dz, third, NT) + dot_exact(amat_t, d_x)
    grad_a = grad_a + grad_z.T / column_top(amat)
    grad_s = amat * (grad_a - jnp.sum(amat * grad_a, axis=1, keepdims=True)) * SCALE
    high, low = halves(grad_s)
    lq = keep_lanes(lq_ref[...], which)
    lk = keep_lanes(lk_ref[...], which)
    q_ref[...] = dot(high, lk) + dot(low, lk)
    k_ref[...] = dot(high.T, lq) + dot(low.T, lq)


def attend_kernel(n, heads, me_ref, fb_ref, top_ref, cot_ref, *refs):
    size = bit_groups(n)[-1][1]
    parts = n // heads
    cols = DH // parts
    reply_refs = refs[:size]
    attn_ref, mixer_ref, norm_ref, center_ref = refs[size : size + 4]
    out_refs = refs[size + 4 : 2 * size + 4]
    w_ref, d_ref, e_ref, sum_ref, all_ref = refs[2 * size + 4 :]
    pair = pl.program_id(0)

    @pl.when(pair == 0)
    def _():
        for m in range(size):
            for t in range(n // size):
                reply = reply_refs[m][t].astype(F32)
                at = (t * size + m) ^ me_ref[0]
                w_ref[at] = reply[:cols]
                d_ref[at] = reply[cols : 2 * cols]
                e_ref[at] = reply[2 * cols : 2 * cols + 8]
        for h in range(heads):
            cut = slice(h * parts, (h + 1) * parts)
            span = slice(h * DH, (h + 1) * DH)
            mixer_ref[span, :] = w_ref[cut].reshape(DH, LANDMARKS).astype(BF16)
            extra = e_ref[cut]
            top = top_ref[h // 2, h % 2 : h % 2 + 1, :]
            factor = jnp.exp(top - extra[0, 0:1, :])
            norm_ref[span, :] = (d_ref[cut].reshape(DH, LANDMARKS) * factor).astype(BF16)
            sums = jnp.sum(extra, axis=0)
            center_ref[h : h + 1, :] = (sums[1:2] + sums[2:3]) * factor

    mixer = mixer_ref[pl.ds(pl.multiple_of(pair * PAIR, PAIR), PAIR), :]
    attn = dot(fb_ref[:, :LANDMARKS], keep_rows(mixer, 0), NT) + dot(
        fb_ref[:, LANDMARKS:], keep_rows(mixer, 1), NT
    )
    attn = attn.astype(BF16)
    attn_ref[...] = attn
    all_ref[pl.ds(pl.multiple_of(pair * PAIR, PAIR), PAIR), :] = attn.T

    @pl.when(pair == pl.num_programs(0) - 1)
    def _():
        block, split = sum_ref.shape[1], n // sum_ref.shape[0]
        width = cot_ref.shape[1]
        sum_ref[...] = dot(all_ref[...], cot_ref[...]).reshape(sum_ref.shape)
        for m in range(size):
            for t in range(n // size):
                at = (t * size + m) ^ me_ref[0]
                if split == 1:
                    out_refs[m][t] = sum_ref[at].astype(BF16)
                else:
                    side = pl.multiple_of((at % split) * (width // split), width // split)
                    out_refs[m][t] = sum_ref[at // split, :, pl.ds(side, width // split)].astype(BF16)


def query_kernel(own_ref, q_ref, g_ref, fb_ref, lk_ref, mixer_ref, more_ref, out_ref, land_ref, ds_ref):
    rows = q_ref.shape[0]
    lk = lk_ref[...] * SCALE
    for h in range(2):
        span = slice(h * LANDMARKS, (h + 1) * LANDMARKS)
        mixer = keep_rows(mixer_ref[...], h)
        for c in range(0, rows, CHUNK):
            part = slice(c, c + CHUNK)
            f = fb_ref[part, span].astype(F32)
            df = dot(g_ref[part, :], mixer)
            ds_ref[part, span] = (f * (df - jnp.sum(f * df, axis=1, keepdims=True))).astype(BF16)
    out_ref[...] = (
        dot(ds_ref[:, :LANDMARKS], keep_lanes(lk, 0).astype(BF16))
        + dot(ds_ref[:, LANDMARKS:], keep_lanes(lk, 1).astype(BF16))
    ).astype(BF16)
    qt = q_ref[...].T
    sums = jnp.concatenate(
        [dot(qt[:DH], ds_ref[:, :LANDMARKS]), dot(qt[DH:], ds_ref[:, LANDMARKS:])], axis=0
    )
    here = (own_ref[0] == pl.program_id(0)).astype(F32)
    land_ref[...] = (sums.T * SCALE + more_ref[...] * here).astype(BF16)


def key_half_kernel(
    first, own_ref, k_ref, v_ref, pb_ref, lq_ref, norm_ref, center_ref, more_ref, *refs
):
    out_ref, value_ref, land_ref, ds_ref = refs[-4:]
    key_pair(first, own_ref, k_ref, v_ref, pb_ref, lq_ref, norm_ref, center_ref, more_ref, out_ref, value_ref, land_ref, ds_ref)


def key_rest_kernel(
    first, own_ref, k_ref, v_ref, pb_ref, lq_ref, norm_ref, center_ref, more_ref, *refs
):
    early_ref, other_ref, _, _, out_ref, value_ref = refs[:6]
    out_refs, (land_ref, ds_ref) = refs[6:-2], refs[-2:]
    size = len(out_refs)
    columns = other_ref.shape[1]
    pair = pl.program_id(0)
    at_pair = pl.ds(pl.multiple_of(pair * PAIR, PAIR), PAIR)
    key_pair(
        first, own_ref, k_ref, v_ref, pb_ref, lq_ref, norm_ref, center_ref, more_ref,
        out_ref, value_ref, land_ref.at[:, at_pair], ds_ref,
    )

    @pl.when(pair == pl.num_programs(0) - 1)
    def _():
        early = early_ref.shape[1]
        for m in range(size):
            held, height, _ = out_refs[m].shape
            for t in range(held):
                at = pl.multiple_of(((t * size + m) ^ own_ref[2]) * height, height)
                out_refs[m][t, :, :early] = early_ref[pl.ds(at, height), :]
                out_refs[m][t, :, early:columns] = land_ref[pl.ds(at, height), :]
                out_refs[m][t, :, columns:] = other_ref[pl.ds(at, height), :]


def key_pair(
    first, own_ref, k_ref, v_ref, pb_ref, lq_ref, norm_ref, center_ref, more_ref, out_ref, value_ref, land_ref, ds_ref
):
    rows = k_ref.shape[0]
    lq = lq_ref[...] * SCALE
    pair = first + pl.program_id(0)
    for h in range(2):
        span = slice(h * LANDMARKS, (h + 1) * LANDMARKS)
        norm = keep_rows(norm_ref[...], h)
        center = center_ref[pl.ds(2 * pair + h, 1), :]
        for c in range(0, rows, CHUNK):
            part = slice(c, c + CHUNK)
            dp = dot(v_ref[part, :], norm)
            ds_ref[part, span] = (pb_ref[part, span].astype(F32) * (dp - center)).astype(BF16)
    out_ref[...] = (
        dot(ds_ref[:, :LANDMARKS], keep_lanes(lq, 0).astype(BF16))
        + dot(ds_ref[:, LANDMARKS:], keep_lanes(lq, 1).astype(BF16))
    ).astype(BF16)
    value_ref[...] = (
        dot(pb_ref[:, :LANDMARKS], keep_rows(norm_ref[...], 0), NT)
        + dot(pb_ref[:, LANDMARKS:], keep_rows(norm_ref[...], 1), NT)
    ).astype(BF16)
    kt = k_ref[...].T
    sums = jnp.concatenate(
        [dot(kt[:DH], ds_ref[:, :LANDMARKS]), dot(kt[DH:], ds_ref[:, LANDMARKS:])], axis=0
    )
    here = (own_ref[0] == pair).astype(F32)
    land_ref[...] = (sums.T * SCALE + more_ref[...] * here).astype(BF16)


def unpack_kernel(split, me_ref, *refs):
    in_refs, (out_ref, wide_ref, sems) = refs[:-3], refs[-3:]
    size = len(in_refs)
    held, block, width = in_refs[0].shape
    copies = []
    for t in range(held):
        for m in range(size):
            slot = t * size + m
            at = slot ^ me_ref[0]
            row = pl.ds(pl.multiple_of((at // split) * block, block), block)
            if split == 1:
                target = out_ref.at[row]
            else:
                target = out_ref.at[row, pl.ds(pl.multiple_of((at % split) * width, width), width)]
            wide_ref[slot] = in_refs[m][t].astype(F32)
            copies.append(pltpu.make_async_copy(wide_ref.at[slot], target, sems.at[slot]))
            copies[-1].start()
    for copy in copies:
        copy.wait()


def held_in_hbm(x):
    return pltpu.with_memory_space_constraint(x, pltpu.HBM)


def whole(shape):
    return pl.BlockSpec(shape, lambda *_: (0,) * len(shape))


def shape_of(shape, dtype):
    return jax.ShapeDtypeStruct(shape, dtype)


def call(kernel, grid, scalars, ins, in_specs, outs, out_specs, scratch=(), flops=0, name=None, aliases={}):
    return pl.pallas_call(
        kernel,
        grid_spec=pltpu.PrefetchScalarGridSpec(
            num_scalar_prefetch=len(scalars),
            grid=grid,
            in_specs=in_specs,
            out_specs=out_specs,
            scratch_shapes=list(scratch),
        ),
        out_shape=outs,
        compiler_params=PARAMS,
        input_output_aliases=aliases,
        cost_estimate=pl.CostEstimate(flops=flops, bytes_accessed=4 << 20, transcendentals=0),
        name=name,
    )(*scalars, *ins)


def local(queries, key_rows, value_rows, out_weight, cotangent):
    rows, columns = queries.shape
    width = out_weight.shape[1]
    heads = columns // DH
    pairs = columns // PAIR
    n = lax.axis_size("seq")
    me = lax.axis_index("seq")
    mine = lax.axis_index("head")
    land_dev = LANDMARKS // n
    seg_len = rows // land_dev
    parts = n // heads
    cols = DH // parts
    size = bit_groups(n)[-1][1]
    height = 2 * cols + EXTRA
    own_head = me // parts
    own_arr = jnp.stack([own_head // 2, own_head % 2, me * 0 if land_dev % 16 else me]).astype(jnp.int32)

    steps = 4
    in_hbm = pl.BlockSpec(memory_space=pltpu.HBM)
    own = call(
        functools.partial(means_kernel, seg_len),
        (1,),
        [],
        [held_in_hbm(queries), held_in_hbm(key_rows)],
        [in_hbm, in_hbm],
        shape_of((land_dev, 2 * columns), BF16),
        whole((land_dev, 2 * columns)),
        [
            pltpu.VMEM((2, rows, columns), BF16),
            pltpu.VMEM((land_dev, 2 * columns), F32),
            pltpu.SemaphoreType.DMA((2, steps)),
        ],
        name="means",
    )
    grad_attn = dot(cotangent, out_weight, NT).astype(BF16)
    sorted_here = land_dev % 16 == 0
    if sorted_here:
        lands = gather_lists(own, n)
    else:
        lands = [gather_ordered(own, n, me).reshape(LANDMARKS // 16, 16, 2 * columns)]
    me_arr = jnp.stack([me, me if sorted_here else me * 0]).astype(jnp.int32)

    token_pair = pl.BlockSpec((rows, PAIR), lambda j, *_: (0, j))
    factor_pair = pl.BlockSpec((rows, 2 * LANDMARKS), lambda j, *_: (0, j))
    lq_pair = pl.BlockSpec((LANDMARKS, PAIR), lambda j, *_: (0, j))
    lk_pair = pl.BlockSpec((LANDMARKS, PAIR), lambda j, *_: (0, j + pairs))
    factors = pltpu.HBM((rows, heads * LANDMARKS), BF16)
    piece = shape_of((n // size, height, LANDMARKS), BF16)

    fb, pb, tops, land, *pieces = call(
        functools.partial(forward_kernel, n, heads, len(lands)),
        (pairs,),
        [me_arr],
        [held_in_hbm(x) for x in (queries, key_rows, value_rows, grad_attn)] + lands,
        [token_pair] * 4 + [whole(lands[0].shape)] * len(lands),
        [
            factors,
            factors,
            shape_of((pairs, 8, LANDMARKS), F32),
            shape_of((LANDMARKS, 2 * columns), BF16),
        ]
        + [piece] * size,
        [
            factor_pair,
            factor_pair,
            pl.BlockSpec((1, 8, LANDMARKS), lambda j, *_: (j, 0, 0)),
            whole((LANDMARKS, 2 * columns)),
        ]
        + [whole(piece.shape)] * size,
        [
            pltpu.VMEM((rows, LANDMARKS), F32),
            pltpu.VMEM((n, height, LANDMARKS), BF16),
        ],
        flops=8 << 30,
        name="forward",
    )

    square = (LANDMARKS, LANDMARKS)
    own_lq = pl.BlockSpec((LANDMARKS, PAIR), lambda i, own: (0, own[0]))
    own_lk = pl.BlockSpec((LANDMARKS, PAIR), lambda i, own: (0, own[0] + pairs))
    kept = pltpu.VMEM((1 + 4 * ITERS,) + square, F32)
    saved, inverse = call(
        newton_kernel,
        (1,),
        [own_arr],
        [land, land],
        [own_lq, own_lk],
        [kept, shape_of((1,) + square, F32)],
        [whole(kept.shape), whole((1,) + square)],
        flops=4 << 30,
        name="newton",
    )

    groups = bit_groups(n)[::-1]
    for step, (shift, count) in enumerate(groups):
        got = [pieces[0]] + [exchange(pieces[m], m << shift, n) for m in range(1, count)]
        specs = [whole(got[0].shape)] * count
        if step == 0:
            got, inverse, saved = lax.optimization_barrier((got, inverse, saved))
        if step + 1 < len(groups):
            following = groups[step + 1][1]
            piece = shape_of((got[0].shape[0] // following, height, LANDMARKS), BF16)
            pieces = call(
                functools.partial(merge_kernel, cols, count),
                (1,),
                [],
                got,
                specs,
                [piece] * following,
                [whole(piece.shape)] * following,
                name="merge",
            )
    small = shape_of((cols, LANDMARKS), F32)
    reply, values, grads = call(
        functools.partial(mix_kernel, cols, count),
        (1,),
        [],
        got + [inverse],
        specs + [whole((1,) + square)],
        [piece, small, small],
        [whole(piece.shape), whole(small.shape), whole(small.shape)],
        name="mix",
    )
    replies = gather_lists(reply[0], n)

    more = shape_of((LANDMARKS, PAIR), F32)
    more_q, more_k = call(
        newton_grad_kernel,
        (1,),
        [own_arr],
        [pltpu.with_memory_space_constraint(saved, pltpu.VMEM), values, grads, land, land],
        [whole(kept.shape), whole(small.shape), whole(small.shape), own_lq, own_lk],
        [more, more],
        [whole(more.shape)] * 2,
        flops=8 << 30,
        name="newton_grad",
    )

    replies, more_q, more_k = lax.optimization_barrier((replies, more_q, more_k))
    block = max(columns // n, 16)
    split = n * block // columns
    flat = shape_of((columns, LANDMARKS), BF16)
    weight_piece = shape_of((n // size, block, width // split), BF16)
    attn, mixer, norm, center, *weight_pieces = call(
        functools.partial(attend_kernel, n, heads),
        (pairs,),
        [me_arr],
        [fb, tops, cotangent] + replies,
        [factor_pair, whole(tops.shape), whole(cotangent.shape)] + [whole(replies[0].shape)] * size,
        [shape_of((rows, columns), BF16), flat, flat, shape_of((heads, LANDMARKS), F32)]
        + [weight_piece] * size,
        [token_pair, whole(flat.shape), whole(flat.shape), whole((heads, LANDMARKS))]
        + [whole(weight_piece.shape)] * size,
        [
            pltpu.VMEM((n, cols, LANDMARKS), F32),
            pltpu.VMEM((n, cols, LANDMARKS), F32),
            pltpu.VMEM((n, 8, LANDMARKS), F32),
            pltpu.VMEM((columns // block, block, width), F32),
            pltpu.VMEM((columns, rows), BF16),
        ],
        flops=4 << 30,
        name="attend",
    )
    (shift, count), later = groups[0], groups[1:]
    weight_sum = scatter_step(weight_pieces, shift, count, n).astype(BF16)
    (pb, key_rows, value_rows), weight_sum = lax.optimization_barrier(
        ((pb, key_rows, value_rows), weight_sum)
    )
    following = later[0][1]
    weight_sum = weight_sum.reshape((-1, following) + weight_sum.shape[1:])
    weight_own = scatter_pieces([weight_sum[:, m] for m in range(following)], n, later)[0].astype(BF16)
    half = width // 2
    there = dot(attn, lax.dynamic_slice_in_dim(out_weight, (1 - mine) * half, half, 1))
    arrived = lax.ppermute(there.astype(BF16), "head", [(0, 1), (1, 0)])
    here = dot(attn, lax.dynamic_slice_in_dim(out_weight, mine * half, half, 1))
    mixed = (here + arrived.astype(F32)).astype(BF16)

    flat_pair = pl.BlockSpec((PAIR, LANDMARKS), lambda j, *_: (j, 0))
    land_pair = pl.BlockSpec((LANDMARKS, PAIR), lambda j, *_: (0, j))
    tokens = shape_of((rows, columns), BF16)
    land_shape = shape_of((LANDMARKS, columns), BF16)
    products = [pltpu.VMEM((rows, 2 * LANDMARKS), BF16)]
    query_f, land_k = call(
        query_kernel,
        (pairs,),
        [own_arr],
        [queries, grad_attn, fb, land, mixer, more_k],
        [token_pair, token_pair, factor_pair, lk_pair, flat_pair, whole(more.shape)],
        [tokens, land_shape],
        [token_pair, land_pair],
        products,
        flops=6 << 30,
        name="query_grad",
    )
    if sorted_here:
        land_piece, count = shape_of((n // size, land_dev, 2 * columns), BF16), size
    else:
        land_piece, count = shape_of((LANDMARKS // 16, 16, 2 * columns), BF16), 1
    some = pairs // 2
    key_in = [key_rows, value_rows, pb, land, norm, center, more_q]

    def key_specs(first):
        pair_of = lambda j, *_: (0, j + first)
        tokens_at = pl.BlockSpec((rows, PAIR), pair_of)
        factors_at = pl.BlockSpec((rows, 2 * LANDMARKS), pair_of)
        land_at = pl.BlockSpec((LANDMARKS, PAIR), pair_of)
        flat_at = pl.BlockSpec((PAIR, LANDMARKS), lambda j, *_: (j + first, 0))
        return [tokens_at, tokens_at, factors_at, land_at, flat_at, whole((heads, LANDMARKS)), whole(more.shape)]

    specs = key_specs(0)
    half_shape = shape_of((LANDMARKS, some * PAIR), BF16)
    tokens_hbm = pltpu.HBM((rows, columns), BF16)
    key_b, value_grad, land_early = call(
        functools.partial(key_half_kernel, 0),
        (some,),
        [own_arr],
        key_in,
        specs,
        [tokens_hbm, tokens_hbm, half_shape],
        [specs[0], specs[0], land_pair],
        products,
        flops=3 << 30,
        name="key_grad",
    )
    (pb, land_early), weight_own = lax.optimization_barrier(((pb, land_early), weight_own))
    key_in[2] = pb
    specs = key_specs(some)
    key_b, value_grad, *land_pieces = call(
        functools.partial(key_rest_kernel, some),
        (pairs - some,),
        [own_arr],
        key_in + [land_early, land_k, held_in_hbm(key_b), held_in_hbm(value_grad)],
        specs + [whole(half_shape.shape), whole(land_shape.shape), in_hbm, in_hbm],
        [tokens_hbm, tokens_hbm] + [land_piece] * count,
        [specs[0], specs[0]] + [whole(land_piece.shape)] * count,
        [pltpu.VMEM((LANDMARKS, (pairs - some) * PAIR), BF16)] + products,
        flops=3 << 30,
        name="key_grad_rest",
        aliases={len(key_in) + 3: 0, len(key_in) + 4: 1},
    )
    if not sorted_here:
        land_pieces = split_by_partner(land_pieces[0].reshape(n, land_dev, 2 * columns), n, me)
    weights = gather_first(weight_own, n)
    weights, land_pieces = lax.optimization_barrier((weights, land_pieces))
    weights = gather_rest(weights, n)
    land_own = scatter_pieces(land_pieces, n, groups)[0] * (1.0 / seg_len)

    def finish(token_part, land_part):
        return (
            (token_part.reshape(land_dev, seg_len, columns) + land_part[:, None, :])
            .astype(BF16)
            .reshape(rows, columns)
        )

    weights, mixed = lax.optimization_barrier((weights, mixed))
    weight_grad = call(
        functools.partial(unpack_kernel, split),
        (1,),
        [me_arr],
        weights,
        [whole(weights[0].shape)] * size,
        pltpu.HBM((columns, width), F32),
        in_hbm,
        [pltpu.VMEM((n,) + weights[0].shape[1:], F32), pltpu.SemaphoreType.DMA((n,))],
        name="unpack",
    )
    query_grad = finish(query_f, land_own[:, :columns])
    key_grad = finish(key_b, land_own[:, columns:])
    return (mixed, query_grad, key_grad, value_grad, weight_grad)


def solution(mesh):
    return jax.shard_map(
        local,
        mesh=mesh,
        in_specs=(
            P("seq", "head"),
            P("seq", "head"),
            P("seq", "head"),
            P("head", None),
            P("seq", None),
        ),
        out_specs=(
            P("seq", "head"),
            P("seq", "head"),
            P("seq", "head"),
            P("seq", "head"),
            P("head", None),
        ),
        check_vma=False,
    )
```

```python
import functools

import jax
import jax.numpy as jnp
from jax import lax
from jax.experimental import pallas as pl
from jax.experimental.pallas import tpu as pltpu
from jax.sharding import PartitionSpec as P

DH = 64
PAIR = 2 * DH
LANDMARKS = 256
ITERS = 2
SCALE = 0.125
CHUNK = 256
EXTRA = 16
F32 = jnp.float32
BF16 = jnp.bfloat16
PARAMS = pltpu.CompilerParams(vmem_limit_bytes=24 * 1024 * 1024)


def dot(left, right, dims=((1,), (0,))):
    return lax.dot_general(left, right, (dims, ((), ())), preferred_element_type=F32)


NT = ((1,), (1,))
TN = ((0,), (0,))


def halves(value):
    high = value.astype(BF16)
    return high, (value - high.astype(F32)).astype(BF16)


def dot_exact(left, right, dims=((1,), (0,))):
    return dot(left[0], right[0], dims) + (
        dot(left[0], right[1], dims) + dot(left[1], right[0], dims)
    )


def turned(pair):
    return pair[0].T, pair[1].T


def keep_rows(block, which):
    rows = lax.broadcasted_iota(jnp.int32, block.shape, 0) // DH
    return jnp.where(rows == which, block, jnp.zeros_like(block))


def keep_lanes(block, which):
    lanes = lax.broadcasted_iota(jnp.int32, block.shape, 1) // DH
    return jnp.where(lanes == which, block, jnp.zeros_like(block))


def fold(block, op):
    parts = block.reshape(block.shape[0] // 8, 8, block.shape[1])
    return op(parts, axis=0)


def exchange(block, mask, n):
    return lax.ppermute(block, "seq", [(i, i ^ mask) for i in range(n)])


def bit_groups(n):
    bits = n.bit_length() - 1
    groups = []
    while bits > 0:
        take = 2 if bits % 2 == 0 else 1
        bits -= take
        groups.append((bits, 1 << take))
    return groups


def gather_first(block, n):
    shift, size = bit_groups(n)[0]
    held = block[None]
    return [held] + [exchange(held, m << shift, n) for m in range(1, size)]


def gather_rest(got, n):
    for shift, size in bit_groups(n)[1:]:
        held = jnp.stack(got, axis=1).reshape((-1,) + got[0].shape[1:])
        got = [held] + [exchange(held, m << shift, n) for m in range(1, size)]
    return got


def gather_lists(block, n):
    return gather_rest(gather_first(block, n), n)


def gather_ordered(block, n, me):
    got = gather_lists(block, n)
    held = jnp.stack(got, axis=1).reshape((n,) + block.shape)
    return held.at[jnp.arange(n) ^ me].get(mode="promise_in_bounds")


def split_by_partner(blocks, n, me):
    size = bit_groups(n)[-1][1]
    return [
        blocks.at[(jnp.arange(n // size) * size + m) ^ me].get(mode="promise_in_bounds")
        for m in range(size)
    ]


def scatter_step(pieces, shift, size, n):
    got = [pieces[0]] + [exchange(pieces[m], m << shift, n) for m in range(1, size)]
    return sum(part.astype(F32) for part in got)


def scatter_pieces(pieces, n, groups):
    for step, (shift, size) in enumerate(groups):
        held = scatter_step(pieces, shift, size, n)
        if step + 1 < len(groups):
            following = groups[step + 1][1]
            held = held.astype(BF16).reshape((-1, following) + held.shape[1:])
            pieces = [held[:, m] for m in range(following)]
    return held


def means_kernel(seg_len, q_ref, k_ref, out_ref, in_ref, sum_ref, sems):
    rows, columns = q_ref.shape
    steps = sems.shape[1]
    height = rows // steps
    copies = {}
    for c in range(steps):
        part = pl.ds(c * height, height)
        for side, ref in enumerate((q_ref, k_ref)):
            copies[side, c] = pltpu.make_async_copy(ref.at[part], in_ref.at[side, part], sems.at[side, c])
            copies[side, c].start()
    for c in range(steps):
        for side in range(2):
            copies[side, c].wait()
            span = slice(side * columns, (side + 1) * columns)
            for s in range(c * height // seg_len, (c + 1) * height // seg_len):
                total = fold(in_ref[side, s * seg_len : (s + 1) * seg_len, :].astype(F32), jnp.sum)
                sum_ref[s : s + 1, span] = jnp.sum(total, axis=0, keepdims=True)
    out_ref[...] = (sum_ref[...] * (1.0 / seg_len)).astype(BF16)


def forward_kernel(n, heads, count, me_ref, q_ref, k_ref, v_ref, g_ref, *refs):
    size = bit_groups(n)[-1][1]
    in_refs = refs[:count]
    fb_ref, pb_ref, top_ref, land_ref = refs[count : count + 4]
    out_refs = refs[count + 4 : count + 4 + size]
    score_ref, message_ref = refs[count + 4 + size :]
    pair = pl.program_id(0)
    columns = land_ref.shape[1] // 2

    @pl.when(pair == 0)
    def _():
        for m in range(count):
            held, height, _ = in_refs[m].shape
            for t in range(held):
                at = pl.multiple_of(((t * count + m) ^ me_ref[1]) * height, height)
                land_ref[pl.ds(at, height), :] = in_refs[m][t]

    here = pl.multiple_of(pair * PAIR, PAIR)
    lq_pair = land_ref[:, pl.ds(here, PAIR)]
    lk_pair = land_ref[:, pl.ds(columns + here, PAIR)]
    rows = q_ref.shape[0]
    parts = n // heads
    cols = DH // parts
    gt = g_ref[...].T
    vt = v_ref[...].T
    for h in range(2):
        lk = keep_lanes(lk_pair * SCALE, h).astype(BF16)
        lq = keep_lanes(lq_pair * SCALE, h).astype(BF16)
        span = slice(h * LANDMARKS, (h + 1) * LANDMARKS)
        top = None
        for c in range(0, rows, CHUNK):
            part = slice(c, c + CHUNK)
            sb = dot(k_ref[part, :], lq, NT)
            score_ref[part, :] = sb
            high = fold(sb, jnp.max)
            top = high if top is None else jnp.maximum(top, high)
            sf = dot(q_ref[part, :], lk, NT)
            e = jnp.exp(sf - jnp.max(sf, axis=1, keepdims=True))
            fb_ref[part, span] = (e * (1.0 / jnp.sum(e, axis=1, keepdims=True))).astype(BF16)
        top = jnp.max(top, axis=0, keepdims=True).astype(BF16).astype(F32)
        total = None
        for c in range(0, rows, CHUNK):
            part = slice(c, c + CHUNK)
            p = jnp.exp(score_ref[part, :] - top)
            add = fold(p, jnp.sum)
            total = add if total is None else total + add
            pb_ref[part, span] = p.astype(BF16)
        total = jnp.sum(total, axis=0, keepdims=True)
        top_ref[0, h : h + 1, :] = top
        grads = dot(gt[h * DH : (h + 1) * DH], fb_ref[:, span])
        vals = dot(vt[h * DH : (h + 1) * DH], pb_ref[:, span])
        high, low = halves(total)
        extra = three_rows(top, high.astype(F32), low.astype(F32))
        for p in range(parts):
            cut = slice(p * cols, (p + 1) * cols)
            message_ref[(2 * pair + h) * parts + p] = jnp.concatenate(
                [vals[cut], grads[cut], extra], axis=0
            ).astype(BF16)

    @pl.when(pair == pl.num_programs(0) - 1)
    def _():
        for m in range(size):
            for t in range(n // size):
                out_refs[m][t] = message_ref[(t * size + m) ^ me_ref[0]]


def merge(items, cols):
    tops = [item[2 * cols : 2 * cols + 1] for item in items]
    peak = functools.reduce(jnp.maximum, tops)
    vals = grads = total = 0.0
    for item, top in zip(items, tops):
        factor = jnp.exp(top - peak)
        vals = vals + item[:cols] * factor
        grads = grads + item[cols : 2 * cols]
        total = total + (
            item[2 * cols + 1 : 2 * cols + 2] + item[2 * cols + 2 : 2 * cols + 3]
        ) * factor
    return vals, grads, peak, total


def three_rows(first, second, third):
    row = lax.broadcasted_iota(jnp.int32, (EXTRA, LANDMARKS), 0)
    return jnp.where(row == 0, first, jnp.where(row == 1, second, jnp.where(row == 2, third, 0.0)))


def merge_kernel(cols, count, *refs):
    in_refs, out_refs = refs[:count], refs[count:]
    following = len(out_refs)
    for t in range(in_refs[0].shape[0]):
        vals, grads, peak, total = merge([ref[t].astype(F32) for ref in in_refs], cols)
        high, low = halves(total)
        extra = three_rows(peak, high.astype(F32), low.astype(F32))
        out_refs[t % following][t // following] = jnp.concatenate(
            [vals, grads, extra], axis=0
        ).astype(BF16)


def mix_kernel(cols, count, *refs):
    in_refs, z_ref = refs[:count], refs[count]
    reply_ref, values_ref, grads_ref = refs[count + 1 :]
    vals, grads, peak, total = merge([ref[0].astype(F32) for ref in in_refs], cols)
    inverse = halves(z_ref[0])
    values = vals / total
    mixer = dot_exact(halves(values), inverse, NT)
    norm = dot_exact(halves(grads), inverse) / total
    high, low = halves(jnp.sum(norm * values, axis=0, keepdims=True))
    extra = three_rows(peak, high.astype(F32), low.astype(F32))
    reply_ref[0] = jnp.concatenate([mixer, norm, extra], axis=0).astype(BF16)
    values_ref[...] = values
    grads_ref[...] = grads


def soft_rows(scores):
    e = jnp.exp(scores - jnp.max(scores, axis=1, keepdims=True))
    return e / jnp.sum(e, axis=1, keepdims=True)


def eye():
    shape = (LANDMARKS, LANDMARKS)
    same = lax.broadcasted_iota(jnp.int32, shape, 0) == lax.broadcasted_iota(jnp.int32, shape, 1)
    return same.astype(F32)


def column_top(amat):
    return jnp.max(jnp.sum(amat, axis=0, keepdims=True), axis=1, keepdims=True)


def newton_kernel(own_ref, lq_ref, lk_ref, saved_ref, z_ref):
    which = own_ref[1]
    amat = soft_rows(dot(keep_lanes(lq_ref[...] * SCALE, which).astype(BF16), lk_ref[...], NT))
    saved_ref[0] = amat
    current = amat.T / column_top(amat)
    ident = eye()
    amat = halves(amat)
    for i in range(ITERS):
        saved_ref[1 + 4 * i] = current
        z = halves(current)
        x_full = dot_exact(amat, z)
        saved_ref[2 + 4 * i] = x_full
        x = halves(x_full)
        inner = 15.0 * ident - dot_exact(x, halves(7.0 * ident - x_full))
        saved_ref[3 + 4 * i] = inner
        inner = 13.0 * ident - dot_exact(x, halves(inner))
        saved_ref[4 + 4 * i] = inner
        current = 0.25 * dot_exact(z, halves(inner))
    z_ref[0] = current


def newton_grad_kernel(own_ref, saved_ref, values_ref, grads_ref, lq_ref, lk_ref, q_ref, k_ref):
    which = own_ref[1]
    ident = eye()
    amat = saved_ref[0]
    amat_t = turned(halves(amat))
    grad_z = dot_exact(halves(grads_ref[...]), halves(values_ref[...]), TN)
    grad_a = jnp.zeros_like(amat)
    for i in reversed(range(ITERS)):
        z = halves(saved_ref[1 + 4 * i])
        x_full = saved_ref[2 + 4 * i]
        x_t = turned(halves(x_full))
        first = halves(7.0 * ident - x_full)
        second = halves(saved_ref[3 + 4 * i])
        third = halves(saved_ref[4 + 4 * i])
        dz = halves(0.25 * grad_z)
        d_third = halves(dot_exact(turned(z), dz))
        d_second = halves(-dot_exact(x_t, d_third))
        d_x = -dot_exact(d_third, second, NT) - dot_exact(d_second, first, NT)
        d_x = halves(d_x + dot_exact(x_t, d_second))
        grad_a = grad_a + dot_exact(d_x, z, NT)
        grad_z = dot_exact(dz, third, NT) + dot_exact(amat_t, d_x)
    grad_a = grad_a + grad_z.T / column_top(amat)
    grad_s = amat * (grad_a - jnp.sum(amat * grad_a, axis=1, keepdims=True)) * SCALE
    high, low = halves(grad_s)
    lq = keep_lanes(lq_ref[...], which)
    lk = keep_lanes(lk_ref[...], which)
    q_ref[...] = dot(high, lk) + dot(low, lk)
    k_ref[...] = dot(high.T, lq) + dot(low.T, lq)


def attend_kernel(n, heads, me_ref, fb_ref, top_ref, cot_ref, *refs):
    size = bit_groups(n)[-1][1]
    parts = n // heads
    cols = DH // parts
    reply_refs = refs[:size]
    attn_ref, mixer_ref, norm_ref, center_ref = refs[size : size + 4]
    out_refs = refs[size + 4 : 2 * size + 4]
    w_ref, d_ref, e_ref, sum_ref, all_ref = refs[2 * size + 4 :]
    pair = pl.program_id(0)

    @pl.when(pair == 0)
    def _():
        for m in range(size):
            for t in range(n // size):
                reply = reply_refs[m][t].astype(F32)
                at = (t * size + m) ^ me_ref[0]
                w_ref[at] = reply[:cols]
                d_ref[at] = reply[cols : 2 * cols]
                e_ref[at] = reply[2 * cols : 2 * cols + 8]
        for h in range(heads):
            cut = slice(h * parts, (h + 1) * parts)
            span = slice(h * DH, (h + 1) * DH)
            mixer_ref[span, :] = w_ref[cut].reshape(DH, LANDMARKS).astype(BF16)
            extra = e_ref[cut]
            top = top_ref[h // 2, h % 2 : h % 2 + 1, :]
            factor = jnp.exp(top - extra[0, 0:1, :])
            norm_ref[span, :] = (d_ref[cut].reshape(DH, LANDMARKS) * factor).astype(BF16)
            sums = jnp.sum(extra, axis=0)
            center_ref[h : h + 1, :] = (sums[1:2] + sums[2:3]) * factor

    mixer = mixer_ref[pl.ds(pl.multiple_of(pair * PAIR, PAIR), PAIR), :]
    attn = dot(fb_ref[:, :LANDMARKS], keep_rows(mixer, 0), NT) + dot(
        fb_ref[:, LANDMARKS:], keep_rows(mixer, 1), NT
    )
    attn = attn.astype(BF16)
    attn_ref[...] = attn
    all_ref[pl.ds(pl.multiple_of(pair * PAIR, PAIR), PAIR), :] = attn.T

    @pl.when(pair == pl.num_programs(0) - 1)
    def _():
        block, split = sum_ref.shape[1], n // sum_ref.shape[0]
        width = cot_ref.shape[1]
        sum_ref[...] = dot(all_ref[...], cot_ref[...]).reshape(sum_ref.shape)
        for m in range(size):
            for t in range(n // size):
                at = (t * size + m) ^ me_ref[0]
                if split == 1:
                    out_refs[m][t] = sum_ref[at].astype(BF16)
                else:
                    side = pl.multiple_of((at % split) * (width // split), width // split)
                    out_refs[m][t] = sum_ref[at // split, :, pl.ds(side, width // split)].astype(BF16)


def query_kernel(own_ref, q_ref, g_ref, fb_ref, lk_ref, mixer_ref, more_ref, out_ref, land_ref, ds_ref):
    rows = q_ref.shape[0]
    lk = lk_ref[...] * SCALE
    for h in range(2):
        span = slice(h * LANDMARKS, (h + 1) * LANDMARKS)
        mixer = keep_rows(mixer_ref[...], h)
        for c in range(0, rows, CHUNK):
            part = slice(c, c + CHUNK)
            f = fb_ref[part, span].astype(F32)
            df = dot(g_ref[part, :], mixer)
            ds_ref[part, span] = (f * (df - jnp.sum(f * df, axis=1, keepdims=True))).astype(BF16)
    out_ref[...] = (
        dot(ds_ref[:, :LANDMARKS], keep_lanes(lk, 0).astype(BF16))
        + dot(ds_ref[:, LANDMARKS:], keep_lanes(lk, 1).astype(BF16))
    ).astype(BF16)
    qt = q_ref[...].T
    sums = jnp.concatenate(
        [dot(qt[:DH], ds_ref[:, :LANDMARKS]), dot(qt[DH:], ds_ref[:, LANDMARKS:])], axis=0
    )
    here = (own_ref[0] == pl.program_id(0)).astype(F32)
    land_ref[...] = (sums.T * SCALE + more_ref[...] * here).astype(BF16)


def key_kernel(own_ref, k_ref, v_ref, pb_ref, lq_ref, norm_ref, center_ref, more_ref, other_ref, *refs):
    out_ref, value_ref = refs[:2]
    out_refs, (land_ref, ds_ref) = refs[2:-2], refs[-2:]
    size = len(out_refs)
    columns = other_ref.shape[1]
    pair = pl.program_id(0)
    rows = k_ref.shape[0]
    lq = lq_ref[...] * SCALE
    for h in range(2):
        span = slice(h * LANDMARKS, (h + 1) * LANDMARKS)
        norm = keep_rows(norm_ref[...], h)
        center = center_ref[pl.ds(2 * pair + h, 1), :]
        for c in range(0, rows, CHUNK):
            part = slice(c, c + CHUNK)
            dp = dot(v_ref[part, :], norm)
            ds_ref[part, span] = (pb_ref[part, span].astype(F32) * (dp - center)).astype(BF16)
    out_ref[...] = (
        dot(ds_ref[:, :LANDMARKS], keep_lanes(lq, 0).astype(BF16))
        + dot(ds_ref[:, LANDMARKS:], keep_lanes(lq, 1).astype(BF16))
    ).astype(BF16)
    value_ref[...] = (
        dot(pb_ref[:, :LANDMARKS], keep_rows(norm_ref[...], 0), NT)
        + dot(pb_ref[:, LANDMARKS:], keep_rows(norm_ref[...], 1), NT)
    ).astype(BF16)
    kt = k_ref[...].T
    sums = jnp.concatenate(
        [dot(kt[:DH], ds_ref[:, :LANDMARKS]), dot(kt[DH:], ds_ref[:, LANDMARKS:])], axis=0
    )
    here = (own_ref[0] == pair).astype(F32)
    land_ref[:, pl.ds(pl.multiple_of(pair * PAIR, PAIR), PAIR)] = (
        sums.T * SCALE + more_ref[...] * here
    ).astype(BF16)

    @pl.when(pair == pl.num_programs(0) - 1)
    def _():
        for m in range(size):
            held, height, _ = out_refs[m].shape
            for t in range(held):
                at = pl.multiple_of(((t * size + m) ^ own_ref[2]) * height, height)
                out_refs[m][t, :, :columns] = land_ref[pl.ds(at, height), :]
                out_refs[m][t, :, columns:] = other_ref[pl.ds(at, height), :]


def part_kernel(_, attn_ref, weight_ref, out_ref):
    out_ref[...] = dot(attn_ref[...], weight_ref[...]).astype(BF16)


def mixed_kernel(_, attn_ref, weight_ref, other_ref, out_ref):
    out_ref[...] = (dot(attn_ref[...], weight_ref[...]) + other_ref[...].astype(F32)).astype(BF16)


def unpack_kernel(split, me_ref, *refs):
    in_refs, (out_ref, wide_ref, sems) = refs[:-3], refs[-3:]
    size = len(in_refs)
    held, block, width = in_refs[0].shape
    copies = []
    for t in range(held):
        for m in range(size):
            slot = t * size + m
            at = slot ^ me_ref[0]
            row = pl.ds(pl.multiple_of((at // split) * block, block), block)
            if split == 1:
                target = out_ref.at[row]
            else:
                target = out_ref.at[row, pl.ds(pl.multiple_of((at % split) * width, width), width)]
            wide_ref[slot] = in_refs[m][t].astype(F32)
            copies.append(pltpu.make_async_copy(wide_ref.at[slot], target, sems.at[slot]))
            copies[-1].start()
    for copy in copies:
        copy.wait()


def held_in_hbm(x):
    return pltpu.with_memory_space_constraint(x, pltpu.HBM)


def whole(shape):
    return pl.BlockSpec(shape, lambda *_: (0,) * len(shape))


def shape_of(shape, dtype):
    return jax.ShapeDtypeStruct(shape, dtype)


def call(kernel, grid, scalars, ins, in_specs, outs, out_specs, scratch=(), flops=0, name=None, aliases={}):
    return pl.pallas_call(
        kernel,
        grid_spec=pltpu.PrefetchScalarGridSpec(
            num_scalar_prefetch=len(scalars),
            grid=grid,
            in_specs=in_specs,
            out_specs=out_specs,
            scratch_shapes=list(scratch),
        ),
        out_shape=outs,
        compiler_params=PARAMS,
        input_output_aliases=aliases,
        cost_estimate=pl.CostEstimate(flops=flops, bytes_accessed=4 << 20, transcendentals=0),
        name=name,
    )(*scalars, *ins)


def local(queries, key_rows, value_rows, out_weight, cotangent):
    rows, columns = queries.shape
    width = out_weight.shape[1]
    heads = columns // DH
    pairs = columns // PAIR
    n = lax.axis_size("seq")
    me = lax.axis_index("seq")
    mine = lax.axis_index("head")
    land_dev = LANDMARKS // n
    seg_len = rows // land_dev
    parts = n // heads
    cols = DH // parts
    size = bit_groups(n)[-1][1]
    height = 2 * cols + EXTRA
    own_head = me // parts
    own_arr = jnp.stack([own_head // 2, own_head % 2, me * 0 if land_dev % 16 else me]).astype(jnp.int32)

    steps = 4
    in_hbm = pl.BlockSpec(memory_space=pltpu.HBM)
    own = call(
        functools.partial(means_kernel, seg_len),
        (1,),
        [],
        [held_in_hbm(queries), held_in_hbm(key_rows)],
        [in_hbm, in_hbm],
        shape_of((land_dev, 2 * columns), BF16),
        whole((land_dev, 2 * columns)),
        [
            pltpu.VMEM((2, rows, columns), BF16),
            pltpu.VMEM((land_dev, 2 * columns), F32),
            pltpu.SemaphoreType.DMA((2, steps)),
        ],
        name="means",
    )
    grad_attn = dot(cotangent, out_weight, NT).astype(BF16)
    sorted_here = land_dev % 16 == 0
    if sorted_here:
        lands = gather_lists(own, n)
    else:
        lands = [gather_ordered(own, n, me).reshape(LANDMARKS // 16, 16, 2 * columns)]
    me_arr = jnp.stack([me, me if sorted_here else me * 0]).astype(jnp.int32)

    token_pair = pl.BlockSpec((rows, PAIR), lambda j, *_: (0, j))
    factor_pair = pl.BlockSpec((rows, 2 * LANDMARKS), lambda j, *_: (0, j))
    lq_pair = pl.BlockSpec((LANDMARKS, PAIR), lambda j, *_: (0, j))
    lk_pair = pl.BlockSpec((LANDMARKS, PAIR), lambda j, *_: (0, j + pairs))
    factors = pltpu.HBM((rows, heads * LANDMARKS), BF16)
    piece = shape_of((n // size, height, LANDMARKS), BF16)

    fb, pb, tops, land, *pieces = call(
        functools.partial(forward_kernel, n, heads, len(lands)),
        (pairs,),
        [me_arr],
        [held_in_hbm(x) for x in (queries, key_rows, value_rows, grad_attn)] + lands,
        [token_pair] * 4 + [whole(lands[0].shape)] * len(lands),
        [
            factors,
            factors,
            shape_of((pairs, 8, LANDMARKS), F32),
            shape_of((LANDMARKS, 2 * columns), BF16),
        ]
        + [piece] * size,
        [
            factor_pair,
            factor_pair,
            pl.BlockSpec((1, 8, LANDMARKS), lambda j, *_: (j, 0, 0)),
            whole((LANDMARKS, 2 * columns)),
        ]
        + [whole(piece.shape)] * size,
        [
            pltpu.VMEM((rows, LANDMARKS), F32),
            pltpu.VMEM((n, height, LANDMARKS), BF16),
        ],
        flops=8 << 30,
        name="forward",
    )

    square = (LANDMARKS, LANDMARKS)
    own_lq = pl.BlockSpec((LANDMARKS, PAIR), lambda i, own: (0, own[0]))
    own_lk = pl.BlockSpec((LANDMARKS, PAIR), lambda i, own: (0, own[0] + pairs))
    kept = pltpu.VMEM((1 + 4 * ITERS,) + square, F32)
    saved, inverse = call(
        newton_kernel,
        (1,),
        [own_arr],
        [land, land],
        [own_lq, own_lk],
        [kept, shape_of((1,) + square, F32)],
        [whole(kept.shape), whole((1,) + square)],
        flops=4 << 30,
        name="newton",
    )

    groups = bit_groups(n)[::-1]
    for step, (shift, count) in enumerate(groups):
        got = [pieces[0]] + [exchange(pieces[m], m << shift, n) for m in range(1, count)]
        specs = [whole(got[0].shape)] * count
        if step == 0:
            got, inverse, saved = lax.optimization_barrier((got, inverse, saved))
        if step + 1 < len(groups):
            following = groups[step + 1][1]
            piece = shape_of((got[0].shape[0] // following, height, LANDMARKS), BF16)
            pieces = call(
                functools.partial(merge_kernel, cols, count),
                (1,),
                [],
                got,
                specs,
                [piece] * following,
                [whole(piece.shape)] * following,
                name="merge",
            )
    small = shape_of((cols, LANDMARKS), F32)
    reply, values, grads = call(
        functools.partial(mix_kernel, cols, count),
        (1,),
        [],
        got + [inverse],
        specs + [whole((1,) + square)],
        [piece, small, small],
        [whole(piece.shape), whole(small.shape), whole(small.shape)],
        name="mix",
    )
    replies = gather_lists(reply[0], n)

    more = shape_of((LANDMARKS, PAIR), F32)
    more_q, more_k = call(
        newton_grad_kernel,
        (1,),
        [own_arr],
        [pltpu.with_memory_space_constraint(saved, pltpu.VMEM), values, grads, land, land],
        [whole(kept.shape), whole(small.shape), whole(small.shape), own_lq, own_lk],
        [more, more],
        [whole(more.shape)] * 2,
        flops=8 << 30,
        name="newton_grad",
    )

    replies, more_q, more_k = lax.optimization_barrier((replies, more_q, more_k))
    block = max(columns // n, 16)
    split = n * block // columns
    flat = shape_of((columns, LANDMARKS), BF16)
    weight_piece = shape_of((n // size, block, width // split), BF16)
    attn, mixer, norm, center, *weight_pieces = call(
        functools.partial(attend_kernel, n, heads),
        (pairs,),
        [me_arr],
        [fb, tops, cotangent] + replies,
        [factor_pair, whole(tops.shape), whole(cotangent.shape)] + [whole(replies[0].shape)] * size,
        [shape_of((rows, columns), BF16), flat, flat, shape_of((heads, LANDMARKS), F32)]
        + [weight_piece] * size,
        [token_pair, whole(flat.shape), whole(flat.shape), whole((heads, LANDMARKS))]
        + [whole(weight_piece.shape)] * size,
        [
            pltpu.VMEM((n, cols, LANDMARKS), F32),
            pltpu.VMEM((n, cols, LANDMARKS), F32),
            pltpu.VMEM((n, 8, LANDMARKS), F32),
            pltpu.VMEM((columns // block, block, width), F32),
            pltpu.VMEM((columns, rows), BF16),
        ],
        flops=4 << 30,
        name="attend",
    )
    (shift, count), later = groups[0], groups[1:]
    weight_sum = scatter_step(weight_pieces, shift, count, n).astype(BF16)
    half = width // 2
    mine_arr = mine.reshape(1).astype(jnp.int32)
    row_block = pl.BlockSpec((rows // 4, columns), lambda j, _: (j, 0))
    half_block = pl.BlockSpec((rows // 4, half), lambda j, _: (j, 0))
    there = call(
        part_kernel,
        (4,),
        [mine_arr],
        [attn, out_weight],
        [row_block, pl.BlockSpec((columns, half), lambda j, mine: (0, 1 - mine[0]))],
        shape_of((rows, half), BF16),
        half_block,
        flops=1 << 30,
        name="part",
    )
    (pb, key_rows, value_rows), weight_sum, there = lax.optimization_barrier(
        ((pb, key_rows, value_rows), weight_sum, there)
    )
    arrived = lax.ppermute(there, "head", [(0, 1), (1, 0)])
    following = later[0][1]
    weight_sum = weight_sum.reshape((-1, following) + weight_sum.shape[1:])
    weight_own = scatter_pieces([weight_sum[:, m] for m in range(following)], n, later)[0].astype(BF16)
    flat_pair = pl.BlockSpec((PAIR, LANDMARKS), lambda j, *_: (j, 0))
    land_pair = pl.BlockSpec((LANDMARKS, PAIR), lambda j, *_: (0, j))
    tokens = shape_of((rows, columns), BF16)
    land_shape = shape_of((LANDMARKS, columns), BF16)
    products = [pltpu.VMEM((rows, 2 * LANDMARKS), BF16)]
    query_f, land_k = call(
        query_kernel,
        (pairs,),
        [own_arr],
        [queries, grad_attn, fb, land, mixer, more_k],
        [token_pair, token_pair, factor_pair, lk_pair, flat_pair, whole(more.shape)],
        [tokens, land_shape],
        [token_pair, land_pair],
        products,
        flops=6 << 30,
        name="query_grad",
    )
    if sorted_here:
        land_piece, count = shape_of((n // size, land_dev, 2 * columns), BF16), size
    else:
        land_piece, count = shape_of((LANDMARKS // 16, 16, 2 * columns), BF16), 1
    key_b, value_grad, *land_pieces = call(
        key_kernel,
        (pairs,),
        [own_arr],
        [key_rows, value_rows, pb, land, norm, center, more_q, land_k],
        [token_pair, token_pair, factor_pair, lq_pair, flat_pair, whole((heads, LANDMARKS))]
        + [whole(more.shape), whole(land_shape.shape)],
        [tokens, tokens] + [land_piece] * count,
        [token_pair, token_pair] + [whole(land_piece.shape)] * count,
        [pltpu.VMEM(land_shape.shape, BF16)] + products,
        flops=6 << 30,
        name="key_grad",
    )
    if not sorted_here:
        land_pieces = split_by_partner(land_pieces[0].reshape(n, land_dev, 2 * columns), n, me)
    mixed = call(
        mixed_kernel,
        (4,),
        [mine_arr],
        [attn, out_weight, arrived],
        [row_block, pl.BlockSpec((columns, half), lambda j, mine: (0, mine[0])), half_block],
        shape_of((rows, half), BF16),
        half_block,
        flops=1 << 30,
        name="mixed",
    )
    weights = gather_first(weight_own, n)
    (shift, count), later = groups[0], groups[1:]
    land_sum = scatter_step(land_pieces, shift, count, n).astype(BF16)
    weights, land_sum, mixed = lax.optimization_barrier((weights, land_sum, mixed))
    weights = gather_rest(weights, n)
    land_sum = land_sum.reshape((-1, following) + land_sum.shape[1:])
    land_own = scatter_pieces([land_sum[:, m] for m in range(following)], n, later)[0] * (1.0 / seg_len)

    def finish(token_part, land_part):
        return (
            (token_part.reshape(land_dev, seg_len, columns) + land_part[:, None, :])
            .astype(BF16)
            .reshape(rows, columns)
        )

    weight_grad = call(
        functools.partial(unpack_kernel, split),
        (1,),
        [me_arr],
        weights,
        [whole(weights[0].shape)] * size,
        pltpu.HBM((columns, width), F32),
        in_hbm,
        [pltpu.VMEM((n,) + weights[0].shape[1:], F32), pltpu.SemaphoreType.DMA((n,))],
        name="unpack",
    )
    query_grad = finish(query_f, land_own[:, :columns])
    key_grad = finish(key_b, land_own[:, columns:])
    return (mixed, query_grad, key_grad, value_grad, weight_grad)


def solution(mesh):
    return jax.shard_map(
        local,
        mesh=mesh,
        in_specs=(
            P("seq", "head"),
            P("seq", "head"),
            P("seq", "head"),
            P("head", None),
            P("seq", None),
        ),
        out_specs=(
            P("seq", "head"),
            P("seq", "head"),
            P("seq", "head"),
            P("seq", "head"),
            P("head", None),
        ),
        check_vma=False,
    )
```

```python
import functools

import jax
import jax.numpy as jnp
from jax import lax
from jax.experimental import pallas as pl
from jax.experimental.pallas import tpu as pltpu
from jax.sharding import PartitionSpec as P

DH = 64
PAIR = 2 * DH
LANDMARKS = 256
ITERS = 2
SCALE = 0.125
CHUNK = 256
EXTRA = 8
F32 = jnp.float32
BF16 = jnp.bfloat16
PARAMS = pltpu.CompilerParams(vmem_limit_bytes=24 * 1024 * 1024)


def dot(left, right, dims=((1,), (0,))):
    return lax.dot_general(left, right, (dims, ((), ())), preferred_element_type=F32)


NT = ((1,), (1,))
TN = ((0,), (0,))


def halves(value):
    high = value.astype(BF16)
    return high, (value - high.astype(F32)).astype(BF16)


def dot_exact(left, right, dims=((1,), (0,))):
    return dot(left[0], right[0], dims) + (
        dot(left[0], right[1], dims) + dot(left[1], right[0], dims)
    )


def turned(pair):
    return pair[0].T, pair[1].T


def keep_rows(block, which):
    rows = lax.broadcasted_iota(jnp.int32, block.shape, 0) // DH
    return jnp.where(rows == which, block, jnp.zeros_like(block))


def keep_lanes(block, which):
    lanes = lax.broadcasted_iota(jnp.int32, block.shape, 1) // DH
    return jnp.where(lanes == which, block, jnp.zeros_like(block))


def fold(block, op):
    parts = block.reshape(block.shape[0] // 8, 8, block.shape[1])
    return op(parts, axis=0)


def exchange(block, mask, n):
    return lax.ppermute(block, "seq", [(i, i ^ mask) for i in range(n)])


def bit_groups(n):
    bits = n.bit_length() - 1
    groups = []
    while bits > 0:
        take = 2 if bits % 2 == 0 else 1
        bits -= take
        groups.append((bits, 1 << take))
    return groups


def gather_first(block, n):
    shift, size = bit_groups(n)[0]
    held = block[None]
    return [held] + [exchange(held, m << shift, n) for m in range(1, size)]


def gather_rest(got, n):
    for shift, size in bit_groups(n)[1:]:
        held = jnp.stack(got, axis=1).reshape((-1,) + got[0].shape[1:])
        got = [held] + [exchange(held, m << shift, n) for m in range(1, size)]
    return got


def gather_lists(block, n):
    return gather_rest(gather_first(block, n), n)


def gather_ordered(block, n, me):
    got = gather_lists(block, n)
    held = jnp.stack(got, axis=1).reshape((n,) + block.shape)
    return held.at[jnp.arange(n) ^ me].get(mode="promise_in_bounds")


def split_by_partner(blocks, n, me):
    size = bit_groups(n)[-1][1]
    return [
        blocks.at[(jnp.arange(n // size) * size + m) ^ me].get(mode="promise_in_bounds")
        for m in range(size)
    ]


def scatter_step(pieces, shift, size, n):
    got = [pieces[0]] + [exchange(pieces[m], m << shift, n) for m in range(1, size)]
    return sum(part.astype(F32) for part in got)


def scatter_pieces(pieces, n, groups):
    for step, (shift, size) in enumerate(groups):
        held = scatter_step(pieces, shift, size, n)
        if step + 1 < len(groups):
            following = groups[step + 1][1]
            held = held.astype(BF16).reshape((-1, following) + held.shape[1:])
            pieces = [held[:, m] for m in range(following)]
    return held


def means_kernel(seg_len, q_ref, k_ref, out_ref, in_ref, sum_ref, sems):
    rows, columns = q_ref.shape
    steps = sems.shape[1]
    height = rows // steps
    copies = {}
    for c in range(steps):
        part = pl.ds(c * height, height)
        for side, ref in enumerate((q_ref, k_ref)):
            copies[side, c] = pltpu.make_async_copy(ref.at[part], in_ref.at[side, part], sems.at[side, c])
            copies[side, c].start()
    for c in range(steps):
        for side in range(2):
            copies[side, c].wait()
            span = slice(side * columns, (side + 1) * columns)
            for s in range(c * height // seg_len, (c + 1) * height // seg_len):
                total = fold(in_ref[side, s * seg_len : (s + 1) * seg_len, :].astype(F32), jnp.sum)
                sum_ref[s : s + 1, span] = jnp.sum(total, axis=0, keepdims=True)
    out_ref[...] = (sum_ref[...] * (1.0 / seg_len)).astype(BF16)


def forward_kernel(n, heads, count, me_ref, q_ref, k_ref, v_ref, g_ref, *refs):
    size = bit_groups(n)[-1][1]
    in_refs = refs[:count]
    fb_ref, pb_ref, top_ref, land_ref = refs[count : count + 4]
    out_refs = refs[count + 4 : count + 4 + size]
    score_ref, message_ref = refs[count + 4 + size :]
    pair = pl.program_id(0)
    columns = land_ref.shape[1] // 2

    @pl.when(pair == 0)
    def _():
        for m in range(count):
            held, height, _ = in_refs[m].shape
            for t in range(held):
                at = pl.multiple_of(((t * count + m) ^ me_ref[1]) * height, height)
                land_ref[pl.ds(at, height), :] = in_refs[m][t]

    here = pl.multiple_of(pair * PAIR, PAIR)
    lq_pair = land_ref[:, pl.ds(here, PAIR)]
    lk_pair = land_ref[:, pl.ds(columns + here, PAIR)]
    rows = q_ref.shape[0]
    parts = n // heads
    cols = DH // parts
    gt = g_ref[...].T
    vt = v_ref[...].T
    for h in range(2):
        lk = keep_lanes(lk_pair * SCALE, h).astype(BF16)
        lq = keep_lanes(lq_pair * SCALE, h).astype(BF16)
        span = slice(h * LANDMARKS, (h + 1) * LANDMARKS)
        top = None
        for c in range(0, rows, CHUNK):
            part = slice(c, c + CHUNK)
            sb = dot(k_ref[part, :], lq, NT)
            score_ref[part, :] = sb
            high = fold(sb, jnp.max)
            top = high if top is None else jnp.maximum(top, high)
            sf = dot(q_ref[part, :], lk, NT)
            e = jnp.exp(sf - jnp.max(sf, axis=1, keepdims=True))
            fb_ref[part, span] = (e * (1.0 / jnp.sum(e, axis=1, keepdims=True))).astype(BF16)
        top = jnp.max(top, axis=0, keepdims=True).astype(BF16).astype(F32)
        total = None
        for c in range(0, rows, CHUNK):
            part = slice(c, c + CHUNK)
            p = jnp.exp(score_ref[part, :] - top)
            add = fold(p, jnp.sum)
            total = add if total is None else total + add
            pb_ref[part, span] = p.astype(BF16)
        total = jnp.sum(total, axis=0, keepdims=True)
        top_ref[0, h : h + 1, :] = top
        grads = dot(gt[h * DH : (h + 1) * DH], fb_ref[:, span])
        vals = dot(vt[h * DH : (h + 1) * DH], pb_ref[:, span])
        high, low = halves(total)
        extra = three_rows(top, high.astype(F32), low.astype(F32))
        for p in range(parts):
            cut = slice(p * cols, (p + 1) * cols)
            message_ref[(2 * pair + h) * parts + p] = jnp.concatenate(
                [vals[cut], grads[cut], extra], axis=0
            ).astype(BF16)

    @pl.when(pair == pl.num_programs(0) - 1)
    def _():
        for m in range(size):
            for t in range(n // size):
                out_refs[m][t] = message_ref[(t * size + m) ^ me_ref[0]]


def merge(items, cols):
    tops = [item[2 * cols : 2 * cols + 1] for item in items]
    peak = functools.reduce(jnp.maximum, tops)
    vals = grads = total = 0.0
    for item, top in zip(items, tops):
        factor = jnp.exp(top - peak)
        vals = vals + item[:cols] * factor
        grads = grads + item[cols : 2 * cols]
        total = total + (
            item[2 * cols + 1 : 2 * cols + 2] + item[2 * cols + 2 : 2 * cols + 3]
        ) * factor
    return vals, grads, peak, total


def three_rows(first, second, third):
    row = lax.broadcasted_iota(jnp.int32, (EXTRA, LANDMARKS), 0)
    return jnp.where(row == 0, first, jnp.where(row == 1, second, jnp.where(row == 2, third, 0.0)))


def merge_kernel(cols, count, *refs):
    in_refs, out_refs = refs[:count], refs[count:]
    following = len(out_refs)
    for t in range(in_refs[0].shape[0]):
        vals, grads, peak, total = merge([ref[t].astype(F32) for ref in in_refs], cols)
        high, low = halves(total)
        extra = three_rows(peak, high.astype(F32), low.astype(F32))
        out_refs[t % following][t // following] = jnp.concatenate(
            [vals, grads, extra], axis=0
        ).astype(BF16)


def mix_kernel(cols, count, *refs):
    in_refs, z_ref = refs[:count], refs[count]
    reply_ref, values_ref, grads_ref = refs[count + 1 :]
    vals, grads, peak, total = merge([ref[0].astype(F32) for ref in in_refs], cols)
    inverse = halves(z_ref[0])
    values = vals / total
    mixer = dot_exact(halves(values), inverse, NT)
    norm = dot_exact(halves(grads), inverse) / total
    high, low = halves(jnp.sum(norm * values, axis=0, keepdims=True))
    extra = three_rows(peak, high.astype(F32), low.astype(F32))
    reply_ref[0] = jnp.concatenate([mixer, norm, extra], axis=0).astype(BF16)
    values_ref[...] = values
    grads_ref[...] = grads


def soft_rows(scores):
    e = jnp.exp(scores - jnp.max(scores, axis=1, keepdims=True))
    return e / jnp.sum(e, axis=1, keepdims=True)


def eye():
    shape = (LANDMARKS, LANDMARKS)
    same = lax.broadcasted_iota(jnp.int32, shape, 0) == lax.broadcasted_iota(jnp.int32, shape, 1)
    return same.astype(F32)


def column_top(amat):
    return jnp.max(jnp.sum(amat, axis=0, keepdims=True), axis=1, keepdims=True)


def newton_kernel(own_ref, lq_ref, lk_ref, saved_ref, z_ref):
    which = own_ref[1]
    amat = soft_rows(dot(keep_lanes(lq_ref[...] * SCALE, which).astype(BF16), lk_ref[...], NT))
    saved_ref[0] = amat
    current = amat.T / column_top(amat)
    ident = eye()
    amat = halves(amat)
    for i in range(ITERS):
        saved_ref[1 + 4 * i] = current
        z = halves(current)
        x_full = dot_exact(amat, z)
        saved_ref[2 + 4 * i] = x_full
        x = halves(x_full)
        inner = 15.0 * ident - dot_exact(x, halves(7.0 * ident - x_full))
        saved_ref[3 + 4 * i] = inner
        inner = 13.0 * ident - dot_exact(x, halves(inner))
        saved_ref[4 + 4 * i] = inner
        current = 0.25 * dot_exact(z, halves(inner))
    z_ref[0] = current


def newton_grad_kernel(own_ref, saved_ref, values_ref, grads_ref, lq_ref, lk_ref, q_ref, k_ref):
    which = own_ref[1]
    ident = eye()
    amat = saved_ref[0]
    amat_t = turned(halves(amat))
    grad_z = dot_exact(halves(grads_ref[...]), halves(values_ref[...]), TN)
    grad_a = jnp.zeros_like(amat)
    for i in reversed(range(ITERS)):
        z = halves(saved_ref[1 + 4 * i])
        x_full = saved_ref[2 + 4 * i]
        x_t = turned(halves(x_full))
        first = halves(7.0 * ident - x_full)
        second = halves(saved_ref[3 + 4 * i])
        third = halves(saved_ref[4 + 4 * i])
        dz = halves(0.25 * grad_z)
        d_third = halves(dot_exact(turned(z), dz))
        d_second = halves(-dot_exact(x_t, d_third))
        d_x = -dot_exact(d_third, second, NT) - dot_exact(d_second, first, NT)
        d_x = halves(d_x + dot_exact(x_t, d_second))
        grad_a = grad_a + dot_exact(d_x, z, NT)
        grad_z = dot_exact(dz, third, NT) + dot_exact(amat_t, d_x)
    grad_a = grad_a + grad_z.T / column_top(amat)
    grad_s = amat * (grad_a - jnp.sum(amat * grad_a, axis=1, keepdims=True)) * SCALE
    high, low = halves(grad_s)
    lq = keep_lanes(lq_ref[...], which)
    lk = keep_lanes(lk_ref[...], which)
    q_ref[...] = dot(high, lk) + dot(low, lk)
    k_ref[...] = dot(high.T, lq) + dot(low.T, lq)


def attend_kernel(n, heads, me_ref, fb_ref, top_ref, cot_ref, *refs):
    size = bit_groups(n)[-1][1]
    parts = n // heads
    cols = DH // parts
    reply_refs = refs[:size]
    attn_ref, mixer_ref, norm_ref, center_ref = refs[size : size + 4]
    out_refs = refs[size + 4 : 2 * size + 4]
    w_ref, d_ref, e_ref, sum_ref, all_ref = refs[2 * size + 4 :]
    pair = pl.program_id(0)

    @pl.when(pair == 0)
    def _():
        for m in range(size):
            for t in range(n // size):
                reply = reply_refs[m][t].astype(F32)
                at = (t * size + m) ^ me_ref[0]
                w_ref[at] = reply[:cols]
                d_ref[at] = reply[cols : 2 * cols]
                e_ref[at] = reply[2 * cols : 2 * cols + 8]
        for h in range(heads):
            cut = slice(h * parts, (h + 1) * parts)
            span = slice(h * DH, (h + 1) * DH)
            mixer_ref[span, :] = w_ref[cut].reshape(DH, LANDMARKS).astype(BF16)
            extra = e_ref[cut]
            top = top_ref[h // 2, h % 2 : h % 2 + 1, :]
            factor = jnp.exp(top - extra[0, 0:1, :])
            norm_ref[span, :] = (d_ref[cut].reshape(DH, LANDMARKS) * factor).astype(BF16)
            sums = jnp.sum(extra, axis=0)
            center_ref[h : h + 1, :] = (sums[1:2] + sums[2:3]) * factor

    mixer = mixer_ref[pl.ds(pl.multiple_of(pair * PAIR, PAIR), PAIR), :]
    attn = dot(fb_ref[:, :LANDMARKS], keep_rows(mixer, 0), NT) + dot(
        fb_ref[:, LANDMARKS:], keep_rows(mixer, 1), NT
    )
    attn = attn.astype(BF16)
    attn_ref[...] = attn
    all_ref[pl.ds(pl.multiple_of(pair * PAIR, PAIR), PAIR), :] = attn.T

    @pl.when(pair == pl.num_programs(0) - 1)
    def _():
        block, split = sum_ref.shape[1], n // sum_ref.shape[0]
        width = cot_ref.shape[1]
        sum_ref[...] = dot(all_ref[...], cot_ref[...]).reshape(sum_ref.shape)
        for m in range(size):
            for t in range(n // size):
                at = (t * size + m) ^ me_ref[0]
                if split == 1:
                    out_refs[m][t] = sum_ref[at].astype(BF16)
                else:
                    side = pl.multiple_of((at % split) * (width // split), width // split)
                    out_refs[m][t] = sum_ref[at // split, :, pl.ds(side, width // split)].astype(BF16)


def query_kernel(own_ref, q_ref, g_ref, fb_ref, lk_ref, mixer_ref, more_ref, out_ref, land_ref, ds_ref):
    rows = q_ref.shape[0]
    lk = lk_ref[...] * SCALE
    for h in range(2):
        span = slice(h * LANDMARKS, (h + 1) * LANDMARKS)
        mixer = keep_rows(mixer_ref[...], h)
        for c in range(0, rows, CHUNK):
            part = slice(c, c + CHUNK)
            f = fb_ref[part, span].astype(F32)
            df = dot(g_ref[part, :], mixer)
            ds_ref[part, span] = (f * (df - jnp.sum(f * df, axis=1, keepdims=True))).astype(BF16)
    out_ref[...] = (
        dot(ds_ref[:, :LANDMARKS], keep_lanes(lk, 0).astype(BF16))
        + dot(ds_ref[:, LANDMARKS:], keep_lanes(lk, 1).astype(BF16))
    ).astype(BF16)
    qt = q_ref[...].T
    sums = jnp.concatenate(
        [dot(qt[:DH], ds_ref[:, :LANDMARKS]), dot(qt[DH:], ds_ref[:, LANDMARKS:])], axis=0
    )
    here = (own_ref[0] == pl.program_id(0)).astype(F32)
    land_ref[...] = (sums.T * SCALE + more_ref[...] * here).astype(BF16)


def key_half_kernel(
    first, own_ref, k_ref, v_ref, pb_ref, lq_ref, norm_ref, center_ref, more_ref, *refs
):
    out_ref, value_ref, land_ref, ds_ref = refs[-4:]
    key_pair(first, own_ref, k_ref, v_ref, pb_ref, lq_ref, norm_ref, center_ref, more_ref, out_ref, value_ref, land_ref, ds_ref)


def key_rest_kernel(
    first, own_ref, k_ref, v_ref, pb_ref, lq_ref, norm_ref, center_ref, more_ref, *refs
):
    early_ref, other_ref, _, _, out_ref, value_ref = refs[:6]
    out_refs, (land_ref, ds_ref) = refs[6:-2], refs[-2:]
    size = len(out_refs)
    columns = other_ref.shape[1]
    pair = pl.program_id(0)
    at_pair = pl.ds(pl.multiple_of(pair * PAIR, PAIR), PAIR)
    key_pair(
        first, own_ref, k_ref, v_ref, pb_ref, lq_ref, norm_ref, center_ref, more_ref,
        out_ref, value_ref, land_ref.at[:, at_pair], ds_ref,
    )

    @pl.when(pair == pl.num_programs(0) - 1)
    def _():
        early = early_ref.shape[1]
        for m in range(size):
            held, height, _ = out_refs[m].shape
            for t in range(held):
                at = pl.multiple_of(((t * size + m) ^ own_ref[2]) * height, height)
                out_refs[m][t, :, :early] = early_ref[pl.ds(at, height), :]
                out_refs[m][t, :, early:columns] = land_ref[pl.ds(at, height), :]
                out_refs[m][t, :, columns:] = other_ref[pl.ds(at, height), :]


def key_pair(
    first, own_ref, k_ref, v_ref, pb_ref, lq_ref, norm_ref, center_ref, more_ref, out_ref, value_ref, land_ref, ds_ref
):
    rows = k_ref.shape[0]
    lq = lq_ref[...] * SCALE
    pair = first + pl.program_id(0)
    for h in range(2):
        span = slice(h * LANDMARKS, (h + 1) * LANDMARKS)
        norm = keep_rows(norm_ref[...], h)
        center = center_ref[pl.ds(2 * pair + h, 1), :]
        for c in range(0, rows, CHUNK):
            part = slice(c, c + CHUNK)
            dp = dot(v_ref[part, :], norm)
            ds_ref[part, span] = (pb_ref[part, span].astype(F32) * (dp - center)).astype(BF16)
    out_ref[...] = (
        dot(ds_ref[:, :LANDMARKS], keep_lanes(lq, 0).astype(BF16))
        + dot(ds_ref[:, LANDMARKS:], keep_lanes(lq, 1).astype(BF16))
    ).astype(BF16)
    value_ref[...] = (
        dot(pb_ref[:, :LANDMARKS], keep_rows(norm_ref[...], 0), NT)
        + dot(pb_ref[:, LANDMARKS:], keep_rows(norm_ref[...], 1), NT)
    ).astype(BF16)
    kt = k_ref[...].T
    sums = jnp.concatenate(
        [dot(kt[:DH], ds_ref[:, :LANDMARKS]), dot(kt[DH:], ds_ref[:, LANDMARKS:])], axis=0
    )
    here = (own_ref[0] == pair).astype(F32)
    land_ref[...] = (sums.T * SCALE + more_ref[...] * here).astype(BF16)


def part_kernel(_, attn_ref, weight_ref, out_ref):
    out_ref[...] = dot(attn_ref[...], weight_ref[...]).astype(BF16)


def mixed_kernel(_, attn_ref, weight_ref, other_ref, out_ref):
    out_ref[...] = (dot(attn_ref[...], weight_ref[...]) + other_ref[...].astype(F32)).astype(BF16)


def unpack_kernel(split, me_ref, *refs):
    in_refs, (out_ref, wide_ref, sems) = refs[:-3], refs[-3:]
    size = len(in_refs)
    held, block, width = in_refs[0].shape
    copies = []
    for t in range(held):
        for m in range(size):
            slot = t * size + m
            at = slot ^ me_ref[0]
            row = pl.ds(pl.multiple_of((at // split) * block, block), block)
            if split == 1:
                target = out_ref.at[row]
            else:
                target = out_ref.at[row, pl.ds(pl.multiple_of((at % split) * width, width), width)]
            wide_ref[slot] = in_refs[m][t].astype(F32)
            copies.append(pltpu.make_async_copy(wide_ref.at[slot], target, sems.at[slot]))
            copies[-1].start()
    for copy in copies:
        copy.wait()


def held_in_hbm(x):
    return pltpu.with_memory_space_constraint(x, pltpu.HBM)


def whole(shape):
    return pl.BlockSpec(shape, lambda *_: (0,) * len(shape))


def shape_of(shape, dtype):
    return jax.ShapeDtypeStruct(shape, dtype)


def call(kernel, grid, scalars, ins, in_specs, outs, out_specs, scratch=(), flops=0, name=None, aliases={}):
    return pl.pallas_call(
        kernel,
        grid_spec=pltpu.PrefetchScalarGridSpec(
            num_scalar_prefetch=len(scalars),
            grid=grid,
            in_specs=in_specs,
            out_specs=out_specs,
            scratch_shapes=list(scratch),
        ),
        out_shape=outs,
        compiler_params=PARAMS,
        input_output_aliases=aliases,
        cost_estimate=pl.CostEstimate(flops=flops, bytes_accessed=4 << 20, transcendentals=0),
        name=name,
    )(*scalars, *ins)


def local(queries, key_rows, value_rows, out_weight, cotangent):
    rows, columns = queries.shape
    width = out_weight.shape[1]
    heads = columns // DH
    pairs = columns // PAIR
    n = lax.axis_size("seq")
    me = lax.axis_index("seq")
    mine = lax.axis_index("head")
    land_dev = LANDMARKS // n
    seg_len = rows // land_dev
    parts = n // heads
    cols = DH // parts
    size = bit_groups(n)[-1][1]
    height = 2 * cols + EXTRA
    own_head = me // parts

    sorted_here = land_dev % 16 == 0
    me_arr = jnp.stack([me, me if sorted_here else me * 0]).astype(jnp.int32)
    mine_arr = mine.reshape(1).astype(jnp.int32)
    own_arr = jnp.stack([own_head // 2, own_head % 2, me * 0 if land_dev % 16 else me]).astype(jnp.int32)
    steps = 4
    in_hbm = pl.BlockSpec(memory_space=pltpu.HBM)
    own = call(
        functools.partial(means_kernel, seg_len),
        (1,),
        [],
        [held_in_hbm(queries), held_in_hbm(key_rows)],
        [in_hbm, in_hbm],
        shape_of((land_dev, 2 * columns), BF16),
        whole((land_dev, 2 * columns)),
        [
            pltpu.VMEM((2, rows, columns), BF16),
            pltpu.VMEM((land_dev, 2 * columns), F32),
            pltpu.SemaphoreType.DMA((2, steps)),
        ],
        name="means",
    )
    own, me_arr, mine_arr, own_arr = lax.optimization_barrier((own, me_arr, mine_arr, own_arr))
    grad_attn = dot(cotangent, out_weight, NT).astype(BF16)
    if sorted_here:
        lands = gather_lists(own, n)
    else:
        lands = [gather_ordered(own, n, me).reshape(LANDMARKS // 16, 16, 2 * columns)]

    token_pair = pl.BlockSpec((rows, PAIR), lambda j, *_: (0, j))
    factor_pair = pl.BlockSpec((rows, 2 * LANDMARKS), lambda j, *_: (0, j))
    lq_pair = pl.BlockSpec((LANDMARKS, PAIR), lambda j, *_: (0, j))
    lk_pair = pl.BlockSpec((LANDMARKS, PAIR), lambda j, *_: (0, j + pairs))
    factors = shape_of((rows, heads * LANDMARKS), BF16)
    piece = shape_of((n // size, height, LANDMARKS), BF16)

    fb, pb, tops, land, *pieces = call(
        functools.partial(forward_kernel, n, heads, len(lands)),
        (pairs,),
        [me_arr],
        [queries, key_rows, value_rows, grad_attn] + lands,
        [token_pair] * 4 + [whole(lands[0].shape)] * len(lands),
        [
            factors,
            factors,
            shape_of((pairs, 8, LANDMARKS), F32),
            shape_of((LANDMARKS, 2 * columns), BF16),
        ]
        + [piece] * size,
        [
            factor_pair,
            factor_pair,
            pl.BlockSpec((1, 8, LANDMARKS), lambda j, *_: (j, 0, 0)),
            whole((LANDMARKS, 2 * columns)),
        ]
        + [whole(piece.shape)] * size,
        [
            pltpu.VMEM((rows, LANDMARKS), F32),
            pltpu.VMEM((n, height, LANDMARKS), BF16),
        ],
        flops=8 << 30,
        name="forward",
    )

    square = (LANDMARKS, LANDMARKS)
    own_lq = pl.BlockSpec((LANDMARKS, PAIR), lambda i, own: (0, own[0]))
    own_lk = pl.BlockSpec((LANDMARKS, PAIR), lambda i, own: (0, own[0] + pairs))
    kept = shape_of((1 + 4 * ITERS,) + square, F32)
    saved, inverse = call(
        newton_kernel,
        (1,),
        [own_arr],
        [land, land],
        [own_lq, own_lk],
        [kept, shape_of((1,) + square, F32)],
        [whole(kept.shape), whole((1,) + square)],
        flops=4 << 30,
        name="newton",
    )

    groups = bit_groups(n)[::-1]
    for step, (shift, count) in enumerate(groups):
        got = [pieces[0]] + [exchange(pieces[m], m << shift, n) for m in range(1, count)]
        specs = [whole(got[0].shape)] * count
        if step == 0:
            got, inverse = lax.optimization_barrier((got, inverse))
        if step + 1 < len(groups):
            following = groups[step + 1][1]
            piece = shape_of((got[0].shape[0] // following, height, LANDMARKS), BF16)
            pieces = call(
                functools.partial(merge_kernel, cols, count),
                (1,),
                [],
                got,
                specs,
                [piece] * following,
                [whole(piece.shape)] * following,
                name="merge",
            )
    small = shape_of((cols, LANDMARKS), F32)
    reply, values, grads = call(
        functools.partial(mix_kernel, cols, count),
        (1,),
        [],
        got + [inverse],
        specs + [whole((1,) + square)],
        [piece, small, small],
        [whole(piece.shape), whole(small.shape), whole(small.shape)],
        name="mix",
    )
    replies = gather_lists(reply[0], n)

    more = shape_of((LANDMARKS, PAIR), F32)
    more_q, more_k = call(
        newton_grad_kernel,
        (1,),
        [own_arr],
        [saved, values, grads, land, land],
        [whole(kept.shape), whole(small.shape), whole(small.shape), own_lq, own_lk],
        [more, more],
        [whole(more.shape)] * 2,
        flops=8 << 30,
        name="newton_grad",
    )

    replies, more_q, more_k = lax.optimization_barrier((replies, more_q, more_k))
    block = max(columns // n, 16)
    split = n * block // columns
    flat = shape_of((columns, LANDMARKS), BF16)
    weight_piece = shape_of((n // size, block, width // split), BF16)
    attn, mixer, norm, center, *weight_pieces = call(
        functools.partial(attend_kernel, n, heads),
        (pairs,),
        [me_arr],
        [fb, tops, cotangent] + replies,
        [factor_pair, whole(tops.shape), whole(cotangent.shape)] + [whole(replies[0].shape)] * size,
        [shape_of((rows, columns), BF16), flat, flat, shape_of((heads, LANDMARKS), F32)]
        + [weight_piece] * size,
        [token_pair, whole(flat.shape), whole(flat.shape), whole((heads, LANDMARKS))]
        + [whole(weight_piece.shape)] * size,
        [
            pltpu.VMEM((n, cols, LANDMARKS), F32),
            pltpu.VMEM((n, cols, LANDMARKS), F32),
            pltpu.VMEM((n, 8, LANDMARKS), F32),
            pltpu.VMEM((columns // block, block, width), F32),
            pltpu.VMEM((columns, rows), BF16),
        ],
        flops=4 << 30,
        name="attend",
    )
    (shift, count), later = groups[0], groups[1:]
    weight_sum = scatter_step(weight_pieces, shift, count, n).astype(BF16)
    (pb, key_rows, value_rows), weight_sum = lax.optimization_barrier(
        ((pb, key_rows, value_rows), weight_sum)
    )
    following = later[0][1]
    weight_sum = weight_sum.reshape((-1, following) + weight_sum.shape[1:])
    weight_own = scatter_pieces([weight_sum[:, m] for m in range(following)], n, later)[0].astype(BF16)
    half = width // 2
    row_block = pl.BlockSpec((rows // 4, columns), lambda j, _: (j, 0))
    half_block = pl.BlockSpec((rows // 4, half), lambda j, _: (j, 0))
    there = call(
        part_kernel,
        (4,),
        [mine_arr],
        [attn, out_weight],
        [row_block, pl.BlockSpec((columns, half), lambda j, mine: (0, 1 - mine[0]))],
        shape_of((rows, half), BF16),
        half_block,
        flops=1 << 30,
        name="part",
    )
    arrived = lax.ppermute(there, "head", [(0, 1), (1, 0)])
    mixed = call(
        mixed_kernel,
        (4,),
        [mine_arr],
        [attn, out_weight, arrived],
        [row_block, pl.BlockSpec((columns, half), lambda j, mine: (0, mine[0])), half_block],
        shape_of((rows, half), BF16),
        half_block,
        flops=1 << 30,
        name="mixed",
    )

    flat_pair = pl.BlockSpec((PAIR, LANDMARKS), lambda j, *_: (j, 0))
    land_pair = pl.BlockSpec((LANDMARKS, PAIR), lambda j, *_: (0, j))
    tokens = shape_of((rows, columns), BF16)
    land_shape = shape_of((LANDMARKS, columns), BF16)
    products = [pltpu.VMEM((rows, 2 * LANDMARKS), BF16)]
    query_f, land_k = call(
        query_kernel,
        (pairs,),
        [own_arr],
        [queries, grad_attn, fb, land, mixer, more_k],
        [token_pair, token_pair, factor_pair, lk_pair, flat_pair, whole(more.shape)],
        [tokens, land_shape],
        [token_pair, land_pair],
        products,
        flops=6 << 30,
        name="query_grad",
    )
    if sorted_here:
        land_piece, count = shape_of((n // size, land_dev, 2 * columns), BF16), size
    else:
        land_piece, count = shape_of((LANDMARKS // 16, 16, 2 * columns), BF16), 1
    some = pairs // 2
    key_in = [key_rows, value_rows, pb, land, norm, center, more_q]

    def key_specs(first):
        pair_of = lambda j, *_: (0, j + first)
        tokens_at = pl.BlockSpec((rows, PAIR), pair_of)
        factors_at = pl.BlockSpec((rows, 2 * LANDMARKS), pair_of)
        land_at = pl.BlockSpec((LANDMARKS, PAIR), pair_of)
        flat_at = pl.BlockSpec((PAIR, LANDMARKS), lambda j, *_: (j + first, 0))
        return [tokens_at, tokens_at, factors_at, land_at, flat_at, whole((heads, LANDMARKS)), whole(more.shape)]

    specs = key_specs(0)
    half_shape = shape_of((LANDMARKS, some * PAIR), BF16)
    tokens_hbm = pltpu.HBM((rows, columns), BF16)
    key_b, value_grad, land_early = call(
        functools.partial(key_half_kernel, 0),
        (some,),
        [own_arr],
        key_in,
        specs,
        [tokens_hbm, tokens_hbm, half_shape],
        [specs[0], specs[0], land_pair],
        products,
        flops=3 << 30,
        name="key_grad",
    )
    (pb, land_early), weight_own = lax.optimization_barrier(((pb, land_early), weight_own))
    key_in[2] = pb
    specs = key_specs(some)
    key_b, value_grad, *land_pieces = call(
        functools.partial(key_rest_kernel, some),
        (pairs - some,),
        [own_arr],
        key_in + [land_early, land_k, held_in_hbm(key_b), held_in_hbm(value_grad)],
        specs + [whole(half_shape.shape), whole(land_shape.shape), in_hbm, in_hbm],
        [tokens_hbm, tokens_hbm] + [land_piece] * count,
        [specs[0], specs[0]] + [whole(land_piece.shape)] * count,
        [pltpu.VMEM((LANDMARKS, (pairs - some) * PAIR), BF16)] + products,
        flops=3 << 30,
        name="key_grad_rest",
        aliases={len(key_in) + 3: 0, len(key_in) + 4: 1},
    )
    if not sorted_here:
        land_pieces = split_by_partner(land_pieces[0].reshape(n, land_dev, 2 * columns), n, me)
    weights = gather_first(weight_own, n)
    weights, land_pieces = lax.optimization_barrier((weights, land_pieces))
    weights = gather_rest(weights, n)
    land_own = scatter_pieces(land_pieces, n, groups)[0] * (1.0 / seg_len)

    def finish(token_part, land_part):
        return (
            (token_part.reshape(land_dev, seg_len, columns) + land_part[:, None, :])
            .astype(BF16)
            .reshape(rows, columns)
        )

    weights, mixed = lax.optimization_barrier((weights, mixed))
    weight_grad = call(
        functools.partial(unpack_kernel, split),
        (1,),
        [me_arr],
        weights,
        [whole(weights[0].shape)] * size,
        pltpu.HBM((columns, width), F32),
        in_hbm,
        [pltpu.VMEM((n,) + weights[0].shape[1:], F32), pltpu.SemaphoreType.DMA((n,))],
        name="unpack",
    )
    query_grad = finish(query_f, land_own[:, :columns])
    key_grad = finish(key_b, land_own[:, columns:])
    return (mixed, query_grad, key_grad, value_grad, weight_grad)


def solution(mesh):
    return jax.shard_map(
        local,
        mesh=mesh,
        in_specs=(
            P("seq", "head"),
            P("seq", "head"),
            P("seq", "head"),
            P("head", None),
            P("seq", None),
        ),
        out_specs=(
            P("seq", "head"),
            P("seq", "head"),
            P("seq", "head"),
            P("seq", "head"),
            P("head", None),
        ),
        check_vma=False,
    )
```

```python
import functools

import jax
import jax.numpy as jnp
from jax import lax
from jax.experimental import pallas as pl
from jax.experimental.pallas import tpu as pltpu
from jax.sharding import PartitionSpec as P

DH = 64
PAIR = 2 * DH
LANDMARKS = 256
ITERS = 2
SCALE = 0.125
CHUNK = 256
EXTRA = 8
F32 = jnp.float32
BF16 = jnp.bfloat16
PARAMS = pltpu.CompilerParams(vmem_limit_bytes=24 * 1024 * 1024)


def dot(left, right, dims=((1,), (0,))):
    return lax.dot_general(left, right, (dims, ((), ())), preferred_element_type=F32)


NT = ((1,), (1,))
TN = ((0,), (0,))


def halves(value):
    high = value.astype(BF16)
    return high, (value - high.astype(F32)).astype(BF16)


def dot_exact(left, right, dims=((1,), (0,))):
    return dot(left[0], right[0], dims) + (
        dot(left[0], right[1], dims) + dot(left[1], right[0], dims)
    )


def turned(pair):
    return pair[0].T, pair[1].T


def keep_rows(block, which):
    rows = lax.broadcasted_iota(jnp.int32, block.shape, 0) // DH
    return jnp.where(rows == which, block, jnp.zeros_like(block))


def keep_lanes(block, which):
    lanes = lax.broadcasted_iota(jnp.int32, block.shape, 1) // DH
    return jnp.where(lanes == which, block, jnp.zeros_like(block))


def fold(block, op):
    parts = block.reshape(block.shape[0] // 8, 8, block.shape[1])
    return op(parts, axis=0)


def exchange(block, mask, n):
    return lax.ppermute(block, "seq", [(i, i ^ mask) for i in range(n)])


def bit_groups(n):
    bits = n.bit_length() - 1
    groups = []
    while bits > 0:
        take = 2 if bits % 2 == 0 else 1
        bits -= take
        groups.append((bits, 1 << take))
    return groups


def gather_first(block, n):
    shift, size = bit_groups(n)[0]
    held = block[None]
    return [held] + [exchange(held, m << shift, n) for m in range(1, size)]


def gather_rest(got, n):
    for shift, size in bit_groups(n)[1:]:
        held = jnp.stack(got, axis=1).reshape((-1,) + got[0].shape[1:])
        got = [held] + [exchange(held, m << shift, n) for m in range(1, size)]
    return got


def gather_lists(block, n):
    return gather_rest(gather_first(block, n), n)


def gather_ordered(block, n, me):
    got = gather_lists(block, n)
    held = jnp.stack(got, axis=1).reshape((n,) + block.shape)
    return held.at[jnp.arange(n) ^ me].get(mode="promise_in_bounds")


def split_by_partner(blocks, n, me):
    size = bit_groups(n)[-1][1]
    return [
        blocks.at[(jnp.arange(n // size) * size + m) ^ me].get(mode="promise_in_bounds")
        for m in range(size)
    ]


def scatter_step(pieces, shift, size, n):
    got = [pieces[0]] + [exchange(pieces[m], m << shift, n) for m in range(1, size)]
    return sum(part.astype(F32) for part in got)


def scatter_pieces(pieces, n, groups):
    for step, (shift, size) in enumerate(groups):
        held = scatter_step(pieces, shift, size, n)
        if step + 1 < len(groups):
            following = groups[step + 1][1]
            held = held.astype(BF16).reshape((-1, following) + held.shape[1:])
            pieces = [held[:, m] for m in range(following)]
    return held


def means_kernel(seg_len, q_ref, k_ref, out_ref, in_ref, sum_ref, sems):
    rows, columns = q_ref.shape
    steps = sems.shape[1]
    height = rows // steps
    copies = {}
    for c in range(steps):
        part = pl.ds(c * height, height)
        for side, ref in enumerate((q_ref, k_ref)):
            copies[side, c] = pltpu.make_async_copy(ref.at[part], in_ref.at[side, part], sems.at[side, c])
            copies[side, c].start()
    for c in range(steps):
        for side in range(2):
            copies[side, c].wait()
            span = slice(side * columns, (side + 1) * columns)
            for s in range(c * height // seg_len, (c + 1) * height // seg_len):
                total = fold(in_ref[side, s * seg_len : (s + 1) * seg_len, :].astype(F32), jnp.sum)
                sum_ref[s : s + 1, span] = jnp.sum(total, axis=0, keepdims=True)
    out_ref[...] = (sum_ref[...] * (1.0 / seg_len)).astype(BF16)


def forward_kernel(n, heads, count, me_ref, q_ref, k_ref, v_ref, g_ref, *refs):
    size = bit_groups(n)[-1][1]
    in_refs = refs[:count]
    fb_ref, pb_ref, top_ref, land_ref = refs[count : count + 4]
    out_refs = refs[count + 4 : count + 4 + size]
    score_ref, message_ref = refs[count + 4 + size :]
    pair = pl.program_id(0)
    columns = land_ref.shape[1] // 2

    @pl.when(pair == 0)
    def _():
        for m in range(count):
            held, height, _ = in_refs[m].shape
            for t in range(held):
                at = pl.multiple_of(((t * count + m) ^ me_ref[1]) * height, height)
                land_ref[pl.ds(at, height), :] = in_refs[m][t]

    here = pl.multiple_of(pair * PAIR, PAIR)
    lq_pair = land_ref[:, pl.ds(here, PAIR)]
    lk_pair = land_ref[:, pl.ds(columns + here, PAIR)]
    rows = q_ref.shape[0]
    parts = n // heads
    cols = DH // parts
    gt = g_ref[...].T
    vt = v_ref[...].T
    for h in range(2):
        lk = keep_lanes(lk_pair * SCALE, h).astype(BF16)
        lq = keep_lanes(lq_pair * SCALE, h).astype(BF16)
        span = slice(h * LANDMARKS, (h + 1) * LANDMARKS)
        top = None
        for c in range(0, rows, CHUNK):
            part = slice(c, c + CHUNK)
            sb = dot(k_ref[part, :], lq, NT)
            score_ref[part, :] = sb
            high = fold(sb, jnp.max)
            top = high if top is None else jnp.maximum(top, high)
            sf = dot(q_ref[part, :], lk, NT)
            e = jnp.exp(sf - jnp.max(sf, axis=1, keepdims=True))
            fb_ref[part, span] = (e * (1.0 / jnp.sum(e, axis=1, keepdims=True))).astype(BF16)
        top = jnp.max(top, axis=0, keepdims=True).astype(BF16).astype(F32)
        total = None
        for c in range(0, rows, CHUNK):
            part = slice(c, c + CHUNK)
            p = jnp.exp(score_ref[part, :] - top)
            add = fold(p, jnp.sum)
            total = add if total is None else total + add
            pb_ref[part, span] = p.astype(BF16)
        total = jnp.sum(total, axis=0, keepdims=True)
        top_ref[0, h : h + 1, :] = top
        grads = dot(gt[h * DH : (h + 1) * DH], fb_ref[:, span])
        vals = dot(vt[h * DH : (h + 1) * DH], pb_ref[:, span])
        high, low = halves(total)
        extra = three_rows(top, high.astype(F32), low.astype(F32))
        for p in range(parts):
            cut = slice(p * cols, (p + 1) * cols)
            message_ref[(2 * pair + h) * parts + p] = jnp.concatenate(
                [vals[cut], grads[cut], extra], axis=0
            ).astype(BF16)

    @pl.when(pair == pl.num_programs(0) - 1)
    def _():
        for m in range(size):
            for t in range(n // size):
                out_refs[m][t] = message_ref[(t * size + m) ^ me_ref[0]]


def merge(items, cols):
    tops = [item[2 * cols : 2 * cols + 1] for item in items]
    peak = functools.reduce(jnp.maximum, tops)
    vals = grads = total = 0.0
    for item, top in zip(items, tops):
        factor = jnp.exp(top - peak)
        vals = vals + item[:cols] * factor
        grads = grads + item[cols : 2 * cols]
        total = total + (
            item[2 * cols + 1 : 2 * cols + 2] + item[2 * cols + 2 : 2 * cols + 3]
        ) * factor
    return vals, grads, peak, total


def three_rows(first, second, third):
    row = lax.broadcasted_iota(jnp.int32, (EXTRA, LANDMARKS), 0)
    return jnp.where(row == 0, first, jnp.where(row == 1, second, jnp.where(row == 2, third, 0.0)))


def merge_kernel(cols, count, *refs):
    in_refs, out_refs = refs[:count], refs[count:]
    following = len(out_refs)
    for t in range(in_refs[0].shape[0]):
        vals, grads, peak, total = merge([ref[t].astype(F32) for ref in in_refs], cols)
        high, low = halves(total)
        extra = three_rows(peak, high.astype(F32), low.astype(F32))
        out_refs[t % following][t // following] = jnp.concatenate(
            [vals, grads, extra], axis=0
        ).astype(BF16)


def mix_kernel(cols, count, *refs):
    in_refs, z_ref = refs[:count], refs[count]
    reply_ref, values_ref, grads_ref = refs[count + 1 :]
    vals, grads, peak, total = merge([ref[0].astype(F32) for ref in in_refs], cols)
    inverse = halves(z_ref[0])
    values = vals / total
    mixer = dot_exact(halves(values), inverse, NT)
    norm = dot_exact(halves(grads), inverse) / total
    high, low = halves(jnp.sum(norm * values, axis=0, keepdims=True))
    extra = three_rows(peak, high.astype(F32), low.astype(F32))
    reply_ref[0] = jnp.concatenate([mixer, norm, extra], axis=0).astype(BF16)
    values_ref[...] = values
    grads_ref[...] = grads


def soft_rows(scores):
    e = jnp.exp(scores - jnp.max(scores, axis=1, keepdims=True))
    return e / jnp.sum(e, axis=1, keepdims=True)


def eye():
    shape = (LANDMARKS, LANDMARKS)
    same = lax.broadcasted_iota(jnp.int32, shape, 0) == lax.broadcasted_iota(jnp.int32, shape, 1)
    return same.astype(F32)


def column_top(amat):
    return jnp.max(jnp.sum(amat, axis=0, keepdims=True), axis=1, keepdims=True)


def newton_kernel(own_ref, lq_ref, lk_ref, saved_ref, z_ref):
    which = own_ref[1]
    amat = soft_rows(dot(keep_lanes(lq_ref[...] * SCALE, which).astype(BF16), lk_ref[...], NT))
    saved_ref[0] = amat
    current = amat.T / column_top(amat)
    ident = eye()
    amat = halves(amat)
    for i in range(ITERS):
        saved_ref[1 + 4 * i] = current
        z = halves(current)
        x_full = dot_exact(amat, z)
        saved_ref[2 + 4 * i] = x_full
        x = halves(x_full)
        inner = 15.0 * ident - dot_exact(x, halves(7.0 * ident - x_full))
        saved_ref[3 + 4 * i] = inner
        inner = 13.0 * ident - dot_exact(x, halves(inner))
        saved_ref[4 + 4 * i] = inner
        current = 0.25 * dot_exact(z, halves(inner))
    z_ref[0] = current


def newton_grad_kernel(own_ref, saved_ref, values_ref, grads_ref, lq_ref, lk_ref, q_ref, k_ref):
    which = own_ref[1]
    ident = eye()
    amat = saved_ref[0]
    amat_t = turned(halves(amat))
    grad_z = dot_exact(halves(grads_ref[...]), halves(values_ref[...]), TN)
    grad_a = jnp.zeros_like(amat)
    for i in reversed(range(ITERS)):
        z = halves(saved_ref[1 + 4 * i])
        x_full = saved_ref[2 + 4 * i]
        x_t = turned(halves(x_full))
        first = halves(7.0 * ident - x_full)
        second = halves(saved_ref[3 + 4 * i])
        third = halves(saved_ref[4 + 4 * i])
        dz = halves(0.25 * grad_z)
        d_third = halves(dot_exact(turned(z), dz))
        d_second = halves(-dot_exact(x_t, d_third))
        d_x = -dot_exact(d_third, second, NT) - dot_exact(d_second, first, NT)
        d_x = halves(d_x + dot_exact(x_t, d_second))
        grad_a = grad_a + dot_exact(d_x, z, NT)
        grad_z = dot_exact(dz, third, NT) + dot_exact(amat_t, d_x)
    grad_a = grad_a + grad_z.T / column_top(amat)
    grad_s = amat * (grad_a - jnp.sum(amat * grad_a, axis=1, keepdims=True)) * SCALE
    high, low = halves(grad_s)
    lq = keep_lanes(lq_ref[...], which)
    lk = keep_lanes(lk_ref[...], which)
    q_ref[...] = dot(high, lk) + dot(low, lk)
    k_ref[...] = dot(high.T, lq) + dot(low.T, lq)


def attend_kernel(n, heads, me_ref, fb_ref, top_ref, cot_ref, *refs):
    size = bit_groups(n)[-1][1]
    parts = n // heads
    cols = DH // parts
    reply_refs = refs[:size]
    attn_ref, mixer_ref, norm_ref, center_ref = refs[size : size + 4]
    out_refs = refs[size + 4 : 2 * size + 4]
    w_ref, d_ref, e_ref, sum_ref, all_ref = refs[2 * size + 4 :]
    pair = pl.program_id(0)

    @pl.when(pair == 0)
    def _():
        for m in range(size):
            for t in range(n // size):
                reply = reply_refs[m][t].astype(F32)
                at = (t * size + m) ^ me_ref[0]
                w_ref[at] = reply[:cols]
                d_ref[at] = reply[cols : 2 * cols]
                e_ref[at] = reply[2 * cols : 2 * cols + 8]
        for h in range(heads):
            cut = slice(h * parts, (h + 1) * parts)
            span = slice(h * DH, (h + 1) * DH)
            mixer_ref[span, :] = w_ref[cut].reshape(DH, LANDMARKS).astype(BF16)
            extra = e_ref[cut]
            top = top_ref[h // 2, h % 2 : h % 2 + 1, :]
            factor = jnp.exp(top - extra[0, 0:1, :])
            norm_ref[span, :] = (d_ref[cut].reshape(DH, LANDMARKS) * factor).astype(BF16)
            sums = jnp.sum(extra, axis=0)
            center_ref[h : h + 1, :] = (sums[1:2] + sums[2:3]) * factor

    mixer = mixer_ref[pl.ds(pl.multiple_of(pair * PAIR, PAIR), PAIR), :]
    attn = dot(fb_ref[:, :LANDMARKS], keep_rows(mixer, 0), NT) + dot(
        fb_ref[:, LANDMARKS:], keep_rows(mixer, 1), NT
    )
    attn = attn.astype(BF16)
    attn_ref[...] = attn
    all_ref[pl.ds(pl.multiple_of(pair * PAIR, PAIR), PAIR), :] = attn.T

    @pl.when(pair == pl.num_programs(0) - 1)
    def _():
        block, split = sum_ref.shape[1], n // sum_ref.shape[0]
        width = cot_ref.shape[1]
        sum_ref[...] = dot(all_ref[...], cot_ref[...]).reshape(sum_ref.shape)
        for m in range(size):
            for t in range(n // size):
                at = (t * size + m) ^ me_ref[0]
                if split == 1:
                    out_refs[m][t] = sum_ref[at].astype(BF16)
                else:
                    side = pl.multiple_of((at % split) * (width // split), width // split)
                    out_refs[m][t] = sum_ref[at // split, :, pl.ds(side, width // split)].astype(BF16)


def soft_grad(fb_ref, g_ref, mixer_ref, ds_ref):
    for h in range(2):
        span = slice(h * LANDMARKS, (h + 1) * LANDMARKS)
        mixer = keep_rows(mixer_ref[...], h)
        for c in range(0, fb_ref.shape[0], CHUNK):
            part = slice(c, c + CHUNK)
            f = fb_ref[part, span].astype(F32)
            df = dot(g_ref[part, :], mixer)
            ds_ref[part, span] = (f * (df - jnp.sum(f * df, axis=1, keepdims=True))).astype(BF16)


def weight_soft_grad(pb_ref, v_ref, norm_ref, center_ref, ds_ref):
    for h in range(2):
        span = slice(h * LANDMARKS, (h + 1) * LANDMARKS)
        norm = keep_rows(norm_ref[...], h)
        center = center_ref[pl.ds(2 * pl.program_id(0) + h, 1), :]
        for c in range(0, pb_ref.shape[0], CHUNK):
            part = slice(c, c + CHUNK)
            dp = dot(v_ref[part, :], norm)
            ds_ref[part, span] = (pb_ref[part, span].astype(F32) * (dp - center)).astype(BF16)


def land_sums(ds_ref, x_ref, own_ref, more_ref):
    xt = x_ref[...].T
    sums = jnp.concatenate(
        [dot(xt[:DH], ds_ref[:, :LANDMARKS]), dot(xt[DH:], ds_ref[:, LANDMARKS:])], axis=0
    )
    here = (own_ref[0] == pl.program_id(0)).astype(F32)
    return (sums.T * SCALE + more_ref[...] * here).astype(BF16)


def token_part(ds_ref, land_ref, out_ref):
    land = land_ref[...] * SCALE
    total = dot(ds_ref[:, :LANDMARKS], keep_lanes(land, 0).astype(BF16)) + dot(
        ds_ref[:, LANDMARKS:], keep_lanes(land, 1).astype(BF16)
    )
    out_ref[...] = total.astype(BF16)


def query_land_kernel(own_ref, q_ref, g_ref, fb_ref, mixer_ref, more_ref, land_ref, ds_ref):
    soft_grad(fb_ref, g_ref, mixer_ref, ds_ref)
    land_ref[...] = land_sums(ds_ref, q_ref, own_ref, more_ref)


def key_land_kernel(own_ref, k_ref, v_ref, pb_ref, norm_ref, center_ref, more_ref, other_ref, *refs):
    ds_ref, out_refs, land_ref = refs[0], refs[1:-1], refs[-1]
    size = len(out_refs)
    columns = other_ref.shape[1]
    pair = pl.program_id(0)
    weight_soft_grad(pb_ref, v_ref, norm_ref, center_ref, ds_ref)
    land_ref[:, pl.ds(pl.multiple_of(pair * PAIR, PAIR), PAIR)] = land_sums(
        ds_ref, k_ref, own_ref, more_ref
    )

    @pl.when(pair == pl.num_programs(0) - 1)
    def _():
        for m in range(size):
            held, height, _ = out_refs[m].shape
            for t in range(held):
                at = pl.multiple_of(((t * size + m) ^ own_ref[2]) * height, height)
                out_refs[m][t, :, :columns] = land_ref[pl.ds(at, height), :]
                out_refs[m][t, :, columns:] = other_ref[pl.ds(at, height), :]


def query_kernel(ds_ref, lk_ref, out_ref):
    token_part(ds_ref, lk_ref, out_ref)


def key_kernel(ds_ref, pb_ref, lq_ref, norm_ref, out_ref, value_ref):
    token_part(ds_ref, lq_ref, out_ref)
    value_ref[...] = (
        dot(pb_ref[:, :LANDMARKS], keep_rows(norm_ref[...], 0), NT)
        + dot(pb_ref[:, LANDMARKS:], keep_rows(norm_ref[...], 1), NT)
    ).astype(BF16)


def part_kernel(_, attn_ref, weight_ref, out_ref):
    out_ref[...] = dot(attn_ref[...], weight_ref[...]).astype(BF16)


def mixed_kernel(_, attn_ref, weight_ref, other_ref, out_ref):
    out_ref[...] = (dot(attn_ref[...], weight_ref[...]) + other_ref[...].astype(F32)).astype(BF16)


def unpack_kernel(split, me_ref, *refs):
    in_refs, (out_ref, wide_ref, sems) = refs[:-3], refs[-3:]
    size = len(in_refs)
    held, block, width = in_refs[0].shape
    copies = []
    for t in range(held):
        for m in range(size):
            slot = t * size + m
            at = slot ^ me_ref[0]
            row = pl.ds(pl.multiple_of((at // split) * block, block), block)
            if split == 1:
                target = out_ref.at[row]
            else:
                target = out_ref.at[row, pl.ds(pl.multiple_of((at % split) * width, width), width)]
            wide_ref[slot] = in_refs[m][t].astype(F32)
            copies.append(pltpu.make_async_copy(wide_ref.at[slot], target, sems.at[slot]))
            copies[-1].start()
    for copy in copies:
        copy.wait()


def held_in_hbm(x):
    return pltpu.with_memory_space_constraint(x, pltpu.HBM)


def whole(shape):
    return pl.BlockSpec(shape, lambda *_: (0,) * len(shape))


def shape_of(shape, dtype):
    return jax.ShapeDtypeStruct(shape, dtype)


def call(kernel, grid, scalars, ins, in_specs, outs, out_specs, scratch=(), flops=0, name=None, aliases={}):
    return pl.pallas_call(
        kernel,
        grid_spec=pltpu.PrefetchScalarGridSpec(
            num_scalar_prefetch=len(scalars),
            grid=grid,
            in_specs=in_specs,
            out_specs=out_specs,
            scratch_shapes=list(scratch),
        ),
        out_shape=outs,
        compiler_params=PARAMS,
        input_output_aliases=aliases,
        cost_estimate=pl.CostEstimate(flops=flops, bytes_accessed=4 << 20, transcendentals=0),
        name=name,
    )(*scalars, *ins)


def local(queries, key_rows, value_rows, out_weight, cotangent):
    rows, columns = queries.shape
    width = out_weight.shape[1]
    heads = columns // DH
    pairs = columns // PAIR
    n = lax.axis_size("seq")
    me = lax.axis_index("seq")
    mine = lax.axis_index("head")
    land_dev = LANDMARKS // n
    seg_len = rows // land_dev
    parts = n // heads
    cols = DH // parts
    size = bit_groups(n)[-1][1]
    height = 2 * cols + EXTRA
    own_head = me // parts

    sorted_here = land_dev % 16 == 0
    me_arr = jnp.stack([me, me if sorted_here else me * 0]).astype(jnp.int32)
    mine_arr = mine.reshape(1).astype(jnp.int32)
    own_arr = jnp.stack([own_head // 2, own_head % 2, me * 0 if land_dev % 16 else me]).astype(jnp.int32)
    steps = 4
    in_hbm = pl.BlockSpec(memory_space=pltpu.HBM)
    own = call(
        functools.partial(means_kernel, seg_len),
        (1,),
        [],
        [held_in_hbm(queries), held_in_hbm(key_rows)],
        [in_hbm, in_hbm],
        shape_of((land_dev, 2 * columns), BF16),
        whole((land_dev, 2 * columns)),
        [
            pltpu.VMEM((2, rows, columns), BF16),
            pltpu.VMEM((land_dev, 2 * columns), F32),
            pltpu.SemaphoreType.DMA((2, steps)),
        ],
        name="means",
    )
    own, me_arr, mine_arr, own_arr = lax.optimization_barrier((own, me_arr, mine_arr, own_arr))
    grad_attn = dot(cotangent, out_weight, NT).astype(BF16)
    if sorted_here:
        lands = gather_lists(own, n)
    else:
        lands = [gather_ordered(own, n, me).reshape(LANDMARKS // 16, 16, 2 * columns)]

    token_pair = pl.BlockSpec((rows, PAIR), lambda j, *_: (0, j))
    factor_pair = pl.BlockSpec((rows, 2 * LANDMARKS), lambda j, *_: (0, j))
    lq_pair = pl.BlockSpec((LANDMARKS, PAIR), lambda j, *_: (0, j))
    lk_pair = pl.BlockSpec((LANDMARKS, PAIR), lambda j, *_: (0, j + pairs))
    factors = shape_of((rows, heads * LANDMARKS), BF16)
    piece = shape_of((n // size, height, LANDMARKS), BF16)

    fb, pb, tops, land, *pieces = call(
        functools.partial(forward_kernel, n, heads, len(lands)),
        (pairs,),
        [me_arr],
        [queries, key_rows, value_rows, grad_attn] + lands,
        [token_pair] * 4 + [whole(lands[0].shape)] * len(lands),
        [
            factors,
            factors,
            shape_of((pairs, 8, LANDMARKS), F32),
            shape_of((LANDMARKS, 2 * columns), BF16),
        ]
        + [piece] * size,
        [
            factor_pair,
            factor_pair,
            pl.BlockSpec((1, 8, LANDMARKS), lambda j, *_: (j, 0, 0)),
            whole((LANDMARKS, 2 * columns)),
        ]
        + [whole(piece.shape)] * size,
        [
            pltpu.VMEM((rows, LANDMARKS), F32),
            pltpu.VMEM((n, height, LANDMARKS), BF16),
        ],
        flops=8 << 30,
        name="forward",
    )

    square = (LANDMARKS, LANDMARKS)
    own_lq = pl.BlockSpec((LANDMARKS, PAIR), lambda i, own: (0, own[0]))
    own_lk = pl.BlockSpec((LANDMARKS, PAIR), lambda i, own: (0, own[0] + pairs))
    kept = shape_of((1 + 4 * ITERS,) + square, F32)
    saved, inverse = call(
        newton_kernel,
        (1,),
        [own_arr],
        [land, land],
        [own_lq, own_lk],
        [kept, shape_of((1,) + square, F32)],
        [whole(kept.shape), whole((1,) + square)],
        flops=4 << 30,
        name="newton",
    )

    groups = bit_groups(n)[::-1]
    for step, (shift, count) in enumerate(groups):
        got = [pieces[0]] + [exchange(pieces[m], m << shift, n) for m in range(1, count)]
        specs = [whole(got[0].shape)] * count
        if step == 0:
            got, inverse = lax.optimization_barrier((got, inverse))
        if step + 1 < len(groups):
            following = groups[step + 1][1]
            piece = shape_of((got[0].shape[0] // following, height, LANDMARKS), BF16)
            pieces = call(
                functools.partial(merge_kernel, cols, count),
                (1,),
                [],
                got,
                specs,
                [piece] * following,
                [whole(piece.shape)] * following,
                name="merge",
            )
    small = shape_of((cols, LANDMARKS), F32)
    reply, values, grads = call(
        functools.partial(mix_kernel, cols, count),
        (1,),
        [],
        got + [inverse],
        specs + [whole((1,) + square)],
        [piece, small, small],
        [whole(piece.shape), whole(small.shape), whole(small.shape)],
        name="mix",
    )
    replies = gather_lists(reply[0], n)

    more = shape_of((LANDMARKS, PAIR), F32)
    more_q, more_k = call(
        newton_grad_kernel,
        (1,),
        [own_arr],
        [saved, values, grads, land, land],
        [whole(kept.shape), whole(small.shape), whole(small.shape), own_lq, own_lk],
        [more, more],
        [whole(more.shape)] * 2,
        flops=8 << 30,
        name="newton_grad",
    )

    replies, more_q, more_k = lax.optimization_barrier((replies, more_q, more_k))
    block = max(columns // n, 16)
    split = n * block // columns
    flat = shape_of((columns, LANDMARKS), BF16)
    weight_piece = shape_of((n // size, block, width // split), BF16)
    attn, mixer, norm, center, *weight_pieces = call(
        functools.partial(attend_kernel, n, heads),
        (pairs,),
        [me_arr],
        [fb, tops, cotangent] + replies,
        [factor_pair, whole(tops.shape), whole(cotangent.shape)] + [whole(replies[0].shape)] * size,
        [shape_of((rows, columns), BF16), flat, flat, shape_of((heads, LANDMARKS), F32)]
        + [weight_piece] * size,
        [token_pair, whole(flat.shape), whole(flat.shape), whole((heads, LANDMARKS))]
        + [whole(weight_piece.shape)] * size,
        [
            pltpu.VMEM((n, cols, LANDMARKS), F32),
            pltpu.VMEM((n, cols, LANDMARKS), F32),
            pltpu.VMEM((n, 8, LANDMARKS), F32),
            pltpu.VMEM((columns // block, block, width), F32),
            pltpu.VMEM((columns, rows), BF16),
        ],
        flops=4 << 30,
        name="attend",
    )
    (shift, count), later = groups[0], groups[1:]
    weight_sum = scatter_step(weight_pieces, shift, count, n).astype(BF16)
    (pb, key_rows, value_rows), weight_sum = lax.optimization_barrier(
        ((pb, key_rows, value_rows), weight_sum)
    )
    following = later[0][1]
    weight_sum = weight_sum.reshape((-1, following) + weight_sum.shape[1:])
    weight_own = scatter_pieces([weight_sum[:, m] for m in range(following)], n, later)[0].astype(BF16)
    flat_pair = pl.BlockSpec((PAIR, LANDMARKS), lambda j, *_: (j, 0))
    land_pair = pl.BlockSpec((LANDMARKS, PAIR), lambda j, *_: (0, j))
    centers = whole((heads, LANDMARKS))
    tokens = shape_of((rows, columns), BF16)
    land_shape = shape_of((LANDMARKS, columns), BF16)
    land_k, grad_sf = call(
        query_land_kernel,
        (pairs,),
        [own_arr],
        [queries, grad_attn, fb, mixer, more_k],
        [token_pair, token_pair, factor_pair, flat_pair, whole(more.shape)],
        [land_shape, factors],
        [land_pair, factor_pair],
        flops=4 << 30,
        name="query_land",
    )
    (shift, count), later = groups[0], groups[1:]
    following = later[0][1]
    weight_sum = scatter_step(weight_pieces, shift, count, n).astype(BF16)
    (pb, key_rows, value_rows), weight_sum, land_k = lax.optimization_barrier(
        ((pb, key_rows, value_rows), weight_sum, land_k)
    )
    if sorted_here:
        land_piece, pieces_count = shape_of((n // size, land_dev, 2 * columns), BF16), size
    else:
        land_piece, pieces_count = shape_of((LANDMARKS // 16, 16, 2 * columns), BF16), 1
    grad_sb, *land_pieces = call(
        key_land_kernel,
        (pairs,),
        [own_arr],
        [key_rows, value_rows, pb, norm, center, more_q, land_k],
        [token_pair, token_pair, factor_pair, flat_pair, centers, whole(more.shape)]
        + [whole(land_shape.shape)],
        [factors] + [land_piece] * pieces_count,
        [factor_pair] + [whole(land_piece.shape)] * pieces_count,
        [pltpu.VMEM(land_shape.shape, BF16)],
        flops=4 << 30,
        name="key_land",
    )
    land_pieces, grad_sf, attn = lax.optimization_barrier((land_pieces, grad_sf, attn))
    query_f = call(
        query_kernel,
        (pairs,),
        [],
        [grad_sf, land],
        [factor_pair, lk_pair],
        tokens,
        token_pair,
        flops=2 << 30,
        name="query_grad",
    )
    half = width // 2
    row_block = pl.BlockSpec((rows // 4, columns), lambda j, _: (j, 0))
    half_block = pl.BlockSpec((rows // 4, half), lambda j, _: (j, 0))
    there = call(
        part_kernel,
        (4,),
        [mine_arr],
        [attn, out_weight],
        [row_block, pl.BlockSpec((columns, half), lambda j, mine: (0, 1 - mine[0]))],
        shape_of((rows, half), BF16),
        half_block,
        flops=1 << 30,
        name="part",
    )

    if not sorted_here:
        land_pieces = split_by_partner(land_pieces[0].reshape(n, land_dev, 2 * columns), n, me)
    weight_sum = weight_sum.reshape((-1, following) + weight_sum.shape[1:])
    weight_own = scatter_pieces([weight_sum[:, m] for m in range(following)], n, later)[0].astype(BF16)
    land_pieces, weight_own = lax.optimization_barrier((land_pieces, weight_own))
    land_sum = scatter_step(land_pieces, shift, count, n).astype(BF16)
    land_sum, weight_own, query_f, there = lax.optimization_barrier(
        (land_sum, weight_own, query_f, there)
    )
    land_sum, weight_own, grad_sb = lax.optimization_barrier((land_sum, weight_own, grad_sb))
    key_b, value_grad = call(
        key_kernel,
        (pairs,),
        [],
        [grad_sb, pb, land, norm],
        [factor_pair, factor_pair, lq_pair, flat_pair],
        [tokens, tokens],
        [token_pair, token_pair],
        flops=4 << 30,
        name="key_grad",
    )

    arrived = lax.ppermute(there, "head", [(0, 1), (1, 0)])
    mixed = call(
        mixed_kernel,
        (4,),
        [mine_arr],
        [attn, out_weight, arrived],
        [row_block, pl.BlockSpec((columns, half), lambda j, mine: (0, mine[0])), half_block],
        shape_of((rows, half), BF16),
        half_block,
        flops=1 << 30,
        name="mixed",
    )
    if len(later) == 1 and weight_own.shape[1] == land_sum.shape[2]:
        (shift, count), tall = later[0], weight_own.shape[0]
        got = [
            exchange(jnp.concatenate([weight_own, land_sum[m]], axis=0), m << shift, n)
            for m in range(1, count)
        ]
        weights = [weight_own[None]] + [part[None, :tall] for part in got]
        land_own = sum(part.astype(F32) for part in [land_sum[0]] + [part[tall:] for part in got])
    else:
        weights = gather_first(weight_own, n)
        land_sum = land_sum.reshape((-1, following) + land_sum.shape[1:])
        land_own = scatter_pieces([land_sum[:, m] for m in range(following)], n, later)[0]
    land_own = land_own * (1.0 / seg_len)
    weights, key_b = lax.optimization_barrier((weights, key_b))
    weights = gather_rest(weights, n)
    weights, mixed = lax.optimization_barrier((weights, mixed))
    weight_grad = call(
        functools.partial(unpack_kernel, split),
        (1,),
        [me_arr],
        weights,
        [whole(weights[0].shape)] * size,
        pltpu.HBM((columns, width), F32),
        in_hbm,
        [pltpu.VMEM((n,) + weights[0].shape[1:], F32), pltpu.SemaphoreType.DMA((n,))],
        name="unpack",
    )

    def finish(token_part, land_part):
        return (
            (token_part.reshape(land_dev, seg_len, columns) + land_part[:, None, :])
            .astype(BF16)
            .reshape(rows, columns)
        )

    query_grad = finish(query_f, land_own[:, :columns])
    key_grad = finish(key_b, land_own[:, columns:])
    return (mixed, query_grad, key_grad, value_grad, weight_grad)


def solution(mesh):
    return jax.shard_map(
        local,
        mesh=mesh,
        in_specs=(
            P("seq", "head"),
            P("seq", "head"),
            P("seq", "head"),
            P("head", None),
            P("seq", None),
        ),
        out_specs=(
            P("seq", "head"),
            P("seq", "head"),
            P("seq", "head"),
            P("seq", "head"),
            P("head", None),
        ),
        check_vma=False,
    )
```

```python
import functools

import jax
import jax.numpy as jnp
from jax import lax
from jax.experimental import pallas as pl
from jax.experimental.pallas import tpu as pltpu
from jax.sharding import PartitionSpec as P

DH = 64
PAIR = 2 * DH
LANDMARKS = 256
ITERS = 2
SCALE = 0.125
CHUNK = 256
EXTRA = 8
F32 = jnp.float32
BF16 = jnp.bfloat16
PARAMS = pltpu.CompilerParams(vmem_limit_bytes=24 * 1024 * 1024)


def dot(left, right, dims=((1,), (0,))):
    return lax.dot_general(left, right, (dims, ((), ())), preferred_element_type=F32)


NT = ((1,), (1,))
TN = ((0,), (0,))


def halves(value):
    high = value.astype(BF16)
    return high, (value - high.astype(F32)).astype(BF16)


def dot_exact(left, right, dims=((1,), (0,))):
    return dot(left[0], right[0], dims) + (
        dot(left[0], right[1], dims) + dot(left[1], right[0], dims)
    )


def turned(pair):
    return pair[0].T, pair[1].T


def keep_rows(block, which):
    rows = lax.broadcasted_iota(jnp.int32, block.shape, 0) // DH
    return jnp.where(rows == which, block, jnp.zeros_like(block))


def keep_lanes(block, which):
    lanes = lax.broadcasted_iota(jnp.int32, block.shape, 1) // DH
    return jnp.where(lanes == which, block, jnp.zeros_like(block))


def fold(block, op):
    parts = block.reshape(block.shape[0] // 8, 8, block.shape[1])
    return op(parts, axis=0)


def exchange(block, mask, n):
    return lax.ppermute(block, "seq", [(i, i ^ mask) for i in range(n)])


def bit_groups(n):
    bits = n.bit_length() - 1
    groups = []
    while bits > 0:
        take = 2 if bits % 2 == 0 else 1
        bits -= take
        groups.append((bits, 1 << take))
    return groups


def gather_first(block, n):
    shift, size = bit_groups(n)[0]
    held = block[None]
    return [held] + [exchange(held, m << shift, n) for m in range(1, size)]


def gather_rest(got, n):
    for shift, size in bit_groups(n)[1:]:
        held = jnp.stack(got, axis=1).reshape((-1,) + got[0].shape[1:])
        got = [held] + [exchange(held, m << shift, n) for m in range(1, size)]
    return got


def gather_lists(block, n):
    return gather_rest(gather_first(block, n), n)


def gather_ordered(block, n, me):
    got = gather_lists(block, n)
    held = jnp.stack(got, axis=1).reshape((n,) + block.shape)
    return held.at[jnp.arange(n) ^ me].get(mode="promise_in_bounds")


def split_by_partner(blocks, n, me):
    size = bit_groups(n)[-1][1]
    return [
        blocks.at[(jnp.arange(n // size) * size + m) ^ me].get(mode="promise_in_bounds")
        for m in range(size)
    ]


def scatter_step(pieces, shift, size, n):
    got = [pieces[0]] + [exchange(pieces[m], m << shift, n) for m in range(1, size)]
    return sum(part.astype(F32) for part in got)


def scatter_pieces(pieces, n, groups):
    for step, (shift, size) in enumerate(groups):
        held = scatter_step(pieces, shift, size, n)
        if step + 1 < len(groups):
            following = groups[step + 1][1]
            held = held.astype(BF16).reshape((-1, following) + held.shape[1:])
            pieces = [held[:, m] for m in range(following)]
    return held


def means_kernel(seg_len, q_ref, k_ref, out_ref, in_ref, sum_ref, sems):
    rows, columns = q_ref.shape
    steps = sems.shape[1]
    height = rows // steps
    copies = {}
    for c in range(steps):
        part = pl.ds(c * height, height)
        for side, ref in enumerate((q_ref, k_ref)):
            copies[side, c] = pltpu.make_async_copy(ref.at[part], in_ref.at[side, part], sems.at[side, c])
            copies[side, c].start()
    for c in range(steps):
        for side in range(2):
            copies[side, c].wait()
            span = slice(side * columns, (side + 1) * columns)
            for s in range(c * height // seg_len, (c + 1) * height // seg_len):
                total = fold(in_ref[side, s * seg_len : (s + 1) * seg_len, :].astype(F32), jnp.sum)
                sum_ref[s : s + 1, span] = jnp.sum(total, axis=0, keepdims=True)
    out_ref[...] = (sum_ref[...] * (1.0 / seg_len)).astype(BF16)


def forward_kernel(n, heads, count, me_ref, q_ref, k_ref, v_ref, g_ref, *refs):
    size = bit_groups(n)[-1][1]
    in_refs = refs[:count]
    fb_ref, pb_ref, top_ref, land_ref = refs[count : count + 4]
    out_refs = refs[count + 4 : count + 4 + size]
    score_ref, message_ref = refs[count + 4 + size :]
    pair = pl.program_id(0)
    columns = land_ref.shape[1] // 2

    @pl.when(pair == 0)
    def _():
        for m in range(count):
            held, height, _ = in_refs[m].shape
            for t in range(held):
                at = pl.multiple_of(((t * count + m) ^ me_ref[1]) * height, height)
                land_ref[pl.ds(at, height), :] = in_refs[m][t]

    here = pl.multiple_of(pair * PAIR, PAIR)
    lq_pair = land_ref[:, pl.ds(here, PAIR)]
    lk_pair = land_ref[:, pl.ds(columns + here, PAIR)]
    rows = q_ref.shape[0]
    parts = n // heads
    cols = DH // parts
    gt = g_ref[...].T
    vt = v_ref[...].T
    for h in range(2):
        lk = keep_lanes(lk_pair * SCALE, h).astype(BF16)
        lq = keep_lanes(lq_pair * SCALE, h).astype(BF16)
        span = slice(h * LANDMARKS, (h + 1) * LANDMARKS)
        top = None
        for c in range(0, rows, CHUNK):
            part = slice(c, c + CHUNK)
            sb = dot(k_ref[part, :], lq, NT)
            score_ref[part, :] = sb
            high = fold(sb, jnp.max)
            top = high if top is None else jnp.maximum(top, high)
            sf = dot(q_ref[part, :], lk, NT)
            e = jnp.exp(sf - jnp.max(sf, axis=1, keepdims=True))
            fb_ref[part, span] = (e * (1.0 / jnp.sum(e, axis=1, keepdims=True))).astype(BF16)
        top = jnp.max(top, axis=0, keepdims=True).astype(BF16).astype(F32)
        total = None
        for c in range(0, rows, CHUNK):
            part = slice(c, c + CHUNK)
            p = jnp.exp(score_ref[part, :] - top)
            add = fold(p, jnp.sum)
            total = add if total is None else total + add
            pb_ref[part, span] = p.astype(BF16)
        total = jnp.sum(total, axis=0, keepdims=True)
        top_ref[0, h : h + 1, :] = top
        grads = dot(gt[h * DH : (h + 1) * DH], fb_ref[:, span])
        vals = dot(vt[h * DH : (h + 1) * DH], pb_ref[:, span])
        high, low = halves(total)
        extra = three_rows(top, high.astype(F32), low.astype(F32))
        for p in range(parts):
            cut = slice(p * cols, (p + 1) * cols)
            message_ref[(2 * pair + h) * parts + p] = jnp.concatenate(
                [vals[cut], grads[cut], extra], axis=0
            ).astype(BF16)

    @pl.when(pair == pl.num_programs(0) - 1)
    def _():
        for m in range(size):
            for t in range(n // size):
                out_refs[m][t] = message_ref[(t * size + m) ^ me_ref[0]]


def merge(items, cols):
    tops = [item[2 * cols : 2 * cols + 1] for item in items]
    peak = functools.reduce(jnp.maximum, tops)
    vals = grads = total = 0.0
    for item, top in zip(items, tops):
        factor = jnp.exp(top - peak)
        vals = vals + item[:cols] * factor
        grads = grads + item[cols : 2 * cols]
        total = total + (
            item[2 * cols + 1 : 2 * cols + 2] + item[2 * cols + 2 : 2 * cols + 3]
        ) * factor
    return vals, grads, peak, total


def three_rows(first, second, third):
    row = lax.broadcasted_iota(jnp.int32, (EXTRA, LANDMARKS), 0)
    return jnp.where(row == 0, first, jnp.where(row == 1, second, jnp.where(row == 2, third, 0.0)))


def merge_kernel(cols, count, *refs):
    in_refs, out_refs = refs[:count], refs[count:]
    following = len(out_refs)
    for t in range(in_refs[0].shape[0]):
        vals, grads, peak, total = merge([ref[t].astype(F32) for ref in in_refs], cols)
        high, low = halves(total)
        extra = three_rows(peak, high.astype(F32), low.astype(F32))
        out_refs[t % following][t // following] = jnp.concatenate(
            [vals, grads, extra], axis=0
        ).astype(BF16)


def mix_kernel(cols, count, *refs):
    in_refs, z_ref = refs[:count], refs[count]
    reply_ref, values_ref, grads_ref = refs[count + 1 :]
    vals, grads, peak, total = merge([ref[0].astype(F32) for ref in in_refs], cols)
    inverse = halves(z_ref[0])
    values = vals / total
    mixer = dot_exact(halves(values), inverse, NT)
    norm = dot_exact(halves(grads), inverse) / total
    high, low = halves(jnp.sum(norm * values, axis=0, keepdims=True))
    extra = three_rows(peak, high.astype(F32), low.astype(F32))
    reply_ref[0] = jnp.concatenate([mixer, norm, extra], axis=0).astype(BF16)
    values_ref[...] = values
    grads_ref[...] = grads


def soft_rows(scores):
    e = jnp.exp(scores - jnp.max(scores, axis=1, keepdims=True))
    return e / jnp.sum(e, axis=1, keepdims=True)


def eye():
    shape = (LANDMARKS, LANDMARKS)
    same = lax.broadcasted_iota(jnp.int32, shape, 0) == lax.broadcasted_iota(jnp.int32, shape, 1)
    return same.astype(F32)


def column_top(amat):
    return jnp.max(jnp.sum(amat, axis=0, keepdims=True), axis=1, keepdims=True)


def newton_kernel(own_ref, lq_ref, lk_ref, saved_ref, z_ref):
    which = own_ref[1]
    amat = soft_rows(dot(keep_lanes(lq_ref[...] * SCALE, which).astype(BF16), lk_ref[...], NT))
    saved_ref[0] = amat
    current = amat.T / column_top(amat)
    ident = eye()
    amat = halves(amat)
    for i in range(ITERS):
        saved_ref[1 + 4 * i] = current
        z = halves(current)
        x_full = dot_exact(amat, z)
        saved_ref[2 + 4 * i] = x_full
        x = halves(x_full)
        inner = 15.0 * ident - dot_exact(x, halves(7.0 * ident - x_full))
        saved_ref[3 + 4 * i] = inner
        inner = 13.0 * ident - dot_exact(x, halves(inner))
        saved_ref[4 + 4 * i] = inner
        current = 0.25 * dot_exact(z, halves(inner))
    z_ref[0] = current


def newton_grad_kernel(own_ref, saved_ref, values_ref, grads_ref, lq_ref, lk_ref, q_ref, k_ref):
    which = own_ref[1]
    ident = eye()
    amat = saved_ref[0]
    amat_t = turned(halves(amat))
    grad_z = dot_exact(halves(grads_ref[...]), halves(values_ref[...]), TN)
    grad_a = jnp.zeros_like(amat)
    for i in reversed(range(ITERS)):
        z = halves(saved_ref[1 + 4 * i])
        x_full = saved_ref[2 + 4 * i]
        x_t = turned(halves(x_full))
        first = halves(7.0 * ident - x_full)
        second = halves(saved_ref[3 + 4 * i])
        third = halves(saved_ref[4 + 4 * i])
        dz = halves(0.25 * grad_z)
        d_third = halves(dot_exact(turned(z), dz))
        d_second = halves(-dot_exact(x_t, d_third))
        d_x = -dot_exact(d_third, second, NT) - dot_exact(d_second, first, NT)
        d_x = halves(d_x + dot_exact(x_t, d_second))
        grad_a = grad_a + dot_exact(d_x, z, NT)
        grad_z = dot_exact(dz, third, NT) + dot_exact(amat_t, d_x)
    grad_a = grad_a + grad_z.T / column_top(amat)
    grad_s = amat * (grad_a - jnp.sum(amat * grad_a, axis=1, keepdims=True)) * SCALE
    high, low = halves(grad_s)
    lq = keep_lanes(lq_ref[...], which)
    lk = keep_lanes(lk_ref[...], which)
    q_ref[...] = dot(high, lk) + dot(low, lk)
    k_ref[...] = dot(high.T, lq) + dot(low.T, lq)


def attend_kernel(n, heads, me_ref, fb_ref, top_ref, cot_ref, *refs):
    size = bit_groups(n)[-1][1]
    parts = n // heads
    cols = DH // parts
    reply_refs = refs[:size]
    attn_ref, mixer_ref, norm_ref, center_ref = refs[size : size + 4]
    out_refs = refs[size + 4 : 2 * size + 4]
    w_ref, d_ref, e_ref, sum_ref, all_ref = refs[2 * size + 4 :]
    pair = pl.program_id(0)

    @pl.when(pair == 0)
    def _():
        for m in range(size):
            for t in range(n // size):
                reply = reply_refs[m][t].astype(F32)
                at = (t * size + m) ^ me_ref[0]
                w_ref[at] = reply[:cols]
                d_ref[at] = reply[cols : 2 * cols]
                e_ref[at] = reply[2 * cols : 2 * cols + 8]
        for h in range(heads):
            cut = slice(h * parts, (h + 1) * parts)
            span = slice(h * DH, (h + 1) * DH)
            mixer_ref[span, :] = w_ref[cut].reshape(DH, LANDMARKS).astype(BF16)
            extra = e_ref[cut]
            top = top_ref[h // 2, h % 2 : h % 2 + 1, :]
            factor = jnp.exp(top - extra[0, 0:1, :])
            norm_ref[span, :] = (d_ref[cut].reshape(DH, LANDMARKS) * factor).astype(BF16)
            sums = jnp.sum(extra, axis=0)
            center_ref[h : h + 1, :] = (sums[1:2] + sums[2:3]) * factor

    mixer = mixer_ref[pl.ds(pl.multiple_of(pair * PAIR, PAIR), PAIR), :]
    attn = dot(fb_ref[:, :LANDMARKS], keep_rows(mixer, 0), NT) + dot(
        fb_ref[:, LANDMARKS:], keep_rows(mixer, 1), NT
    )
    attn = attn.astype(BF16)
    attn_ref[...] = attn
    all_ref[pl.ds(pl.multiple_of(pair * PAIR, PAIR), PAIR), :] = attn.T

    @pl.when(pair == pl.num_programs(0) - 1)
    def _():
        block, split = sum_ref.shape[1], n // sum_ref.shape[0]
        width = cot_ref.shape[1]
        sum_ref[...] = dot(all_ref[...], cot_ref[...]).reshape(sum_ref.shape)
        for m in range(size):
            for t in range(n // size):
                at = (t * size + m) ^ me_ref[0]
                if split == 1:
                    out_refs[m][t] = sum_ref[at].astype(BF16)
                else:
                    side = pl.multiple_of((at % split) * (width // split), width // split)
                    out_refs[m][t] = sum_ref[at // split, :, pl.ds(side, width // split)].astype(BF16)


def soft_grad(fb_ref, g_ref, mixer_ref, ds_ref):
    for h in range(2):
        span = slice(h * LANDMARKS, (h + 1) * LANDMARKS)
        mixer = keep_rows(mixer_ref[...], h)
        for c in range(0, fb_ref.shape[0], CHUNK):
            part = slice(c, c + CHUNK)
            f = fb_ref[part, span].astype(F32)
            df = dot(g_ref[part, :], mixer)
            ds_ref[part, span] = (f * (df - jnp.sum(f * df, axis=1, keepdims=True))).astype(BF16)


def weight_soft_grad(pb_ref, v_ref, norm_ref, center_ref, ds_ref):
    for h in range(2):
        span = slice(h * LANDMARKS, (h + 1) * LANDMARKS)
        norm = keep_rows(norm_ref[...], h)
        center = center_ref[pl.ds(2 * pl.program_id(0) + h, 1), :]
        for c in range(0, pb_ref.shape[0], CHUNK):
            part = slice(c, c + CHUNK)
            dp = dot(v_ref[part, :], norm)
            ds_ref[part, span] = (pb_ref[part, span].astype(F32) * (dp - center)).astype(BF16)


def land_sums(ds_ref, x_ref, own_ref, more_ref):
    xt = x_ref[...].T
    sums = jnp.concatenate(
        [dot(xt[:DH], ds_ref[:, :LANDMARKS]), dot(xt[DH:], ds_ref[:, LANDMARKS:])], axis=0
    )
    here = (own_ref[0] == pl.program_id(0)).astype(F32)
    return (sums.T * SCALE + more_ref[...] * here).astype(BF16)


def token_part(ds_ref, land_ref, out_ref):
    land = land_ref[...] * SCALE
    total = dot(ds_ref[:, :LANDMARKS], keep_lanes(land, 0).astype(BF16)) + dot(
        ds_ref[:, LANDMARKS:], keep_lanes(land, 1).astype(BF16)
    )
    out_ref[...] = total.astype(BF16)


def query_land_kernel(own_ref, q_ref, g_ref, fb_ref, mixer_ref, more_ref, land_ref, ds_ref):
    soft_grad(fb_ref, g_ref, mixer_ref, ds_ref)
    land_ref[...] = land_sums(ds_ref, q_ref, own_ref, more_ref)


def key_land_kernel(own_ref, k_ref, v_ref, pb_ref, norm_ref, center_ref, more_ref, other_ref, *refs):
    ds_ref, out_refs, land_ref = refs[0], refs[1:-1], refs[-1]
    size = len(out_refs)
    columns = other_ref.shape[1]
    pair = pl.program_id(0)
    weight_soft_grad(pb_ref, v_ref, norm_ref, center_ref, ds_ref)
    land_ref[:, pl.ds(pl.multiple_of(pair * PAIR, PAIR), PAIR)] = land_sums(
        ds_ref, k_ref, own_ref, more_ref
    )

    @pl.when(pair == pl.num_programs(0) - 1)
    def _():
        for m in range(size):
            held, height, _ = out_refs[m].shape
            for t in range(held):
                at = pl.multiple_of(((t * size + m) ^ own_ref[2]) * height, height)
                out_refs[m][t, :, :columns] = land_ref[pl.ds(at, height), :]
                out_refs[m][t, :, columns:] = other_ref[pl.ds(at, height), :]


def query_kernel(ds_ref, lk_ref, out_ref):
    token_part(ds_ref, lk_ref, out_ref)


def key_kernel(ds_ref, pb_ref, lq_ref, norm_ref, out_ref, value_ref):
    token_part(ds_ref, lq_ref, out_ref)
    value_ref[...] = (
        dot(pb_ref[:, :LANDMARKS], keep_rows(norm_ref[...], 0), NT)
        + dot(pb_ref[:, LANDMARKS:], keep_rows(norm_ref[...], 1), NT)
    ).astype(BF16)


def part_kernel(_, attn_ref, weight_ref, out_ref):
    out_ref[...] = dot(attn_ref[...], weight_ref[...]).astype(BF16)


def mixed_kernel(_, attn_ref, weight_ref, other_ref, out_ref):
    out_ref[...] = (dot(attn_ref[...], weight_ref[...]) + other_ref[...].astype(F32)).astype(BF16)


def unpack_kernel(split, me_ref, *refs):
    in_refs, (out_ref, wide_ref, sems) = refs[:-3], refs[-3:]
    size = len(in_refs)
    held, block, width = in_refs[0].shape
    copies = []
    for t in range(held):
        for m in range(size):
            slot = t * size + m
            at = slot ^ me_ref[0]
            row = pl.ds(pl.multiple_of((at // split) * block, block), block)
            if split == 1:
                target = out_ref.at[row]
            else:
                target = out_ref.at[row, pl.ds(pl.multiple_of((at % split) * width, width), width)]
            wide_ref[slot] = in_refs[m][t].astype(F32)
            copies.append(pltpu.make_async_copy(wide_ref.at[slot], target, sems.at[slot]))
            copies[-1].start()
    for copy in copies:
        copy.wait()


def held_in_hbm(x):
    return pltpu.with_memory_space_constraint(x, pltpu.HBM)


def whole(shape):
    return pl.BlockSpec(shape, lambda *_: (0,) * len(shape))


def shape_of(shape, dtype):
    return jax.ShapeDtypeStruct(shape, dtype)


def call(kernel, grid, scalars, ins, in_specs, outs, out_specs, scratch=(), flops=0, name=None, aliases={}):
    return pl.pallas_call(
        kernel,
        grid_spec=pltpu.PrefetchScalarGridSpec(
            num_scalar_prefetch=len(scalars),
            grid=grid,
            in_specs=in_specs,
            out_specs=out_specs,
            scratch_shapes=list(scratch),
        ),
        out_shape=outs,
        compiler_params=PARAMS,
        input_output_aliases=aliases,
        cost_estimate=pl.CostEstimate(flops=flops, bytes_accessed=4 << 20, transcendentals=0),
        name=name,
    )(*scalars, *ins)


def local(queries, key_rows, value_rows, out_weight, cotangent):
    rows, columns = queries.shape
    width = out_weight.shape[1]
    heads = columns // DH
    pairs = columns // PAIR
    n = lax.axis_size("seq")
    me = lax.axis_index("seq")
    mine = lax.axis_index("head")
    land_dev = LANDMARKS // n
    seg_len = rows // land_dev
    parts = n // heads
    cols = DH // parts
    size = bit_groups(n)[-1][1]
    height = 2 * cols + EXTRA
    own_head = me // parts

    sorted_here = land_dev % 16 == 0
    me_arr = jnp.stack([me, me if sorted_here else me * 0]).astype(jnp.int32)
    mine_arr = mine.reshape(1).astype(jnp.int32)
    own_arr = jnp.stack([own_head // 2, own_head % 2, me * 0 if land_dev % 16 else me]).astype(jnp.int32)
    steps = 4
    in_hbm = pl.BlockSpec(memory_space=pltpu.HBM)
    own = call(
        functools.partial(means_kernel, seg_len),
        (1,),
        [],
        [held_in_hbm(queries), held_in_hbm(key_rows)],
        [in_hbm, in_hbm],
        shape_of((land_dev, 2 * columns), BF16),
        whole((land_dev, 2 * columns)),
        [
            pltpu.VMEM((2, rows, columns), BF16),
            pltpu.VMEM((land_dev, 2 * columns), F32),
            pltpu.SemaphoreType.DMA((2, steps)),
        ],
        name="means",
    )
    own, me_arr, mine_arr, own_arr = lax.optimization_barrier((own, me_arr, mine_arr, own_arr))
    grad_attn = dot(cotangent, out_weight, NT).astype(BF16)
    if sorted_here:
        lands = gather_lists(own, n)
    else:
        lands = [gather_ordered(own, n, me).reshape(LANDMARKS // 16, 16, 2 * columns)]

    token_pair = pl.BlockSpec((rows, PAIR), lambda j, *_: (0, j))
    factor_pair = pl.BlockSpec((rows, 2 * LANDMARKS), lambda j, *_: (0, j))
    lq_pair = pl.BlockSpec((LANDMARKS, PAIR), lambda j, *_: (0, j))
    lk_pair = pl.BlockSpec((LANDMARKS, PAIR), lambda j, *_: (0, j + pairs))
    factors = shape_of((rows, heads * LANDMARKS), BF16)
    piece = shape_of((n // size, height, LANDMARKS), BF16)

    fb, pb, tops, land, *pieces = call(
        functools.partial(forward_kernel, n, heads, len(lands)),
        (pairs,),
        [me_arr],
        [queries, key_rows, value_rows, grad_attn] + lands,
        [token_pair] * 4 + [whole(lands[0].shape)] * len(lands),
        [
            factors,
            factors,
            shape_of((pairs, 8, LANDMARKS), F32),
            shape_of((LANDMARKS, 2 * columns), BF16),
        ]
        + [piece] * size,
        [
            factor_pair,
            factor_pair,
            pl.BlockSpec((1, 8, LANDMARKS), lambda j, *_: (j, 0, 0)),
            whole((LANDMARKS, 2 * columns)),
        ]
        + [whole(piece.shape)] * size,
        [
            pltpu.VMEM((rows, LANDMARKS), F32),
            pltpu.VMEM((n, height, LANDMARKS), BF16),
        ],
        flops=8 << 30,
        name="forward",
    )

    square = (LANDMARKS, LANDMARKS)
    own_lq = pl.BlockSpec((LANDMARKS, PAIR), lambda i, own: (0, own[0]))
    own_lk = pl.BlockSpec((LANDMARKS, PAIR), lambda i, own: (0, own[0] + pairs))
    kept = shape_of((1 + 4 * ITERS,) + square, F32)
    saved, inverse = call(
        newton_kernel,
        (1,),
        [own_arr],
        [land, land],
        [own_lq, own_lk],
        [kept, shape_of((1,) + square, F32)],
        [whole(kept.shape), whole((1,) + square)],
        flops=4 << 30,
        name="newton",
    )

    groups = bit_groups(n)[::-1]
    for step, (shift, count) in enumerate(groups):
        got = [pieces[0]] + [exchange(pieces[m], m << shift, n) for m in range(1, count)]
        specs = [whole(got[0].shape)] * count
        if step == 0:
            got, inverse = lax.optimization_barrier((got, inverse))
        if step + 1 < len(groups):
            following = groups[step + 1][1]
            piece = shape_of((got[0].shape[0] // following, height, LANDMARKS), BF16)
            pieces = call(
                functools.partial(merge_kernel, cols, count),
                (1,),
                [],
                got,
                specs,
                [piece] * following,
                [whole(piece.shape)] * following,
                name="merge",
            )
    small = shape_of((cols, LANDMARKS), F32)
    reply, values, grads = call(
        functools.partial(mix_kernel, cols, count),
        (1,),
        [],
        got + [inverse],
        specs + [whole((1,) + square)],
        [piece, small, small],
        [whole(piece.shape), whole(small.shape), whole(small.shape)],
        name="mix",
    )
    replies = gather_lists(reply[0], n)

    more = shape_of((LANDMARKS, PAIR), F32)
    more_q, more_k = call(
        newton_grad_kernel,
        (1,),
        [own_arr],
        [saved, values, grads, land, land],
        [whole(kept.shape), whole(small.shape), whole(small.shape), own_lq, own_lk],
        [more, more],
        [whole(more.shape)] * 2,
        flops=8 << 30,
        name="newton_grad",
    )

    replies, more_q, more_k = lax.optimization_barrier((replies, more_q, more_k))
    block = max(columns // n, 16)
    split = n * block // columns
    flat = shape_of((columns, LANDMARKS), BF16)
    weight_piece = shape_of((n // size, block, width // split), BF16)
    attn, mixer, norm, center, *weight_pieces = call(
        functools.partial(attend_kernel, n, heads),
        (pairs,),
        [me_arr],
        [fb, tops, cotangent] + replies,
        [factor_pair, whole(tops.shape), whole(cotangent.shape)] + [whole(replies[0].shape)] * size,
        [shape_of((rows, columns), BF16), flat, flat, shape_of((heads, LANDMARKS), F32)]
        + [weight_piece] * size,
        [token_pair, whole(flat.shape), whole(flat.shape), whole((heads, LANDMARKS))]
        + [whole(weight_piece.shape)] * size,
        [
            pltpu.VMEM((n, cols, LANDMARKS), F32),
            pltpu.VMEM((n, cols, LANDMARKS), F32),
            pltpu.VMEM((n, 8, LANDMARKS), F32),
            pltpu.VMEM((columns // block, block, width), F32),
            pltpu.VMEM((columns, rows), BF16),
        ],
        flops=4 << 30,
        name="attend",
    )
    (shift, count), later = groups[0], groups[1:]
    weight_sum = scatter_step(weight_pieces, shift, count, n).astype(BF16)
    (pb, key_rows, value_rows), weight_sum = lax.optimization_barrier(
        ((pb, key_rows, value_rows), weight_sum)
    )
    following = later[0][1]
    weight_sum = weight_sum.reshape((-1, following) + weight_sum.shape[1:])
    weight_own = scatter_pieces([weight_sum[:, m] for m in range(following)], n, later)[0].astype(BF16)
    flat_pair = pl.BlockSpec((PAIR, LANDMARKS), lambda j, *_: (j, 0))
    land_pair = pl.BlockSpec((LANDMARKS, PAIR), lambda j, *_: (0, j))
    centers = whole((heads, LANDMARKS))
    tokens = shape_of((rows, columns), BF16)
    land_shape = shape_of((LANDMARKS, columns), BF16)
    land_k, grad_sf = call(
        query_land_kernel,
        (pairs,),
        [own_arr],
        [queries, grad_attn, fb, mixer, more_k],
        [token_pair, token_pair, factor_pair, flat_pair, whole(more.shape)],
        [land_shape, factors],
        [land_pair, factor_pair],
        flops=4 << 30,
        name="query_land",
    )
    (shift, count), later = groups[0], groups[1:]
    following = later[0][1]
    weight_sum = scatter_step(weight_pieces, shift, count, n).astype(BF16)
    (pb, key_rows, value_rows), weight_sum, land_k = lax.optimization_barrier(
        ((pb, key_rows, value_rows), weight_sum, land_k)
    )
    if sorted_here:
        land_piece, pieces_count = shape_of((n // size, land_dev, 2 * columns), BF16), size
    else:
        land_piece, pieces_count = shape_of((LANDMARKS // 16, 16, 2 * columns), BF16), 1
    grad_sb, *land_pieces = call(
        key_land_kernel,
        (pairs,),
        [own_arr],
        [key_rows, value_rows, pb, norm, center, more_q, land_k],
        [token_pair, token_pair, factor_pair, flat_pair, centers, whole(more.shape)]
        + [whole(land_shape.shape)],
        [factors] + [land_piece] * pieces_count,
        [factor_pair] + [whole(land_piece.shape)] * pieces_count,
        [pltpu.VMEM(land_shape.shape, BF16)],
        flops=4 << 30,
        name="key_land",
    )
    land_pieces, grad_sf, attn = lax.optimization_barrier((land_pieces, grad_sf, attn))
    query_f = call(
        query_kernel,
        (pairs,),
        [],
        [grad_sf, land],
        [factor_pair, lk_pair],
        tokens,
        token_pair,
        flops=2 << 30,
        name="query_grad",
    )
    half = width // 2
    row_block = pl.BlockSpec((rows // 4, columns), lambda j, _: (j, 0))
    half_block = pl.BlockSpec((rows // 4, half), lambda j, _: (j, 0))
    there = call(
        part_kernel,
        (4,),
        [mine_arr],
        [attn, out_weight],
        [row_block, pl.BlockSpec((columns, half), lambda j, mine: (0, 1 - mine[0]))],
        shape_of((rows, half), BF16),
        half_block,
        flops=1 << 30,
        name="part",
    )

    if not sorted_here:
        land_pieces = split_by_partner(land_pieces[0].reshape(n, land_dev, 2 * columns), n, me)
    weight_sum = weight_sum.reshape((-1, following) + weight_sum.shape[1:])
    weight_own = scatter_pieces([weight_sum[:, m] for m in range(following)], n, later)[0].astype(BF16)
    land_pieces, weight_own = lax.optimization_barrier((land_pieces, weight_own))
    land_sum = scatter_step(land_pieces, shift, count, n).astype(BF16)
    land_sum, weight_own, query_f, there = lax.optimization_barrier(
        (land_sum, weight_own, query_f, there)
    )
    land_sum, weight_own, grad_sb = lax.optimization_barrier((land_sum, weight_own, grad_sb))
    arrived = lax.ppermute(there, "head", [(0, 1), (1, 0)])
    arrived, grad_sb = lax.optimization_barrier((arrived, grad_sb))
    key_b, value_grad = call(
        key_kernel,
        (pairs,),
        [],
        [grad_sb, pb, land, norm],
        [factor_pair, factor_pair, lq_pair, flat_pair],
        [tokens, tokens],
        [token_pair, token_pair],
        flops=4 << 30,
        name="key_grad",
    )

    mixed = call(
        mixed_kernel,
        (4,),
        [mine_arr],
        [attn, out_weight, arrived],
        [row_block, pl.BlockSpec((columns, half), lambda j, mine: (0, mine[0])), half_block],
        shape_of((rows, half), BF16),
        half_block,
        flops=1 << 30,
        name="mixed",
    )
    if len(later) == 1 and weight_own.shape[1] == land_sum.shape[2]:
        (shift, count), tall = later[0], weight_own.shape[0]
        got = [
            exchange(jnp.concatenate([weight_own, land_sum[m]], axis=0), m << shift, n)
            for m in range(1, count)
        ]
        weights = [weight_own[None]] + [part[None, :tall] for part in got]
        land_own = sum(part.astype(F32) for part in [land_sum[0]] + [part[tall:] for part in got])
    else:
        weights = gather_first(weight_own, n)
        land_sum = land_sum.reshape((-1, following) + land_sum.shape[1:])
        land_own = scatter_pieces([land_sum[:, m] for m in range(following)], n, later)[0]
    land_own = land_own * (1.0 / seg_len)
    weights, key_b = lax.optimization_barrier((weights, key_b))
    weights = gather_rest(weights, n)
    weights, mixed = lax.optimization_barrier((weights, mixed))
    weight_grad = call(
        functools.partial(unpack_kernel, split),
        (1,),
        [me_arr],
        weights,
        [whole(weights[0].shape)] * size,
        pltpu.HBM((columns, width), F32),
        in_hbm,
        [pltpu.VMEM((n,) + weights[0].shape[1:], F32), pltpu.SemaphoreType.DMA((n,))],
        name="unpack",
    )

    def finish(token_part, land_part):
        return (
            (token_part.reshape(land_dev, seg_len, columns) + land_part[:, None, :])
            .astype(BF16)
            .reshape(rows, columns)
        )

    query_grad = finish(query_f, land_own[:, :columns])
    key_grad = finish(key_b, land_own[:, columns:])
    return (mixed, query_grad, key_grad, value_grad, weight_grad)


def solution(mesh):
    return jax.shard_map(
        local,
        mesh=mesh,
        in_specs=(
            P("seq", "head"),
            P("seq", "head"),
            P("seq", "head"),
            P("head", None),
            P("seq", None),
        ),
        out_specs=(
            P("seq", "head"),
            P("seq", "head"),
            P("seq", "head"),
            P("seq", "head"),
            P("head", None),
        ),
        check_vma=False,
    )
```

```python
import functools

import jax
import jax.numpy as jnp
from jax import lax
from jax.experimental import pallas as pl
from jax.experimental.pallas import tpu as pltpu
from jax.sharding import PartitionSpec as P

DH = 64
PAIR = 2 * DH
LANDMARKS = 256
ITERS = 2
SCALE = 0.125
CHUNK = 256
EXTRA = 8
F32 = jnp.float32
BF16 = jnp.bfloat16
PARAMS = pltpu.CompilerParams(vmem_limit_bytes=24 * 1024 * 1024)


def dot(left, right, dims=((1,), (0,))):
    return lax.dot_general(left, right, (dims, ((), ())), preferred_element_type=F32)


NT = ((1,), (1,))
TN = ((0,), (0,))


def halves(value):
    high = value.astype(BF16)
    return high, (value - high.astype(F32)).astype(BF16)


def dot_exact(left, right, dims=((1,), (0,))):
    return dot(left[0], right[0], dims) + (
        dot(left[0], right[1], dims) + dot(left[1], right[0], dims)
    )


def turned(pair):
    return pair[0].T, pair[1].T


def keep_rows(block, which):
    rows = lax.broadcasted_iota(jnp.int32, block.shape, 0) // DH
    return jnp.where(rows == which, block, jnp.zeros_like(block))


def keep_lanes(block, which):
    lanes = lax.broadcasted_iota(jnp.int32, block.shape, 1) // DH
    return jnp.where(lanes == which, block, jnp.zeros_like(block))


def fold(block, op):
    parts = block.reshape(block.shape[0] // 8, 8, block.shape[1])
    return op(parts, axis=0)


def exchange(block, mask, n):
    return lax.ppermute(block, "seq", [(i, i ^ mask) for i in range(n)])


def bit_groups(n):
    bits = n.bit_length() - 1
    groups = []
    while bits > 0:
        take = 2 if bits % 2 == 0 else 1
        bits -= take
        groups.append((bits, 1 << take))
    return groups


def gather_first(block, n):
    shift, size = bit_groups(n)[0]
    held = block[None]
    return [held] + [exchange(held, m << shift, n) for m in range(1, size)]


def gather_rest(got, n):
    for shift, size in bit_groups(n)[1:]:
        held = jnp.stack(got, axis=1).reshape((-1,) + got[0].shape[1:])
        got = [held] + [exchange(held, m << shift, n) for m in range(1, size)]
    return got


def gather_lists(block, n):
    return gather_rest(gather_first(block, n), n)


def gather_ordered(block, n, me):
    got = gather_lists(block, n)
    held = jnp.stack(got, axis=1).reshape((n,) + block.shape)
    return held.at[jnp.arange(n) ^ me].get(mode="promise_in_bounds")


def split_by_partner(blocks, n, me):
    size = bit_groups(n)[-1][1]
    return [
        blocks.at[(jnp.arange(n // size) * size + m) ^ me].get(mode="promise_in_bounds")
        for m in range(size)
    ]


def scatter_step(pieces, shift, size, n):
    got = [pieces[0]] + [exchange(pieces[m], m << shift, n) for m in range(1, size)]
    return sum(part.astype(F32) for part in got)


def scatter_pieces(pieces, n, groups):
    for step, (shift, size) in enumerate(groups):
        held = scatter_step(pieces, shift, size, n)
        if step + 1 < len(groups):
            following = groups[step + 1][1]
            held = held.astype(BF16).reshape((-1, following) + held.shape[1:])
            pieces = [held[:, m] for m in range(following)]
    return held


def means_kernel(seg_len, q_ref, k_ref, out_ref, in_ref, sum_ref, sems):
    rows, columns = q_ref.shape
    steps = sems.shape[1]
    height = rows // steps
    copies = {}
    for c in range(steps):
        part = pl.ds(c * height, height)
        for side, ref in enumerate((q_ref, k_ref)):
            copies[side, c] = pltpu.make_async_copy(ref.at[part], in_ref.at[side, part], sems.at[side, c])
            copies[side, c].start()
    for c in range(steps):
        for side in range(2):
            copies[side, c].wait()
            span = slice(side * columns, (side + 1) * columns)
            for s in range(c * height // seg_len, (c + 1) * height // seg_len):
                total = fold(in_ref[side, s * seg_len : (s + 1) * seg_len, :].astype(F32), jnp.sum)
                sum_ref[s : s + 1, span] = jnp.sum(total, axis=0, keepdims=True)
    out_ref[...] = (sum_ref[...] * (1.0 / seg_len)).astype(BF16)


def forward_kernel(n, heads, count, me_ref, q_ref, k_ref, v_ref, g_ref, *refs):
    size = bit_groups(n)[-1][1]
    in_refs = refs[:count]
    fb_ref, pb_ref, top_ref, land_ref = refs[count : count + 4]
    out_refs = refs[count + 4 : count + 4 + size]
    score_ref, message_ref = refs[count + 4 + size :]
    pair = pl.program_id(0)
    columns = land_ref.shape[1] // 2

    @pl.when(pair == 0)
    def _():
        for m in range(count):
            held, height, _ = in_refs[m].shape
            for t in range(held):
                at = pl.multiple_of(((t * count + m) ^ me_ref[1]) * height, height)
                land_ref[pl.ds(at, height), :] = in_refs[m][t]

    here = pl.multiple_of(pair * PAIR, PAIR)
    lq_pair = land_ref[:, pl.ds(here, PAIR)]
    lk_pair = land_ref[:, pl.ds(columns + here, PAIR)]
    rows = q_ref.shape[0]
    parts = n // heads
    cols = DH // parts
    gt = g_ref[...].T
    vt = v_ref[...].T
    for h in range(2):
        lk = keep_lanes(lk_pair * SCALE, h).astype(BF16)
        lq = keep_lanes(lq_pair * SCALE, h).astype(BF16)
        span = slice(h * LANDMARKS, (h + 1) * LANDMARKS)
        top = None
        for c in range(0, rows, CHUNK):
            part = slice(c, c + CHUNK)
            sb = dot(k_ref[part, :], lq, NT)
            score_ref[part, :] = sb
            high = fold(sb, jnp.max)
            top = high if top is None else jnp.maximum(top, high)
            sf = dot(q_ref[part, :], lk, NT)
            e = jnp.exp(sf - jnp.max(sf, axis=1, keepdims=True))
            fb_ref[part, span] = (e * (1.0 / jnp.sum(e, axis=1, keepdims=True))).astype(BF16)
        top = jnp.max(top, axis=0, keepdims=True).astype(BF16).astype(F32)
        total = None
        for c in range(0, rows, CHUNK):
            part = slice(c, c + CHUNK)
            p = jnp.exp(score_ref[part, :] - top)
            add = fold(p, jnp.sum)
            total = add if total is None else total + add
            pb_ref[part, span] = p.astype(BF16)
        total = jnp.sum(total, axis=0, keepdims=True)
        top_ref[0, h : h + 1, :] = top
        grads = dot(gt[h * DH : (h + 1) * DH], fb_ref[:, span])
        vals = dot(vt[h * DH : (h + 1) * DH], pb_ref[:, span])
        high, low = halves(total)
        extra = three_rows(top, high.astype(F32), low.astype(F32))
        for p in range(parts):
            cut = slice(p * cols, (p + 1) * cols)
            message_ref[(2 * pair + h) * parts + p] = jnp.concatenate(
                [vals[cut], grads[cut], extra], axis=0
            ).astype(BF16)

    @pl.when(pair == pl.num_programs(0) - 1)
    def _():
        for m in range(size):
            for t in range(n // size):
                out_refs[m][t] = message_ref[(t * size + m) ^ me_ref[0]]


def merge(items, cols):
    tops = [item[2 * cols : 2 * cols + 1] for item in items]
    peak = functools.reduce(jnp.maximum, tops)
    vals = grads = total = 0.0
    for item, top in zip(items, tops):
        factor = jnp.exp(top - peak)
        vals = vals + item[:cols] * factor
        grads = grads + item[cols : 2 * cols]
        total = total + (
            item[2 * cols + 1 : 2 * cols + 2] + item[2 * cols + 2 : 2 * cols + 3]
        ) * factor
    return vals, grads, peak, total


def three_rows(first, second, third):
    row = lax.broadcasted_iota(jnp.int32, (EXTRA, LANDMARKS), 0)
    return jnp.where(row == 0, first, jnp.where(row == 1, second, jnp.where(row == 2, third, 0.0)))


def merge_kernel(cols, count, *refs):
    in_refs, out_refs = refs[:count], refs[count:]
    following = len(out_refs)
    for t in range(in_refs[0].shape[0]):
        vals, grads, peak, total = merge([ref[t].astype(F32) for ref in in_refs], cols)
        high, low = halves(total)
        extra = three_rows(peak, high.astype(F32), low.astype(F32))
        out_refs[t % following][t // following] = jnp.concatenate(
            [vals, grads, extra], axis=0
        ).astype(BF16)


def mix_kernel(cols, count, *refs):
    in_refs, z_ref = refs[:count], refs[count]
    reply_ref, values_ref, grads_ref = refs[count + 1 :]
    vals, grads, peak, total = merge([ref[0].astype(F32) for ref in in_refs], cols)
    inverse = halves(z_ref[0])
    values = vals / total
    mixer = dot_exact(halves(values), inverse, NT)
    norm = dot_exact(halves(grads), inverse) / total
    high, low = halves(jnp.sum(norm * values, axis=0, keepdims=True))
    extra = three_rows(peak, high.astype(F32), low.astype(F32))
    reply_ref[0] = jnp.concatenate([mixer, norm, extra], axis=0).astype(BF16)
    values_ref[...] = values
    grads_ref[...] = grads


def soft_rows(scores):
    e = jnp.exp(scores - jnp.max(scores, axis=1, keepdims=True))
    return e / jnp.sum(e, axis=1, keepdims=True)


def eye():
    shape = (LANDMARKS, LANDMARKS)
    same = lax.broadcasted_iota(jnp.int32, shape, 0) == lax.broadcasted_iota(jnp.int32, shape, 1)
    return same.astype(F32)


def column_top(amat):
    return jnp.max(jnp.sum(amat, axis=0, keepdims=True), axis=1, keepdims=True)


def newton_kernel(own_ref, lq_ref, lk_ref, saved_ref, z_ref):
    which = own_ref[1]
    amat = soft_rows(dot(keep_lanes(lq_ref[...] * SCALE, which).astype(BF16), lk_ref[...], NT))
    saved_ref[0] = amat
    current = amat.T / column_top(amat)
    ident = eye()
    amat = halves(amat)
    for i in range(ITERS):
        saved_ref[1 + 4 * i] = current
        z = halves(current)
        x_full = dot_exact(amat, z)
        saved_ref[2 + 4 * i] = x_full
        x = halves(x_full)
        inner = 15.0 * ident - dot_exact(x, halves(7.0 * ident - x_full))
        saved_ref[3 + 4 * i] = inner
        inner = 13.0 * ident - dot_exact(x, halves(inner))
        saved_ref[4 + 4 * i] = inner
        current = 0.25 * dot_exact(z, halves(inner))
    z_ref[0] = current


def newton_grad_kernel(own_ref, saved_ref, values_ref, grads_ref, lq_ref, lk_ref, q_ref, k_ref):
    which = own_ref[1]
    ident = eye()
    amat = saved_ref[0]
    amat_t = turned(halves(amat))
    grad_z = dot_exact(halves(grads_ref[...]), halves(values_ref[...]), TN)
    grad_a = jnp.zeros_like(amat)
    for i in reversed(range(ITERS)):
        z = halves(saved_ref[1 + 4 * i])
        x_full = saved_ref[2 + 4 * i]
        x_t = turned(halves(x_full))
        first = halves(7.0 * ident - x_full)
        second = halves(saved_ref[3 + 4 * i])
        third = halves(saved_ref[4 + 4 * i])
        dz = halves(0.25 * grad_z)
        d_third = halves(dot_exact(turned(z), dz))
        d_second = halves(-dot_exact(x_t, d_third))
        d_x = -dot_exact(d_third, second, NT) - dot_exact(d_second, first, NT)
        d_x = halves(d_x + dot_exact(x_t, d_second))
        grad_a = grad_a + dot_exact(d_x, z, NT)
        grad_z = dot_exact(dz, third, NT) + dot_exact(amat_t, d_x)
    grad_a = grad_a + grad_z.T / column_top(amat)
    grad_s = amat * (grad_a - jnp.sum(amat * grad_a, axis=1, keepdims=True)) * SCALE
    high, low = halves(grad_s)
    lq = keep_lanes(lq_ref[...], which)
    lk = keep_lanes(lk_ref[...], which)
    q_ref[...] = dot(high, lk) + dot(low, lk)
    k_ref[...] = dot(high.T, lq) + dot(low.T, lq)


def attend_kernel(n, heads, me_ref, fb_ref, top_ref, cot_ref, *refs):
    size = bit_groups(n)[-1][1]
    parts = n // heads
    cols = DH // parts
    reply_refs = refs[:size]
    attn_ref, mixer_ref, norm_ref, center_ref = refs[size : size + 4]
    out_refs = refs[size + 4 : 2 * size + 4]
    w_ref, d_ref, e_ref, sum_ref, all_ref = refs[2 * size + 4 :]
    pair = pl.program_id(0)

    @pl.when(pair == 0)
    def _():
        for m in range(size):
            for t in range(n // size):
                reply = reply_refs[m][t].astype(F32)
                at = (t * size + m) ^ me_ref[0]
                w_ref[at] = reply[:cols]
                d_ref[at] = reply[cols : 2 * cols]
                e_ref[at] = reply[2 * cols : 2 * cols + 8]
        for h in range(heads):
            cut = slice(h * parts, (h + 1) * parts)
            span = slice(h * DH, (h + 1) * DH)
            mixer_ref[span, :] = w_ref[cut].reshape(DH, LANDMARKS).astype(BF16)
            extra = e_ref[cut]
            top = top_ref[h // 2, h % 2 : h % 2 + 1, :]
            factor = jnp.exp(top - extra[0, 0:1, :])
            norm_ref[span, :] = (d_ref[cut].reshape(DH, LANDMARKS) * factor).astype(BF16)
            sums = jnp.sum(extra, axis=0)
            center_ref[h : h + 1, :] = (sums[1:2] + sums[2:3]) * factor

    mixer = mixer_ref[pl.ds(pl.multiple_of(pair * PAIR, PAIR), PAIR), :]
    attn = dot(fb_ref[:, :LANDMARKS], keep_rows(mixer, 0), NT) + dot(
        fb_ref[:, LANDMARKS:], keep_rows(mixer, 1), NT
    )
    attn = attn.astype(BF16)
    attn_ref[...] = attn
    all_ref[pl.ds(pl.multiple_of(pair * PAIR, PAIR), PAIR), :] = attn.T

    @pl.when(pair == pl.num_programs(0) - 1)
    def _():
        block, split = sum_ref.shape[1], n // sum_ref.shape[0]
        width = cot_ref.shape[1]
        sum_ref[...] = dot(all_ref[...], cot_ref[...]).reshape(sum_ref.shape)
        for m in range(size):
            for t in range(n // size):
                at = (t * size + m) ^ me_ref[0]
                if split == 1:
                    out_refs[m][t] = sum_ref[at].astype(BF16)
                else:
                    side = pl.multiple_of((at % split) * (width // split), width // split)
                    out_refs[m][t] = sum_ref[at // split, :, pl.ds(side, width // split)].astype(BF16)


def soft_grad(fb_ref, g_ref, mixer_ref, ds_ref):
    for h in range(2):
        span = slice(h * LANDMARKS, (h + 1) * LANDMARKS)
        mixer = keep_rows(mixer_ref[...], h)
        for c in range(0, fb_ref.shape[0], CHUNK):
            part = slice(c, c + CHUNK)
            f = fb_ref[part, span].astype(F32)
            df = dot(g_ref[part, :], mixer)
            ds_ref[part, span] = (f * (df - jnp.sum(f * df, axis=1, keepdims=True))).astype(BF16)


def weight_soft_grad(pb_ref, v_ref, norm_ref, center_ref, ds_ref):
    for h in range(2):
        span = slice(h * LANDMARKS, (h + 1) * LANDMARKS)
        norm = keep_rows(norm_ref[...], h)
        center = center_ref[pl.ds(2 * pl.program_id(0) + h, 1), :]
        for c in range(0, pb_ref.shape[0], CHUNK):
            part = slice(c, c + CHUNK)
            dp = dot(v_ref[part, :], norm)
            ds_ref[part, span] = (pb_ref[part, span].astype(F32) * (dp - center)).astype(BF16)


def land_sums(ds_ref, x_ref, own_ref, more_ref):
    xt = x_ref[...].T
    sums = jnp.concatenate(
        [dot(xt[:DH], ds_ref[:, :LANDMARKS]), dot(xt[DH:], ds_ref[:, LANDMARKS:])], axis=0
    )
    here = (own_ref[0] == pl.program_id(0)).astype(F32)
    return (sums.T * SCALE + more_ref[...] * here).astype(BF16)


def token_part(ds_ref, land_ref, out_ref):
    land = land_ref[...] * SCALE
    total = dot(ds_ref[:, :LANDMARKS], keep_lanes(land, 0).astype(BF16)) + dot(
        ds_ref[:, LANDMARKS:], keep_lanes(land, 1).astype(BF16)
    )
    out_ref[...] = total.astype(BF16)


def query_land_kernel(own_ref, q_ref, g_ref, fb_ref, mixer_ref, more_ref, land_ref, ds_ref):
    soft_grad(fb_ref, g_ref, mixer_ref, ds_ref)
    land_ref[...] = land_sums(ds_ref, q_ref, own_ref, more_ref)


def key_land_kernel(own_ref, k_ref, v_ref, pb_ref, norm_ref, center_ref, more_ref, other_ref, *refs):
    ds_ref, out_refs, land_ref = refs[0], refs[1:-1], refs[-1]
    size = len(out_refs)
    columns = other_ref.shape[1]
    pair = pl.program_id(0)
    weight_soft_grad(pb_ref, v_ref, norm_ref, center_ref, ds_ref)
    land_ref[:, pl.ds(pl.multiple_of(pair * PAIR, PAIR), PAIR)] = land_sums(
        ds_ref, k_ref, own_ref, more_ref
    )

    @pl.when(pair == pl.num_programs(0) - 1)
    def _():
        for m in range(size):
            held, height, _ = out_refs[m].shape
            for t in range(held):
                at = pl.multiple_of(((t * size + m) ^ own_ref[2]) * height, height)
                out_refs[m][t, :, :columns] = land_ref[pl.ds(at, height), :]
                out_refs[m][t, :, columns:] = other_ref[pl.ds(at, height), :]


def query_kernel(ds_ref, lk_ref, out_ref):
    token_part(ds_ref, lk_ref, out_ref)


def key_kernel(ds_ref, pb_ref, lq_ref, norm_ref, out_ref, value_ref):
    token_part(ds_ref, lq_ref, out_ref)
    value_ref[...] = (
        dot(pb_ref[:, :LANDMARKS], keep_rows(norm_ref[...], 0), NT)
        + dot(pb_ref[:, LANDMARKS:], keep_rows(norm_ref[...], 1), NT)
    ).astype(BF16)


def part_kernel(_, attn_ref, weight_ref, out_ref):
    out_ref[...] = dot(attn_ref[...], weight_ref[...]).astype(BF16)


def mixed_kernel(_, attn_ref, weight_ref, other_ref, out_ref):
    out_ref[...] = (dot(attn_ref[...], weight_ref[...]) + other_ref[...].astype(F32)).astype(BF16)


def unpack_kernel(split, me_ref, *refs):
    in_refs, (out_ref, wide_ref, sems) = refs[:-3], refs[-3:]
    size = len(in_refs)
    held, block, width = in_refs[0].shape
    copies = []
    for t in range(held):
        for m in range(size):
            slot = t * size + m
            at = slot ^ me_ref[0]
            row = pl.ds(pl.multiple_of((at // split) * block, block), block)
            if split == 1:
                target = out_ref.at[row]
            else:
                target = out_ref.at[row, pl.ds(pl.multiple_of((at % split) * width, width), width)]
            wide_ref[slot] = in_refs[m][t].astype(F32)
            copies.append(pltpu.make_async_copy(wide_ref.at[slot], target, sems.at[slot]))
            copies[-1].start()
    for copy in copies:
        copy.wait()


def held_in_hbm(x):
    return pltpu.with_memory_space_constraint(x, pltpu.HBM)


def whole(shape):
    return pl.BlockSpec(shape, lambda *_: (0,) * len(shape))


def shape_of(shape, dtype):
    return jax.ShapeDtypeStruct(shape, dtype)


def call(kernel, grid, scalars, ins, in_specs, outs, out_specs, scratch=(), flops=0, name=None, aliases={}):
    return pl.pallas_call(
        kernel,
        grid_spec=pltpu.PrefetchScalarGridSpec(
            num_scalar_prefetch=len(scalars),
            grid=grid,
            in_specs=in_specs,
            out_specs=out_specs,
            scratch_shapes=list(scratch),
        ),
        out_shape=outs,
        compiler_params=PARAMS,
        input_output_aliases=aliases,
        cost_estimate=pl.CostEstimate(flops=flops, bytes_accessed=4 << 20, transcendentals=0),
        name=name,
    )(*scalars, *ins)


def local(queries, key_rows, value_rows, out_weight, cotangent):
    rows, columns = queries.shape
    width = out_weight.shape[1]
    heads = columns // DH
    pairs = columns // PAIR
    n = lax.axis_size("seq")
    me = lax.axis_index("seq")
    mine = lax.axis_index("head")
    land_dev = LANDMARKS // n
    seg_len = rows // land_dev
    parts = n // heads
    cols = DH // parts
    size = bit_groups(n)[-1][1]
    height = 2 * cols + EXTRA
    own_head = me // parts

    sorted_here = land_dev % 16 == 0
    me_arr = jnp.stack([me, me if sorted_here else me * 0]).astype(jnp.int32)
    mine_arr = mine.reshape(1).astype(jnp.int32)
    own_arr = jnp.stack([own_head // 2, own_head % 2, me * 0 if land_dev % 16 else me]).astype(jnp.int32)
    steps = 4
    in_hbm = pl.BlockSpec(memory_space=pltpu.HBM)
    own = call(
        functools.partial(means_kernel, seg_len),
        (1,),
        [],
        [held_in_hbm(queries), held_in_hbm(key_rows)],
        [in_hbm, in_hbm],
        shape_of((land_dev, 2 * columns), BF16),
        whole((land_dev, 2 * columns)),
        [
            pltpu.VMEM((2, rows, columns), BF16),
            pltpu.VMEM((land_dev, 2 * columns), F32),
            pltpu.SemaphoreType.DMA((2, steps)),
        ],
        name="means",
    )
    own, me_arr, mine_arr, own_arr = lax.optimization_barrier((own, me_arr, mine_arr, own_arr))
    grad_attn = dot(cotangent, out_weight, NT).astype(BF16)
    if sorted_here:
        lands = gather_lists(own, n)
    else:
        lands = [gather_ordered(own, n, me).reshape(LANDMARKS // 16, 16, 2 * columns)]

    token_pair = pl.BlockSpec((rows, PAIR), lambda j, *_: (0, j))
    factor_pair = pl.BlockSpec((rows, 2 * LANDMARKS), lambda j, *_: (0, j))
    lq_pair = pl.BlockSpec((LANDMARKS, PAIR), lambda j, *_: (0, j))
    lk_pair = pl.BlockSpec((LANDMARKS, PAIR), lambda j, *_: (0, j + pairs))
    factors = shape_of((rows, heads * LANDMARKS), BF16)
    piece = shape_of((n // size, height, LANDMARKS), BF16)

    fb, pb, tops, land, *pieces = call(
        functools.partial(forward_kernel, n, heads, len(lands)),
        (pairs,),
        [me_arr],
        [queries, key_rows, value_rows, grad_attn] + lands,
        [token_pair] * 4 + [whole(lands[0].shape)] * len(lands),
        [
            factors,
            factors,
            shape_of((pairs, 8, LANDMARKS), F32),
            shape_of((LANDMARKS, 2 * columns), BF16),
        ]
        + [piece] * size,
        [
            factor_pair,
            factor_pair,
            pl.BlockSpec((1, 8, LANDMARKS), lambda j, *_: (j, 0, 0)),
            whole((LANDMARKS, 2 * columns)),
        ]
        + [whole(piece.shape)] * size,
        [
            pltpu.VMEM((rows, LANDMARKS), F32),
            pltpu.VMEM((n, height, LANDMARKS), BF16),
        ],
        flops=8 << 30,
        name="forward",
    )

    square = (LANDMARKS, LANDMARKS)
    own_lq = pl.BlockSpec((LANDMARKS, PAIR), lambda i, own: (0, own[0]))
    own_lk = pl.BlockSpec((LANDMARKS, PAIR), lambda i, own: (0, own[0] + pairs))
    kept = shape_of((1 + 4 * ITERS,) + square, F32)
    saved, inverse = call(
        newton_kernel,
        (1,),
        [own_arr],
        [land, land],
        [own_lq, own_lk],
        [kept, shape_of((1,) + square, F32)],
        [whole(kept.shape), whole((1,) + square)],
        flops=4 << 30,
        name="newton",
    )

    groups = bit_groups(n)[::-1]
    for step, (shift, count) in enumerate(groups):
        got = [pieces[0]] + [exchange(pieces[m], m << shift, n) for m in range(1, count)]
        specs = [whole(got[0].shape)] * count
        if step == 0:
            got, inverse = lax.optimization_barrier((got, inverse))
        if step + 1 < len(groups):
            following = groups[step + 1][1]
            piece = shape_of((got[0].shape[0] // following, height, LANDMARKS), BF16)
            pieces = call(
                functools.partial(merge_kernel, cols, count),
                (1,),
                [],
                got,
                specs,
                [piece] * following,
                [whole(piece.shape)] * following,
                name="merge",
            )
    small = shape_of((cols, LANDMARKS), F32)
    reply, values, grads = call(
        functools.partial(mix_kernel, cols, count),
        (1,),
        [],
        got + [inverse],
        specs + [whole((1,) + square)],
        [piece, small, small],
        [whole(piece.shape), whole(small.shape), whole(small.shape)],
        name="mix",
    )
    replies = gather_lists(reply[0], n)

    more = shape_of((LANDMARKS, PAIR), F32)
    more_q, more_k = call(
        newton_grad_kernel,
        (1,),
        [own_arr],
        [saved, values, grads, land, land],
        [whole(kept.shape), whole(small.shape), whole(small.shape), own_lq, own_lk],
        [more, more],
        [whole(more.shape)] * 2,
        flops=8 << 30,
        name="newton_grad",
    )

    replies, more_q, more_k = lax.optimization_barrier((replies, more_q, more_k))
    block = max(columns // n, 16)
    split = n * block // columns
    flat = shape_of((columns, LANDMARKS), BF16)
    weight_piece = shape_of((n // size, block, width // split), BF16)
    attn, mixer, norm, center, *weight_pieces = call(
        functools.partial(attend_kernel, n, heads),
        (pairs,),
        [me_arr],
        [fb, tops, cotangent] + replies,
        [factor_pair, whole(tops.shape), whole(cotangent.shape)] + [whole(replies[0].shape)] * size,
        [shape_of((rows, columns), BF16), flat, flat, shape_of((heads, LANDMARKS), F32)]
        + [weight_piece] * size,
        [token_pair, whole(flat.shape), whole(flat.shape), whole((heads, LANDMARKS))]
        + [whole(weight_piece.shape)] * size,
        [
            pltpu.VMEM((n, cols, LANDMARKS), F32),
            pltpu.VMEM((n, cols, LANDMARKS), F32),
            pltpu.VMEM((n, 8, LANDMARKS), F32),
            pltpu.VMEM((columns // block, block, width), F32),
            pltpu.VMEM((columns, rows), BF16),
        ],
        flops=4 << 30,
        name="attend",
    )
    (shift, count), later = groups[0], groups[1:]
    weight_sum = scatter_step(weight_pieces, shift, count, n).astype(BF16)
    (pb, key_rows, value_rows), weight_sum = lax.optimization_barrier(
        ((pb, key_rows, value_rows), weight_sum)
    )
    following = later[0][1]
    weight_sum = weight_sum.reshape((-1, following) + weight_sum.shape[1:])
    weight_own = scatter_pieces([weight_sum[:, m] for m in range(following)], n, later)[0].astype(BF16)
    flat_pair = pl.BlockSpec((PAIR, LANDMARKS), lambda j, *_: (j, 0))
    land_pair = pl.BlockSpec((LANDMARKS, PAIR), lambda j, *_: (0, j))
    centers = whole((heads, LANDMARKS))
    tokens = shape_of((rows, columns), BF16)
    land_shape = shape_of((LANDMARKS, columns), BF16)
    land_k, grad_sf = call(
        query_land_kernel,
        (pairs,),
        [own_arr],
        [queries, grad_attn, fb, mixer, more_k],
        [token_pair, token_pair, factor_pair, flat_pair, whole(more.shape)],
        [land_shape, factors],
        [land_pair, factor_pair],
        flops=4 << 30,
        name="query_land",
    )
    (shift, count), later = groups[0], groups[1:]
    following = later[0][1]
    weight_sum = scatter_step(weight_pieces, shift, count, n).astype(BF16)
    (pb, key_rows, value_rows), weight_sum, land_k = lax.optimization_barrier(
        ((pb, key_rows, value_rows), weight_sum, land_k)
    )
    if sorted_here:
        land_piece, pieces_count = shape_of((n // size, land_dev, 2 * columns), BF16), size
    else:
        land_piece, pieces_count = shape_of((LANDMARKS // 16, 16, 2 * columns), BF16), 1
    grad_sb, *land_pieces = call(
        key_land_kernel,
        (pairs,),
        [own_arr],
        [key_rows, value_rows, pb, norm, center, more_q, land_k],
        [token_pair, token_pair, factor_pair, flat_pair, centers, whole(more.shape)]
        + [whole(land_shape.shape)],
        [factors] + [land_piece] * pieces_count,
        [factor_pair] + [whole(land_piece.shape)] * pieces_count,
        [pltpu.VMEM(land_shape.shape, BF16)],
        flops=4 << 30,
        name="key_land",
    )
    land_pieces, grad_sf, attn = lax.optimization_barrier((land_pieces, grad_sf, attn))
    query_f = call(
        query_kernel,
        (pairs,),
        [],
        [grad_sf, land],
        [factor_pair, lk_pair],
        tokens,
        token_pair,
        flops=2 << 30,
        name="query_grad",
    )
    half = width // 2
    row_block = pl.BlockSpec((rows // 4, columns), lambda j, _: (j, 0))
    half_block = pl.BlockSpec((rows // 4, half), lambda j, _: (j, 0))
    there = call(
        part_kernel,
        (4,),
        [mine_arr],
        [attn, out_weight],
        [row_block, pl.BlockSpec((columns, half), lambda j, mine: (0, 1 - mine[0]))],
        shape_of((rows, half), BF16),
        half_block,
        flops=1 << 30,
        name="part",
    )

    if not sorted_here:
        land_pieces = split_by_partner(land_pieces[0].reshape(n, land_dev, 2 * columns), n, me)
    weight_sum = weight_sum.reshape((-1, following) + weight_sum.shape[1:])
    weight_own = scatter_pieces([weight_sum[:, m] for m in range(following)], n, later)[0].astype(BF16)
    land_pieces, weight_own = lax.optimization_barrier((land_pieces, weight_own))
    land_sum = scatter_step(land_pieces, shift, count, n).astype(BF16)
    land_sum, weight_own, query_f, there = lax.optimization_barrier(
        (land_sum, weight_own, query_f, there)
    )
    land_sum, weight_own, grad_sb = lax.optimization_barrier((land_sum, weight_own, grad_sb))
    key_b, value_grad = call(
        key_kernel,
        (pairs,),
        [],
        [grad_sb, pb, land, norm],
        [factor_pair, factor_pair, lq_pair, flat_pair],
        [tokens, tokens],
        [token_pair, token_pair],
        flops=4 << 30,
        name="key_grad",
    )

    arrived = lax.ppermute(there, "head", [(0, 1), (1, 0)])
    if len(later) == 1 and weight_own.shape[1] == land_sum.shape[2]:
        (shift, count), tall = later[0], weight_own.shape[0]
        got = [
            exchange(jnp.concatenate([weight_own, land_sum[m]], axis=0), m << shift, n)
            for m in range(1, count)
        ]
        weights = [weight_own[None]] + [part[None, :tall] for part in got]
        land_own = sum(part.astype(F32) for part in [land_sum[0]] + [part[tall:] for part in got])
    else:
        weights = gather_first(weight_own, n)
        land_sum = land_sum.reshape((-1, following) + land_sum.shape[1:])
        land_own = scatter_pieces([land_sum[:, m] for m in range(following)], n, later)[0]
    land_own = land_own * (1.0 / seg_len)
    weights, key_b, arrived = lax.optimization_barrier((weights, key_b, arrived))
    mixed = call(
        mixed_kernel,
        (4,),
        [mine_arr],
        [attn, out_weight, arrived],
        [row_block, pl.BlockSpec((columns, half), lambda j, mine: (0, mine[0])), half_block],
        shape_of((rows, half), BF16),
        half_block,
        flops=1 << 30,
        name="mixed",
    )
    weights = gather_rest(weights, n)
    weights, mixed = lax.optimization_barrier((weights, mixed))
    weight_grad = call(
        functools.partial(unpack_kernel, split),
        (1,),
        [me_arr],
        weights,
        [whole(weights[0].shape)] * size,
        pltpu.HBM((columns, width), F32),
        in_hbm,
        [pltpu.VMEM((n,) + weights[0].shape[1:], F32), pltpu.SemaphoreType.DMA((n,))],
        name="unpack",
    )

    def finish(token_part, land_part):
        return (
            (token_part.reshape(land_dev, seg_len, columns) + land_part[:, None, :])
            .astype(BF16)
            .reshape(rows, columns)
        )

    query_grad = finish(query_f, land_own[:, :columns])
    key_grad = finish(key_b, land_own[:, columns:])
    return (mixed, query_grad, key_grad, value_grad, weight_grad)


def solution(mesh):
    return jax.shard_map(
        local,
        mesh=mesh,
        in_specs=(
            P("seq", "head"),
            P("seq", "head"),
            P("seq", "head"),
            P("head", None),
            P("seq", None),
        ),
        out_specs=(
            P("seq", "head"),
            P("seq", "head"),
            P("seq", "head"),
            P("seq", "head"),
            P("head", None),
        ),
        check_vma=False,
    )
```

```python
import functools

import jax
import jax.numpy as jnp
from jax import lax
from jax.experimental import pallas as pl
from jax.experimental.pallas import tpu as pltpu
from jax.sharding import PartitionSpec as P

DH = 64
PAIR = 2 * DH
LANDMARKS = 256
ITERS = 2
SCALE = 0.125
CHUNK = 256
EXTRA = 8
F32 = jnp.float32
BF16 = jnp.bfloat16
PARAMS = pltpu.CompilerParams(vmem_limit_bytes=24 * 1024 * 1024)


def dot(left, right, dims=((1,), (0,))):
    return lax.dot_general(left, right, (dims, ((), ())), preferred_element_type=F32)


NT = ((1,), (1,))
TN = ((0,), (0,))


def halves(value):
    high = value.astype(BF16)
    return high, (value - high.astype(F32)).astype(BF16)


def dot_exact(left, right, dims=((1,), (0,))):
    return dot(left[0], right[0], dims) + (
        dot(left[0], right[1], dims) + dot(left[1], right[0], dims)
    )


def turned(pair):
    return pair[0].T, pair[1].T


def keep_rows(block, which):
    rows = lax.broadcasted_iota(jnp.int32, block.shape, 0) // DH
    return jnp.where(rows == which, block, jnp.zeros_like(block))


def keep_lanes(block, which):
    lanes = lax.broadcasted_iota(jnp.int32, block.shape, 1) // DH
    return jnp.where(lanes == which, block, jnp.zeros_like(block))


def fold(block, op):
    parts = block.reshape(block.shape[0] // 8, 8, block.shape[1])
    return op(parts, axis=0)


def exchange(block, mask, n):
    return lax.ppermute(block, "seq", [(i, i ^ mask) for i in range(n)])


def bit_groups(n):
    bits = n.bit_length() - 1
    groups = []
    while bits > 0:
        take = 2 if bits % 2 == 0 else 1
        bits -= take
        groups.append((bits, 1 << take))
    return groups


def gather_first(block, n):
    shift, size = bit_groups(n)[0]
    held = block[None]
    return [held] + [exchange(held, m << shift, n) for m in range(1, size)]


def gather_rest(got, n):
    for shift, size in bit_groups(n)[1:]:
        held = jnp.stack(got, axis=1).reshape((-1,) + got[0].shape[1:])
        got = [held] + [exchange(held, m << shift, n) for m in range(1, size)]
    return got


def gather_lists(block, n):
    return gather_rest(gather_first(block, n), n)


def gather_ordered(block, n, me):
    got = gather_lists(block, n)
    held = jnp.stack(got, axis=1).reshape((n,) + block.shape)
    return held.at[jnp.arange(n) ^ me].get(mode="promise_in_bounds")


def split_by_partner(blocks, n, me):
    size = bit_groups(n)[-1][1]
    return [
        blocks.at[(jnp.arange(n // size) * size + m) ^ me].get(mode="promise_in_bounds")
        for m in range(size)
    ]


def scatter_step(pieces, shift, size, n):
    got = [pieces[0]] + [exchange(pieces[m], m << shift, n) for m in range(1, size)]
    return sum(part.astype(F32) for part in got)


def scatter_pieces(pieces, n, groups):
    for step, (shift, size) in enumerate(groups):
        held = scatter_step(pieces, shift, size, n)
        if step + 1 < len(groups):
            following = groups[step + 1][1]
            held = held.astype(BF16).reshape((-1, following) + held.shape[1:])
            pieces = [held[:, m] for m in range(following)]
    return held


def means_kernel(seg_len, q_ref, k_ref, out_ref, in_ref, sum_ref, sems):
    rows, columns = q_ref.shape
    steps = sems.shape[1]
    height = rows // steps
    copies = {}
    for c in range(steps):
        part = pl.ds(c * height, height)
        for side, ref in enumerate((q_ref, k_ref)):
            copies[side, c] = pltpu.make_async_copy(ref.at[part], in_ref.at[side, part], sems.at[side, c])
            copies[side, c].start()
    for c in range(steps):
        for side in range(2):
            copies[side, c].wait()
            span = slice(side * columns, (side + 1) * columns)
            for s in range(c * height // seg_len, (c + 1) * height // seg_len):
                total = fold(in_ref[side, s * seg_len : (s + 1) * seg_len, :].astype(F32), jnp.sum)
                sum_ref[s : s + 1, span] = jnp.sum(total, axis=0, keepdims=True)
    out_ref[...] = (sum_ref[...] * (1.0 / seg_len)).astype(BF16)


def forward_kernel(n, heads, count, me_ref, q_ref, k_ref, v_ref, g_ref, *refs):
    size = bit_groups(n)[-1][1]
    in_refs = refs[:count]
    fb_ref, pb_ref, top_ref, land_ref = refs[count : count + 4]
    out_refs = refs[count + 4 : count + 4 + size]
    score_ref, message_ref = refs[count + 4 + size :]
    pair = pl.program_id(0)
    columns = land_ref.shape[1] // 2

    @pl.when(pair == 0)
    def _():
        for m in range(count):
            held, height, _ = in_refs[m].shape
            for t in range(held):
                at = pl.multiple_of(((t * count + m) ^ me_ref[1]) * height, height)
                land_ref[pl.ds(at, height), :] = in_refs[m][t]

    here = pl.multiple_of(pair * PAIR, PAIR)
    lq_pair = land_ref[:, pl.ds(here, PAIR)]
    lk_pair = land_ref[:, pl.ds(columns + here, PAIR)]
    rows = q_ref.shape[0]
    parts = n // heads
    cols = DH // parts
    gt = g_ref[...].T
    vt = v_ref[...].T
    for h in range(2):
        lk = keep_lanes(lk_pair * SCALE, h).astype(BF16)
        lq = keep_lanes(lq_pair * SCALE, h).astype(BF16)
        span = slice(h * LANDMARKS, (h + 1) * LANDMARKS)
        top = None
        for c in range(0, rows, CHUNK):
            part = slice(c, c + CHUNK)
            sb = dot(k_ref[part, :], lq, NT)
            score_ref[part, :] = sb
            high = fold(sb, jnp.max)
            top = high if top is None else jnp.maximum(top, high)
            sf = dot(q_ref[part, :], lk, NT)
            e = jnp.exp(sf - jnp.max(sf, axis=1, keepdims=True))
            fb_ref[part, span] = (e * (1.0 / jnp.sum(e, axis=1, keepdims=True))).astype(BF16)
        top = jnp.max(top, axis=0, keepdims=True).astype(BF16).astype(F32)
        total = None
        for c in range(0, rows, CHUNK):
            part = slice(c, c + CHUNK)
            p = jnp.exp(score_ref[part, :] - top)
            add = fold(p, jnp.sum)
            total = add if total is None else total + add
            pb_ref[part, span] = p.astype(BF16)
        total = jnp.sum(total, axis=0, keepdims=True)
        top_ref[0, h : h + 1, :] = top
        grads = dot(gt[h * DH : (h + 1) * DH], fb_ref[:, span])
        vals = dot(vt[h * DH : (h + 1) * DH], pb_ref[:, span])
        high, low = halves(total)
        extra = three_rows(top, high.astype(F32), low.astype(F32))
        for p in range(parts):
            cut = slice(p * cols, (p + 1) * cols)
            message_ref[(2 * pair + h) * parts + p] = jnp.concatenate(
                [vals[cut], grads[cut], extra], axis=0
            ).astype(BF16)

    @pl.when(pair == pl.num_programs(0) - 1)
    def _():
        for m in range(size):
            for t in range(n // size):
                out_refs[m][t] = message_ref[(t * size + m) ^ me_ref[0]]


def merge(items, cols):
    tops = [item[2 * cols : 2 * cols + 1] for item in items]
    peak = functools.reduce(jnp.maximum, tops)
    vals = grads = total = 0.0
    for item, top in zip(items, tops):
        factor = jnp.exp(top - peak)
        vals = vals + item[:cols] * factor
        grads = grads + item[cols : 2 * cols]
        total = total + (
            item[2 * cols + 1 : 2 * cols + 2] + item[2 * cols + 2 : 2 * cols + 3]
        ) * factor
    return vals, grads, peak, total


def three_rows(first, second, third):
    row = lax.broadcasted_iota(jnp.int32, (EXTRA, LANDMARKS), 0)
    return jnp.where(row == 0, first, jnp.where(row == 1, second, jnp.where(row == 2, third, 0.0)))


def merge_kernel(cols, count, *refs):
    in_refs, out_refs = refs[:count], refs[count:]
    following = len(out_refs)
    for t in range(in_refs[0].shape[0]):
        vals, grads, peak, total = merge([ref[t].astype(F32) for ref in in_refs], cols)
        high, low = halves(total)
        extra = three_rows(peak, high.astype(F32), low.astype(F32))
        out_refs[t % following][t // following] = jnp.concatenate(
            [vals, grads, extra], axis=0
        ).astype(BF16)


def mix_kernel(cols, count, *refs):
    in_refs, z_ref = refs[:count], refs[count]
    reply_ref, values_ref, grads_ref = refs[count + 1 :]
    vals, grads, peak, total = merge([ref[0].astype(F32) for ref in in_refs], cols)
    inverse = halves(z_ref[0])
    values = vals / total
    mixer = dot_exact(halves(values), inverse, NT)
    norm = dot_exact(halves(grads), inverse) / total
    high, low = halves(jnp.sum(norm * values, axis=0, keepdims=True))
    extra = three_rows(peak, high.astype(F32), low.astype(F32))
    reply_ref[0] = jnp.concatenate([mixer, norm, extra], axis=0).astype(BF16)
    values_ref[...] = values
    grads_ref[...] = grads


def soft_rows(scores):
    e = jnp.exp(scores - jnp.max(scores, axis=1, keepdims=True))
    return e / jnp.sum(e, axis=1, keepdims=True)


def eye():
    shape = (LANDMARKS, LANDMARKS)
    same = lax.broadcasted_iota(jnp.int32, shape, 0) == lax.broadcasted_iota(jnp.int32, shape, 1)
    return same.astype(F32)


def column_top(amat):
    return jnp.max(jnp.sum(amat, axis=0, keepdims=True), axis=1, keepdims=True)


def newton_kernel(own_ref, lq_ref, lk_ref, saved_ref, z_ref):
    which = own_ref[1]
    amat = soft_rows(dot(keep_lanes(lq_ref[...] * SCALE, which).astype(BF16), lk_ref[...], NT))
    saved_ref[0] = amat
    current = amat.T / column_top(amat)
    ident = eye()
    amat = halves(amat)
    for i in range(ITERS):
        saved_ref[1 + 4 * i] = current
        z = halves(current)
        x_full = dot_exact(amat, z)
        saved_ref[2 + 4 * i] = x_full
        x = halves(x_full)
        inner = 15.0 * ident - dot_exact(x, halves(7.0 * ident - x_full))
        saved_ref[3 + 4 * i] = inner
        inner = 13.0 * ident - dot_exact(x, halves(inner))
        saved_ref[4 + 4 * i] = inner
        current = 0.25 * dot_exact(z, halves(inner))
    z_ref[0] = current


def newton_grad_kernel(own_ref, saved_ref, values_ref, grads_ref, lq_ref, lk_ref, q_ref, k_ref):
    which = own_ref[1]
    ident = eye()
    amat = saved_ref[0]
    amat_t = turned(halves(amat))
    grad_z = dot_exact(halves(grads_ref[...]), halves(values_ref[...]), TN)
    grad_a = jnp.zeros_like(amat)
    for i in reversed(range(ITERS)):
        z = halves(saved_ref[1 + 4 * i])
        x_full = saved_ref[2 + 4 * i]
        x_t = turned(halves(x_full))
        first = halves(7.0 * ident - x_full)
        second = halves(saved_ref[3 + 4 * i])
        third = halves(saved_ref[4 + 4 * i])
        dz = halves(0.25 * grad_z)
        d_third = halves(dot_exact(turned(z), dz))
        d_second = halves(-dot_exact(x_t, d_third))
        d_x = -dot_exact(d_third, second, NT) - dot_exact(d_second, first, NT)
        d_x = halves(d_x + dot_exact(x_t, d_second))
        grad_a = grad_a + dot_exact(d_x, z, NT)
        grad_z = dot_exact(dz, third, NT) + dot_exact(amat_t, d_x)
    grad_a = grad_a + grad_z.T / column_top(amat)
    grad_s = amat * (grad_a - jnp.sum(amat * grad_a, axis=1, keepdims=True)) * SCALE
    high, low = halves(grad_s)
    lq = keep_lanes(lq_ref[...], which)
    lk = keep_lanes(lk_ref[...], which)
    q_ref[...] = dot(high, lk) + dot(low, lk)
    k_ref[...] = dot(high.T, lq) + dot(low.T, lq)


def attend_kernel(n, heads, me_ref, fb_ref, top_ref, cot_ref, *refs):
    size = bit_groups(n)[-1][1]
    parts = n // heads
    cols = DH // parts
    reply_refs = refs[:size]
    attn_ref, mixer_ref, norm_ref, center_ref = refs[size : size + 4]
    out_refs = refs[size + 4 : 2 * size + 4]
    w_ref, d_ref, e_ref, sum_ref, all_ref = refs[2 * size + 4 :]
    pair = pl.program_id(0)

    @pl.when(pair == 0)
    def _():
        for m in range(size):
            for t in range(n // size):
                reply = reply_refs[m][t].astype(F32)
                at = (t * size + m) ^ me_ref[0]
                w_ref[at] = reply[:cols]
                d_ref[at] = reply[cols : 2 * cols]
                e_ref[at] = reply[2 * cols : 2 * cols + 8]
        for h in range(heads):
            cut = slice(h * parts, (h + 1) * parts)
            span = slice(h * DH, (h + 1) * DH)
            mixer_ref[span, :] = w_ref[cut].reshape(DH, LANDMARKS).astype(BF16)
            extra = e_ref[cut]
            top = top_ref[h // 2, h % 2 : h % 2 + 1, :]
            factor = jnp.exp(top - extra[0, 0:1, :])
            norm_ref[span, :] = (d_ref[cut].reshape(DH, LANDMARKS) * factor).astype(BF16)
            sums = jnp.sum(extra, axis=0)
            center_ref[h : h + 1, :] = (sums[1:2] + sums[2:3]) * factor

    mixer = mixer_ref[pl.ds(pl.multiple_of(pair * PAIR, PAIR), PAIR), :]
    attn = dot(fb_ref[:, :LANDMARKS], keep_rows(mixer, 0), NT) + dot(
        fb_ref[:, LANDMARKS:], keep_rows(mixer, 1), NT
    )
    attn = attn.astype(BF16)
    attn_ref[...] = attn
    all_ref[pl.ds(pl.multiple_of(pair * PAIR, PAIR), PAIR), :] = attn.T

    @pl.when(pair == pl.num_programs(0) - 1)
    def _():
        block, split = sum_ref.shape[1], n // sum_ref.shape[0]
        width = cot_ref.shape[1]
        sum_ref[...] = dot(all_ref[...], cot_ref[...]).reshape(sum_ref.shape)
        for m in range(size):
            for t in range(n // size):
                at = (t * size + m) ^ me_ref[0]
                if split == 1:
                    out_refs[m][t] = sum_ref[at].astype(BF16)
                else:
                    side = pl.multiple_of((at % split) * (width // split), width // split)
                    out_refs[m][t] = sum_ref[at // split, :, pl.ds(side, width // split)].astype(BF16)


def soft_grad(fb_ref, g_ref, mixer_ref, ds_ref):
    for h in range(2):
        span = slice(h * LANDMARKS, (h + 1) * LANDMARKS)
        mixer = keep_rows(mixer_ref[...], h)
        for c in range(0, fb_ref.shape[0], CHUNK):
            part = slice(c, c + CHUNK)
            f = fb_ref[part, span].astype(F32)
            df = dot(g_ref[part, :], mixer)
            ds_ref[part, span] = (f * (df - jnp.sum(f * df, axis=1, keepdims=True))).astype(BF16)


def weight_soft_grad(pb_ref, v_ref, norm_ref, center_ref, ds_ref):
    for h in range(2):
        span = slice(h * LANDMARKS, (h + 1) * LANDMARKS)
        norm = keep_rows(norm_ref[...], h)
        center = center_ref[pl.ds(2 * pl.program_id(0) + h, 1), :]
        for c in range(0, pb_ref.shape[0], CHUNK):
            part = slice(c, c + CHUNK)
            dp = dot(v_ref[part, :], norm)
            ds_ref[part, span] = (pb_ref[part, span].astype(F32) * (dp - center)).astype(BF16)


def land_sums(ds_ref, x_ref, own_ref, more_ref):
    xt = x_ref[...].T
    sums = jnp.concatenate(
        [dot(xt[:DH], ds_ref[:, :LANDMARKS]), dot(xt[DH:], ds_ref[:, LANDMARKS:])], axis=0
    )
    here = (own_ref[0] == pl.program_id(0)).astype(F32)
    return (sums.T * SCALE + more_ref[...] * here).astype(BF16)


def token_part(ds_ref, land_ref, out_ref):
    land = land_ref[...] * SCALE
    total = dot(ds_ref[:, :LANDMARKS], keep_lanes(land, 0).astype(BF16)) + dot(
        ds_ref[:, LANDMARKS:], keep_lanes(land, 1).astype(BF16)
    )
    out_ref[...] = total.astype(BF16)


def query_land_kernel(own_ref, q_ref, g_ref, fb_ref, mixer_ref, more_ref, land_ref, ds_ref):
    soft_grad(fb_ref, g_ref, mixer_ref, ds_ref)
    land_ref[...] = land_sums(ds_ref, q_ref, own_ref, more_ref)


def key_land_kernel(own_ref, k_ref, v_ref, pb_ref, norm_ref, center_ref, more_ref, other_ref, *refs):
    ds_ref, out_refs, land_ref = refs[0], refs[1:-1], refs[-1]
    size = len(out_refs)
    columns = other_ref.shape[1]
    pair = pl.program_id(0)
    weight_soft_grad(pb_ref, v_ref, norm_ref, center_ref, ds_ref)
    land_ref[:, pl.ds(pl.multiple_of(pair * PAIR, PAIR), PAIR)] = land_sums(
        ds_ref, k_ref, own_ref, more_ref
    )

    @pl.when(pair == pl.num_programs(0) - 1)
    def _():
        for m in range(size):
            held, height, _ = out_refs[m].shape
            for t in range(held):
                at = pl.multiple_of(((t * size + m) ^ own_ref[2]) * height, height)
                out_refs[m][t, :, :columns] = land_ref[pl.ds(at, height), :]
                out_refs[m][t, :, columns:] = other_ref[pl.ds(at, height), :]


def query_kernel(ds_ref, lk_ref, out_ref):
    token_part(ds_ref, lk_ref, out_ref)


def key_kernel(ds_ref, pb_ref, lq_ref, norm_ref, out_ref, value_ref):
    token_part(ds_ref, lq_ref, out_ref)
    value_ref[...] = (
        dot(pb_ref[:, :LANDMARKS], keep_rows(norm_ref[...], 0), NT)
        + dot(pb_ref[:, LANDMARKS:], keep_rows(norm_ref[...], 1), NT)
    ).astype(BF16)


def part_kernel(_, attn_ref, weight_ref, out_ref):
    out_ref[...] = dot(attn_ref[...], weight_ref[...]).astype(BF16)


def mixed_kernel(_, attn_ref, weight_ref, other_ref, out_ref):
    out_ref[...] = (dot(attn_ref[...], weight_ref[...]) + other_ref[...].astype(F32)).astype(BF16)


def unpack_kernel(split, me_ref, *refs):
    in_refs, (out_ref, wide_ref, sems) = refs[:-3], refs[-3:]
    size = len(in_refs)
    held, block, width = in_refs[0].shape
    copies = []
    for t in range(held):
        for m in range(size):
            slot = t * size + m
            at = slot ^ me_ref[0]
            row = pl.ds(pl.multiple_of((at // split) * block, block), block)
            if split == 1:
                target = out_ref.at[row]
            else:
                target = out_ref.at[row, pl.ds(pl.multiple_of((at % split) * width, width), width)]
            wide_ref[slot] = in_refs[m][t].astype(F32)
            copies.append(pltpu.make_async_copy(wide_ref.at[slot], target, sems.at[slot]))
            copies[-1].start()
    for copy in copies:
        copy.wait()


def held_in_hbm(x):
    return pltpu.with_memory_space_constraint(x, pltpu.HBM)


def whole(shape):
    return pl.BlockSpec(shape, lambda *_: (0,) * len(shape))


def shape_of(shape, dtype):
    return jax.ShapeDtypeStruct(shape, dtype)


def call(kernel, grid, scalars, ins, in_specs, outs, out_specs, scratch=(), flops=0, name=None, aliases={}):
    return pl.pallas_call(
        kernel,
        grid_spec=pltpu.PrefetchScalarGridSpec(
            num_scalar_prefetch=len(scalars),
            grid=grid,
            in_specs=in_specs,
            out_specs=out_specs,
            scratch_shapes=list(scratch),
        ),
        out_shape=outs,
        compiler_params=PARAMS,
        input_output_aliases=aliases,
        cost_estimate=pl.CostEstimate(flops=flops, bytes_accessed=4 << 20, transcendentals=0),
        name=name,
    )(*scalars, *ins)


def local(queries, key_rows, value_rows, out_weight, cotangent):
    rows, columns = queries.shape
    width = out_weight.shape[1]
    heads = columns // DH
    pairs = columns // PAIR
    n = lax.axis_size("seq")
    me = lax.axis_index("seq")
    mine = lax.axis_index("head")
    land_dev = LANDMARKS // n
    seg_len = rows // land_dev
    parts = n // heads
    cols = DH // parts
    size = bit_groups(n)[-1][1]
    height = 2 * cols + EXTRA
    own_head = me // parts

    sorted_here = land_dev % 16 == 0
    me_arr = jnp.stack([me, me if sorted_here else me * 0]).astype(jnp.int32)
    mine_arr = mine.reshape(1).astype(jnp.int32)
    own_arr = jnp.stack([own_head // 2, own_head % 2, me * 0 if land_dev % 16 else me]).astype(jnp.int32)
    steps = 4
    in_hbm = pl.BlockSpec(memory_space=pltpu.HBM)
    own = call(
        functools.partial(means_kernel, seg_len),
        (1,),
        [],
        [held_in_hbm(queries), held_in_hbm(key_rows)],
        [in_hbm, in_hbm],
        shape_of((land_dev, 2 * columns), BF16),
        whole((land_dev, 2 * columns)),
        [
            pltpu.VMEM((2, rows, columns), BF16),
            pltpu.VMEM((land_dev, 2 * columns), F32),
            pltpu.SemaphoreType.DMA((2, steps)),
        ],
        name="means",
    )
    own, me_arr, mine_arr, own_arr = lax.optimization_barrier((own, me_arr, mine_arr, own_arr))
    grad_attn = dot(cotangent, out_weight, NT).astype(BF16)
    if sorted_here:
        lands = gather_lists(own, n)
    else:
        lands = [gather_ordered(own, n, me).reshape(LANDMARKS // 16, 16, 2 * columns)]

    token_pair = pl.BlockSpec((rows, PAIR), lambda j, *_: (0, j))
    factor_pair = pl.BlockSpec((rows, 2 * LANDMARKS), lambda j, *_: (0, j))
    lq_pair = pl.BlockSpec((LANDMARKS, PAIR), lambda j, *_: (0, j))
    lk_pair = pl.BlockSpec((LANDMARKS, PAIR), lambda j, *_: (0, j + pairs))
    factors = shape_of((rows, heads * LANDMARKS), BF16)
    piece = shape_of((n // size, height, LANDMARKS), BF16)

    fb, pb, tops, land, *pieces = call(
        functools.partial(forward_kernel, n, heads, len(lands)),
        (pairs,),
        [me_arr],
        [queries, key_rows, value_rows, grad_attn] + lands,
        [token_pair] * 4 + [whole(lands[0].shape)] * len(lands),
        [
            factors,
            factors,
            shape_of((pairs, 8, LANDMARKS), F32),
            shape_of((LANDMARKS, 2 * columns), BF16),
        ]
        + [piece] * size,
        [
            factor_pair,
            factor_pair,
            pl.BlockSpec((1, 8, LANDMARKS), lambda j, *_: (j, 0, 0)),
            whole((LANDMARKS, 2 * columns)),
        ]
        + [whole(piece.shape)] * size,
        [
            pltpu.VMEM((rows, LANDMARKS), F32),
            pltpu.VMEM((n, height, LANDMARKS), BF16),
        ],
        flops=8 << 30,
        name="forward",
    )

    square = (LANDMARKS, LANDMARKS)
    own_lq = pl.BlockSpec((LANDMARKS, PAIR), lambda i, own: (0, own[0]))
    own_lk = pl.BlockSpec((LANDMARKS, PAIR), lambda i, own: (0, own[0] + pairs))
    kept = shape_of((1 + 4 * ITERS,) + square, F32)
    saved, inverse = call(
        newton_kernel,
        (1,),
        [own_arr],
        [land, land],
        [own_lq, own_lk],
        [kept, shape_of((1,) + square, F32)],
        [whole(kept.shape), whole((1,) + square)],
        flops=4 << 30,
        name="newton",
    )

    groups = bit_groups(n)[::-1]
    for step, (shift, count) in enumerate(groups):
        got = [pieces[0]] + [exchange(pieces[m], m << shift, n) for m in range(1, count)]
        specs = [whole(got[0].shape)] * count
        if step == 0:
            got, inverse = lax.optimization_barrier((got, inverse))
        if step + 1 < len(groups):
            following = groups[step + 1][1]
            piece = shape_of((got[0].shape[0] // following, height, LANDMARKS), BF16)
            pieces = call(
                functools.partial(merge_kernel, cols, count),
                (1,),
                [],
                got,
                specs,
                [piece] * following,
                [whole(piece.shape)] * following,
                name="merge",
            )
    small = shape_of((cols, LANDMARKS), F32)
    reply, values, grads = call(
        functools.partial(mix_kernel, cols, count),
        (1,),
        [],
        got + [inverse],
        specs + [whole((1,) + square)],
        [piece, small, small],
        [whole(piece.shape), whole(small.shape), whole(small.shape)],
        name="mix",
    )
    replies = gather_lists(reply[0], n)

    more = shape_of((LANDMARKS, PAIR), F32)
    more_q, more_k = call(
        newton_grad_kernel,
        (1,),
        [own_arr],
        [saved, values, grads, land, land],
        [whole(kept.shape), whole(small.shape), whole(small.shape), own_lq, own_lk],
        [more, more],
        [whole(more.shape)] * 2,
        flops=8 << 30,
        name="newton_grad",
    )

    replies, more_q, more_k = lax.optimization_barrier((replies, more_q, more_k))
    block = max(columns // n, 16)
    split = n * block // columns
    flat = shape_of((columns, LANDMARKS), BF16)
    weight_piece = shape_of((n // size, block, width // split), BF16)
    attn, mixer, norm, center, *weight_pieces = call(
        functools.partial(attend_kernel, n, heads),
        (pairs,),
        [me_arr],
        [fb, tops, cotangent] + replies,
        [factor_pair, whole(tops.shape), whole(cotangent.shape)] + [whole(replies[0].shape)] * size,
        [shape_of((rows, columns), BF16), flat, flat, shape_of((heads, LANDMARKS), F32)]
        + [weight_piece] * size,
        [token_pair, whole(flat.shape), whole(flat.shape), whole((heads, LANDMARKS))]
        + [whole(weight_piece.shape)] * size,
        [
            pltpu.VMEM((n, cols, LANDMARKS), F32),
            pltpu.VMEM((n, cols, LANDMARKS), F32),
            pltpu.VMEM((n, 8, LANDMARKS), F32),
            pltpu.VMEM((columns // block, block, width), F32),
            pltpu.VMEM((columns, rows), BF16),
        ],
        flops=4 << 30,
        name="attend",
    )
    (shift, count), later = groups[0], groups[1:]
    weight_sum = scatter_step(weight_pieces, shift, count, n).astype(BF16)
    (pb, key_rows, value_rows), weight_sum = lax.optimization_barrier(
        ((pb, key_rows, value_rows), weight_sum)
    )
    following = later[0][1]
    weight_sum = weight_sum.reshape((-1, following) + weight_sum.shape[1:])
    weight_own = scatter_pieces([weight_sum[:, m] for m in range(following)], n, later)[0].astype(BF16)
    flat_pair = pl.BlockSpec((PAIR, LANDMARKS), lambda j, *_: (j, 0))
    land_pair = pl.BlockSpec((LANDMARKS, PAIR), lambda j, *_: (0, j))
    centers = whole((heads, LANDMARKS))
    tokens = shape_of((rows, columns), BF16)
    land_shape = shape_of((LANDMARKS, columns), BF16)
    land_k, grad_sf = call(
        query_land_kernel,
        (pairs,),
        [own_arr],
        [queries, grad_attn, fb, mixer, more_k],
        [token_pair, token_pair, factor_pair, flat_pair, whole(more.shape)],
        [land_shape, factors],
        [land_pair, factor_pair],
        flops=4 << 30,
        name="query_land",
    )
    (shift, count), later = groups[0], groups[1:]
    following = later[0][1]
    weight_sum = scatter_step(weight_pieces, shift, count, n).astype(BF16)
    (pb, key_rows, value_rows), weight_sum, land_k = lax.optimization_barrier(
        ((pb, key_rows, value_rows), weight_sum, land_k)
    )
    if sorted_here:
        land_piece, pieces_count = shape_of((n // size, land_dev, 2 * columns), BF16), size
    else:
        land_piece, pieces_count = shape_of((LANDMARKS // 16, 16, 2 * columns), BF16), 1
    grad_sb, *land_pieces = call(
        key_land_kernel,
        (pairs,),
        [own_arr],
        [key_rows, value_rows, pb, norm, center, more_q, land_k],
        [token_pair, token_pair, factor_pair, flat_pair, centers, whole(more.shape)]
        + [whole(land_shape.shape)],
        [factors] + [land_piece] * pieces_count,
        [factor_pair] + [whole(land_piece.shape)] * pieces_count,
        [pltpu.VMEM(land_shape.shape, BF16)],
        flops=4 << 30,
        name="key_land",
    )
    land_pieces, grad_sf, attn = lax.optimization_barrier((land_pieces, grad_sf, attn))
    query_f = call(
        query_kernel,
        (pairs,),
        [],
        [grad_sf, land],
        [factor_pair, lk_pair],
        tokens,
        token_pair,
        flops=2 << 30,
        name="query_grad",
    )
    half = width // 2
    row_block = pl.BlockSpec((rows // 4, columns), lambda j, _: (j, 0))
    half_block = pl.BlockSpec((rows // 4, half), lambda j, _: (j, 0))
    there = call(
        part_kernel,
        (4,),
        [mine_arr],
        [attn, out_weight],
        [row_block, pl.BlockSpec((columns, half), lambda j, mine: (0, 1 - mine[0]))],
        shape_of((rows, half), BF16),
        half_block,
        flops=1 << 30,
        name="part",
    )

    if not sorted_here:
        land_pieces = split_by_partner(land_pieces[0].reshape(n, land_dev, 2 * columns), n, me)
    weight_sum = weight_sum.reshape((-1, following) + weight_sum.shape[1:])
    weight_own = scatter_pieces([weight_sum[:, m] for m in range(following)], n, later)[0].astype(BF16)
    land_pieces, weight_own = lax.optimization_barrier((land_pieces, weight_own))
    land_sum = scatter_step(land_pieces, shift, count, n).astype(BF16)
    weights = gather_first(weight_own, n)
    land_sum, weights, query_f, there = lax.optimization_barrier((land_sum, weights, query_f, there))
    land_sum, weights, grad_sb = lax.optimization_barrier((land_sum, weights, grad_sb))
    key_b, value_grad = call(
        key_kernel,
        (pairs,),
        [],
        [grad_sb, pb, land, norm],
        [factor_pair, factor_pair, lq_pair, flat_pair],
        [tokens, tokens],
        [token_pair, token_pair],
        flops=4 << 30,
        name="key_grad",
    )

    arrived = lax.ppermute(there, "head", [(0, 1), (1, 0)])
    mask = size
    while land_sum.shape[0] > 1:
        given = exchange(land_sum[1::2], mask, n)
        land_sum = (land_sum[::2].astype(F32) + given.astype(F32)).astype(BF16)
        mask *= 2
    land_own = land_sum[0].astype(F32)
    land_own = land_own * (1.0 / seg_len)
    mixed = call(
        mixed_kernel,
        (4,),
        [mine_arr],
        [attn, out_weight, arrived],
        [row_block, pl.BlockSpec((columns, half), lambda j, mine: (0, mine[0])), half_block],
        shape_of((rows, half), BF16),
        half_block,
        flops=1 << 30,
        name="mixed",
    )
    weights = gather_rest(weights, n)
    weights, mixed = lax.optimization_barrier((weights, mixed))
    weight_grad = call(
        functools.partial(unpack_kernel, split),
        (1,),
        [me_arr],
        weights,
        [whole(weights[0].shape)] * size,
        pltpu.HBM((columns, width), F32),
        in_hbm,
        [pltpu.VMEM((n,) + weights[0].shape[1:], F32), pltpu.SemaphoreType.DMA((n,))],
        name="unpack",
    )

    def finish(token_part, land_part):
        return (
            (token_part.reshape(land_dev, seg_len, columns) + land_part[:, None, :])
            .astype(BF16)
            .reshape(rows, columns)
        )

    query_grad = finish(query_f, land_own[:, :columns])
    key_grad = finish(key_b, land_own[:, columns:])
    return (mixed, query_grad, key_grad, value_grad, weight_grad)


def solution(mesh):
    return jax.shard_map(
        local,
        mesh=mesh,
        in_specs=(
            P("seq", "head"),
            P("seq", "head"),
            P("seq", "head"),
            P("head", None),
            P("seq", None),
        ),
        out_specs=(
            P("seq", "head"),
            P("seq", "head"),
            P("seq", "head"),
            P("seq", "head"),
            P("head", None),
        ),
        check_vma=False,
    )
```

```python
import functools

import jax
import jax.numpy as jnp
from jax import lax
from jax.experimental import pallas as pl
from jax.experimental.pallas import tpu as pltpu
from jax.sharding import PartitionSpec as P

DH = 64
PAIR = 2 * DH
LANDMARKS = 256
ITERS = 2
SCALE = 0.125
CHUNK = 256
EXTRA = 8
F32 = jnp.float32
BF16 = jnp.bfloat16
PARAMS = pltpu.CompilerParams(vmem_limit_bytes=24 * 1024 * 1024)


def dot(left, right, dims=((1,), (0,))):
    return lax.dot_general(left, right, (dims, ((), ())), preferred_element_type=F32)


NT = ((1,), (1,))
TN = ((0,), (0,))


def halves(value):
    high = value.astype(BF16)
    return high, (value - high.astype(F32)).astype(BF16)


def dot_exact(left, right, dims=((1,), (0,))):
    return dot(left[0], right[0], dims) + (
        dot(left[0], right[1], dims) + dot(left[1], right[0], dims)
    )


def turned(pair):
    return pair[0].T, pair[1].T


def keep_rows(block, which):
    rows = lax.broadcasted_iota(jnp.int32, block.shape, 0) // DH
    return jnp.where(rows == which, block, jnp.zeros_like(block))


def keep_lanes(block, which):
    lanes = lax.broadcasted_iota(jnp.int32, block.shape, 1) // DH
    return jnp.where(lanes == which, block, jnp.zeros_like(block))


def fold(block, op):
    parts = block.reshape(block.shape[0] // 8, 8, block.shape[1])
    return op(parts, axis=0)


def exchange(block, mask, n):
    return lax.ppermute(block, "seq", [(i, i ^ mask) for i in range(n)])


def bit_groups(n):
    bits = n.bit_length() - 1
    groups = []
    while bits > 0:
        take = 2 if bits % 2 == 0 else 1
        bits -= take
        groups.append((bits, 1 << take))
    return groups


def gather_first(block, n):
    shift, size = bit_groups(n)[0]
    held = block[None]
    return [held] + [exchange(held, m << shift, n) for m in range(1, size)]


def gather_rest(got, n):
    for shift, size in bit_groups(n)[1:]:
        held = jnp.stack(got, axis=1).reshape((-1,) + got[0].shape[1:])
        got = [held] + [exchange(held, m << shift, n) for m in range(1, size)]
    return got


def gather_lists(block, n):
    return gather_rest(gather_first(block, n), n)


def gather_ordered(block, n, me):
    got = gather_lists(block, n)
    held = jnp.stack(got, axis=1).reshape((n,) + block.shape)
    return held.at[jnp.arange(n) ^ me].get(mode="promise_in_bounds")


def split_by_partner(blocks, n, me):
    size = bit_groups(n)[-1][1]
    return [
        blocks.at[(jnp.arange(n // size) * size + m) ^ me].get(mode="promise_in_bounds")
        for m in range(size)
    ]


def scatter_step(pieces, shift, size, n):
    got = [pieces[0]] + [exchange(pieces[m], m << shift, n) for m in range(1, size)]
    return sum(part.astype(F32) for part in got)


def scatter_pieces(pieces, n, groups):
    for step, (shift, size) in enumerate(groups):
        held = scatter_step(pieces, shift, size, n)
        if step + 1 < len(groups):
            following = groups[step + 1][1]
            held = held.astype(BF16).reshape((-1, following) + held.shape[1:])
            pieces = [held[:, m] for m in range(following)]
    return held


def means_kernel(seg_len, q_ref, k_ref, out_ref, in_ref, sum_ref, sems):
    rows, columns = q_ref.shape
    steps = sems.shape[1]
    height = rows // steps
    copies = {}
    for c in range(steps):
        part = pl.ds(c * height, height)
        for side, ref in enumerate((q_ref, k_ref)):
            copies[side, c] = pltpu.make_async_copy(ref.at[part], in_ref.at[side, part], sems.at[side, c])
            copies[side, c].start()
    for c in range(steps):
        for side in range(2):
            copies[side, c].wait()
            span = slice(side * columns, (side + 1) * columns)
            for s in range(c * height // seg_len, (c + 1) * height // seg_len):
                total = fold(in_ref[side, s * seg_len : (s + 1) * seg_len, :].astype(F32), jnp.sum)
                sum_ref[s : s + 1, span] = jnp.sum(total, axis=0, keepdims=True)
    out_ref[...] = (sum_ref[...] * (1.0 / seg_len)).astype(BF16)


def forward_kernel(n, heads, count, me_ref, q_ref, k_ref, v_ref, g_ref, *refs):
    size = bit_groups(n)[-1][1]
    in_refs = refs[:count]
    fb_ref, pb_ref, top_ref, land_ref = refs[count : count + 4]
    out_refs = refs[count + 4 : count + 4 + size]
    score_ref, message_ref = refs[count + 4 + size :]
    pair = pl.program_id(0)
    columns = land_ref.shape[1] // 2

    @pl.when(pair == 0)
    def _():
        for m in range(count):
            held, height, _ = in_refs[m].shape
            for t in range(held):
                at = pl.multiple_of(((t * count + m) ^ me_ref[1]) * height, height)
                land_ref[pl.ds(at, height), :] = in_refs[m][t]

    here = pl.multiple_of(pair * PAIR, PAIR)
    lq_pair = land_ref[:, pl.ds(here, PAIR)]
    lk_pair = land_ref[:, pl.ds(columns + here, PAIR)]
    rows = q_ref.shape[0]
    parts = n // heads
    cols = DH // parts
    gt = g_ref[...].T
    vt = v_ref[...].T
    for h in range(2):
        lk = keep_lanes(lk_pair * SCALE, h).astype(BF16)
        lq = keep_lanes(lq_pair * SCALE, h).astype(BF16)
        span = slice(h * LANDMARKS, (h + 1) * LANDMARKS)
        top = None
        for c in range(0, rows, CHUNK):
            part = slice(c, c + CHUNK)
            sb = dot(k_ref[part, :], lq, NT)
            score_ref[part, :] = sb
            high = fold(sb, jnp.max)
            top = high if top is None else jnp.maximum(top, high)
            sf = dot(q_ref[part, :], lk, NT)
            e = jnp.exp(sf - jnp.max(sf, axis=1, keepdims=True))
            fb_ref[part, span] = (e * (1.0 / jnp.sum(e, axis=1, keepdims=True))).astype(BF16)
        top = jnp.max(top, axis=0, keepdims=True).astype(BF16).astype(F32)
        total = None
        for c in range(0, rows, CHUNK):
            part = slice(c, c + CHUNK)
            p = jnp.exp(score_ref[part, :] - top)
            add = fold(p, jnp.sum)
            total = add if total is None else total + add
            pb_ref[part, span] = p.astype(BF16)
        total = jnp.sum(total, axis=0, keepdims=True)
        top_ref[0, h : h + 1, :] = top
        grads = dot(gt[h * DH : (h + 1) * DH], fb_ref[:, span])
        vals = dot(vt[h * DH : (h + 1) * DH], pb_ref[:, span])
        high, low = halves(total)
        extra = three_rows(top, high.astype(F32), low.astype(F32))
        for p in range(parts):
            cut = slice(p * cols, (p + 1) * cols)
            message_ref[(2 * pair + h) * parts + p] = jnp.concatenate(
                [vals[cut], grads[cut], extra], axis=0
            ).astype(BF16)

    @pl.when(pair == pl.num_programs(0) - 1)
    def _():
        for m in range(size):
            for t in range(n // size):
                out_refs[m][t] = message_ref[(t * size + m) ^ me_ref[0]]


def merge(items, cols):
    tops = [item[2 * cols : 2 * cols + 1] for item in items]
    peak = functools.reduce(jnp.maximum, tops)
    vals = grads = total = 0.0
    for item, top in zip(items, tops):
        factor = jnp.exp(top - peak)
        vals = vals + item[:cols] * factor
        grads = grads + item[cols : 2 * cols]
        total = total + (
            item[2 * cols + 1 : 2 * cols + 2] + item[2 * cols + 2 : 2 * cols + 3]
        ) * factor
    return vals, grads, peak, total


def three_rows(first, second, third):
    row = lax.broadcasted_iota(jnp.int32, (EXTRA, LANDMARKS), 0)
    return jnp.where(row == 0, first, jnp.where(row == 1, second, jnp.where(row == 2, third, 0.0)))


def merge_kernel(cols, count, *refs):
    in_refs, out_refs = refs[:count], refs[count:]
    following = len(out_refs)
    for t in range(in_refs[0].shape[0]):
        vals, grads, peak, total = merge([ref[t].astype(F32) for ref in in_refs], cols)
        high, low = halves(total)
        extra = three_rows(peak, high.astype(F32), low.astype(F32))
        out_refs[t % following][t // following] = jnp.concatenate(
            [vals, grads, extra], axis=0
        ).astype(BF16)


def mix_kernel(cols, count, *refs):
    in_refs, z_ref = refs[:count], refs[count]
    reply_ref, values_ref, grads_ref = refs[count + 1 :]
    vals, grads, peak, total = merge([ref[0].astype(F32) for ref in in_refs], cols)
    inverse = halves(z_ref[0])
    values = vals / total
    mixer = dot_exact(halves(values), inverse, NT)
    norm = dot_exact(halves(grads), inverse) / total
    high, low = halves(jnp.sum(norm * values, axis=0, keepdims=True))
    extra = three_rows(peak, high.astype(F32), low.astype(F32))
    reply_ref[0] = jnp.concatenate([mixer, norm, extra], axis=0).astype(BF16)
    values_ref[...] = values
    grads_ref[...] = grads


def soft_rows(scores):
    e = jnp.exp(scores - jnp.max(scores, axis=1, keepdims=True))
    return e / jnp.sum(e, axis=1, keepdims=True)


def eye():
    shape = (LANDMARKS, LANDMARKS)
    same = lax.broadcasted_iota(jnp.int32, shape, 0) == lax.broadcasted_iota(jnp.int32, shape, 1)
    return same.astype(F32)


def column_top(amat):
    return jnp.max(jnp.sum(amat, axis=0, keepdims=True), axis=1, keepdims=True)


def newton_kernel(own_ref, lq_ref, lk_ref, saved_ref, z_ref):
    which = own_ref[1]
    amat = soft_rows(dot(keep_lanes(lq_ref[...] * SCALE, which).astype(BF16), lk_ref[...], NT))
    saved_ref[0] = amat
    current = amat.T / column_top(amat)
    ident = eye()
    amat = halves(amat)
    for i in range(ITERS):
        saved_ref[1 + 4 * i] = current
        z = halves(current)
        x_full = dot_exact(amat, z)
        saved_ref[2 + 4 * i] = x_full
        x = halves(x_full)
        inner = 15.0 * ident - dot_exact(x, halves(7.0 * ident - x_full))
        saved_ref[3 + 4 * i] = inner
        inner = 13.0 * ident - dot_exact(x, halves(inner))
        saved_ref[4 + 4 * i] = inner
        current = 0.25 * dot_exact(z, halves(inner))
    z_ref[0] = current


def newton_grad_kernel(own_ref, saved_ref, values_ref, grads_ref, lq_ref, lk_ref, q_ref, k_ref):
    which = own_ref[1]
    ident = eye()
    amat = saved_ref[0]
    amat_t = turned(halves(amat))
    grad_z = dot_exact(halves(grads_ref[...]), halves(values_ref[...]), TN)
    grad_a = jnp.zeros_like(amat)
    for i in reversed(range(ITERS)):
        z = halves(saved_ref[1 + 4 * i])
        x_full = saved_ref[2 + 4 * i]
        x_t = turned(halves(x_full))
        first = halves(7.0 * ident - x_full)
        second = halves(saved_ref[3 + 4 * i])
        third = halves(saved_ref[4 + 4 * i])
        dz = halves(0.25 * grad_z)
        d_third = halves(dot_exact(turned(z), dz))
        d_second = halves(-dot_exact(x_t, d_third))
        d_x = -dot_exact(d_third, second, NT) - dot_exact(d_second, first, NT)
        d_x = halves(d_x + dot_exact(x_t, d_second))
        grad_a = grad_a + dot_exact(d_x, z, NT)
        grad_z = dot_exact(dz, third, NT) + dot_exact(amat_t, d_x)
    grad_a = grad_a + grad_z.T / column_top(amat)
    grad_s = amat * (grad_a - jnp.sum(amat * grad_a, axis=1, keepdims=True)) * SCALE
    high, low = halves(grad_s)
    lq = keep_lanes(lq_ref[...], which)
    lk = keep_lanes(lk_ref[...], which)
    q_ref[...] = dot(high, lk) + dot(low, lk)
    k_ref[...] = dot(high.T, lq) + dot(low.T, lq)


def attend_kernel(n, heads, me_ref, fb_ref, top_ref, cot_ref, *refs):
    size = bit_groups(n)[-1][1]
    parts = n // heads
    cols = DH // parts
    reply_refs = refs[:size]
    attn_ref, mixer_ref, norm_ref, center_ref = refs[size : size + 4]
    out_refs = refs[size + 4 : 2 * size + 4]
    w_ref, d_ref, e_ref, sum_ref, all_ref = refs[2 * size + 4 :]
    pair = pl.program_id(0)

    @pl.when(pair == 0)
    def _():
        for m in range(size):
            for t in range(n // size):
                reply = reply_refs[m][t].astype(F32)
                at = (t * size + m) ^ me_ref[0]
                w_ref[at] = reply[:cols]
                d_ref[at] = reply[cols : 2 * cols]
                e_ref[at] = reply[2 * cols : 2 * cols + 8]
        for h in range(heads):
            cut = slice(h * parts, (h + 1) * parts)
            span = slice(h * DH, (h + 1) * DH)
            mixer_ref[span, :] = w_ref[cut].reshape(DH, LANDMARKS).astype(BF16)
            extra = e_ref[cut]
            top = top_ref[h // 2, h % 2 : h % 2 + 1, :]
            factor = jnp.exp(top - extra[0, 0:1, :])
            norm_ref[span, :] = (d_ref[cut].reshape(DH, LANDMARKS) * factor).astype(BF16)
            sums = jnp.sum(extra, axis=0)
            center_ref[h : h + 1, :] = (sums[1:2] + sums[2:3]) * factor

    mixer = mixer_ref[pl.ds(pl.multiple_of(pair * PAIR, PAIR), PAIR), :]
    attn = dot(fb_ref[:, :LANDMARKS], keep_rows(mixer, 0), NT) + dot(
        fb_ref[:, LANDMARKS:], keep_rows(mixer, 1), NT
    )
    attn = attn.astype(BF16)
    attn_ref[...] = attn
    all_ref[pl.ds(pl.multiple_of(pair * PAIR, PAIR), PAIR), :] = attn.T

    @pl.when(pair == pl.num_programs(0) - 1)
    def _():
        block, split = sum_ref.shape[1], n // sum_ref.shape[0]
        width = cot_ref.shape[1]
        sum_ref[...] = dot(all_ref[...], cot_ref[...]).reshape(sum_ref.shape)
        for m in range(size):
            for t in range(n // size):
                at = (t * size + m) ^ me_ref[0]
                if split == 1:
                    out_refs[m][t] = sum_ref[at].astype(BF16)
                else:
                    side = pl.multiple_of((at % split) * (width // split), width // split)
                    out_refs[m][t] = sum_ref[at // split, :, pl.ds(side, width // split)].astype(BF16)


def soft_grad(fb_ref, g_ref, mixer_ref, ds_ref):
    for h in range(2):
        span = slice(h * LANDMARKS, (h + 1) * LANDMARKS)
        mixer = keep_rows(mixer_ref[...], h)
        for c in range(0, fb_ref.shape[0], CHUNK):
            part = slice(c, c + CHUNK)
            f = fb_ref[part, span].astype(F32)
            df = dot(g_ref[part, :], mixer)
            ds_ref[part, span] = (f * (df - jnp.sum(f * df, axis=1, keepdims=True))).astype(BF16)


def weight_soft_grad(pb_ref, v_ref, norm_ref, center_ref, ds_ref):
    for h in range(2):
        span = slice(h * LANDMARKS, (h + 1) * LANDMARKS)
        norm = keep_rows(norm_ref[...], h)
        center = center_ref[pl.ds(2 * pl.program_id(0) + h, 1), :]
        for c in range(0, pb_ref.shape[0], CHUNK):
            part = slice(c, c + CHUNK)
            dp = dot(v_ref[part, :], norm)
            ds_ref[part, span] = (pb_ref[part, span].astype(F32) * (dp - center)).astype(BF16)


def land_sums(ds_ref, x_ref, own_ref, more_ref):
    xt = x_ref[...].T
    sums = jnp.concatenate(
        [dot(xt[:DH], ds_ref[:, :LANDMARKS]), dot(xt[DH:], ds_ref[:, LANDMARKS:])], axis=0
    )
    here = (own_ref[0] == pl.program_id(0)).astype(F32)
    return (sums.T * SCALE + more_ref[...] * here).astype(BF16)


def token_part(ds_ref, land_ref, out_ref):
    land = land_ref[...] * SCALE
    total = dot(ds_ref[:, :LANDMARKS], keep_lanes(land, 0).astype(BF16)) + dot(
        ds_ref[:, LANDMARKS:], keep_lanes(land, 1).astype(BF16)
    )
    out_ref[...] = total.astype(BF16)


def query_land_kernel(own_ref, q_ref, g_ref, fb_ref, mixer_ref, more_ref, land_ref, ds_ref):
    soft_grad(fb_ref, g_ref, mixer_ref, ds_ref)
    land_ref[...] = land_sums(ds_ref, q_ref, own_ref, more_ref)


def key_land_kernel(own_ref, k_ref, v_ref, pb_ref, norm_ref, center_ref, more_ref, other_ref, *refs):
    ds_ref, out_refs, land_ref = refs[0], refs[1:-1], refs[-1]
    size = len(out_refs)
    columns = other_ref.shape[1]
    pair = pl.program_id(0)
    weight_soft_grad(pb_ref, v_ref, norm_ref, center_ref, ds_ref)
    land_ref[:, pl.ds(pl.multiple_of(pair * PAIR, PAIR), PAIR)] = land_sums(
        ds_ref, k_ref, own_ref, more_ref
    )

    @pl.when(pair == pl.num_programs(0) - 1)
    def _():
        for m in range(size):
            held, height, _ = out_refs[m].shape
            for t in range(held):
                at = pl.multiple_of(((t * size + m) ^ own_ref[2]) * height, height)
                out_refs[m][t, :, :columns] = land_ref[pl.ds(at, height), :]
                out_refs[m][t, :, columns:] = other_ref[pl.ds(at, height), :]


def query_kernel(ds_ref, lk_ref, out_ref):
    token_part(ds_ref, lk_ref, out_ref)


def key_kernel(ds_ref, pb_ref, lq_ref, norm_ref, out_ref, value_ref):
    token_part(ds_ref, lq_ref, out_ref)
    value_ref[...] = (
        dot(pb_ref[:, :LANDMARKS], keep_rows(norm_ref[...], 0), NT)
        + dot(pb_ref[:, LANDMARKS:], keep_rows(norm_ref[...], 1), NT)
    ).astype(BF16)


def part_kernel(_, attn_ref, weight_ref, out_ref):
    out_ref[...] = dot(attn_ref[...], weight_ref[...]).astype(BF16)


def mixed_kernel(_, attn_ref, weight_ref, other_ref, out_ref):
    out_ref[...] = (dot(attn_ref[...], weight_ref[...]) + other_ref[...].astype(F32)).astype(BF16)


def unpack_kernel(split, me_ref, *refs):
    in_refs, (out_ref, wide_ref, sems) = refs[:-3], refs[-3:]
    size = len(in_refs)
    held, block, width = in_refs[0].shape
    copies = []
    for t in range(held):
        for m in range(size):
            slot = t * size + m
            at = slot ^ me_ref[0]
            row = pl.ds(pl.multiple_of((at // split) * block, block), block)
            if split == 1:
                target = out_ref.at[row]
            else:
                target = out_ref.at[row, pl.ds(pl.multiple_of((at % split) * width, width), width)]
            wide_ref[slot] = in_refs[m][t].astype(F32)
            copies.append(pltpu.make_async_copy(wide_ref.at[slot], target, sems.at[slot]))
            copies[-1].start()
    for copy in copies:
        copy.wait()


def held_in_hbm(x):
    return pltpu.with_memory_space_constraint(x, pltpu.HBM)


def whole(shape):
    return pl.BlockSpec(shape, lambda *_: (0,) * len(shape))


def shape_of(shape, dtype):
    return jax.ShapeDtypeStruct(shape, dtype)


def call(kernel, grid, scalars, ins, in_specs, outs, out_specs, scratch=(), flops=0, name=None, aliases={}):
    return pl.pallas_call(
        kernel,
        grid_spec=pltpu.PrefetchScalarGridSpec(
            num_scalar_prefetch=len(scalars),
            grid=grid,
            in_specs=in_specs,
            out_specs=out_specs,
            scratch_shapes=list(scratch),
        ),
        out_shape=outs,
        compiler_params=PARAMS,
        input_output_aliases=aliases,
        cost_estimate=pl.CostEstimate(flops=flops, bytes_accessed=4 << 20, transcendentals=0),
        name=name,
    )(*scalars, *ins)


def local(queries, key_rows, value_rows, out_weight, cotangent):
    rows, columns = queries.shape
    width = out_weight.shape[1]
    heads = columns // DH
    pairs = columns // PAIR
    n = lax.axis_size("seq")
    me = lax.axis_index("seq")
    mine = lax.axis_index("head")
    land_dev = LANDMARKS // n
    seg_len = rows // land_dev
    parts = n // heads
    cols = DH // parts
    size = bit_groups(n)[-1][1]
    height = 2 * cols + EXTRA
    own_head = me // parts

    sorted_here = land_dev % 16 == 0
    me_arr = jnp.stack([me, me if sorted_here else me * 0]).astype(jnp.int32)
    mine_arr = mine.reshape(1).astype(jnp.int32)
    own_arr = jnp.stack([own_head // 2, own_head % 2, me * 0 if land_dev % 16 else me]).astype(jnp.int32)
    steps = 4
    in_hbm = pl.BlockSpec(memory_space=pltpu.HBM)
    own = call(
        functools.partial(means_kernel, seg_len),
        (1,),
        [],
        [held_in_hbm(queries), held_in_hbm(key_rows)],
        [in_hbm, in_hbm],
        shape_of((land_dev, 2 * columns), BF16),
        whole((land_dev, 2 * columns)),
        [
            pltpu.VMEM((2, rows, columns), BF16),
            pltpu.VMEM((land_dev, 2 * columns), F32),
            pltpu.SemaphoreType.DMA((2, steps)),
        ],
        name="means",
    )
    own, me_arr, mine_arr, own_arr = lax.optimization_barrier((own, me_arr, mine_arr, own_arr))
    grad_attn = dot(cotangent, out_weight, NT).astype(BF16)
    if sorted_here:
        lands = gather_lists(own, n)
    else:
        lands = [gather_ordered(own, n, me).reshape(LANDMARKS // 16, 16, 2 * columns)]

    token_pair = pl.BlockSpec((rows, PAIR), lambda j, *_: (0, j))
    factor_pair = pl.BlockSpec((rows, 2 * LANDMARKS), lambda j, *_: (0, j))
    lq_pair = pl.BlockSpec((LANDMARKS, PAIR), lambda j, *_: (0, j))
    lk_pair = pl.BlockSpec((LANDMARKS, PAIR), lambda j, *_: (0, j + pairs))
    factors = shape_of((rows, heads * LANDMARKS), BF16)
    piece = shape_of((n // size, height, LANDMARKS), BF16)

    fb, pb, tops, land, *pieces = call(
        functools.partial(forward_kernel, n, heads, len(lands)),
        (pairs,),
        [me_arr],
        [queries, key_rows, value_rows, grad_attn] + lands,
        [token_pair] * 4 + [whole(lands[0].shape)] * len(lands),
        [
            factors,
            factors,
            shape_of((pairs, 8, LANDMARKS), F32),
            shape_of((LANDMARKS, 2 * columns), BF16),
        ]
        + [piece] * size,
        [
            factor_pair,
            factor_pair,
            pl.BlockSpec((1, 8, LANDMARKS), lambda j, *_: (j, 0, 0)),
            whole((LANDMARKS, 2 * columns)),
        ]
        + [whole(piece.shape)] * size,
        [
            pltpu.VMEM((rows, LANDMARKS), F32),
            pltpu.VMEM((n, height, LANDMARKS), BF16),
        ],
        flops=8 << 30,
        name="forward",
    )

    square = (LANDMARKS, LANDMARKS)
    own_lq = pl.BlockSpec((LANDMARKS, PAIR), lambda i, own: (0, own[0]))
    own_lk = pl.BlockSpec((LANDMARKS, PAIR), lambda i, own: (0, own[0] + pairs))
    kept = shape_of((1 + 4 * ITERS,) + square, F32)
    saved, inverse = call(
        newton_kernel,
        (1,),
        [own_arr],
        [land, land],
        [own_lq, own_lk],
        [kept, shape_of((1,) + square, F32)],
        [whole(kept.shape), whole((1,) + square)],
        flops=4 << 30,
        name="newton",
    )

    groups = bit_groups(n)[::-1]
    for step, (shift, count) in enumerate(groups):
        got = [pieces[0]] + [exchange(pieces[m], m << shift, n) for m in range(1, count)]
        specs = [whole(got[0].shape)] * count
        if step == 0:
            got, inverse = lax.optimization_barrier((got, inverse))
        if step + 1 < len(groups):
            following = groups[step + 1][1]
            piece = shape_of((got[0].shape[0] // following, height, LANDMARKS), BF16)
            pieces = call(
                functools.partial(merge_kernel, cols, count),
                (1,),
                [],
                got,
                specs,
                [piece] * following,
                [whole(piece.shape)] * following,
                name="merge",
            )
    small = shape_of((cols, LANDMARKS), F32)
    reply, values, grads = call(
        functools.partial(mix_kernel, cols, count),
        (1,),
        [],
        got + [inverse],
        specs + [whole((1,) + square)],
        [piece, small, small],
        [whole(piece.shape), whole(small.shape), whole(small.shape)],
        name="mix",
    )
    replies = gather_lists(reply[0], n)

    more = shape_of((LANDMARKS, PAIR), F32)
    more_q, more_k = call(
        newton_grad_kernel,
        (1,),
        [own_arr],
        [saved, values, grads, land, land],
        [whole(kept.shape), whole(small.shape), whole(small.shape), own_lq, own_lk],
        [more, more],
        [whole(more.shape)] * 2,
        flops=8 << 30,
        name="newton_grad",
    )

    replies, more_q, more_k = lax.optimization_barrier((replies, more_q, more_k))
    block = max(columns // n, 16)
    split = n * block // columns
    flat = shape_of((columns, LANDMARKS), BF16)
    weight_piece = shape_of((n // size, block, width // split), BF16)
    attn, mixer, norm, center, *weight_pieces = call(
        functools.partial(attend_kernel, n, heads),
        (pairs,),
        [me_arr],
        [fb, tops, cotangent] + replies,
        [factor_pair, whole(tops.shape), whole(cotangent.shape)] + [whole(replies[0].shape)] * size,
        [shape_of((rows, columns), BF16), flat, flat, shape_of((heads, LANDMARKS), F32)]
        + [weight_piece] * size,
        [token_pair, whole(flat.shape), whole(flat.shape), whole((heads, LANDMARKS))]
        + [whole(weight_piece.shape)] * size,
        [
            pltpu.VMEM((n, cols, LANDMARKS), F32),
            pltpu.VMEM((n, cols, LANDMARKS), F32),
            pltpu.VMEM((n, 8, LANDMARKS), F32),
            pltpu.VMEM((columns // block, block, width), F32),
            pltpu.VMEM((columns, rows), BF16),
        ],
        flops=4 << 30,
        name="attend",
    )
    (shift, count), later = groups[0], groups[1:]
    weight_sum = scatter_step(weight_pieces, shift, count, n).astype(BF16)
    (pb, key_rows, value_rows), weight_sum = lax.optimization_barrier(
        ((pb, key_rows, value_rows), weight_sum)
    )
    following = later[0][1]
    weight_sum = weight_sum.reshape((-1, following) + weight_sum.shape[1:])
    weight_own = scatter_pieces([weight_sum[:, m] for m in range(following)], n, later)[0].astype(BF16)
    flat_pair = pl.BlockSpec((PAIR, LANDMARKS), lambda j, *_: (j, 0))
    land_pair = pl.BlockSpec((LANDMARKS, PAIR), lambda j, *_: (0, j))
    centers = whole((heads, LANDMARKS))
    tokens = shape_of((rows, columns), BF16)
    land_shape = shape_of((LANDMARKS, columns), BF16)
    land_k, grad_sf = call(
        query_land_kernel,
        (pairs,),
        [own_arr],
        [queries, grad_attn, fb, mixer, more_k],
        [token_pair, token_pair, factor_pair, flat_pair, whole(more.shape)],
        [land_shape, factors],
        [land_pair, factor_pair],
        flops=4 << 30,
        name="query_land",
    )
    (shift, count), later = groups[0], groups[1:]
    following = later[0][1]
    weight_sum = scatter_step(weight_pieces, shift, count, n).astype(BF16)
    (pb, key_rows, value_rows), weight_sum, land_k = lax.optimization_barrier(
        ((pb, key_rows, value_rows), weight_sum, land_k)
    )
    if sorted_here:
        land_piece, pieces_count = shape_of((n // size, land_dev, 2 * columns), BF16), size
    else:
        land_piece, pieces_count = shape_of((LANDMARKS // 16, 16, 2 * columns), BF16), 1
    grad_sb, *land_pieces = call(
        key_land_kernel,
        (pairs,),
        [own_arr],
        [key_rows, value_rows, pb, norm, center, more_q, land_k],
        [token_pair, token_pair, factor_pair, flat_pair, centers, whole(more.shape)]
        + [whole(land_shape.shape)],
        [factors] + [land_piece] * pieces_count,
        [factor_pair] + [whole(land_piece.shape)] * pieces_count,
        [pltpu.VMEM(land_shape.shape, BF16)],
        flops=4 << 30,
        name="key_land",
    )
    land_pieces, attn = lax.optimization_barrier((land_pieces, attn))
    half = width // 2
    row_block = pl.BlockSpec((rows // 4, columns), lambda j, _: (j, 0))
    half_block = pl.BlockSpec((rows // 4, half), lambda j, _: (j, 0))
    there = call(
        part_kernel,
        (4,),
        [mine_arr],
        [attn, out_weight],
        [row_block, pl.BlockSpec((columns, half), lambda j, mine: (0, 1 - mine[0]))],
        shape_of((rows, half), BF16),
        half_block,
        flops=1 << 30,
        name="part",
    )

    if not sorted_here:
        land_pieces = split_by_partner(land_pieces[0].reshape(n, land_dev, 2 * columns), n, me)
    weight_sum = weight_sum.reshape((-1, following) + weight_sum.shape[1:])
    weight_own = scatter_pieces([weight_sum[:, m] for m in range(following)], n, later)[0].astype(BF16)
    land_pieces, weight_own = lax.optimization_barrier((land_pieces, weight_own))
    land_sum = scatter_step(land_pieces, shift, count, n).astype(BF16)
    weights = gather_first(weight_own, n)
    land_sum, grad_sf = lax.optimization_barrier((land_sum, grad_sf))
    query_f = call(
        query_kernel,
        (pairs,),
        [],
        [grad_sf, land],
        [factor_pair, lk_pair],
        tokens,
        token_pair,
        flops=2 << 30,
        name="query_grad",
    )
    land_sum, weights, query_f, there = lax.optimization_barrier((land_sum, weights, query_f, there))
    land_sum, weights, grad_sb = lax.optimization_barrier((land_sum, weights, grad_sb))
    key_b, value_grad = call(
        key_kernel,
        (pairs,),
        [],
        [grad_sb, pb, land, norm],
        [factor_pair, factor_pair, lq_pair, flat_pair],
        [tokens, tokens],
        [token_pair, token_pair],
        flops=4 << 30,
        name="key_grad",
    )

    arrived = lax.ppermute(there, "head", [(0, 1), (1, 0)])
    mask = size
    while land_sum.shape[0] > 1:
        given = exchange(land_sum[1::2], mask, n)
        land_sum = (land_sum[::2].astype(F32) + given.astype(F32)).astype(BF16)
        mask *= 2
    land_own = land_sum[0].astype(F32)
    land_own = land_own * (1.0 / seg_len)
    mixed = call(
        mixed_kernel,
        (4,),
        [mine_arr],
        [attn, out_weight, arrived],
        [row_block, pl.BlockSpec((columns, half), lambda j, mine: (0, mine[0])), half_block],
        shape_of((rows, half), BF16),
        half_block,
        flops=1 << 30,
        name="mixed",
    )
    weights = gather_rest(weights, n)
    weights, mixed = lax.optimization_barrier((weights, mixed))
    weight_grad = call(
        functools.partial(unpack_kernel, split),
        (1,),
        [me_arr],
        weights,
        [whole(weights[0].shape)] * size,
        pltpu.HBM((columns, width), F32),
        in_hbm,
        [pltpu.VMEM((n,) + weights[0].shape[1:], F32), pltpu.SemaphoreType.DMA((n,))],
        name="unpack",
    )

    def finish(token_part, land_part):
        return (
            (token_part.reshape(land_dev, seg_len, columns) + land_part[:, None, :])
            .astype(BF16)
            .reshape(rows, columns)
        )

    query_grad = finish(query_f, land_own[:, :columns])
    key_grad = finish(key_b, land_own[:, columns:])
    return (mixed, query_grad, key_grad, value_grad, weight_grad)


def solution(mesh):
    return jax.shard_map(
        local,
        mesh=mesh,
        in_specs=(
            P("seq", "head"),
            P("seq", "head"),
            P("seq", "head"),
            P("head", None),
            P("seq", None),
        ),
        out_specs=(
            P("seq", "head"),
            P("seq", "head"),
            P("seq", "head"),
            P("seq", "head"),
            P("head", None),
        ),
        check_vma=False,
    )
```

```python
import functools

import jax
import jax.numpy as jnp
from jax import lax
from jax.experimental import pallas as pl
from jax.experimental.pallas import tpu as pltpu
from jax.sharding import PartitionSpec as P

DH = 64
PAIR = 2 * DH
LANDMARKS = 256
ITERS = 2
SCALE = 0.125
CHUNK = 256
EXTRA = 8
F32 = jnp.float32
BF16 = jnp.bfloat16
PARAMS = pltpu.CompilerParams(vmem_limit_bytes=24 * 1024 * 1024)


def dot(left, right, dims=((1,), (0,))):
    return lax.dot_general(left, right, (dims, ((), ())), preferred_element_type=F32)


NT = ((1,), (1,))
TN = ((0,), (0,))


def halves(value):
    high = value.astype(BF16)
    return high, (value - high.astype(F32)).astype(BF16)


def dot_exact(left, right, dims=((1,), (0,))):
    return dot(left[0], right[0], dims) + (
        dot(left[0], right[1], dims) + dot(left[1], right[0], dims)
    )


def turned(pair):
    return pair[0].T, pair[1].T


def keep_rows(block, which):
    rows = lax.broadcasted_iota(jnp.int32, block.shape, 0) // DH
    return jnp.where(rows == which, block, jnp.zeros_like(block))


def keep_lanes(block, which):
    lanes = lax.broadcasted_iota(jnp.int32, block.shape, 1) // DH
    return jnp.where(lanes == which, block, jnp.zeros_like(block))


def fold(block, op):
    parts = block.reshape(block.shape[0] // 8, 8, block.shape[1])
    return op(parts, axis=0)


def exchange(block, mask, n):
    return lax.ppermute(block, "seq", [(i, i ^ mask) for i in range(n)])


def bit_groups(n):
    bits = n.bit_length() - 1
    groups = []
    while bits > 0:
        take = 2 if bits % 2 == 0 else 1
        bits -= take
        groups.append((bits, 1 << take))
    return groups


def gather_first(block, n):
    shift, size = bit_groups(n)[0]
    held = block[None]
    return [held] + [exchange(held, m << shift, n) for m in range(1, size)]


def gather_rest(got, n):
    for shift, size in bit_groups(n)[1:]:
        held = jnp.stack(got, axis=1).reshape((-1,) + got[0].shape[1:])
        got = [held] + [exchange(held, m << shift, n) for m in range(1, size)]
    return got


def gather_lists(block, n):
    return gather_rest(gather_first(block, n), n)


def gather_ordered(block, n, me):
    got = gather_lists(block, n)
    held = jnp.stack(got, axis=1).reshape((n,) + block.shape)
    return held.at[jnp.arange(n) ^ me].get(mode="promise_in_bounds")


def split_by_partner(blocks, n, me):
    size = bit_groups(n)[-1][1]
    return [
        blocks.at[(jnp.arange(n // size) * size + m) ^ me].get(mode="promise_in_bounds")
        for m in range(size)
    ]


def scatter_step(pieces, shift, size, n):
    got = [pieces[0]] + [exchange(pieces[m], m << shift, n) for m in range(1, size)]
    return sum(part.astype(F32) for part in got)


def scatter_pieces(pieces, n, groups):
    for step, (shift, size) in enumerate(groups):
        held = scatter_step(pieces, shift, size, n)
        if step + 1 < len(groups):
            following = groups[step + 1][1]
            held = held.astype(BF16).reshape((-1, following) + held.shape[1:])
            pieces = [held[:, m] for m in range(following)]
    return held


def means_kernel(seg_len, q_ref, k_ref, out_ref, in_ref, sum_ref, sems):
    rows, columns = q_ref.shape
    steps = sems.shape[1]
    height = rows // steps
    copies = {}
    for c in range(steps):
        part = pl.ds(c * height, height)
        for side, ref in enumerate((q_ref, k_ref)):
            copies[side, c] = pltpu.make_async_copy(ref.at[part], in_ref.at[side, part], sems.at[side, c])
            copies[side, c].start()
    for c in range(steps):
        for side in range(2):
            copies[side, c].wait()
            span = slice(side * columns, (side + 1) * columns)
            for s in range(c * height // seg_len, (c + 1) * height // seg_len):
                total = fold(in_ref[side, s * seg_len : (s + 1) * seg_len, :].astype(F32), jnp.sum)
                sum_ref[s : s + 1, span] = jnp.sum(total, axis=0, keepdims=True)
    out_ref[...] = (sum_ref[...] * (1.0 / seg_len)).astype(BF16)


def forward_kernel(n, heads, count, me_ref, q_ref, k_ref, v_ref, g_ref, *refs):
    size = bit_groups(n)[-1][1]
    in_refs = refs[:count]
    fb_ref, pb_ref, top_ref, land_ref = refs[count : count + 4]
    out_refs = refs[count + 4 : count + 4 + size]
    score_ref, message_ref = refs[count + 4 + size :]
    pair = pl.program_id(0)
    columns = land_ref.shape[1] // 2

    @pl.when(pair == 0)
    def _():
        for m in range(count):
            held, height, _ = in_refs[m].shape
            for t in range(held):
                at = pl.multiple_of(((t * count + m) ^ me_ref[1]) * height, height)
                land_ref[pl.ds(at, height), :] = in_refs[m][t]

    here = pl.multiple_of(pair * PAIR, PAIR)
    lq_pair = land_ref[:, pl.ds(here, PAIR)]
    lk_pair = land_ref[:, pl.ds(columns + here, PAIR)]
    rows = q_ref.shape[0]
    parts = n // heads
    cols = DH // parts
    gt = g_ref[...].T
    vt = v_ref[...].T
    for h in range(2):
        lk = keep_lanes(lk_pair * SCALE, h).astype(BF16)
        lq = keep_lanes(lq_pair * SCALE, h).astype(BF16)
        span = slice(h * LANDMARKS, (h + 1) * LANDMARKS)
        top = None
        for c in range(0, rows, CHUNK):
            part = slice(c, c + CHUNK)
            sb = dot(k_ref[part, :], lq, NT)
            score_ref[part, :] = sb
            high = fold(sb, jnp.max)
            top = high if top is None else jnp.maximum(top, high)
            sf = dot(q_ref[part, :], lk, NT)
            e = jnp.exp(sf - jnp.max(sf, axis=1, keepdims=True))
            fb_ref[part, span] = (e * (1.0 / jnp.sum(e, axis=1, keepdims=True))).astype(BF16)
        top = jnp.max(top, axis=0, keepdims=True).astype(BF16).astype(F32)
        total = None
        for c in range(0, rows, CHUNK):
            part = slice(c, c + CHUNK)
            p = jnp.exp(score_ref[part, :] - top)
            add = fold(p, jnp.sum)
            total = add if total is None else total + add
            pb_ref[part, span] = p.astype(BF16)
        total = jnp.sum(total, axis=0, keepdims=True)
        top_ref[0, h : h + 1, :] = top
        grads = dot(gt[h * DH : (h + 1) * DH], fb_ref[:, span])
        vals = dot(vt[h * DH : (h + 1) * DH], pb_ref[:, span])
        high, low = halves(total)
        extra = three_rows(top, high.astype(F32), low.astype(F32))
        for p in range(parts):
            cut = slice(p * cols, (p + 1) * cols)
            message_ref[(2 * pair + h) * parts + p] = jnp.concatenate(
                [vals[cut], grads[cut], extra], axis=0
            ).astype(BF16)

    @pl.when(pair == pl.num_programs(0) - 1)
    def _():
        for m in range(size):
            for t in range(n // size):
                out_refs[m][t] = message_ref[(t * size + m) ^ me_ref[0]]


def merge(items, cols):
    tops = [item[2 * cols : 2 * cols + 1] for item in items]
    peak = functools.reduce(jnp.maximum, tops)
    vals = grads = total = 0.0
    for item, top in zip(items, tops):
        factor = jnp.exp(top - peak)
        vals = vals + item[:cols] * factor
        grads = grads + item[cols : 2 * cols]
        total = total + (
            item[2 * cols + 1 : 2 * cols + 2] + item[2 * cols + 2 : 2 * cols + 3]
        ) * factor
    return vals, grads, peak, total


def three_rows(first, second, third):
    row = lax.broadcasted_iota(jnp.int32, (EXTRA, LANDMARKS), 0)
    return jnp.where(row == 0, first, jnp.where(row == 1, second, jnp.where(row == 2, third, 0.0)))


def merge_kernel(cols, count, *refs):
    in_refs, out_refs = refs[:count], refs[count:]
    following = len(out_refs)
    for t in range(in_refs[0].shape[0]):
        vals, grads, peak, total = merge([ref[t].astype(F32) for ref in in_refs], cols)
        high, low = halves(total)
        extra = three_rows(peak, high.astype(F32), low.astype(F32))
        out_refs[t % following][t // following] = jnp.concatenate(
            [vals, grads, extra], axis=0
        ).astype(BF16)


def mix_kernel(cols, count, *refs):
    in_refs, z_ref = refs[:count], refs[count]
    reply_ref, values_ref, grads_ref = refs[count + 1 :]
    vals, grads, peak, total = merge([ref[0].astype(F32) for ref in in_refs], cols)
    inverse = halves(z_ref[0])
    values = vals / total
    mixer = dot_exact(halves(values), inverse, NT)
    norm = dot_exact(halves(grads), inverse) / total
    high, low = halves(jnp.sum(norm * values, axis=0, keepdims=True))
    extra = three_rows(peak, high.astype(F32), low.astype(F32))
    reply_ref[0] = jnp.concatenate([mixer, norm, extra], axis=0).astype(BF16)
    values_ref[...] = values
    grads_ref[...] = grads


def soft_rows(scores):
    e = jnp.exp(scores - jnp.max(scores, axis=1, keepdims=True))
    return e / jnp.sum(e, axis=1, keepdims=True)


def eye():
    shape = (LANDMARKS, LANDMARKS)
    same = lax.broadcasted_iota(jnp.int32, shape, 0) == lax.broadcasted_iota(jnp.int32, shape, 1)
    return same.astype(F32)


def column_top(amat):
    return jnp.max(jnp.sum(amat, axis=0, keepdims=True), axis=1, keepdims=True)


def newton_kernel(own_ref, lq_ref, lk_ref, saved_ref, z_ref):
    which = own_ref[1]
    amat = soft_rows(dot(keep_lanes(lq_ref[...] * SCALE, which).astype(BF16), lk_ref[...], NT))
    saved_ref[0] = amat
    current = amat.T / column_top(amat)
    ident = eye()
    amat = halves(amat)
    for i in range(ITERS):
        saved_ref[1 + 4 * i] = current
        z = halves(current)
        x_full = dot_exact(amat, z)
        saved_ref[2 + 4 * i] = x_full
        x = halves(x_full)
        inner = 15.0 * ident - dot_exact(x, halves(7.0 * ident - x_full))
        saved_ref[3 + 4 * i] = inner
        inner = 13.0 * ident - dot_exact(x, halves(inner))
        saved_ref[4 + 4 * i] = inner
        current = 0.25 * dot_exact(z, halves(inner))
    z_ref[0] = current


def newton_grad_kernel(own_ref, saved_ref, values_ref, grads_ref, lq_ref, lk_ref, q_ref, k_ref):
    which = own_ref[1]
    ident = eye()
    amat = saved_ref[0]
    amat_t = turned(halves(amat))
    grad_z = dot_exact(halves(grads_ref[...]), halves(values_ref[...]), TN)
    grad_a = jnp.zeros_like(amat)
    for i in reversed(range(ITERS)):
        z = halves(saved_ref[1 + 4 * i])
        x_full = saved_ref[2 + 4 * i]
        x_t = turned(halves(x_full))
        first = halves(7.0 * ident - x_full)
        second = halves(saved_ref[3 + 4 * i])
        third = halves(saved_ref[4 + 4 * i])
        dz = halves(0.25 * grad_z)
        d_third = halves(dot_exact(turned(z), dz))
        d_second = halves(-dot_exact(x_t, d_third))
        d_x = -dot_exact(d_third, second, NT) - dot_exact(d_second, first, NT)
        d_x = halves(d_x + dot_exact(x_t, d_second))
        grad_a = grad_a + dot_exact(d_x, z, NT)
        grad_z = dot_exact(dz, third, NT) + dot_exact(amat_t, d_x)
    grad_a = grad_a + grad_z.T / column_top(amat)
    grad_s = amat * (grad_a - jnp.sum(amat * grad_a, axis=1, keepdims=True)) * SCALE
    high, low = halves(grad_s)
    lq = keep_lanes(lq_ref[...], which)
    lk = keep_lanes(lk_ref[...], which)
    q_ref[...] = dot(high, lk) + dot(low, lk)
    k_ref[...] = dot(high.T, lq) + dot(low.T, lq)


def attend_kernel(n, heads, me_ref, fb_ref, top_ref, cot_ref, *refs):
    size = bit_groups(n)[-1][1]
    parts = n // heads
    cols = DH // parts
    reply_refs = refs[:size]
    attn_ref, mixer_ref, norm_ref, center_ref = refs[size : size + 4]
    out_refs = refs[size + 4 : 2 * size + 4]
    w_ref, d_ref, e_ref, sum_ref, all_ref = refs[2 * size + 4 :]
    pair = pl.program_id(0)

    @pl.when(pair == 0)
    def _():
        for m in range(size):
            for t in range(n // size):
                reply = reply_refs[m][t].astype(F32)
                at = (t * size + m) ^ me_ref[0]
                w_ref[at] = reply[:cols]
                d_ref[at] = reply[cols : 2 * cols]
                e_ref[at] = reply[2 * cols : 2 * cols + 8]
        for h in range(heads):
            cut = slice(h * parts, (h + 1) * parts)
            span = slice(h * DH, (h + 1) * DH)
            mixer_ref[span, :] = w_ref[cut].reshape(DH, LANDMARKS).astype(BF16)
            extra = e_ref[cut]
            top = top_ref[h // 2, h % 2 : h % 2 + 1, :]
            factor = jnp.exp(top - extra[0, 0:1, :])
            norm_ref[span, :] = (d_ref[cut].reshape(DH, LANDMARKS) * factor).astype(BF16)
            sums = jnp.sum(extra, axis=0)
            center_ref[h : h + 1, :] = (sums[1:2] + sums[2:3]) * factor

    mixer = mixer_ref[pl.ds(pl.multiple_of(pair * PAIR, PAIR), PAIR), :]
    attn = dot(fb_ref[:, :LANDMARKS], keep_rows(mixer, 0), NT) + dot(
        fb_ref[:, LANDMARKS:], keep_rows(mixer, 1), NT
    )
    attn = attn.astype(BF16)
    attn_ref[...] = attn
    all_ref[pl.ds(pl.multiple_of(pair * PAIR, PAIR), PAIR), :] = attn.T

    @pl.when(pair == pl.num_programs(0) - 1)
    def _():
        block, split = sum_ref.shape[1], n // sum_ref.shape[0]
        width = cot_ref.shape[1]
        sum_ref[...] = dot(all_ref[...], cot_ref[...]).reshape(sum_ref.shape)
        for m in range(size):
            for t in range(n // size):
                at = (t * size + m) ^ me_ref[0]
                if split == 1:
                    out_refs[m][t] = sum_ref[at].astype(BF16)
                else:
                    side = pl.multiple_of((at % split) * (width // split), width // split)
                    out_refs[m][t] = sum_ref[at // split, :, pl.ds(side, width // split)].astype(BF16)


def soft_grad(fb_ref, g_ref, mixer_ref, ds_ref):
    for h in range(2):
        span = slice(h * LANDMARKS, (h + 1) * LANDMARKS)
        mixer = keep_rows(mixer_ref[...], h)
        for c in range(0, fb_ref.shape[0], CHUNK):
            part = slice(c, c + CHUNK)
            f = fb_ref[part, span].astype(F32)
            df = dot(g_ref[part, :], mixer)
            ds_ref[part, span] = (f * (df - jnp.sum(f * df, axis=1, keepdims=True))).astype(BF16)


def weight_soft_grad(pb_ref, v_ref, norm_ref, center_ref, ds_ref):
    for h in range(2):
        span = slice(h * LANDMARKS, (h + 1) * LANDMARKS)
        norm = keep_rows(norm_ref[...], h)
        center = center_ref[pl.ds(2 * pl.program_id(0) + h, 1), :]
        for c in range(0, pb_ref.shape[0], CHUNK):
            part = slice(c, c + CHUNK)
            dp = dot(v_ref[part, :], norm)
            ds_ref[part, span] = (pb_ref[part, span].astype(F32) * (dp - center)).astype(BF16)


def land_sums(ds_ref, x_ref, own_ref, more_ref):
    xt = x_ref[...].T
    sums = jnp.concatenate(
        [dot(xt[:DH], ds_ref[:, :LANDMARKS]), dot(xt[DH:], ds_ref[:, LANDMARKS:])], axis=0
    )
    here = (own_ref[0] == pl.program_id(0)).astype(F32)
    return (sums.T * SCALE + more_ref[...] * here).astype(BF16)


def token_part(ds_ref, land_ref, out_ref):
    land = land_ref[...] * SCALE
    total = dot(ds_ref[:, :LANDMARKS], keep_lanes(land, 0).astype(BF16)) + dot(
        ds_ref[:, LANDMARKS:], keep_lanes(land, 1).astype(BF16)
    )
    out_ref[...] = total.astype(BF16)


def query_land_kernel(own_ref, q_ref, g_ref, fb_ref, mixer_ref, more_ref, land_ref, ds_ref):
    soft_grad(fb_ref, g_ref, mixer_ref, ds_ref)
    land_ref[...] = land_sums(ds_ref, q_ref, own_ref, more_ref)


def key_land_kernel(own_ref, k_ref, v_ref, pb_ref, norm_ref, center_ref, more_ref, other_ref, *refs):
    ds_ref, out_refs, land_ref = refs[0], refs[1:-1], refs[-1]
    size = len(out_refs)
    columns = other_ref.shape[1]
    pair = pl.program_id(0)
    weight_soft_grad(pb_ref, v_ref, norm_ref, center_ref, ds_ref)
    land_ref[:, pl.ds(pl.multiple_of(pair * PAIR, PAIR), PAIR)] = land_sums(
        ds_ref, k_ref, own_ref, more_ref
    )

    @pl.when(pair == pl.num_programs(0) - 1)
    def _():
        for m in range(size):
            held, height, _ = out_refs[m].shape
            for t in range(held):
                at = pl.multiple_of(((t * size + m) ^ own_ref[2]) * height, height)
                out_refs[m][t, :, :columns] = land_ref[pl.ds(at, height), :]
                out_refs[m][t, :, columns:] = other_ref[pl.ds(at, height), :]


def query_kernel(ds_ref, lk_ref, out_ref):
    token_part(ds_ref, lk_ref, out_ref)


def key_kernel(ds_ref, pb_ref, lq_ref, norm_ref, out_ref, value_ref):
    token_part(ds_ref, lq_ref, out_ref)
    value_ref[...] = (
        dot(pb_ref[:, :LANDMARKS], keep_rows(norm_ref[...], 0), NT)
        + dot(pb_ref[:, LANDMARKS:], keep_rows(norm_ref[...], 1), NT)
    ).astype(BF16)


def finish_kernel(query_ref, key_ref, query_own_ref, key_own_ref, query_out_ref, key_out_ref):
    for in_ref, own_ref, out_ref in (
        (query_ref, query_own_ref, query_out_ref),
        (key_ref, key_own_ref, key_out_ref),
    ):
        own = own_ref[...]
        segments = (own.shape[0], in_ref.shape[0] // own.shape[0], PAIR)
        total = in_ref[...].astype(F32).reshape(segments) + own[:, None, :]
        out_ref[...] = total.reshape(in_ref.shape).astype(BF16)


def part_kernel(_, attn_ref, weight_ref, out_ref):
    out_ref[...] = dot(attn_ref[...], weight_ref[...]).astype(BF16)


def mixed_kernel(_, attn_ref, weight_ref, other_ref, out_ref):
    out_ref[...] = (dot(attn_ref[...], weight_ref[...]) + other_ref[...].astype(F32)).astype(BF16)


def unpack_kernel(split, me_ref, *refs):
    in_refs, (out_ref, wide_ref, sems) = refs[:-3], refs[-3:]
    size = len(in_refs)
    held, block, width = in_refs[0].shape
    copies = []
    for t in range(held):
        for m in range(size):
            slot = t * size + m
            at = slot ^ me_ref[0]
            row = pl.ds(pl.multiple_of((at // split) * block, block), block)
            if split == 1:
                target = out_ref.at[row]
            else:
                target = out_ref.at[row, pl.ds(pl.multiple_of((at % split) * width, width), width)]
            wide_ref[slot] = in_refs[m][t].astype(F32)
            copies.append(pltpu.make_async_copy(wide_ref.at[slot], target, sems.at[slot]))
            copies[-1].start()
    for copy in copies:
        copy.wait()


def held_in_hbm(x):
    return pltpu.with_memory_space_constraint(x, pltpu.HBM)


def whole(shape):
    return pl.BlockSpec(shape, lambda *_: (0,) * len(shape))


def shape_of(shape, dtype):
    return jax.ShapeDtypeStruct(shape, dtype)


def call(kernel, grid, scalars, ins, in_specs, outs, out_specs, scratch=(), flops=0, name=None, aliases={}):
    return pl.pallas_call(
        kernel,
        grid_spec=pltpu.PrefetchScalarGridSpec(
            num_scalar_prefetch=len(scalars),
            grid=grid,
            in_specs=in_specs,
            out_specs=out_specs,
            scratch_shapes=list(scratch),
        ),
        out_shape=outs,
        compiler_params=PARAMS,
        input_output_aliases=aliases,
        cost_estimate=pl.CostEstimate(flops=flops, bytes_accessed=4 << 20, transcendentals=0),
        name=name,
    )(*scalars, *ins)


def local(queries, key_rows, value_rows, out_weight, cotangent):
    rows, columns = queries.shape
    width = out_weight.shape[1]
    heads = columns // DH
    pairs = columns // PAIR
    n = lax.axis_size("seq")
    me = lax.axis_index("seq")
    mine = lax.axis_index("head")
    land_dev = LANDMARKS // n
    seg_len = rows // land_dev
    parts = n // heads
    cols = DH // parts
    size = bit_groups(n)[-1][1]
    height = 2 * cols + EXTRA
    own_head = me // parts

    sorted_here = land_dev % 16 == 0
    me_arr = jnp.stack([me, me if sorted_here else me * 0]).astype(jnp.int32)
    mine_arr = mine.reshape(1).astype(jnp.int32)
    own_arr = jnp.stack([own_head // 2, own_head % 2, me * 0 if land_dev % 16 else me]).astype(jnp.int32)
    steps = 4
    in_hbm = pl.BlockSpec(memory_space=pltpu.HBM)
    own = call(
        functools.partial(means_kernel, seg_len),
        (1,),
        [],
        [held_in_hbm(queries), held_in_hbm(key_rows)],
        [in_hbm, in_hbm],
        shape_of((land_dev, 2 * columns), BF16),
        whole((land_dev, 2 * columns)),
        [
            pltpu.VMEM((2, rows, columns), BF16),
            pltpu.VMEM((land_dev, 2 * columns), F32),
            pltpu.SemaphoreType.DMA((2, steps)),
        ],
        name="means",
    )
    own, me_arr, mine_arr, own_arr = lax.optimization_barrier((own, me_arr, mine_arr, own_arr))
    grad_attn = dot(cotangent, out_weight, NT).astype(BF16)
    if sorted_here:
        lands = gather_lists(own, n)
    else:
        lands = [gather_ordered(own, n, me).reshape(LANDMARKS // 16, 16, 2 * columns)]

    token_pair = pl.BlockSpec((rows, PAIR), lambda j, *_: (0, j))
    factor_pair = pl.BlockSpec((rows, 2 * LANDMARKS), lambda j, *_: (0, j))
    lq_pair = pl.BlockSpec((LANDMARKS, PAIR), lambda j, *_: (0, j))
    lk_pair = pl.BlockSpec((LANDMARKS, PAIR), lambda j, *_: (0, j + pairs))
    factors = shape_of((rows, heads * LANDMARKS), BF16)
    piece = shape_of((n // size, height, LANDMARKS), BF16)

    fb, pb, tops, land, *pieces = call(
        functools.partial(forward_kernel, n, heads, len(lands)),
        (pairs,),
        [me_arr],
        [queries, key_rows, value_rows, grad_attn] + lands,
        [token_pair] * 4 + [whole(lands[0].shape)] * len(lands),
        [
            factors,
            factors,
            shape_of((pairs, 8, LANDMARKS), F32),
            shape_of((LANDMARKS, 2 * columns), BF16),
        ]
        + [piece] * size,
        [
            factor_pair,
            factor_pair,
            pl.BlockSpec((1, 8, LANDMARKS), lambda j, *_: (j, 0, 0)),
            whole((LANDMARKS, 2 * columns)),
        ]
        + [whole(piece.shape)] * size,
        [
            pltpu.VMEM((rows, LANDMARKS), F32),
            pltpu.VMEM((n, height, LANDMARKS), BF16),
        ],
        flops=8 << 30,
        name="forward",
    )

    square = (LANDMARKS, LANDMARKS)
    own_lq = pl.BlockSpec((LANDMARKS, PAIR), lambda i, own: (0, own[0]))
    own_lk = pl.BlockSpec((LANDMARKS, PAIR), lambda i, own: (0, own[0] + pairs))
    kept = shape_of((1 + 4 * ITERS,) + square, F32)
    saved, inverse = call(
        newton_kernel,
        (1,),
        [own_arr],
        [land, land],
        [own_lq, own_lk],
        [kept, shape_of((1,) + square, F32)],
        [whole(kept.shape), whole((1,) + square)],
        flops=4 << 30,
        name="newton",
    )

    groups = bit_groups(n)[::-1]
    for step, (shift, count) in enumerate(groups):
        got = [pieces[0]] + [exchange(pieces[m], m << shift, n) for m in range(1, count)]
        specs = [whole(got[0].shape)] * count
        if step == 0:
            got, inverse = lax.optimization_barrier((got, inverse))
        if step + 1 < len(groups):
            following = groups[step + 1][1]
            piece = shape_of((got[0].shape[0] // following, height, LANDMARKS), BF16)
            pieces = call(
                functools.partial(merge_kernel, cols, count),
                (1,),
                [],
                got,
                specs,
                [piece] * following,
                [whole(piece.shape)] * following,
                name="merge",
            )
    small = shape_of((cols, LANDMARKS), F32)
    reply, values, grads = call(
        functools.partial(mix_kernel, cols, count),
        (1,),
        [],
        got + [inverse],
        specs + [whole((1,) + square)],
        [piece, small, small],
        [whole(piece.shape), whole(small.shape), whole(small.shape)],
        name="mix",
    )
    replies = gather_lists(reply[0], n)

    more = shape_of((LANDMARKS, PAIR), F32)
    more_q, more_k = call(
        newton_grad_kernel,
        (1,),
        [own_arr],
        [saved, values, grads, land, land],
        [whole(kept.shape), whole(small.shape), whole(small.shape), own_lq, own_lk],
        [more, more],
        [whole(more.shape)] * 2,
        flops=8 << 30,
        name="newton_grad",
    )

    replies, more_q, more_k = lax.optimization_barrier((replies, more_q, more_k))
    block = max(columns // n, 16)
    split = n * block // columns
    flat = shape_of((columns, LANDMARKS), BF16)
    weight_piece = shape_of((n // size, block, width // split), BF16)
    attn, mixer, norm, center, *weight_pieces = call(
        functools.partial(attend_kernel, n, heads),
        (pairs,),
        [me_arr],
        [fb, tops, cotangent] + replies,
        [factor_pair, whole(tops.shape), whole(cotangent.shape)] + [whole(replies[0].shape)] * size,
        [shape_of((rows, columns), BF16), flat, flat, shape_of((heads, LANDMARKS), F32)]
        + [weight_piece] * size,
        [token_pair, whole(flat.shape), whole(flat.shape), whole((heads, LANDMARKS))]
        + [whole(weight_piece.shape)] * size,
        [
            pltpu.VMEM((n, cols, LANDMARKS), F32),
            pltpu.VMEM((n, cols, LANDMARKS), F32),
            pltpu.VMEM((n, 8, LANDMARKS), F32),
            pltpu.VMEM((columns // block, block, width), F32),
            pltpu.VMEM((columns, rows), BF16),
        ],
        flops=4 << 30,
        name="attend",
    )
    (shift, count), later = groups[0], groups[1:]
    weight_sum = scatter_step(weight_pieces, shift, count, n).astype(BF16)
    (pb, key_rows, value_rows), weight_sum = lax.optimization_barrier(
        ((pb, key_rows, value_rows), weight_sum)
    )
    following = later[0][1]
    weight_sum = weight_sum.reshape((-1, following) + weight_sum.shape[1:])
    weight_own = scatter_pieces([weight_sum[:, m] for m in range(following)], n, later)[0].astype(BF16)
    flat_pair = pl.BlockSpec((PAIR, LANDMARKS), lambda j, *_: (j, 0))
    land_pair = pl.BlockSpec((LANDMARKS, PAIR), lambda j, *_: (0, j))
    centers = whole((heads, LANDMARKS))
    tokens = shape_of((rows, columns), BF16)
    land_shape = shape_of((LANDMARKS, columns), BF16)
    land_k, grad_sf = call(
        query_land_kernel,
        (pairs,),
        [own_arr],
        [queries, grad_attn, fb, mixer, more_k],
        [token_pair, token_pair, factor_pair, flat_pair, whole(more.shape)],
        [land_shape, factors],
        [land_pair, factor_pair],
        flops=4 << 30,
        name="query_land",
    )
    (shift, count), later = groups[0], groups[1:]
    following = later[0][1]
    weight_sum = scatter_step(weight_pieces, shift, count, n).astype(BF16)
    (pb, key_rows, value_rows), weight_sum, land_k = lax.optimization_barrier(
        ((pb, key_rows, value_rows), weight_sum, land_k)
    )
    if sorted_here:
        land_piece, pieces_count = shape_of((n // size, land_dev, 2 * columns), BF16), size
    else:
        land_piece, pieces_count = shape_of((LANDMARKS // 16, 16, 2 * columns), BF16), 1
    grad_sb, *land_pieces = call(
        key_land_kernel,
        (pairs,),
        [own_arr],
        [key_rows, value_rows, pb, norm, center, more_q, land_k],
        [token_pair, token_pair, factor_pair, flat_pair, centers, whole(more.shape)]
        + [whole(land_shape.shape)],
        [factors] + [land_piece] * pieces_count,
        [factor_pair] + [whole(land_piece.shape)] * pieces_count,
        [pltpu.VMEM(land_shape.shape, BF16)],
        flops=4 << 30,
        name="key_land",
    )
    half = width // 2
    row_block = pl.BlockSpec((rows // 4, columns), lambda j, _: (j, 0))
    half_block = pl.BlockSpec((rows // 4, half), lambda j, _: (j, 0))

    if not sorted_here:
        land_pieces = split_by_partner(land_pieces[0].reshape(n, land_dev, 2 * columns), n, me)
    weight_sum = weight_sum.reshape((-1, following) + weight_sum.shape[1:])
    weight_own = scatter_pieces([weight_sum[:, m] for m in range(following)], n, later)[0].astype(BF16)
    land_pieces, weight_own = lax.optimization_barrier((land_pieces, weight_own))
    land_sum = scatter_step(land_pieces, shift, count, n).astype(BF16)
    weights = gather_first(weight_own, n)
    land_sum, grad_sf, attn = lax.optimization_barrier((land_sum, grad_sf, attn))
    query_f = call(
        query_kernel,
        (pairs,),
        [],
        [grad_sf, land],
        [factor_pair, lk_pair],
        tokens,
        token_pair,
        flops=2 << 30,
        name="query_grad",
    )
    there = call(
        part_kernel,
        (4,),
        [mine_arr],
        [attn, out_weight],
        [row_block, pl.BlockSpec((columns, half), lambda j, mine: (0, 1 - mine[0]))],
        shape_of((rows, half), BF16),
        half_block,
        flops=1 << 30,
        name="part",
    )
    land_sum, weights, query_f, there = lax.optimization_barrier((land_sum, weights, query_f, there))
    land_sum, weights, grad_sb = lax.optimization_barrier((land_sum, weights, grad_sb))
    key_b, value_grad = call(
        key_kernel,
        (pairs,),
        [],
        [grad_sb, pb, land, norm],
        [factor_pair, factor_pair, lq_pair, flat_pair],
        [tokens, tokens],
        [token_pair, token_pair],
        flops=4 << 30,
        name="key_grad",
    )

    arrived = lax.ppermute(there, "head", [(0, 1), (1, 0)])
    mask = size
    while land_sum.shape[0] > 1:
        given = exchange(land_sum[1::2], mask, n)
        land_sum = (land_sum[::2].astype(F32) + given.astype(F32)).astype(BF16)
        mask *= 2
    land_own = land_sum[0].astype(F32)
    land_own = land_own * (1.0 / seg_len)
    mixed = call(
        mixed_kernel,
        (4,),
        [mine_arr],
        [attn, out_weight, arrived],
        [row_block, pl.BlockSpec((columns, half), lambda j, mine: (0, mine[0])), half_block],
        shape_of((rows, half), BF16),
        half_block,
        flops=1 << 30,
        name="mixed",
    )
    weights = gather_rest(weights, n)
    weights, mixed = lax.optimization_barrier((weights, mixed))
    weight_grad = call(
        functools.partial(unpack_kernel, split),
        (1,),
        [me_arr],
        weights,
        [whole(weights[0].shape)] * size,
        pltpu.HBM((columns, width), F32),
        in_hbm,
        [pltpu.VMEM((n,) + weights[0].shape[1:], F32), pltpu.SemaphoreType.DMA((n,))],
        name="unpack",
    )

    def own_pair(first):
        return pl.BlockSpec((land_dev, PAIR), lambda j, *_: (0, j + first))

    query_grad, key_grad = call(
        finish_kernel,
        (pairs,),
        [],
        [query_f, key_b, land_own, land_own],
        [token_pair, token_pair, own_pair(0), own_pair(pairs)],
        [tokens, tokens],
        [token_pair, token_pair],
        name="finish",
    )
    return (mixed, query_grad, key_grad, value_grad, weight_grad)


def solution(mesh):
    return jax.shard_map(
        local,
        mesh=mesh,
        in_specs=(
            P("seq", "head"),
            P("seq", "head"),
            P("seq", "head"),
            P("head", None),
            P("seq", None),
        ),
        out_specs=(
            P("seq", "head"),
            P("seq", "head"),
            P("seq", "head"),
            P("seq", "head"),
            P("head", None),
        ),
        check_vma=False,
    )
```

```python
import functools

import jax
import jax.numpy as jnp
from jax import lax
from jax.experimental import pallas as pl
from jax.experimental.pallas import tpu as pltpu
from jax.sharding import PartitionSpec as P

DH = 64
PAIR = 2 * DH
LANDMARKS = 256
ITERS = 2
SCALE = 0.125
CHUNK = 256
EXTRA = 16
F32 = jnp.float32
BF16 = jnp.bfloat16
PARAMS = pltpu.CompilerParams(vmem_limit_bytes=24 * 1024 * 1024)


def dot(left, right, dims=((1,), (0,))):
    return lax.dot_general(left, right, (dims, ((), ())), preferred_element_type=F32)


NT = ((1,), (1,))
TN = ((0,), (0,))


def halves(value):
    high = value.astype(BF16)
    return high, (value - high.astype(F32)).astype(BF16)


def dot_exact(left, right, dims=((1,), (0,))):
    return dot(left[0], right[0], dims) + (
        dot(left[0], right[1], dims) + dot(left[1], right[0], dims)
    )


def turned(pair):
    return pair[0].T, pair[1].T


def keep_rows(block, which):
    rows = lax.broadcasted_iota(jnp.int32, block.shape, 0) // DH
    return jnp.where(rows == which, block, jnp.zeros_like(block))


def keep_lanes(block, which):
    lanes = lax.broadcasted_iota(jnp.int32, block.shape, 1) // DH
    return jnp.where(lanes == which, block, jnp.zeros_like(block))


def fold(block, op):
    parts = block.reshape(block.shape[0] // 8, 8, block.shape[1])
    return op(parts, axis=0)


def exchange(block, mask, n):
    return lax.ppermute(block, "seq", [(i, i ^ mask) for i in range(n)])


def bit_groups(n):
    bits = n.bit_length() - 1
    groups = []
    while bits > 0:
        take = 2 if bits % 2 == 0 else 1
        bits -= take
        groups.append((bits, 1 << take))
    return groups


def gather_first(block, n):
    shift, size = bit_groups(n)[0]
    held = block[None]
    return [held] + [exchange(held, m << shift, n) for m in range(1, size)]


def gather_rest(got, n):
    for shift, size in bit_groups(n)[1:]:
        held = jnp.stack(got, axis=1).reshape((-1,) + got[0].shape[1:])
        got = [held] + [exchange(held, m << shift, n) for m in range(1, size)]
    return got


def gather_lists(block, n):
    return gather_rest(gather_first(block, n), n)


def gather_ordered(block, n, me):
    got = gather_lists(block, n)
    held = jnp.stack(got, axis=1).reshape((n,) + block.shape)
    return held.at[jnp.arange(n) ^ me].get(mode="promise_in_bounds")


def split_by_partner(blocks, n, me):
    size = bit_groups(n)[-1][1]
    return [
        blocks.at[(jnp.arange(n // size) * size + m) ^ me].get(mode="promise_in_bounds")
        for m in range(size)
    ]


def scatter_step(pieces, shift, size, n):
    got = [pieces[0]] + [exchange(pieces[m], m << shift, n) for m in range(1, size)]
    return sum(part.astype(F32) for part in got)


def scatter_pieces(pieces, n, groups):
    for step, (shift, size) in enumerate(groups):
        held = scatter_step(pieces, shift, size, n)
        if step + 1 < len(groups):
            following = groups[step + 1][1]
            held = held.astype(BF16).reshape((-1, following) + held.shape[1:])
            pieces = [held[:, m] for m in range(following)]
    return held


def means_kernel(seg_len, q_ref, k_ref, out_ref, in_ref, sum_ref, sems):
    rows, columns = q_ref.shape
    steps = sems.shape[1]
    height = rows // steps
    copies = {}
    for c in range(steps):
        part = pl.ds(c * height, height)
        for side, ref in enumerate((q_ref, k_ref)):
            copies[side, c] = pltpu.make_async_copy(ref.at[part], in_ref.at[side, part], sems.at[side, c])
            copies[side, c].start()
    for c in range(steps):
        for side in range(2):
            copies[side, c].wait()
            span = slice(side * columns, (side + 1) * columns)
            for s in range(c * height // seg_len, (c + 1) * height // seg_len):
                total = fold(in_ref[side, s * seg_len : (s + 1) * seg_len, :].astype(F32), jnp.sum)
                sum_ref[s : s + 1, span] = jnp.sum(total, axis=0, keepdims=True)
    out_ref[...] = (sum_ref[...] * (1.0 / seg_len)).astype(BF16)


def forward_kernel(n, heads, count, me_ref, q_ref, k_ref, v_ref, g_ref, *refs):
    size = bit_groups(n)[-1][1]
    in_refs = refs[:count]
    fb_ref, pb_ref, top_ref, land_ref = refs[count : count + 4]
    out_refs = refs[count + 4 : count + 4 + size]
    score_ref, message_ref = refs[count + 4 + size :]
    pair = pl.program_id(0)
    columns = land_ref.shape[1] // 2

    @pl.when(pair == 0)
    def _():
        for m in range(count):
            held, height, _ = in_refs[m].shape
            for t in range(held):
                at = pl.multiple_of(((t * count + m) ^ me_ref[1]) * height, height)
                land_ref[pl.ds(at, height), :] = in_refs[m][t]

    here = pl.multiple_of(pair * PAIR, PAIR)
    lq_pair = land_ref[:, pl.ds(here, PAIR)]
    lk_pair = land_ref[:, pl.ds(columns + here, PAIR)]
    rows = q_ref.shape[0]
    parts = n // heads
    cols = DH // parts
    gt = g_ref[...].T
    vt = v_ref[...].T
    for h in range(2):
        lk = keep_lanes(lk_pair * SCALE, h).astype(BF16)
        lq = keep_lanes(lq_pair * SCALE, h).astype(BF16)
        span = slice(h * LANDMARKS, (h + 1) * LANDMARKS)
        top = None
        for c in range(0, rows, CHUNK):
            part = slice(c, c + CHUNK)
            sb = dot(k_ref[part, :], lq, NT)
            score_ref[part, :] = sb
            high = fold(sb, jnp.max)
            top = high if top is None else jnp.maximum(top, high)
            sf = dot(q_ref[part, :], lk, NT)
            e = jnp.exp(sf - jnp.max(sf, axis=1, keepdims=True))
            fb_ref[part, span] = (e * (1.0 / jnp.sum(e, axis=1, keepdims=True))).astype(BF16)
        top = jnp.max(top, axis=0, keepdims=True).astype(BF16).astype(F32)
        total = None
        for c in range(0, rows, CHUNK):
            part = slice(c, c + CHUNK)
            p = jnp.exp(score_ref[part, :] - top)
            add = fold(p, jnp.sum)
            total = add if total is None else total + add
            pb_ref[part, span] = p.astype(BF16)
        total = jnp.sum(total, axis=0, keepdims=True)
        top_ref[0, h : h + 1, :] = top
        grads = dot(gt[h * DH : (h + 1) * DH], fb_ref[:, span])
        vals = dot(vt[h * DH : (h + 1) * DH], pb_ref[:, span])
        high, low = halves(total)
        extra = three_rows(top, high.astype(F32), low.astype(F32))
        for p in range(parts):
            cut = slice(p * cols, (p + 1) * cols)
            message_ref[(2 * pair + h) * parts + p] = jnp.concatenate(
                [vals[cut], grads[cut], extra], axis=0
            ).astype(BF16)

    @pl.when(pair == pl.num_programs(0) - 1)
    def _():
        for m in range(size):
            for t in range(n // size):
                out_refs[m][t] = message_ref[(t * size + m) ^ me_ref[0]]


def merge(items, cols):
    tops = [item[2 * cols : 2 * cols + 1] for item in items]
    peak = functools.reduce(jnp.maximum, tops)
    vals = grads = total = 0.0
    for item, top in zip(items, tops):
        factor = jnp.exp(top - peak)
        vals = vals + item[:cols] * factor
        grads = grads + item[cols : 2 * cols]
        total = total + (
            item[2 * cols + 1 : 2 * cols + 2] + item[2 * cols + 2 : 2 * cols + 3]
        ) * factor
    return vals, grads, peak, total


def three_rows(first, second, third):
    row = lax.broadcasted_iota(jnp.int32, (EXTRA, LANDMARKS), 0)
    return jnp.where(row == 0, first, jnp.where(row == 1, second, jnp.where(row == 2, third, 0.0)))


def merge_kernel(cols, count, *refs):
    in_refs, out_refs = refs[:count], refs[count:]
    following = len(out_refs)
    for t in range(in_refs[0].shape[0]):
        vals, grads, peak, total = merge([ref[t].astype(F32) for ref in in_refs], cols)
        high, low = halves(total)
        extra = three_rows(peak, high.astype(F32), low.astype(F32))
        out_refs[t % following][t // following] = jnp.concatenate(
            [vals, grads, extra], axis=0
        ).astype(BF16)


def mix_kernel(cols, count, *refs):
    in_refs, z_ref = refs[:count], refs[count]
    reply_ref, values_ref, grads_ref = refs[count + 1 :]
    vals, grads, peak, total = merge([ref[0].astype(F32) for ref in in_refs], cols)
    inverse = halves(z_ref[0])
    values = vals / total
    mixer = dot_exact(halves(values), inverse, NT)
    norm = dot_exact(halves(grads), inverse) / total
    high, low = halves(jnp.sum(norm * values, axis=0, keepdims=True))
    extra = three_rows(peak, high.astype(F32), low.astype(F32))
    reply_ref[0] = jnp.concatenate([mixer, norm, extra], axis=0).astype(BF16)
    values_ref[...] = values
    grads_ref[...] = grads


def soft_rows(scores):
    e = jnp.exp(scores - jnp.max(scores, axis=1, keepdims=True))
    return e / jnp.sum(e, axis=1, keepdims=True)


def eye():
    shape = (LANDMARKS, LANDMARKS)
    same = lax.broadcasted_iota(jnp.int32, shape, 0) == lax.broadcasted_iota(jnp.int32, shape, 1)
    return same.astype(F32)


def column_top(amat):
    return jnp.max(jnp.sum(amat, axis=0, keepdims=True), axis=1, keepdims=True)


def newton_kernel(own_ref, lq_ref, lk_ref, saved_ref, z_ref):
    which = own_ref[1]
    amat = soft_rows(dot(keep_lanes(lq_ref[...] * SCALE, which).astype(BF16), lk_ref[...], NT))
    saved_ref[0] = amat
    current = amat.T / column_top(amat)
    ident = eye()
    amat = halves(amat)
    for i in range(ITERS):
        saved_ref[1 + 4 * i] = current
        z = halves(current)
        x_full = dot_exact(amat, z)
        saved_ref[2 + 4 * i] = x_full
        x = halves(x_full)
        inner = 15.0 * ident - dot_exact(x, halves(7.0 * ident - x_full))
        saved_ref[3 + 4 * i] = inner
        inner = 13.0 * ident - dot_exact(x, halves(inner))
        saved_ref[4 + 4 * i] = inner
        current = 0.25 * dot_exact(z, halves(inner))
    z_ref[0] = current


def newton_grad_kernel(own_ref, saved_ref, values_ref, grads_ref, lq_ref, lk_ref, q_ref, k_ref):
    which = own_ref[1]
    ident = eye()
    amat = saved_ref[0]
    amat_t = turned(halves(amat))
    grad_z = dot_exact(halves(grads_ref[...]), halves(values_ref[...]), TN)
    grad_a = jnp.zeros_like(amat)
    for i in reversed(range(ITERS)):
        z = halves(saved_ref[1 + 4 * i])
        x_full = saved_ref[2 + 4 * i]
        x_t = turned(halves(x_full))
        first = halves(7.0 * ident - x_full)
        second = halves(saved_ref[3 + 4 * i])
        third = halves(saved_ref[4 + 4 * i])
        dz = halves(0.25 * grad_z)
        d_third = halves(dot_exact(turned(z), dz))
        d_second = halves(-dot_exact(x_t, d_third))
        d_x = -dot_exact(d_third, second, NT) - dot_exact(d_second, first, NT)
        d_x = halves(d_x + dot_exact(x_t, d_second))
        grad_a = grad_a + dot_exact(d_x, z, NT)
        grad_z = dot_exact(dz, third, NT) + dot_exact(amat_t, d_x)
    grad_a = grad_a + grad_z.T / column_top(amat)
    grad_s = amat * (grad_a - jnp.sum(amat * grad_a, axis=1, keepdims=True)) * SCALE
    high, low = halves(grad_s)
    lq = keep_lanes(lq_ref[...], which)
    lk = keep_lanes(lk_ref[...], which)
    q_ref[...] = dot(high, lk) + dot(low, lk)
    k_ref[...] = dot(high.T, lq) + dot(low.T, lq)


def attend_kernel(n, heads, me_ref, fb_ref, top_ref, cot_ref, *refs):
    size = bit_groups(n)[-1][1]
    parts = n // heads
    cols = DH // parts
    reply_refs = refs[:size]
    attn_ref, mixer_ref, norm_ref, center_ref = refs[size : size + 4]
    out_refs = refs[size + 4 : 2 * size + 4]
    w_ref, d_ref, e_ref, sum_ref, all_ref = refs[2 * size + 4 :]
    pair = pl.program_id(0)

    @pl.when(pair == 0)
    def _():
        for m in range(size):
            for t in range(n // size):
                reply = reply_refs[m][t].astype(F32)
                at = (t * size + m) ^ me_ref[0]
                w_ref[at] = reply[:cols]
                d_ref[at] = reply[cols : 2 * cols]
                e_ref[at] = reply[2 * cols : 2 * cols + 8]
        for h in range(heads):
            cut = slice(h * parts, (h + 1) * parts)
            span = slice(h * DH, (h + 1) * DH)
            mixer_ref[span, :] = w_ref[cut].reshape(DH, LANDMARKS).astype(BF16)
            extra = e_ref[cut]
            top = top_ref[h // 2, h % 2 : h % 2 + 1, :]
            factor = jnp.exp(top - extra[0, 0:1, :])
            norm_ref[span, :] = (d_ref[cut].reshape(DH, LANDMARKS) * factor).astype(BF16)
            sums = jnp.sum(extra, axis=0)
            center_ref[h : h + 1, :] = (sums[1:2] + sums[2:3]) * factor

    mixer = mixer_ref[pl.ds(pl.multiple_of(pair * PAIR, PAIR), PAIR), :]
    attn = dot(fb_ref[:, :LANDMARKS], keep_rows(mixer, 0), NT) + dot(
        fb_ref[:, LANDMARKS:], keep_rows(mixer, 1), NT
    )
    attn = attn.astype(BF16)
    attn_ref[...] = attn
    all_ref[pl.ds(pl.multiple_of(pair * PAIR, PAIR), PAIR), :] = attn.T

    @pl.when(pair == pl.num_programs(0) - 1)
    def _():
        block, split = sum_ref.shape[1], n // sum_ref.shape[0]
        width = cot_ref.shape[1]
        sum_ref[...] = dot(all_ref[...], cot_ref[...]).reshape(sum_ref.shape)
        for m in range(size):
            for t in range(n // size):
                at = (t * size + m) ^ me_ref[0]
                if split == 1:
                    out_refs[m][t] = sum_ref[at].astype(BF16)
                else:
                    side = pl.multiple_of((at % split) * (width // split), width // split)
                    out_refs[m][t] = sum_ref[at // split, :, pl.ds(side, width // split)].astype(BF16)


def soft_grad(fb_ref, g_ref, mixer_ref, ds_ref):
    for h in range(2):
        span = slice(h * LANDMARKS, (h + 1) * LANDMARKS)
        mixer = keep_rows(mixer_ref[...], h)
        for c in range(0, fb_ref.shape[0], CHUNK):
            part = slice(c, c + CHUNK)
            f = fb_ref[part, span].astype(F32)
            df = dot(g_ref[part, :], mixer)
            ds_ref[part, span] = (f * (df - jnp.sum(f * df, axis=1, keepdims=True))).astype(BF16)


def weight_soft_grad(pb_ref, v_ref, norm_ref, center_ref, ds_ref):
    for h in range(2):
        span = slice(h * LANDMARKS, (h + 1) * LANDMARKS)
        norm = keep_rows(norm_ref[...], h)
        center = center_ref[pl.ds(2 * pl.program_id(0) + h, 1), :]
        for c in range(0, pb_ref.shape[0], CHUNK):
            part = slice(c, c + CHUNK)
            dp = dot(v_ref[part, :], norm)
            ds_ref[part, span] = (pb_ref[part, span].astype(F32) * (dp - center)).astype(BF16)


def land_sums(ds_ref, x_ref, own_ref, more_ref):
    xt = x_ref[...].T
    sums = jnp.concatenate(
        [dot(xt[:DH], ds_ref[:, :LANDMARKS]), dot(xt[DH:], ds_ref[:, LANDMARKS:])], axis=0
    )
    here = (own_ref[0] == pl.program_id(0)).astype(F32)
    return (sums.T * SCALE + more_ref[...] * here).astype(BF16)


def token_part(ds_ref, land_ref, out_ref):
    land = land_ref[...] * SCALE
    total = dot(ds_ref[:, :LANDMARKS], keep_lanes(land, 0).astype(BF16)) + dot(
        ds_ref[:, LANDMARKS:], keep_lanes(land, 1).astype(BF16)
    )
    out_ref[...] = total.astype(BF16)


def query_land_kernel(own_ref, q_ref, g_ref, fb_ref, mixer_ref, more_ref, land_ref, ds_ref):
    soft_grad(fb_ref, g_ref, mixer_ref, ds_ref)
    land_ref[...] = land_sums(ds_ref, q_ref, own_ref, more_ref)


def key_land_kernel(own_ref, k_ref, v_ref, pb_ref, norm_ref, center_ref, more_ref, other_ref, *refs):
    ds_ref, out_refs, land_ref = refs[0], refs[1:-1], refs[-1]
    size = len(out_refs)
    columns = other_ref.shape[1]
    pair = pl.program_id(0)
    weight_soft_grad(pb_ref, v_ref, norm_ref, center_ref, ds_ref)
    land_ref[:, pl.ds(pl.multiple_of(pair * PAIR, PAIR), PAIR)] = land_sums(
        ds_ref, k_ref, own_ref, more_ref
    )

    @pl.when(pair == pl.num_programs(0) - 1)
    def _():
        for m in range(size):
            held, height, _ = out_refs[m].shape
            for t in range(held):
                at = pl.multiple_of(((t * size + m) ^ own_ref[2]) * height, height)
                out_refs[m][t, :, :columns] = land_ref[pl.ds(at, height), :]
                out_refs[m][t, :, columns:] = other_ref[pl.ds(at, height), :]


def query_kernel(ds_ref, lk_ref, out_ref):
    token_part(ds_ref, lk_ref, out_ref)


def key_kernel(ds_ref, pb_ref, lq_ref, norm_ref, out_ref, value_ref):
    token_part(ds_ref, lq_ref, out_ref)
    value_ref[...] = (
        dot(pb_ref[:, :LANDMARKS], keep_rows(norm_ref[...], 0), NT)
        + dot(pb_ref[:, LANDMARKS:], keep_rows(norm_ref[...], 1), NT)
    ).astype(BF16)


def finish_kernel(query_ref, key_ref, query_own_ref, key_own_ref, query_out_ref, key_out_ref):
    for in_ref, own_ref, out_ref in (
        (query_ref, query_own_ref, query_out_ref),
        (key_ref, key_own_ref, key_out_ref),
    ):
        own = own_ref[...]
        segments = (own.shape[0], in_ref.shape[0] // own.shape[0], PAIR)
        total = in_ref[...].astype(F32).reshape(segments) + own[:, None, :]
        out_ref[...] = total.reshape(in_ref.shape).astype(BF16)


def part_kernel(_, attn_ref, weight_ref, out_ref):
    out_ref[...] = dot(attn_ref[...], weight_ref[...]).astype(BF16)


def mixed_kernel(_, attn_ref, weight_ref, other_ref, out_ref):
    out_ref[...] = (dot(attn_ref[...], weight_ref[...]) + other_ref[...].astype(F32)).astype(BF16)


def unpack_kernel(split, me_ref, *refs):
    in_refs, (out_ref, wide_ref, sems) = refs[:-3], refs[-3:]
    size = len(in_refs)
    held, block, width = in_refs[0].shape
    copies = []
    for t in range(held):
        for m in range(size):
            slot = t * size + m
            at = slot ^ me_ref[0]
            row = pl.ds(pl.multiple_of((at // split) * block, block), block)
            if split == 1:
                target = out_ref.at[row]
            else:
                target = out_ref.at[row, pl.ds(pl.multiple_of((at % split) * width, width), width)]
            wide_ref[slot] = in_refs[m][t].astype(F32)
            copies.append(pltpu.make_async_copy(wide_ref.at[slot], target, sems.at[slot]))
            copies[-1].start()
    for copy in copies:
        copy.wait()


def held_in_hbm(x):
    return pltpu.with_memory_space_constraint(x, pltpu.HBM)


def whole(shape):
    return pl.BlockSpec(shape, lambda *_: (0,) * len(shape))


def shape_of(shape, dtype):
    return jax.ShapeDtypeStruct(shape, dtype)


def call(kernel, grid, scalars, ins, in_specs, outs, out_specs, scratch=(), flops=0, name=None, aliases={}):
    return pl.pallas_call(
        kernel,
        grid_spec=pltpu.PrefetchScalarGridSpec(
            num_scalar_prefetch=len(scalars),
            grid=grid,
            in_specs=in_specs,
            out_specs=out_specs,
            scratch_shapes=list(scratch),
        ),
        out_shape=outs,
        compiler_params=PARAMS,
        input_output_aliases=aliases,
        cost_estimate=pl.CostEstimate(flops=flops, bytes_accessed=4 << 20, transcendentals=0),
        name=name,
    )(*scalars, *ins)


def local(queries, key_rows, value_rows, out_weight, cotangent):
    rows, columns = queries.shape
    width = out_weight.shape[1]
    heads = columns // DH
    pairs = columns // PAIR
    n = lax.axis_size("seq")
    me = lax.axis_index("seq")
    mine = lax.axis_index("head")
    land_dev = LANDMARKS // n
    seg_len = rows // land_dev
    parts = n // heads
    cols = DH // parts
    size = bit_groups(n)[-1][1]
    height = 2 * cols + EXTRA
    own_head = me // parts

    sorted_here = land_dev % 16 == 0
    me_arr = jnp.stack([me, me if sorted_here else me * 0]).astype(jnp.int32)
    mine_arr = mine.reshape(1).astype(jnp.int32)
    own_arr = jnp.stack([own_head // 2, own_head % 2, me * 0 if land_dev % 16 else me]).astype(jnp.int32)
    steps = 4
    in_hbm = pl.BlockSpec(memory_space=pltpu.HBM)
    own = call(
        functools.partial(means_kernel, seg_len),
        (1,),
        [],
        [held_in_hbm(queries), held_in_hbm(key_rows)],
        [in_hbm, in_hbm],
        shape_of((land_dev, 2 * columns), BF16),
        whole((land_dev, 2 * columns)),
        [
            pltpu.VMEM((2, rows, columns), BF16),
            pltpu.VMEM((land_dev, 2 * columns), F32),
            pltpu.SemaphoreType.DMA((2, steps)),
        ],
        name="means",
    )
    own, me_arr, mine_arr, own_arr = lax.optimization_barrier((own, me_arr, mine_arr, own_arr))
    grad_attn = dot(cotangent, out_weight, NT).astype(BF16)
    if sorted_here:
        lands = gather_lists(own, n)
    else:
        lands = [gather_ordered(own, n, me).reshape(LANDMARKS // 16, 16, 2 * columns)]

    token_pair = pl.BlockSpec((rows, PAIR), lambda j, *_: (0, j))
    factor_pair = pl.BlockSpec((rows, 2 * LANDMARKS), lambda j, *_: (0, j))
    lq_pair = pl.BlockSpec((LANDMARKS, PAIR), lambda j, *_: (0, j))
    lk_pair = pl.BlockSpec((LANDMARKS, PAIR), lambda j, *_: (0, j + pairs))
    factors = shape_of((rows, heads * LANDMARKS), BF16)
    piece = shape_of((n // size, height, LANDMARKS), BF16)

    fb, pb, tops, land, *pieces = call(
        functools.partial(forward_kernel, n, heads, len(lands)),
        (pairs,),
        [me_arr],
        [queries, key_rows, value_rows, grad_attn] + lands,
        [token_pair] * 4 + [whole(lands[0].shape)] * len(lands),
        [
            factors,
            factors,
            shape_of((pairs, 8, LANDMARKS), F32),
            shape_of((LANDMARKS, 2 * columns), BF16),
        ]
        + [piece] * size,
        [
            factor_pair,
            factor_pair,
            pl.BlockSpec((1, 8, LANDMARKS), lambda j, *_: (j, 0, 0)),
            whole((LANDMARKS, 2 * columns)),
        ]
        + [whole(piece.shape)] * size,
        [
            pltpu.VMEM((rows, LANDMARKS), F32),
            pltpu.VMEM((n, height, LANDMARKS), BF16),
        ],
        flops=8 << 30,
        name="forward",
    )

    square = (LANDMARKS, LANDMARKS)
    own_lq = pl.BlockSpec((LANDMARKS, PAIR), lambda i, own: (0, own[0]))
    own_lk = pl.BlockSpec((LANDMARKS, PAIR), lambda i, own: (0, own[0] + pairs))
    kept = shape_of((1 + 4 * ITERS,) + square, F32)
    saved, inverse = call(
        newton_kernel,
        (1,),
        [own_arr],
        [land, land],
        [own_lq, own_lk],
        [kept, shape_of((1,) + square, F32)],
        [whole(kept.shape), whole((1,) + square)],
        flops=4 << 30,
        name="newton",
    )

    groups = bit_groups(n)[::-1]
    for step, (shift, count) in enumerate(groups):
        got = [pieces[0]] + [exchange(pieces[m], m << shift, n) for m in range(1, count)]
        specs = [whole(got[0].shape)] * count
        if step == 0:
            got, inverse = lax.optimization_barrier((got, inverse))
        if step + 1 < len(groups):
            following = groups[step + 1][1]
            piece = shape_of((got[0].shape[0] // following, height, LANDMARKS), BF16)
            pieces = call(
                functools.partial(merge_kernel, cols, count),
                (1,),
                [],
                got,
                specs,
                [piece] * following,
                [whole(piece.shape)] * following,
                name="merge",
            )
    small = shape_of((cols, LANDMARKS), F32)
    reply, values, grads = call(
        functools.partial(mix_kernel, cols, count),
        (1,),
        [],
        got + [inverse],
        specs + [whole((1,) + square)],
        [piece, small, small],
        [whole(piece.shape), whole(small.shape), whole(small.shape)],
        name="mix",
    )
    replies = gather_lists(reply[0], n)

    more = shape_of((LANDMARKS, PAIR), F32)
    more_q, more_k = call(
        newton_grad_kernel,
        (1,),
        [own_arr],
        [saved, values, grads, land, land],
        [whole(kept.shape), whole(small.shape), whole(small.shape), own_lq, own_lk],
        [more, more],
        [whole(more.shape)] * 2,
        flops=8 << 30,
        name="newton_grad",
    )

    replies, more_q, more_k = lax.optimization_barrier((replies, more_q, more_k))
    block = max(columns // n, 16)
    split = n * block // columns
    flat = shape_of((columns, LANDMARKS), BF16)
    weight_piece = shape_of((n // size, block, width // split), BF16)
    attn, mixer, norm, center, *weight_pieces = call(
        functools.partial(attend_kernel, n, heads),
        (pairs,),
        [me_arr],
        [fb, tops, cotangent] + replies,
        [factor_pair, whole(tops.shape), whole(cotangent.shape)] + [whole(replies[0].shape)] * size,
        [shape_of((rows, columns), BF16), flat, flat, shape_of((heads, LANDMARKS), F32)]
        + [weight_piece] * size,
        [token_pair, whole(flat.shape), whole(flat.shape), whole((heads, LANDMARKS))]
        + [whole(weight_piece.shape)] * size,
        [
            pltpu.VMEM((n, cols, LANDMARKS), F32),
            pltpu.VMEM((n, cols, LANDMARKS), F32),
            pltpu.VMEM((n, 8, LANDMARKS), F32),
            pltpu.VMEM((columns // block, block, width), F32),
            pltpu.VMEM((columns, rows), BF16),
        ],
        flops=4 << 30,
        name="attend",
    )
    (shift, count), later = groups[0], groups[1:]
    weight_sum = scatter_step(weight_pieces, shift, count, n).astype(BF16)
    (pb, key_rows, value_rows), weight_sum = lax.optimization_barrier(
        ((pb, key_rows, value_rows), weight_sum)
    )
    following = later[0][1]
    weight_sum = weight_sum.reshape((-1, following) + weight_sum.shape[1:])
    weight_own = scatter_pieces([weight_sum[:, m] for m in range(following)], n, later)[0].astype(BF16)
    flat_pair = pl.BlockSpec((PAIR, LANDMARKS), lambda j, *_: (j, 0))
    land_pair = pl.BlockSpec((LANDMARKS, PAIR), lambda j, *_: (0, j))
    centers = whole((heads, LANDMARKS))
    tokens = shape_of((rows, columns), BF16)
    land_shape = shape_of((LANDMARKS, columns), BF16)
    land_k, grad_sf = call(
        query_land_kernel,
        (pairs,),
        [own_arr],
        [queries, grad_attn, fb, mixer, more_k],
        [token_pair, token_pair, factor_pair, flat_pair, whole(more.shape)],
        [land_shape, factors],
        [land_pair, factor_pair],
        flops=4 << 30,
        name="query_land",
    )
    (shift, count), later = groups[0], groups[1:]
    following = later[0][1]
    weight_sum = scatter_step(weight_pieces, shift, count, n).astype(BF16)
    (pb, key_rows, value_rows), weight_sum, land_k = lax.optimization_barrier(
        ((pb, key_rows, value_rows), weight_sum, land_k)
    )
    if sorted_here:
        land_piece, pieces_count = shape_of((n // size, land_dev, 2 * columns), BF16), size
    else:
        land_piece, pieces_count = shape_of((LANDMARKS // 16, 16, 2 * columns), BF16), 1
    grad_sb, *land_pieces = call(
        key_land_kernel,
        (pairs,),
        [own_arr],
        [key_rows, value_rows, pb, norm, center, more_q, land_k],
        [token_pair, token_pair, factor_pair, flat_pair, centers, whole(more.shape)]
        + [whole(land_shape.shape)],
        [factors] + [land_piece] * pieces_count,
        [factor_pair] + [whole(land_piece.shape)] * pieces_count,
        [pltpu.VMEM(land_shape.shape, BF16)],
        flops=4 << 30,
        name="key_land",
    )
    half = width // 2
    row_block = pl.BlockSpec((rows // 4, columns), lambda j, _: (j, 0))
    half_block = pl.BlockSpec((rows // 4, half), lambda j, _: (j, 0))

    if not sorted_here:
        land_pieces = split_by_partner(land_pieces[0].reshape(n, land_dev, 2 * columns), n, me)
    weight_sum = weight_sum.reshape((-1, following) + weight_sum.shape[1:])
    weight_own = scatter_pieces([weight_sum[:, m] for m in range(following)], n, later)[0].astype(BF16)
    land_pieces, weight_own = lax.optimization_barrier((land_pieces, weight_own))
    land_sum = scatter_step(land_pieces, shift, count, n).astype(BF16)
    weights = gather_first(weight_own, n)
    land_sum, grad_sf, attn = lax.optimization_barrier((land_sum, grad_sf, attn))
    query_f = call(
        query_kernel,
        (pairs,),
        [],
        [grad_sf, land],
        [factor_pair, lk_pair],
        tokens,
        token_pair,
        flops=2 << 30,
        name="query_grad",
    )
    there = call(
        part_kernel,
        (4,),
        [mine_arr],
        [attn, out_weight],
        [row_block, pl.BlockSpec((columns, half), lambda j, mine: (0, 1 - mine[0]))],
        shape_of((rows, half), BF16),
        half_block,
        flops=1 << 30,
        name="part",
    )
    land_sum, weights, query_f, there = lax.optimization_barrier((land_sum, weights, query_f, there))
    land_sum, weights, grad_sb = lax.optimization_barrier((land_sum, weights, grad_sb))
    key_b, value_grad = call(
        key_kernel,
        (pairs,),
        [],
        [grad_sb, pb, land, norm],
        [factor_pair, factor_pair, lq_pair, flat_pair],
        [tokens, tokens],
        [token_pair, token_pair],
        flops=4 << 30,
        name="key_grad",
    )

    arrived = lax.ppermute(there, "head", [(0, 1), (1, 0)])
    mask = size
    while land_sum.shape[0] > 1:
        given = exchange(land_sum[1::2], mask, n)
        land_sum = (land_sum[::2].astype(F32) + given.astype(F32)).astype(BF16)
        mask *= 2
    land_own = land_sum[0].astype(F32)
    land_own = land_own * (1.0 / seg_len)
    mixed = call(
        mixed_kernel,
        (4,),
        [mine_arr],
        [attn, out_weight, arrived],
        [row_block, pl.BlockSpec((columns, half), lambda j, mine: (0, mine[0])), half_block],
        shape_of((rows, half), BF16),
        half_block,
        flops=1 << 30,
        name="mixed",
    )
    weights = gather_rest(weights, n)
    weights, mixed = lax.optimization_barrier((weights, mixed))
    weight_grad = call(
        functools.partial(unpack_kernel, split),
        (1,),
        [me_arr],
        weights,
        [whole(weights[0].shape)] * size,
        pltpu.HBM((columns, width), F32),
        in_hbm,
        [pltpu.VMEM((n,) + weights[0].shape[1:], F32), pltpu.SemaphoreType.DMA((n,))],
        name="unpack",
    )

    def own_pair(first):
        return pl.BlockSpec((land_dev, PAIR), lambda j, *_: (0, j + first))

    query_grad, key_grad = call(
        finish_kernel,
        (pairs,),
        [],
        [query_f, key_b, land_own, land_own],
        [token_pair, token_pair, own_pair(0), own_pair(pairs)],
        [tokens, tokens],
        [token_pair, token_pair],
        name="finish",
    )
    return (mixed, query_grad, key_grad, value_grad, weight_grad)


def solution(mesh):
    return jax.shard_map(
        local,
        mesh=mesh,
        in_specs=(
            P("seq", "head"),
            P("seq", "head"),
            P("seq", "head"),
            P("head", None),
            P("seq", None),
        ),
        out_specs=(
            P("seq", "head"),
            P("seq", "head"),
            P("seq", "head"),
            P("seq", "head"),
            P("head", None),
        ),
        check_vma=False,
    )
```

```python
import functools

import jax
import jax.numpy as jnp
from jax import lax
from jax.experimental import pallas as pl
from jax.experimental.pallas import tpu as pltpu
from jax.sharding import PartitionSpec as P

DH = 64
PAIR = 2 * DH
LANDMARKS = 256
ITERS = 2
SCALE = 0.125
CHUNK = 256
EXTRA = 16
F32 = jnp.float32
BF16 = jnp.bfloat16
PARAMS = pltpu.CompilerParams(vmem_limit_bytes=24 * 1024 * 1024)


def dot(left, right, dims=((1,), (0,))):
    return lax.dot_general(left, right, (dims, ((), ())), preferred_element_type=F32)


NT = ((1,), (1,))
TN = ((0,), (0,))


def halves(value):
    high = value.astype(BF16)
    return high, (value - high.astype(F32)).astype(BF16)


def dot_exact(left, right, dims=((1,), (0,))):
    return dot(left[0], right[0], dims) + (
        dot(left[0], right[1], dims) + dot(left[1], right[0], dims)
    )


def turned(pair):
    return pair[0].T, pair[1].T


def keep_rows(block, which):
    rows = lax.broadcasted_iota(jnp.int32, block.shape, 0) // DH
    return jnp.where(rows == which, block, jnp.zeros_like(block))


def keep_lanes(block, which):
    lanes = lax.broadcasted_iota(jnp.int32, block.shape, 1) // DH
    return jnp.where(lanes == which, block, jnp.zeros_like(block))


def fold(block, op):
    parts = block.reshape(block.shape[0] // 8, 8, block.shape[1])
    return op(parts, axis=0)


def exchange(block, mask, n):
    return lax.ppermute(block, "seq", [(i, i ^ mask) for i in range(n)])


def bit_groups(n):
    bits = n.bit_length() - 1
    groups = []
    while bits > 0:
        take = 2 if bits % 2 == 0 else 1
        bits -= take
        groups.append((bits, 1 << take))
    return groups


def gather_first(block, n):
    shift, size = bit_groups(n)[0]
    held = block[None]
    return [held] + [exchange(held, m << shift, n) for m in range(1, size)]


def gather_rest(got, n):
    for shift, size in bit_groups(n)[1:]:
        held = jnp.stack(got, axis=1).reshape((-1,) + got[0].shape[1:])
        got = [held] + [exchange(held, m << shift, n) for m in range(1, size)]
    return got


def gather_lists(block, n):
    return gather_rest(gather_first(block, n), n)


def gather_ordered(block, n, me):
    got = gather_lists(block, n)
    held = jnp.stack(got, axis=1).reshape((n,) + block.shape)
    return held.at[jnp.arange(n) ^ me].get(mode="promise_in_bounds")


def split_by_partner(blocks, n, me):
    size = bit_groups(n)[-1][1]
    return [
        blocks.at[(jnp.arange(n // size) * size + m) ^ me].get(mode="promise_in_bounds")
        for m in range(size)
    ]


def scatter_step(pieces, shift, size, n):
    got = [pieces[0]] + [exchange(pieces[m], m << shift, n) for m in range(1, size)]
    return sum(part.astype(F32) for part in got)


def scatter_pieces(pieces, n, groups):
    for step, (shift, size) in enumerate(groups):
        held = scatter_step(pieces, shift, size, n)
        if step + 1 < len(groups):
            following = groups[step + 1][1]
            held = held.astype(BF16).reshape((-1, following) + held.shape[1:])
            pieces = [held[:, m] for m in range(following)]
    return held


def means_kernel(seg_len, q_ref, k_ref, out_ref, in_ref, sum_ref, sems):
    rows, columns = q_ref.shape
    steps = sems.shape[1]
    height = rows // steps
    copies = {}
    for c in range(steps):
        part = pl.ds(c * height, height)
        for side, ref in enumerate((q_ref, k_ref)):
            copies[side, c] = pltpu.make_async_copy(ref.at[part], in_ref.at[side, part], sems.at[side, c])
            copies[side, c].start()
    for c in range(steps):
        for side in range(2):
            copies[side, c].wait()
            span = slice(side * columns, (side + 1) * columns)
            for s in range(c * height // seg_len, (c + 1) * height // seg_len):
                total = fold(in_ref[side, s * seg_len : (s + 1) * seg_len, :].astype(F32), jnp.sum)
                sum_ref[s : s + 1, span] = jnp.sum(total, axis=0, keepdims=True)
    out_ref[...] = (sum_ref[...] * (1.0 / seg_len)).astype(BF16)


def forward_kernel(n, heads, count, me_ref, q_ref, k_ref, v_ref, g_ref, *refs):
    size = bit_groups(n)[-1][1]
    in_refs = refs[:count]
    fb_ref, pb_ref, top_ref, land_ref = refs[count : count + 4]
    out_refs = refs[count + 4 : count + 4 + size]
    score_ref, message_ref = refs[count + 4 + size :]
    pair = pl.program_id(0)
    columns = land_ref.shape[1] // 2

    @pl.when(pair == 0)
    def _():
        for m in range(count):
            held, height, _ = in_refs[m].shape
            for t in range(held):
                at = pl.multiple_of(((t * count + m) ^ me_ref[1]) * height, height)
                land_ref[pl.ds(at, height), :] = in_refs[m][t]

    here = pl.multiple_of(pair * PAIR, PAIR)
    lq_pair = land_ref[:, pl.ds(here, PAIR)]
    lk_pair = land_ref[:, pl.ds(columns + here, PAIR)]
    rows = q_ref.shape[0]
    parts = n // heads
    cols = DH // parts
    gt = g_ref[...].T
    vt = v_ref[...].T
    for h in range(2):
        lk = keep_lanes(lk_pair * SCALE, h).astype(BF16)
        lq = keep_lanes(lq_pair * SCALE, h).astype(BF16)
        span = slice(h * LANDMARKS, (h + 1) * LANDMARKS)
        top = None
        for c in range(0, rows, CHUNK):
            part = slice(c, c + CHUNK)
            sb = dot(k_ref[part, :], lq, NT)
            score_ref[part, :] = sb
            high = fold(sb, jnp.max)
            top = high if top is None else jnp.maximum(top, high)
            sf = dot(q_ref[part, :], lk, NT)
            e = jnp.exp(sf - jnp.max(sf, axis=1, keepdims=True))
            fb_ref[part, span] = (e * (1.0 / jnp.sum(e, axis=1, keepdims=True))).astype(BF16)
        top = jnp.max(top, axis=0, keepdims=True).astype(BF16).astype(F32)
        total = None
        for c in range(0, rows, CHUNK):
            part = slice(c, c + CHUNK)
            p = jnp.exp(score_ref[part, :] - top)
            add = fold(p, jnp.sum)
            total = add if total is None else total + add
            pb_ref[part, span] = p.astype(BF16)
        total = jnp.sum(total, axis=0, keepdims=True)
        top_ref[0, h : h + 1, :] = top
        grads = dot(gt[h * DH : (h + 1) * DH], fb_ref[:, span])
        vals = dot(vt[h * DH : (h + 1) * DH], pb_ref[:, span])
        high, low = halves(total)
        extra = three_rows(top, high.astype(F32), low.astype(F32))
        for p in range(parts):
            cut = slice(p * cols, (p + 1) * cols)
            message_ref[(2 * pair + h) * parts + p] = jnp.concatenate(
                [vals[cut], grads[cut], extra], axis=0
            ).astype(BF16)

    @pl.when(pair == pl.num_programs(0) - 1)
    def _():
        for m in range(size):
            for t in range(n // size):
                out_refs[m][t] = message_ref[(t * size + m) ^ me_ref[0]]


def merge(items, cols):
    tops = [item[2 * cols : 2 * cols + 1] for item in items]
    peak = functools.reduce(jnp.maximum, tops)
    vals = grads = total = 0.0
    for item, top in zip(items, tops):
        factor = jnp.exp(top - peak)
        vals = vals + item[:cols] * factor
        grads = grads + item[cols : 2 * cols]
        total = total + (
            item[2 * cols + 1 : 2 * cols + 2] + item[2 * cols + 2 : 2 * cols + 3]
        ) * factor
    return vals, grads, peak, total


def three_rows(first, second, third):
    row = lax.broadcasted_iota(jnp.int32, (EXTRA, LANDMARKS), 0)
    return jnp.where(row == 0, first, jnp.where(row == 1, second, jnp.where(row == 2, third, 0.0)))


def merge_kernel(cols, count, *refs):
    in_refs, out_refs = refs[:count], refs[count:]
    following = len(out_refs)
    for t in range(in_refs[0].shape[0]):
        vals, grads, peak, total = merge([ref[t].astype(F32) for ref in in_refs], cols)
        high, low = halves(total)
        extra = three_rows(peak, high.astype(F32), low.astype(F32))
        out_refs[t % following][t // following] = jnp.concatenate(
            [vals, grads, extra], axis=0
        ).astype(BF16)


def mix_kernel(cols, count, *refs):
    in_refs, z_ref = refs[:count], refs[count]
    reply_ref, values_ref, grads_ref = refs[count + 1 :]
    vals, grads, peak, total = merge([ref[0].astype(F32) for ref in in_refs], cols)
    inverse = halves(z_ref[0])
    values = vals / total
    mixer = dot_exact(halves(values), inverse, NT)
    norm = dot_exact(halves(grads), inverse) / total
    high, low = halves(jnp.sum(norm * values, axis=0, keepdims=True))
    extra = three_rows(peak, high.astype(F32), low.astype(F32))
    reply_ref[0] = jnp.concatenate([mixer, norm, extra], axis=0).astype(BF16)
    values_ref[...] = values
    grads_ref[...] = grads


def soft_rows(scores):
    e = jnp.exp(scores - jnp.max(scores, axis=1, keepdims=True))
    return e / jnp.sum(e, axis=1, keepdims=True)


def eye():
    shape = (LANDMARKS, LANDMARKS)
    same = lax.broadcasted_iota(jnp.int32, shape, 0) == lax.broadcasted_iota(jnp.int32, shape, 1)
    return same.astype(F32)


def column_top(amat):
    return jnp.max(jnp.sum(amat, axis=0, keepdims=True), axis=1, keepdims=True)


def newton_kernel(own_ref, lq_ref, lk_ref, saved_ref, z_ref):
    which = own_ref[1]
    amat = soft_rows(dot(keep_lanes(lq_ref[...] * SCALE, which).astype(BF16), lk_ref[...], NT))
    saved_ref[0] = amat
    current = amat.T / column_top(amat)
    ident = eye()
    amat = halves(amat)
    for i in range(ITERS):
        saved_ref[1 + 4 * i] = current
        z = halves(current)
        x_full = dot_exact(amat, z)
        saved_ref[2 + 4 * i] = x_full
        x = halves(x_full)
        inner = 15.0 * ident - dot_exact(x, halves(7.0 * ident - x_full))
        saved_ref[3 + 4 * i] = inner
        inner = 13.0 * ident - dot_exact(x, halves(inner))
        saved_ref[4 + 4 * i] = inner
        current = 0.25 * dot_exact(z, halves(inner))
    z_ref[0] = current


def newton_grad_kernel(own_ref, saved_ref, values_ref, grads_ref, lq_ref, lk_ref, q_ref, k_ref):
    which = own_ref[1]
    ident = eye()
    amat = saved_ref[0]
    amat_t = turned(halves(amat))
    grad_z = dot_exact(halves(grads_ref[...]), halves(values_ref[...]), TN)
    grad_a = jnp.zeros_like(amat)
    for i in reversed(range(ITERS)):
        z = halves(saved_ref[1 + 4 * i])
        x_full = saved_ref[2 + 4 * i]
        x_t = turned(halves(x_full))
        first = halves(7.0 * ident - x_full)
        second = halves(saved_ref[3 + 4 * i])
        third = halves(saved_ref[4 + 4 * i])
        dz = halves(0.25 * grad_z)
        d_third = halves(dot_exact(turned(z), dz))
        d_second = halves(-dot_exact(x_t, d_third))
        d_x = -dot_exact(d_third, second, NT) - dot_exact(d_second, first, NT)
        d_x = halves(d_x + dot_exact(x_t, d_second))
        grad_a = grad_a + dot_exact(d_x, z, NT)
        grad_z = dot_exact(dz, third, NT) + dot_exact(amat_t, d_x)
    grad_a = grad_a + grad_z.T / column_top(amat)
    grad_s = amat * (grad_a - jnp.sum(amat * grad_a, axis=1, keepdims=True)) * SCALE
    high, low = halves(grad_s)
    lq = keep_lanes(lq_ref[...], which)
    lk = keep_lanes(lk_ref[...], which)
    q_ref[...] = dot(high, lk) + dot(low, lk)
    k_ref[...] = dot(high.T, lq) + dot(low.T, lq)


def attend_kernel(n, heads, me_ref, fb_ref, top_ref, cot_ref, *refs):
    size = bit_groups(n)[-1][1]
    parts = n // heads
    cols = DH // parts
    reply_refs = refs[:size]
    attn_ref, mixer_ref, norm_ref, center_ref = refs[size : size + 4]
    out_refs = refs[size + 4 : 2 * size + 4]
    w_ref, d_ref, e_ref, sum_ref, all_ref = refs[2 * size + 4 :]
    pair = pl.program_id(0)

    @pl.when(pair == 0)
    def _():
        for m in range(size):
            for t in range(n // size):
                reply = reply_refs[m][t].astype(F32)
                at = (t * size + m) ^ me_ref[0]
                w_ref[at] = reply[:cols]
                d_ref[at] = reply[cols : 2 * cols]
                e_ref[at] = reply[2 * cols : 2 * cols + 8]
        for h in range(heads):
            cut = slice(h * parts, (h + 1) * parts)
            span = slice(h * DH, (h + 1) * DH)
            mixer_ref[span, :] = w_ref[cut].reshape(DH, LANDMARKS).astype(BF16)
            extra = e_ref[cut]
            top = top_ref[h // 2, h % 2 : h % 2 + 1, :]
            factor = jnp.exp(top - extra[0, 0:1, :])
            norm_ref[span, :] = (d_ref[cut].reshape(DH, LANDMARKS) * factor).astype(BF16)
            sums = jnp.sum(extra, axis=0)
            center_ref[h : h + 1, :] = (sums[1:2] + sums[2:3]) * factor

    mixer = mixer_ref[pl.ds(pl.multiple_of(pair * PAIR, PAIR), PAIR), :]
    attn = dot(fb_ref[:, :LANDMARKS], keep_rows(mixer, 0), NT) + dot(
        fb_ref[:, LANDMARKS:], keep_rows(mixer, 1), NT
    )
    attn = attn.astype(BF16)
    attn_ref[...] = attn
    all_ref[pl.ds(pl.multiple_of(pair * PAIR, PAIR), PAIR), :] = attn.T

    @pl.when(pair == pl.num_programs(0) - 1)
    def _():
        block, split = sum_ref.shape[1], n // sum_ref.shape[0]
        width = cot_ref.shape[1]
        sum_ref[...] = dot(all_ref[...], cot_ref[...]).reshape(sum_ref.shape)
        for m in range(size):
            for t in range(n // size):
                at = (t * size + m) ^ me_ref[0]
                if split == 1:
                    out_refs[m][t] = sum_ref[at].astype(BF16)
                else:
                    side = pl.multiple_of((at % split) * (width // split), width // split)
                    out_refs[m][t] = sum_ref[at // split, :, pl.ds(side, width // split)].astype(BF16)


def soft_grad(fb_ref, g_ref, mixer_ref, ds_ref):
    for h in range(2):
        span = slice(h * LANDMARKS, (h + 1) * LANDMARKS)
        mixer = keep_rows(mixer_ref[...], h)
        for c in range(0, fb_ref.shape[0], CHUNK):
            part = slice(c, c + CHUNK)
            f = fb_ref[part, span].astype(F32)
            df = dot(g_ref[part, :], mixer)
            ds_ref[part, span] = (f * (df - jnp.sum(f * df, axis=1, keepdims=True))).astype(BF16)


def weight_soft_grad(pb_ref, v_ref, norm_ref, center_ref, ds_ref):
    for h in range(2):
        span = slice(h * LANDMARKS, (h + 1) * LANDMARKS)
        norm = keep_rows(norm_ref[...], h)
        center = center_ref[pl.ds(2 * pl.program_id(0) + h, 1), :]
        for c in range(0, pb_ref.shape[0], CHUNK):
            part = slice(c, c + CHUNK)
            dp = dot(v_ref[part, :], norm)
            ds_ref[part, span] = (pb_ref[part, span].astype(F32) * (dp - center)).astype(BF16)


def land_sums(ds_ref, x_ref, own_ref, more_ref):
    xt = x_ref[...].T
    sums = jnp.concatenate(
        [dot(xt[:DH], ds_ref[:, :LANDMARKS]), dot(xt[DH:], ds_ref[:, LANDMARKS:])], axis=0
    )
    here = (own_ref[0] == pl.program_id(0)).astype(F32)
    return (sums.T * SCALE + more_ref[...] * here).astype(BF16)


def token_part(ds_ref, land_ref, out_ref):
    land = land_ref[...] * SCALE
    total = dot(ds_ref[:, :LANDMARKS], keep_lanes(land, 0).astype(BF16)) + dot(
        ds_ref[:, LANDMARKS:], keep_lanes(land, 1).astype(BF16)
    )
    out_ref[...] = total.astype(BF16)


def query_land_kernel(own_ref, q_ref, g_ref, fb_ref, mixer_ref, more_ref, land_ref, ds_ref):
    soft_grad(fb_ref, g_ref, mixer_ref, ds_ref)
    land_ref[...] = land_sums(ds_ref, q_ref, own_ref, more_ref)


def key_land_kernel(own_ref, k_ref, v_ref, pb_ref, norm_ref, center_ref, more_ref, other_ref, *refs):
    ds_ref, out_refs, land_ref = refs[0], refs[1:-1], refs[-1]
    size = len(out_refs)
    columns = other_ref.shape[1]
    pair = pl.program_id(0)
    weight_soft_grad(pb_ref, v_ref, norm_ref, center_ref, ds_ref)
    land_ref[:, pl.ds(pl.multiple_of(pair * PAIR, PAIR), PAIR)] = land_sums(
        ds_ref, k_ref, own_ref, more_ref
    )

    @pl.when(pair == pl.num_programs(0) - 1)
    def _():
        for m in range(size):
            held, height, _ = out_refs[m].shape
            for t in range(held):
                at = pl.multiple_of(((t * size + m) ^ own_ref[2]) * height, height)
                out_refs[m][t, :, :columns] = land_ref[pl.ds(at, height), :]
                out_refs[m][t, :, columns:] = other_ref[pl.ds(at, height), :]


def query_kernel(ds_ref, lk_ref, out_ref):
    token_part(ds_ref, lk_ref, out_ref)


def key_kernel(ds_ref, pb_ref, lq_ref, norm_ref, out_ref, value_ref):
    token_part(ds_ref, lq_ref, out_ref)
    value_ref[...] = (
        dot(pb_ref[:, :LANDMARKS], keep_rows(norm_ref[...], 0), NT)
        + dot(pb_ref[:, LANDMARKS:], keep_rows(norm_ref[...], 1), NT)
    ).astype(BF16)


def finish_kernel(query_ref, key_ref, query_own_ref, key_own_ref, query_out_ref, key_out_ref):
    for in_ref, own_ref, out_ref in (
        (query_ref, query_own_ref, query_out_ref),
        (key_ref, key_own_ref, key_out_ref),
    ):
        own = own_ref[...]
        segments = (own.shape[0], in_ref.shape[0] // own.shape[0], PAIR)
        total = in_ref[...].astype(F32).reshape(segments) + own[:, None, :]
        out_ref[...] = total.reshape(in_ref.shape).astype(BF16)


def part_kernel(_, attn_ref, weight_ref, out_ref):
    out_ref[...] = dot(attn_ref[...], weight_ref[...]).astype(BF16)


def mixed_kernel(_, attn_ref, weight_ref, other_ref, out_ref):
    out_ref[...] = (dot(attn_ref[...], weight_ref[...]) + other_ref[...].astype(F32)).astype(BF16)


def unpack_kernel(split, me_ref, *refs):
    in_refs, (out_ref, wide_ref, sems) = refs[:-3], refs[-3:]
    size = len(in_refs)
    held, block, width = in_refs[0].shape
    copies = []
    for t in range(held):
        for m in range(size):
            slot = t * size + m
            at = slot ^ me_ref[0]
            row = pl.ds(pl.multiple_of((at // split) * block, block), block)
            if split == 1:
                target = out_ref.at[row]
            else:
                target = out_ref.at[row, pl.ds(pl.multiple_of((at % split) * width, width), width)]
            wide_ref[slot] = in_refs[m][t].astype(F32)
            copies.append(pltpu.make_async_copy(wide_ref.at[slot], target, sems.at[slot]))
            copies[-1].start()
    for copy in copies:
        copy.wait()


def held_in_hbm(x):
    return pltpu.with_memory_space_constraint(x, pltpu.HBM)


def whole(shape):
    return pl.BlockSpec(shape, lambda *_: (0,) * len(shape))


def shape_of(shape, dtype):
    return jax.ShapeDtypeStruct(shape, dtype)


def call(kernel, grid, scalars, ins, in_specs, outs, out_specs, scratch=(), flops=0, name=None, aliases={}):
    return pl.pallas_call(
        kernel,
        grid_spec=pltpu.PrefetchScalarGridSpec(
            num_scalar_prefetch=len(scalars),
            grid=grid,
            in_specs=in_specs,
            out_specs=out_specs,
            scratch_shapes=list(scratch),
        ),
        out_shape=outs,
        compiler_params=PARAMS,
        input_output_aliases=aliases,
        cost_estimate=pl.CostEstimate(flops=flops, bytes_accessed=4 << 20, transcendentals=0),
        name=name,
    )(*scalars, *ins)


def local(queries, key_rows, value_rows, out_weight, cotangent):
    rows, columns = queries.shape
    width = out_weight.shape[1]
    heads = columns // DH
    pairs = columns // PAIR
    n = lax.axis_size("seq")
    me = lax.axis_index("seq")
    mine = lax.axis_index("head")
    land_dev = LANDMARKS // n
    seg_len = rows // land_dev
    parts = n // heads
    cols = DH // parts
    size = bit_groups(n)[-1][1]
    height = 2 * cols + EXTRA
    own_head = me // parts

    sorted_here = land_dev % 16 == 0
    me_arr = jnp.stack([me, me if sorted_here else me * 0]).astype(jnp.int32)
    mine_arr = mine.reshape(1).astype(jnp.int32)
    own_arr = jnp.stack([own_head // 2, own_head % 2, me * 0 if land_dev % 16 else me]).astype(jnp.int32)
    steps = 4
    in_hbm = pl.BlockSpec(memory_space=pltpu.HBM)
    own = call(
        functools.partial(means_kernel, seg_len),
        (1,),
        [],
        [held_in_hbm(queries), held_in_hbm(key_rows)],
        [in_hbm, in_hbm],
        shape_of((land_dev, 2 * columns), BF16),
        whole((land_dev, 2 * columns)),
        [
            pltpu.VMEM((2, rows, columns), BF16),
            pltpu.VMEM((land_dev, 2 * columns), F32),
            pltpu.SemaphoreType.DMA((2, steps)),
        ],
        name="means",
    )
    own, me_arr, mine_arr, own_arr = lax.optimization_barrier((own, me_arr, mine_arr, own_arr))
    grad_attn = dot(cotangent, out_weight, NT).astype(BF16)
    if sorted_here:
        lands = gather_lists(own, n)
    else:
        lands = [gather_ordered(own, n, me).reshape(LANDMARKS // 16, 16, 2 * columns)]

    token_pair = pl.BlockSpec((rows, PAIR), lambda j, *_: (0, j))
    factor_pair = pl.BlockSpec((rows, 2 * LANDMARKS), lambda j, *_: (0, j))
    lq_pair = pl.BlockSpec((LANDMARKS, PAIR), lambda j, *_: (0, j))
    lk_pair = pl.BlockSpec((LANDMARKS, PAIR), lambda j, *_: (0, j + pairs))
    factors = shape_of((rows, heads * LANDMARKS), BF16)
    piece = shape_of((n // size, height, LANDMARKS), BF16)

    fb, pb, tops, land, *pieces = call(
        functools.partial(forward_kernel, n, heads, len(lands)),
        (pairs,),
        [me_arr],
        [queries, key_rows, value_rows, grad_attn] + lands,
        [token_pair] * 4 + [whole(lands[0].shape)] * len(lands),
        [
            factors,
            factors,
            shape_of((pairs, 8, LANDMARKS), F32),
            shape_of((LANDMARKS, 2 * columns), BF16),
        ]
        + [piece] * size,
        [
            factor_pair,
            factor_pair,
            pl.BlockSpec((1, 8, LANDMARKS), lambda j, *_: (j, 0, 0)),
            whole((LANDMARKS, 2 * columns)),
        ]
        + [whole(piece.shape)] * size,
        [
            pltpu.VMEM((rows, LANDMARKS), F32),
            pltpu.VMEM((n, height, LANDMARKS), BF16),
        ],
        flops=8 << 30,
        name="forward",
    )

    square = (LANDMARKS, LANDMARKS)
    own_lq = pl.BlockSpec((LANDMARKS, PAIR), lambda i, own: (0, own[0]))
    own_lk = pl.BlockSpec((LANDMARKS, PAIR), lambda i, own: (0, own[0] + pairs))
    kept = shape_of((1 + 4 * ITERS,) + square, F32)
    saved, inverse = call(
        newton_kernel,
        (1,),
        [own_arr],
        [land, land],
        [own_lq, own_lk],
        [kept, shape_of((1,) + square, F32)],
        [whole(kept.shape), whole((1,) + square)],
        flops=4 << 30,
        name="newton",
    )

    groups = bit_groups(n)[::-1]
    for step, (shift, count) in enumerate(groups):
        got = [pieces[0]] + [exchange(pieces[m], m << shift, n) for m in range(1, count)]
        specs = [whole(got[0].shape)] * count
        if step == 0:
            got, inverse = lax.optimization_barrier((got, inverse))
        if step + 1 < len(groups):
            following = groups[step + 1][1]
            piece = shape_of((got[0].shape[0] // following, height, LANDMARKS), BF16)
            pieces = call(
                functools.partial(merge_kernel, cols, count),
                (1,),
                [],
                got,
                specs,
                [piece] * following,
                [whole(piece.shape)] * following,
                name="merge",
            )
    small = shape_of((cols, LANDMARKS), F32)
    reply, values, grads = call(
        functools.partial(mix_kernel, cols, count),
        (1,),
        [],
        got + [inverse],
        specs + [whole((1,) + square)],
        [piece, small, small],
        [whole(piece.shape), whole(small.shape), whole(small.shape)],
        name="mix",
    )
    replies = gather_lists(reply[0], n)

    more = shape_of((LANDMARKS, PAIR), F32)
    more_q, more_k = call(
        newton_grad_kernel,
        (1,),
        [own_arr],
        [saved, values, grads, land, land],
        [whole(kept.shape), whole(small.shape), whole(small.shape), own_lq, own_lk],
        [more, more],
        [whole(more.shape)] * 2,
        flops=8 << 30,
        name="newton_grad",
    )

    replies, more_q, more_k = lax.optimization_barrier((replies, more_q, more_k))
    block = max(columns // n, 16)
    split = n * block // columns
    flat = shape_of((columns, LANDMARKS), BF16)
    weight_piece = shape_of((n // size, block, width // split), BF16)
    attn, mixer, norm, center, *weight_pieces = call(
        functools.partial(attend_kernel, n, heads),
        (pairs,),
        [me_arr],
        [fb, tops, cotangent] + replies,
        [factor_pair, whole(tops.shape), whole(cotangent.shape)] + [whole(replies[0].shape)] * size,
        [shape_of((rows, columns), BF16), flat, flat, shape_of((heads, LANDMARKS), F32)]
        + [weight_piece] * size,
        [token_pair, whole(flat.shape), whole(flat.shape), whole((heads, LANDMARKS))]
        + [whole(weight_piece.shape)] * size,
        [
            pltpu.VMEM((n, cols, LANDMARKS), F32),
            pltpu.VMEM((n, cols, LANDMARKS), F32),
            pltpu.VMEM((n, 8, LANDMARKS), F32),
            pltpu.VMEM((columns // block, block, width), F32),
            pltpu.VMEM((columns, rows), BF16),
        ],
        flops=4 << 30,
        name="attend",
    )
    (shift, count), later = groups[0], groups[1:]
    weight_sum = scatter_step(weight_pieces, shift, count, n).astype(BF16)
    (pb, key_rows, value_rows), weight_sum = lax.optimization_barrier(
        ((pb, key_rows, value_rows), weight_sum)
    )
    following = later[0][1]
    weight_sum = weight_sum.reshape((-1, following) + weight_sum.shape[1:])
    weight_own = scatter_pieces([weight_sum[:, m] for m in range(following)], n, later)[0].astype(BF16)
    flat_pair = pl.BlockSpec((PAIR, LANDMARKS), lambda j, *_: (j, 0))
    land_pair = pl.BlockSpec((LANDMARKS, PAIR), lambda j, *_: (0, j))
    centers = whole((heads, LANDMARKS))
    tokens = shape_of((rows, columns), BF16)
    land_shape = shape_of((LANDMARKS, columns), BF16)
    land_k, grad_sf = call(
        query_land_kernel,
        (pairs,),
        [own_arr],
        [queries, grad_attn, fb, mixer, more_k],
        [token_pair, token_pair, factor_pair, flat_pair, whole(more.shape)],
        [land_shape, factors],
        [land_pair, factor_pair],
        flops=4 << 30,
        name="query_land",
    )
    (shift, count), later = groups[0], groups[1:]
    following = later[0][1]
    weight_sum = scatter_step(weight_pieces, shift, count, n).astype(BF16)
    (pb, key_rows, value_rows), weight_sum, land_k = lax.optimization_barrier(
        ((pb, key_rows, value_rows), weight_sum, land_k)
    )
    if sorted_here:
        land_piece, pieces_count = shape_of((n // size, land_dev, 2 * columns), BF16), size
    else:
        land_piece, pieces_count = shape_of((LANDMARKS // 16, 16, 2 * columns), BF16), 1
    grad_sb, *land_pieces = call(
        key_land_kernel,
        (pairs,),
        [own_arr],
        [key_rows, value_rows, pb, norm, center, more_q, land_k],
        [token_pair, token_pair, factor_pair, flat_pair, centers, whole(more.shape)]
        + [whole(land_shape.shape)],
        [factors] + [land_piece] * pieces_count,
        [factor_pair] + [whole(land_piece.shape)] * pieces_count,
        [pltpu.VMEM(land_shape.shape, BF16)],
        flops=4 << 30,
        name="key_land",
    )
    half = width // 2
    row_block = pl.BlockSpec((rows // 2, columns), lambda j, _: (j, 0))
    half_block = pl.BlockSpec((rows // 2, half), lambda j, _: (j, 0))

    if not sorted_here:
        land_pieces = split_by_partner(land_pieces[0].reshape(n, land_dev, 2 * columns), n, me)
    weight_sum = weight_sum.reshape((-1, following) + weight_sum.shape[1:])
    weight_own = scatter_pieces([weight_sum[:, m] for m in range(following)], n, later)[0].astype(BF16)
    land_pieces, weight_own = lax.optimization_barrier((land_pieces, weight_own))
    land_sum = scatter_step(land_pieces, shift, count, n).astype(BF16)
    weights = gather_first(weight_own, n)
    land_sum, grad_sf, attn = lax.optimization_barrier((land_sum, grad_sf, attn))
    query_f = call(
        query_kernel,
        (pairs,),
        [],
        [grad_sf, land],
        [factor_pair, lk_pair],
        tokens,
        token_pair,
        flops=2 << 30,
        name="query_grad",
    )
    there = call(
        part_kernel,
        (2,),
        [mine_arr],
        [attn, out_weight],
        [row_block, pl.BlockSpec((columns, half), lambda j, mine: (0, 1 - mine[0]))],
        shape_of((rows, half), BF16),
        half_block,
        flops=1 << 30,
        name="part",
    )
    land_sum, weights, query_f, there = lax.optimization_barrier((land_sum, weights, query_f, there))
    land_sum, weights, grad_sb = lax.optimization_barrier((land_sum, weights, grad_sb))
    key_b, value_grad = call(
        key_kernel,
        (pairs,),
        [],
        [grad_sb, pb, land, norm],
        [factor_pair, factor_pair, lq_pair, flat_pair],
        [tokens, tokens],
        [token_pair, token_pair],
        flops=4 << 30,
        name="key_grad",
    )

    arrived = lax.ppermute(there, "head", [(0, 1), (1, 0)])
    mask = size
    while land_sum.shape[0] > 1:
        given = exchange(land_sum[1::2], mask, n)
        land_sum = (land_sum[::2].astype(F32) + given.astype(F32)).astype(BF16)
        mask *= 2
    land_own = land_sum[0].astype(F32)
    land_own = land_own * (1.0 / seg_len)
    mixed = call(
        mixed_kernel,
        (2,),
        [mine_arr],
        [attn, out_weight, arrived],
        [row_block, pl.BlockSpec((columns, half), lambda j, mine: (0, mine[0])), half_block],
        shape_of((rows, half), BF16),
        half_block,
        flops=1 << 30,
        name="mixed",
    )
    weights = gather_rest(weights, n)
    weights, mixed = lax.optimization_barrier((weights, mixed))
    weight_grad = call(
        functools.partial(unpack_kernel, split),
        (1,),
        [me_arr],
        weights,
        [whole(weights[0].shape)] * size,
        pltpu.HBM((columns, width), F32),
        in_hbm,
        [pltpu.VMEM((n,) + weights[0].shape[1:], F32), pltpu.SemaphoreType.DMA((n,))],
        name="unpack",
    )

    def own_pair(first):
        return pl.BlockSpec((land_dev, PAIR), lambda j, *_: (0, j + first))

    query_grad, key_grad = call(
        finish_kernel,
        (pairs,),
        [],
        [query_f, key_b, land_own, land_own],
        [token_pair, token_pair, own_pair(0), own_pair(pairs)],
        [tokens, tokens],
        [token_pair, token_pair],
        name="finish",
    )
    return (mixed, query_grad, key_grad, value_grad, weight_grad)


def solution(mesh):
    return jax.shard_map(
        local,
        mesh=mesh,
        in_specs=(
            P("seq", "head"),
            P("seq", "head"),
            P("seq", "head"),
            P("head", None),
            P("seq", None),
        ),
        out_specs=(
            P("seq", "head"),
            P("seq", "head"),
            P("seq", "head"),
            P("seq", "head"),
            P("head", None),
        ),
        check_vma=False,
    )
```
